32 devices in a mesh: dp: 4 (over x, core), expert: 8 (over z, y).
Axes of the slice: x: 2, y: 2, z: 4, core: 2. Of those that a mesh axis runs over, the one named last changes fastest.
Arguments:
- tokens: bfloat16 [32768, 768], P(('dp', 'expert')), may hold values from -6 to 6
- segments: int32 [32, 1024], P(('dp', 'expert')), may hold values from 0 to 7, never falling along the last dimension, each value on 1 to 512 neighbouring positions
- routes: int32 [32768, 1], P(('dp', 'expert')), may hold values from 0 to 7
- cotangent: bfloat16 [32768, 768], P(('dp', 'expert')), may hold values from -6 to 6
- attn_gain: float32 [768], replicated, may hold values from 0.5 to 1.5
- ffn_gain: float32 [768], replicated, may hold values from 0.5 to 1.5
- query_weight: bfloat16 [768, 768], replicated, may hold values from -0.21875 to 0.21875
- key_weight: bfloat16 [768, 768], replicated, may hold values from -0.21875 to 0.21875
- value_weight: bfloat16 [768, 768], replicated, may hold values from -0.21875 to 0.21875
- output_weight: bfloat16 [768, 768], replicated, may hold values from -0.875 to 0.875
- position_bias_grid: float32 [32, 12], replicated, may hold values from -6 to 6
- router_weight: float32 [768, 8], replicated, may hold values from -0.15625 to 0.15625
- expert_in: bfloat16 [8, 768, 3072], P('expert'), may hold values from -0.21875 to 0.21875
- expert_out: bfloat16 [8, 3072, 768], P('expert'), may hold values from -0.875 to 0.875
Outputs:
- mixed: bfloat16 [32768, 768], P(('dp', 'expert'))
- grad_tokens: bfloat16 [32768, 768], P(('dp', 'expert'))
- grad_attn_gain: float32 [768], replicated
- grad_ffn_gain: float32 [768], replicated
- grad_query: float32 [768, 768], replicated
- grad_key: float32 [768, 768], replicated
- grad_value: float32 [768, 768], replicated
- grad_output: float32 [768, 768], replicated
- grad_bias: float32 [32, 12], replicated
- grad_router: float32 [768, 8], replicated
- grad_expert_in: float32 [8, 768, 3072], P('expert', None, 'dp')
- grad_expert_out: float32 [8, 3072, 768], P('expert', 'dp')
The draws below stay inside these ranges and needn't reach their ends.
All inputs are finite; a program needn't handle non-finite values.
Results may differ from the reference program's by a relative error of at most 0.017.
Values may be sent and summed in bfloat16 or wider, within the bound.
A program may use at most 320 MiB of HBM per device.

```python
import math
import jax
import jax.numpy as jnp
import numpy as np
from jax import lax

D = 768
HEADS = 12
HEAD_DIM = 64
FF = 3072
BUCKETS = 32
SEQ = 1024
DOCS = 8
EXPERTS = 8
DEVICES_ALL = 32
TOK_DEV = 1024
NSEQ = 32
TOKENS = 32768
CAP = 160


def level_of(stream_key, extent, cuts, low, largest):
    def one(position, parts):
        steps = jax.random.uniform(jax.random.fold_in(jax.random.fold_in(stream_key, 6), position), (parts,), jnp.float32, low / len(cuts), largest / len(cuts))
        return jnp.repeat(jnp.exp(steps), extent[position] // parts).reshape((-1,) + (1,) * (len(extent) - position - 1))

    gain = one(*cuts[0])
    for cut in cuts[1:]:
        gain = gain * one(*cut)
    return gain


def choose_distinct(rng, rows, amount, top, lift):
    sequence = jax.random.permutation(jax.random.fold_in(rng, 1), amount)
    favour = sequence
    for power in range(3):
        favour = favour * favour // amount
    favour = favour * lift // amount
    chance = jax.random.randint(jax.random.fold_in(rng, 2), (rows, amount), 0, 4096) + favour
    sure = jax.random.permutation(jax.random.fold_in(rng, 3), rows)[jnp.arange(amount) % rows]
    chance = jnp.where(jnp.arange(rows)[:, None] == sure[None, :], 1 << 14, chance)
    score = chance * amount + jnp.arange(amount)
    return lax.top_k(score.astype(jnp.int32), top)[1].astype(jnp.int32)


def length_profile(amount, total, bound, skew):
    weights = [(1 << 20) // math.isqrt(standing ** skew) + 1 for standing in range(2, amount + 1)]
    spare, given = total - bound - (amount - 1), [1] * (amount - 1)
    while spare > 0:
        candidates = [i for i in range(amount - 1) if given[i] < bound]
        whole, left = sum([weights[i] for i in candidates]), spare
        for i in candidates:
            more = min(bound - given[i], max(1, left * weights[i] // whole), spare)
            given[i] = given[i] + more
            spare = spare - more
    return np.array([bound] + given)


def uneven_parts(stream_key, amount, total, limit, skew):
    if amount == 2:
        one = jax.random.randint(stream_key, (), max(1, total - limit), min(limit, total - 1) + 1)
        return jnp.stack([one, total - one])
    lengths = jnp.asarray(length_profile(amount, total, limit, skew), jnp.int32)
    twos = (amount - 1) // 2
    donor, receiver = lengths[1:1 + 2 * twos:2], lengths[2:2 + 2 * twos:2]
    room = jnp.minimum(donor - 1, limit - receiver)
    passed = jax.random.randint(jax.random.fold_in(stream_key, 1), (twos,), 0, 1 << 20) % (room + 1)
    lengths = lengths.at[1:1 + 2 * twos:2].set(donor - passed).at[2:2 + 2 * twos:2].set(receiver + passed)
    return lengths[jax.random.permutation(jax.random.fold_in(stream_key, 2), amount)]


def centred(stream_key, extent, spread, reach, pieces=(), held_as=jnp.bfloat16):
    level = level_of(stream_key, extent, pieces, -0.22, 0.18) if pieces else 1.0
    result = jax.random.normal(stream_key, extent, jnp.float32) * spread * level
    return jnp.minimum(jnp.maximum(result, -reach), reach).astype(held_as)


def setup_inputs(seed: int = 0) -> dict:
    splits = jax.random.split(jax.random.key(seed), 15)
    tokens = centred(splits[0], (TOKENS, D), 1.0, 6.0, ((0, 32),))
    segments = jax.vmap(lambda own: jnp.searchsorted(jnp.cumsum(uneven_parts(own, DOCS, SEQ, SEQ // 2, 1)), jnp.arange(SEQ), side="right"))(jax.random.split(splits[1], NSEQ)).reshape((NSEQ, SEQ)).astype(jnp.int32)
    routes = choose_distinct(splits[2], TOKENS, EXPERTS, 1, 1024)
    cotangent = centred(splits[3], (TOKENS, D), 1.0, 6.0, ((0, 32),))
    attn_gain = jnp.clip(1.0 + 0.1 * jax.random.normal(splits[4], (D,), jnp.float32), 0.5, 1.5)
    ffn_gain = jnp.clip(1.0 + 0.1 * jax.random.normal(splits[5], (D,), jnp.float32), 0.5, 1.5)
    query_weight = centred(splits[6], (D, D), D ** -0.5, 0.21875)
    key_weight = centred(splits[7], (D, D), D ** -0.5, 0.21875)
    value_weight = centred(splits[8], (D, D), D ** -0.5, 0.21875)
    output_weight = centred(splits[9], (D, D), (D // 16) ** -0.5, 0.875)
    position_bias_grid = centred(splits[10], (BUCKETS, HEADS), 1.0, 6.0, (), jnp.float32)
    router_weight = centred(splits[11], (D, EXPERTS), (2 * D) ** -0.5, 0.15625, (), jnp.float32)
    expert_in = centred(splits[12], (EXPERTS, D, FF), D ** -0.5, 0.21875, ((0, 8),))
    expert_out = centred(splits[13], (EXPERTS, FF, D), (max(1, FF // (EXPERTS * EXPERTS))) ** -0.5, 0.875, ((0, 8),))
    return dict(tokens=tokens, segments=segments, routes=routes, cotangent=cotangent, attn_gain=attn_gain, ffn_gain=ffn_gain, query_weight=query_weight, key_weight=key_weight, value_weight=value_weight, output_weight=output_weight, position_bias_grid=position_bias_grid, router_weight=router_weight, expert_in=expert_in, expert_out=expert_out)


@jax.custom_vjp
def low(v):
    return lax.optimization_barrier(v.astype(jnp.bfloat16)).astype(jnp.float32)

@jax.custom_vjp
def low_back(v):
    return v

def low_keep(v):
    return (low(v), None)

def low_pass(kept, grad):
    return (grad,)

def back_keep(v):
    return (v, None)

def back_low(kept, grad):
    return (low(grad),)
low.defvjp(low_keep, low_pass)
low_back.defvjp(back_keep, back_low)
epsilon = 1e-06
masked_score = -1e+30
bucket_bounds = (12, 16, 23, 32, 46, 64, 91)
precise_setting = lax.Precision.HIGHEST

def bucket_of(relative):
    distance = jnp.abs(relative)
    beyond = jnp.zeros_like(distance)
    for threshold in bucket_bounds:
        beyond = beyond + (distance >= threshold).astype(jnp.int32)
    inside = jnp.where(distance < 8, distance, 8 + beyond)
    return inside + 16 * (relative > 0).astype(jnp.int32)

def rms_norm(values, norm_gain):
    return values * lax.rsqrt(lax.optimization_barrier(jnp.mean(values * values, -1, keepdims=True)) + epsilon) * norm_gain

def matmul(left, right):
    return jnp.dot(left, right, precision=precise_setting)

def forward(params, segments, chosen):
    inputs, attn_gain, ffn_gain, query_weight, key_weight, value_weight, output_weight, position_bias_grid, router_weight, expert_in, expert_out = params
    normed = low(rms_norm(inputs, attn_gain))
    queries = low_back(low(matmul(normed, query_weight)))
    key_rows = low_back(low(matmul(normed, key_weight)))
    value_rows = low_back(low(matmul(normed, value_weight)))
    relative = lax.iota(jnp.int32, SEQ)[None, :] - lax.iota(jnp.int32, SEQ)[:, None]
    bias = jnp.transpose(position_bias_grid[bucket_of(relative)], (2, 0, 1))
    seq_shape = (NSEQ, SEQ, HEADS, HEAD_DIM)

    def one_sequence(operands):
        query_seq, key_seq, value_seq, segment_row = operands
        scores = jnp.einsum('qhd,khd->hqk', query_seq, key_seq, precision=precise_setting) * HEAD_DIM ** (-0.5) + bias
        scores = low_back(scores)
        same_doc = segment_row[:, None] == segment_row[None, :]
        scores = jnp.where(same_doc[None], scores, masked_score)
        highest = lax.optimization_barrier(jnp.max(scores, -1, keepdims=True))
        exponents = jnp.exp(scores - highest)
        attention = low(exponents / lax.optimization_barrier(jnp.sum(exponents, -1, keepdims=True)))
        return jnp.einsum('hqk,khd->qhd', attention, value_seq, precision=precise_setting)
    attended = lax.map(jax.checkpoint(one_sequence), (queries.reshape(seq_shape), key_rows.reshape(seq_shape), value_rows.reshape(seq_shape), segments))
    attended = low_back(low(attended.reshape(TOKENS, D)))
    middle = inputs + low_back(matmul(attended, output_weight))
    hidden_two = rms_norm(middle, ffn_gain)
    logits = matmul(hidden_two, router_weight)
    top_logit = lax.optimization_barrier(jnp.max(logits, -1, keepdims=True))
    exponents = jnp.exp(logits - top_logit)
    router_probs = exponents / lax.optimization_barrier(jnp.sum(exponents, -1, keepdims=True))
    expert_hot = (chosen[:, None] == lax.iota(jnp.int32, EXPERTS)[None, :]).astype(jnp.int32)
    blocked = expert_hot.reshape(DEVICES_ALL, TOK_DEV, EXPERTS)
    slot_rank = lax.optimization_barrier(jnp.sum((jnp.cumsum(blocked, 1) - blocked) * blocked, -1)).reshape(TOKENS)
    device_of = lax.iota(jnp.int32, TOKENS) // TOK_DEV
    dump_slot = DEVICES_ALL * EXPERTS * CAP
    token_slot = jnp.where(slot_rank < CAP, (device_of * EXPERTS + chosen) * CAP + slot_rank, dump_slot)
    gate_values = lax.optimization_barrier(jnp.sum(router_probs * expert_hot.astype(jnp.float32), -1))
    sent_rows = low(hidden_two)
    buffer = jnp.zeros((dump_slot + 1, D), jnp.float32).at[token_slot].add(sent_rows)
    buffer = buffer[:dump_slot].reshape(DEVICES_ALL, EXPERTS, CAP, D).transpose(1, 0, 2, 3)
    buffer = low_back(buffer.reshape(EXPERTS, DEVICES_ALL * CAP, D))

    def expert_ffn(operands):
        rows_in, weight_in, weight_out = operands
        pre_act = low_back(matmul(rows_in, weight_in))
        activated = low(jax.nn.gelu(pre_act, approximate=False))
        return low_back(low(matmul(activated, weight_out)))
    produced = lax.map(jax.checkpoint(expert_ffn), (buffer, expert_in, expert_out))
    produced = produced.reshape(EXPERTS, DEVICES_ALL, CAP, D).transpose(1, 0, 2, 3).reshape(dump_slot, D)
    produced = jnp.concatenate([produced, jnp.zeros((1, D), jnp.float32)], 0)
    expert_rows = produced[token_slot]
    return middle + gate_values[:, None] * expert_rows

def reference(tokens, segments, routes, cotangent, attn_gain, ffn_gain, query_weight, key_weight, value_weight, output_weight, position_bias_grid, router_weight, expert_in, expert_out):
    chosen = routes[:, 0]
    floats = (tokens.astype(jnp.float32), attn_gain, ffn_gain, query_weight.astype(jnp.float32), key_weight.astype(jnp.float32), value_weight.astype(jnp.float32), output_weight.astype(jnp.float32), position_bias_grid, router_weight, expert_in.astype(jnp.float32), expert_out.astype(jnp.float32))

    def run(params):
        return forward(params, segments, chosen)
    mixed, pull = jax.vjp(run, floats)
    grads = pull(cotangent.astype(jnp.float32))[0]
    return (mixed.astype(jnp.bfloat16), grads[0].astype(jnp.bfloat16), grads[1], grads[2], grads[3], grads[4], grads[5], grads[6], grads[7], grads[8], grads[9], grads[10])
```

```python
import functools

import jax
import jax.numpy as jnp
from jax import lax
from jax.experimental import pallas as pl
from jax.experimental.pallas import tpu as pltpu
from jax.sharding import PartitionSpec as P

epsilon = 1e-06
precise_setting = lax.Precision.HIGHEST
bucket_bounds = (12, 16, 23, 32, 46, 64, 91)
masked_score = -1e30
LANES = 128
BLOCK = 128
NEAR = 5


def bucket_of(relative):
    distance = jnp.abs(relative)
    beyond = jnp.zeros_like(distance)
    for threshold in bucket_bounds:
        beyond = beyond + (distance >= threshold).astype(jnp.int32)
    inside = jnp.where(distance < 8, distance, 8 + beyond)
    return inside + 16 * (relative > 0).astype(jnp.int32)


def dot_nt(a, b):
    return lax.dot_general(a, b, (((1,), (1,)), ((), ())), preferred_element_type=jnp.float32)


def dot_nn(a, b):
    return lax.dot_general(a, b, (((1,), (0,)), ((), ())), preferred_element_type=jnp.float32)


def split3(x):
    a = x.astype(jnp.bfloat16)
    r = x - a.astype(jnp.float32)
    b = r.astype(jnp.bfloat16)
    c = (r - b.astype(jnp.float32)).astype(jnp.bfloat16)
    return a, b, c


def attn_fwd_kernel(lo_ref, hi_ref, q_ref, k_ref, v_ref, qm_ref, km_ref, diag_ref, o_ref, qx_ref,
                    kext, vext, bias, sc, mx, acc, *, heads):
    pairs = heads // 2
    length = q_ref.shape[0]
    nblk = length // BLOCK
    lane = lax.broadcasted_iota(jnp.int32, (1, LANES), 1)
    low = lane < 64
    for h in range(heads):
        for d in range(NEAR):
            if d in (0, 4):
                col = diag_ref[h : h + 1, 0:1] if d == 0 else diag_ref[h : h + 1, 511:512]
                bias[h, d] = jnp.broadcast_to(col, (BLOCK, BLOCK))
            else:
                v = jnp.broadcast_to(diag_ref[h : h + 1, (d - 1) * 128 : (d - 1) * 128 + 256], (BLOCK, 256))
                bias[h, d] = pltpu.roll(v, 128, 1, stride=1, stride_axis=0)[:, :BLOCK]
    zero = jnp.zeros((BLOCK, LANES), jnp.bfloat16)

    def build(j, _):
        rows = pl.ds(pl.multiple_of(j * BLOCK, BLOCK), BLOCK)
        km = km_ref[rows, :]
        km0 = jnp.where(low, km, 0).astype(jnp.bfloat16)
        km1 = jnp.where((lane < 8) | (lane >= 64), km, 0).astype(jnp.bfloat16)
        one0 = jnp.broadcast_to(low.astype(jnp.bfloat16), (BLOCK, LANES))
        one1 = jnp.broadcast_to((~low).astype(jnp.bfloat16), (BLOCK, LANES))
        for p in range(pairs):
            cols = pl.ds(p * LANES, LANES)
            kk = k_ref[rows, cols]
            vv = v_ref[rows, cols]
            kext[p, j] = jnp.concatenate([
                jnp.concatenate([jnp.where(low, kk, zero), km0], 1),
                jnp.concatenate([jnp.where(low, zero, kk), km1], 1)], 0)
            vext[p, j] = jnp.concatenate([
                jnp.concatenate([jnp.where(low, vv, zero), one0], 1),
                jnp.concatenate([jnp.where(low, zero, vv), one1], 1)], 0)
        return 0
    lax.fori_loop(0, nblk, build, 0)

    def q_block(i, _):
        lo = lo_ref[i]
        hi = hi_ref[i]
        rows = pl.ds(pl.multiple_of(i * BLOCK, BLOCK), BLOCK)
        qm = qm_ref[rows, :]
        mx[...] = jnp.full(mx.shape, -3e38, jnp.float32)

        def pass1(j, _):
            d = jnp.clip(j - i, -2, 2) + 2
            for p in range(pairs):
                qe = jnp.concatenate([q_ref[rows, pl.ds(p * LANES, LANES)], qm], 1)
                s = dot_nt(qe, kext[p, j])
                s0 = s[:, :BLOCK] + bias[2 * p, d]
                s1 = s[:, BLOCK:] + bias[2 * p + 1, d]
                sc[p, j, :, :BLOCK] = s0
                sc[p, j, :, BLOCK:] = s1
                mx[2 * p] = jnp.maximum(mx[2 * p], s0)
                mx[2 * p + 1] = jnp.maximum(mx[2 * p + 1], s1)
            return 0
        lax.fori_loop(lo, hi, pass1, 0)
        for h in range(heads):
            mx[h] = jnp.broadcast_to(jnp.max(mx[h], 1, keepdims=True), (BLOCK, LANES))
        acc[...] = jnp.zeros_like(acc)

        def pass2(j, _):
            for p in range(pairs):
                p0 = jnp.exp(sc[p, j, :, :BLOCK] - mx[2 * p]).astype(jnp.bfloat16)
                p1 = jnp.exp(sc[p, j, :, BLOCK:] - mx[2 * p + 1]).astype(jnp.bfloat16)
                acc[p] += dot_nn(jnp.concatenate([p0, p1], 1), vext[p, j])
            return 0
        lax.fori_loop(lo, hi, pass2, 0)
        m64 = lane % 64
        for p in range(pairs):
            cols = pl.ds(p * LANES, LANES)
            total = acc[p, :, LANES:]
            o_ref[rows, cols] = (acc[p, :, :LANES] / total).astype(jnp.bfloat16)
            lse = jnp.where(low, mx[2 * p], mx[2 * p + 1]) + jnp.log(total)
            a, b, c = split3(lse)
            ext = jnp.where(m64 == 8, -a, jnp.where(m64 == 9, -b, jnp.where(m64 == 10, -c, qm)))
            qx_ref[rows, cols] = ext.astype(jnp.bfloat16)
        return 0
    lax.fori_loop(0, nblk, q_block, 0)


def attn_fwd(lo, hi, q, k, v, qm, km, diag):
    length, width = q.shape
    heads = diag.shape[0]
    pairs = heads // 2
    nblk = length // BLOCK
    smem = pl.BlockSpec(memory_space=pltpu.SMEM)
    vmem = pl.BlockSpec(memory_space=pltpu.VMEM)
    f32, bf16 = jnp.float32, jnp.bfloat16
    return pl.pallas_call(
        functools.partial(attn_fwd_kernel, heads=heads),
        out_shape=(jax.ShapeDtypeStruct((length, width), bf16), jax.ShapeDtypeStruct((length, width), bf16)),
        in_specs=[smem, smem] + [vmem] * 6,
        out_specs=(vmem, vmem),
        scratch_shapes=[
            pltpu.VMEM((pairs, nblk, 2 * BLOCK, 2 * LANES), bf16),
            pltpu.VMEM((pairs, nblk, 2 * BLOCK, 2 * LANES), bf16),
            pltpu.VMEM((heads, NEAR, BLOCK, BLOCK), f32),
            pltpu.VMEM((pairs, nblk, BLOCK, 2 * BLOCK), f32),
            pltpu.VMEM((heads, BLOCK, LANES), f32),
            pltpu.VMEM((pairs, BLOCK, 2 * LANES), f32),
        ],
        compiler_params=pltpu.CompilerParams(vmem_limit_bytes=60 << 20),
        cost_estimate=pl.CostEstimate(flops=4 * length * length * width, bytes_accessed=10 * length * width, transcendentals=length * length * heads),
    )(lo, hi, q, k, v, qm, km, diag)


def attn_bwd_kernel(lo_ref, hi_ref, q_ref, k_ref, v_ref, qx_ref, do_ref, o_ref, km_ref, diag_ref,
                    dq_ref, dk_ref, dv_ref, gsum_ref,
                    qst, dost, bias, gacc, dkacc, dvacc, dqacc, *, heads, scale):
    pairs = heads // 2
    length = q_ref.shape[0]
    nblk = length // BLOCK
    lane = lax.broadcasted_iota(jnp.int32, (1, LANES), 1)
    low = lane < 64
    m64 = lane % 64
    f32, bf16 = jnp.float32, jnp.bfloat16
    for h in range(heads):
        for d in range(NEAR):
            if d in (0, 4):
                col = diag_ref[h : h + 1, 0:1] if d == 0 else diag_ref[h : h + 1, 511:512]
                bias[h, d] = jnp.broadcast_to(col, (BLOCK, BLOCK))
            else:
                base = (3 - d) * BLOCK
                v = jnp.broadcast_to(diag_ref[heads + h : heads + h + 1, base : base + 256], (BLOCK, 256))
                bias[h, d] = pltpu.roll(v, 128, 1, stride=1, stride_axis=0)[:, :BLOCK]
    zero = jnp.zeros((BLOCK, LANES), bf16)
    gacc[...] = jnp.zeros_like(gacc)
    dkacc[...] = jnp.zeros_like(dkacc)
    dvacc[...] = jnp.zeros_like(dvacc)

    def q_block(i, _):
        lo = lo_ref[i]
        hi = hi_ref[i]
        rows = pl.ds(pl.multiple_of(i * BLOCK, BLOCK), BLOCK)
        for p in range(pairs):
            cols = pl.ds(p * LANES, LANES)
            qq = q_ref[rows, cols]
            qx = qx_ref[rows, cols]
            qst[p] = jnp.concatenate([
                jnp.concatenate([jnp.where(low, qq, zero), jnp.where(low, qx, zero)], 1),
                jnp.concatenate([jnp.where(low, zero, qq), jnp.where((lane < 8) | ~low, qx, zero)], 1)], 0)
            dd = do_ref[rows, cols]
            prod = dd.astype(f32) * o_ref[rows, cols].astype(f32)
            in0 = jnp.sum(jnp.where(low, prod, 0.0), 1, keepdims=True)
            in1 = jnp.sum(jnp.where(low, 0.0, prod), 1, keepdims=True)
            inner = jnp.where(low, in0, in1)
            a, b, c = split3(inner)
            ext = jnp.where(m64 == 8, -a, jnp.where(m64 == 9, -b, jnp.where(m64 == 10, -c, zero)))
            dost[p] = jnp.concatenate([
                jnp.concatenate([jnp.where(low, dd, zero), jnp.where(low, ext, zero)], 1),
                jnp.concatenate([jnp.where(low, zero, dd), jnp.where(low, zero, ext)], 1)], 0)
        dqacc[...] = jnp.zeros_like(dqacc)

        def k_block(j, _):
            d = jnp.clip(j - i, -2, 2) + 2
            krows = pl.ds(pl.multiple_of(j * BLOCK, BLOCK), BLOCK)
            km = km_ref[krows, :]
            for p in range(pairs):
                cols = pl.ds(p * LANES, LANES)
                kk = k_ref[krows, cols]
                vv = v_ref[krows, cols]
                qs = qst[p]
                ds_ = dost[p]
                st = dot_nt(jnp.concatenate([kk, km], 1), qs)
                dpt = dot_nt(jnp.concatenate([vv, km], 1), ds_)
                p0 = jnp.exp(st[:, :BLOCK] + bias[2 * p, d])
                p1 = jnp.exp(st[:, BLOCK:] + bias[2 * p + 1, d])
                d0 = p0 * dpt[:, :BLOCK]
                d1 = p1 * dpt[:, BLOCK:]
                gacc[2 * p, d] += d0
                gacc[2 * p + 1, d] += d1
                pb = jnp.concatenate([p0.astype(bf16), p1.astype(bf16)], 1)
                d0b = d0.astype(bf16)
                d1b = d1.astype(bf16)
                db = jnp.concatenate([d0b, d1b], 1)
                dvacc[krows, cols] += dot_nn(pb, ds_[:, :LANES])
                dkacc[krows, cols] += dot_nn(db, qs[:, :LANES])
                dst = jnp.concatenate([d0b.T, d1b.T], 1)
                kz = jnp.concatenate([jnp.where(low, kk, zero), jnp.where(low, zero, kk)], 0)
                dqacc[:, cols] += dot_nn(dst, kz)
            return 0
        lax.fori_loop(lo, hi, k_block, 0)
        dq_ref[rows, :] = (dqacc[...] * scale).astype(bf16)
        return 0
    lax.fori_loop(0, nblk, q_block, 0)
    dk_ref[...] = dkacc[...].astype(bf16)
    dv_ref[...] = dvacc[...].astype(bf16)
    pad = jnp.zeros((BLOCK, LANES), f32)
    sub = lax.broadcasted_iota(jnp.int32, (8, 2 * LANES), 0)
    for h in range(heads):
        for d in range(NEAR):
            t = gacc[h, d]
            if d in (0, 4):
                s = jnp.concatenate([jnp.sum(t, 0, keepdims=True), jnp.zeros((1, LANES), f32)], 1)
            else:
                wide = jnp.concatenate([t, pad], 1)
                s = jnp.zeros((8, 2 * LANES), f32)
                for a in range(BLOCK // 8):
                    s = s + pltpu.roll(wide[8 * a : 8 * a + 8], BLOCK - 8 * a, 1)
                for bit in (1, 2, 4):
                    s = jnp.where((sub & bit) > 0, pltpu.roll(s, 2 * LANES - bit, 1), s)
                s = jnp.sum(s, 0, keepdims=True)
            gsum_ref[h * NEAR + d : h * NEAR + d + 1, :] = s


def attn_bwd(lo, hi, q, k, v, qx, do, o, km, diag, scale):
    length, width = q.shape
    heads = diag.shape[0] // 2
    pairs = heads // 2
    nblk = length // BLOCK
    smem = pl.BlockSpec(memory_space=pltpu.SMEM)
    vmem = pl.BlockSpec(memory_space=pltpu.VMEM)
    f32, bf16 = jnp.float32, jnp.bfloat16
    act = jax.ShapeDtypeStruct((length, width), bf16)
    return pl.pallas_call(
        functools.partial(attn_bwd_kernel, heads=heads, scale=scale),
        out_shape=(act, act, act, jax.ShapeDtypeStruct((heads * NEAR, 256), f32)),
        in_specs=[smem, smem] + [vmem] * 8,
        out_specs=(vmem,) * 4,
        scratch_shapes=[
            pltpu.VMEM((pairs, 2 * BLOCK, 2 * LANES), bf16),
            pltpu.VMEM((pairs, 2 * BLOCK, 2 * LANES), bf16),
            pltpu.VMEM((heads, NEAR, BLOCK, BLOCK), f32),
            pltpu.VMEM((heads, NEAR, BLOCK, BLOCK), f32),
            pltpu.VMEM((length, width), f32),
            pltpu.VMEM((length, width), f32),
            pltpu.VMEM((BLOCK, width), f32),
        ],
        compiler_params=pltpu.CompilerParams(vmem_limit_bytes=60 << 20),
        cost_estimate=pl.CostEstimate(flops=10 * length * length * width, bytes_accessed=20 * length * width, transcendentals=length * length * heads),
    )(lo, hi, q, k, v, qx, do, o, km, diag)


def rms_forward(values, norm_gain):
    inverse = lax.rsqrt(jnp.mean(values * values, -1, keepdims=True) + epsilon)
    return (values * inverse * norm_gain, inverse)


def rms_backward(values, inverse, norm_gain, upstream):
    scaled = upstream * norm_gain
    gain_grad = jnp.sum(upstream * values * inverse, 0)
    input_grad = inverse * (
        scaled - values * inverse * inverse * jnp.mean(scaled * values, -1, keepdims=True)
    )
    return (input_grad, gain_grad)


def matmul(left, right):
    return jnp.dot(left, right, preferred_element_type=jnp.float32)


def matmul_tn(left, right):
    return lax.dot_general(left, right, (((0,), (0,)), ((), ())), preferred_element_type=jnp.float32)


def matmul_nt(left, right):
    return lax.dot_general(left, right, (((1,), (1,)), ((), ())), preferred_element_type=jnp.float32)


def attention_operands(segment_row, bias_grid):
    f32 = jnp.float32
    first, last = segment_row[::BLOCK], segment_row[BLOCK - 1 :: BLOCK]
    lo = jnp.sum(segment_row[None, :] < first[:, None], 1) // BLOCK
    hi = (jnp.sum(segment_row[None, :] <= last[:, None], 1) + BLOCK - 1) // BLOCK
    lane = lax.iota(jnp.int32, LANES)[None, :]
    same = segment_row[:, None] == lane
    query_mask = jnp.where(same, masked_score, 0.0).astype(jnp.bfloat16)
    ones = ((lane % 64 >= 8) & (lane % 64 <= 10)).astype(f32)
    key_mask = jnp.where(lane < 8, 1.0 - same.astype(f32), ones).astype(jnp.bfloat16)
    relative = lax.iota(jnp.int32, 512) - 256
    buckets = bucket_of(jnp.concatenate([relative, 256 - lax.iota(jnp.int32, 512)]))
    hot = (lax.iota(jnp.int32, bias_grid.shape[0])[:, None] == buckets[None, :]).astype(f32)
    along = lax.dot_general(
        bias_grid, hot, (((0,), (0,)), ((), ())), precision=precise_setting
    )
    diag = jnp.concatenate([along[:, :512], along[:, 512:]], 0)
    return lo.astype(jnp.int32), hi.astype(jnp.int32), query_mask, key_mask, diag


def bias_grad(sums, heads, bucket_count):
    near = lax.broadcasted_iota(jnp.int32, (NEAR, 2 * LANES), 0)
    place = lax.broadcasted_iota(jnp.int32, (NEAR, 2 * LANES), 1)
    bucket = bucket_of((near - 2) * BLOCK + BLOCK - place)
    bucket = jnp.where(near == 0, 15, jnp.where(near == NEAR - 1, 31, bucket))
    hot = (bucket.reshape(-1)[:, None] == lax.iota(jnp.int32, bucket_count)[None, :]).astype(jnp.float32)
    return jnp.dot(sums.reshape(heads, -1), hot, precision=precise_setting).T


def per_device(
    tokens,
    segments,
    routes,
    cotangent,
    attn_gain,
    ffn_gain,
    query_weight,
    key_weight,
    value_weight,
    output_weight,
    position_bias_grid,
    router_weight,
    expert_in,
    expert_out,
):
    f32, bf16 = jnp.float32, jnp.bfloat16
    token_count, model_width = tokens.shape
    bucket_count, head_count = position_bias_grid.shape
    head_width = model_width // head_count
    score_scale = head_width ** (-0.5)
    experts_all = router_weight.shape[1]
    capacity = (5 * token_count + 4 * experts_all - 1) // (4 * experts_all)
    slots = experts_all * capacity

    chosen = routes[:, 0]
    expert_hot = chosen[:, None] == lax.iota(jnp.int32, experts_all)[None, :]
    expert_float = expert_hot.astype(f32)
    before = lax.iota(jnp.int32, token_count)[:, None] > lax.iota(jnp.int32, token_count)[None, :]
    ranks = matmul(before.astype(bf16), expert_hot.astype(bf16))
    slot_rank = jnp.sum(ranks * expert_float, 1).astype(jnp.int32)
    token_slot = jnp.where(slot_rank < capacity, chosen * capacity + slot_rank, slots)
    to_slots = (lax.iota(jnp.int32, slots)[:, None] == token_slot[None, :]).astype(bf16)

    inputs = tokens.astype(f32)
    normed, inverse_one = rms_forward(inputs, attn_gain)
    normed_low = normed.astype(bf16)
    queries = (matmul(normed_low, query_weight).astype(bf16) * score_scale).astype(bf16)
    key_rows = matmul(normed_low, key_weight).astype(bf16)
    value_rows = matmul(normed_low, value_weight).astype(bf16)
    lo, hi, query_mask, key_mask, diag = attention_operands(segments[0], position_bias_grid)
    attended, query_extra = attn_fwd(
        lo, hi, queries, key_rows, value_rows, query_mask, key_mask, diag[:head_count]
    )
    middle = inputs + matmul(attended, output_weight)
    hidden_two, inverse_two = rms_forward(middle, ffn_gain)
    logits = jnp.dot(hidden_two, router_weight, precision=precise_setting)
    top_logit = jnp.max(logits, -1, keepdims=True)
    exponents_router = jnp.exp(logits - top_logit)
    router_probs = exponents_router / jnp.sum(exponents_router, -1, keepdims=True)
    gate_values = jnp.sum(router_probs * expert_float, 1)
    upstream = cotangent.astype(f32)

    def exchange(rows):
        rows = rows.reshape(experts_all, capacity, model_width)
        rows = lax.all_to_all(rows, "expert", split_axis=0, concat_axis=0, tiled=True)
        return rows.reshape(slots, model_width)

    arrived = exchange(matmul(to_slots, hidden_two.astype(bf16)).astype(bf16))
    out_grad_rows = (gate_values[:, None] * upstream).astype(bf16)
    grad_arrived = exchange(matmul(to_slots, out_grad_rows).astype(bf16))
    weight_in, weight_out = expert_in[0], expert_out[0]
    pre_act = matmul(arrived, weight_in)
    activated = jax.nn.gelu(pre_act, approximate=False).astype(bf16)
    produced = matmul(activated, weight_out).astype(bf16)
    returned = exchange(produced)
    expert_rows = matmul_tn(to_slots, returned)
    mixed = (middle + gate_values[:, None] * expert_rows).astype(bf16)
    gate_grad = jnp.sum(upstream * expert_rows, 1)

    act_grad = matmul_nt(grad_arrived, weight_out)
    _, gelu_pull = jax.vjp(functools.partial(jax.nn.gelu, approximate=False), pre_act)
    pre_grad = gelu_pull(act_grad)[0].astype(bf16)
    out_weight_grad = matmul_tn(activated, grad_arrived)
    in_weight_grad = matmul_tn(arrived, pre_grad)
    home_grad = exchange(matmul_nt(pre_grad, weight_in).astype(bf16))
    in_weight_grad = lax.psum_scatter(
        in_weight_grad.astype(bf16), "dp", scatter_dimension=1, tiled=True
    ).astype(f32)
    out_weight_grad = lax.psum_scatter(
        out_weight_grad.astype(bf16), "dp", scatter_dimension=0, tiled=True
    ).astype(f32)
    expert_input_grad = matmul_tn(to_slots, home_grad)
    logit_grad = router_probs * (
        expert_float * gate_grad[:, None] - (gate_values * gate_grad)[:, None]
    )
    router_grad = jnp.dot(hidden_two.T, logit_grad, precision=precise_setting)
    hidden_grad = expert_input_grad + jnp.dot(
        logit_grad, router_weight.T, precision=precise_setting
    )
    middle_part, ffn_gain_grad = rms_backward(middle, inverse_two, ffn_gain, hidden_grad)
    middle_grad = upstream + middle_part
    branch_grad = middle_grad.astype(bf16)
    output_weight_grad = matmul_tn(attended, branch_grad)
    attended_grad = matmul_nt(branch_grad, output_weight).astype(bf16)
    query_grad, key_grad, value_grad, diag_sums = attn_bwd(
        lo, hi, queries, key_rows, value_rows, query_extra, attended_grad, attended, key_mask,
        diag, score_scale,
    )
    table_grad = bias_grad(diag_sums, head_count, bucket_count)
    query_weight_grad = matmul_tn(normed_low, query_grad)
    key_weight_grad = matmul_tn(normed_low, key_grad)
    value_weight_grad = matmul_tn(normed_low, value_grad)
    normed_grad = (
        matmul_nt(query_grad, query_weight)
        + matmul_nt(key_grad, key_weight)
        + matmul_nt(value_grad, value_weight)
    )
    input_part, attn_gain_grad = rms_backward(inputs, inverse_one, attn_gain, normed_grad)
    token_grad = (middle_grad + input_part).astype(bf16)
    weights = jnp.concatenate(
        [query_weight_grad, key_weight_grad, value_weight_grad, output_weight_grad], 1
    ).astype(bf16)
    weights = lax.psum(weights, ("dp", "expert")).astype(f32)
    weights = [weights[:, i * model_width : (i + 1) * model_width] for i in range(4)]
    small = lax.psum((table_grad, router_grad, attn_gain_grad, ffn_gain_grad), ("dp", "expert"))
    return (
        mixed,
        token_grad,
        small[2],
        small[3],
        *weights,
        small[0],
        small[1],
        in_weight_grad[None],
        out_weight_grad[None],
    )


def solution(mesh):
    rows = P(("dp", "expert"), None)
    return jax.shard_map(
        per_device,
        mesh=mesh,
        in_specs=(rows,) * 4 + (P(),) * 8 + (P("expert", None, None),) * 2,
        out_specs=(rows,) * 2 + (P(),) * 8 + (P("expert", None, "dp"), P("expert", "dp", None)),
        check_vma=False,
    )
```

```python
import functools

import jax
import jax.numpy as jnp
from jax import lax
from jax.experimental import pallas as pl
from jax.experimental.pallas import tpu as pltpu
from jax.sharding import PartitionSpec as P

epsilon = 1e-06
precise_setting = lax.Precision.HIGHEST
bucket_bounds = (12, 16, 23, 32, 46, 64, 91)
masked_score = -1e30
LANES = 128
BLOCK = 128
NEAR = 5


def bucket_of(relative):
    distance = jnp.abs(relative)
    beyond = jnp.zeros_like(distance)
    for threshold in bucket_bounds:
        beyond = beyond + (distance >= threshold).astype(jnp.int32)
    inside = jnp.where(distance < 8, distance, 8 + beyond)
    return inside + 16 * (relative > 0).astype(jnp.int32)


def dot_nt(a, b):
    return lax.dot_general(a, b, (((1,), (1,)), ((), ())), preferred_element_type=jnp.float32)


def dot_nn(a, b):
    return lax.dot_general(a, b, (((1,), (0,)), ((), ())), preferred_element_type=jnp.float32)


def split3(x):
    a = x.astype(jnp.bfloat16)
    r = x - a.astype(jnp.float32)
    b = r.astype(jnp.bfloat16)
    c = (r - b.astype(jnp.float32)).astype(jnp.bfloat16)
    return a, b, c


def attn_fwd_kernel(lo_ref, hi_ref, q_ref, k_ref, v_ref, qm_ref, km_ref, diag_ref, o_ref, qx_ref,
                    kext, vext, bias, sc, mx, acc, *, heads):
    pairs = heads // 2
    length = q_ref.shape[0]
    nblk = length // BLOCK
    lane = lax.broadcasted_iota(jnp.int32, (1, LANES), 1)
    low = lane < 64
    for h in range(heads):
        for d in range(NEAR):
            if d in (0, 4):
                col = diag_ref[h : h + 1, 0:1] if d == 0 else diag_ref[h : h + 1, 511:512]
                bias[h, d] = jnp.broadcast_to(col, (BLOCK, BLOCK))
            else:
                v = jnp.broadcast_to(diag_ref[h : h + 1, (d - 1) * 128 : (d - 1) * 128 + 256], (BLOCK, 256))
                bias[h, d] = pltpu.roll(v, 128, 1, stride=1, stride_axis=0)[:, :BLOCK]
    zero = jnp.zeros((BLOCK, LANES), jnp.bfloat16)

    def build(j, _):
        rows = pl.ds(pl.multiple_of(j * BLOCK, BLOCK), BLOCK)
        km = km_ref[rows, :]
        km0 = jnp.where(low, km, 0).astype(jnp.bfloat16)
        km1 = jnp.where((lane < 8) | (lane >= 64), km, 0).astype(jnp.bfloat16)
        one0 = jnp.broadcast_to(low.astype(jnp.bfloat16), (BLOCK, LANES))
        one1 = jnp.broadcast_to((~low).astype(jnp.bfloat16), (BLOCK, LANES))
        for p in range(pairs):
            cols = pl.ds(p * LANES, LANES)
            kk = k_ref[rows, cols]
            vv = v_ref[rows, cols]
            kext[p, j] = jnp.concatenate([
                jnp.concatenate([jnp.where(low, kk, zero), km0], 1),
                jnp.concatenate([jnp.where(low, zero, kk), km1], 1)], 0)
            vext[p, j] = jnp.concatenate([
                jnp.concatenate([jnp.where(low, vv, zero), one0], 1),
                jnp.concatenate([jnp.where(low, zero, vv), one1], 1)], 0)
        return 0
    lax.fori_loop(0, nblk, build, 0)

    def q_block(i, _):
        lo = lo_ref[i]
        hi = hi_ref[i]
        rows = pl.ds(pl.multiple_of(i * BLOCK, BLOCK), BLOCK)
        qm = qm_ref[rows, :]
        mx[...] = jnp.full(mx.shape, -3e38, jnp.float32)

        def pass1(j, _):
            d = jnp.clip(j - i, -2, 2) + 2
            for p in range(pairs):
                qe = jnp.concatenate([q_ref[rows, pl.ds(p * LANES, LANES)], qm], 1)
                s = dot_nt(qe, kext[p, j])
                s0 = s[:, :BLOCK] + bias[2 * p, d]
                s1 = s[:, BLOCK:] + bias[2 * p + 1, d]
                sc[p, j, :, :BLOCK] = s0
                sc[p, j, :, BLOCK:] = s1
                mx[2 * p] = jnp.maximum(mx[2 * p], s0)
                mx[2 * p + 1] = jnp.maximum(mx[2 * p + 1], s1)
            return 0
        lax.fori_loop(lo, hi, pass1, 0)
        for h in range(heads):
            mx[h] = jnp.broadcast_to(jnp.max(mx[h], 1, keepdims=True), (BLOCK, LANES))
        acc[...] = jnp.zeros_like(acc)

        def pass2(j, _):
            for p in range(pairs):
                p0 = jnp.exp(sc[p, j, :, :BLOCK] - mx[2 * p]).astype(jnp.bfloat16)
                p1 = jnp.exp(sc[p, j, :, BLOCK:] - mx[2 * p + 1]).astype(jnp.bfloat16)
                acc[p] += dot_nn(jnp.concatenate([p0, p1], 1), vext[p, j])
            return 0
        lax.fori_loop(lo, hi, pass2, 0)
        m64 = lane % 64
        for p in range(pairs):
            cols = pl.ds(p * LANES, LANES)
            total = acc[p, :, LANES:]
            o_ref[rows, cols] = (acc[p, :, :LANES] / total).astype(jnp.bfloat16)
            lse = jnp.where(low, mx[2 * p], mx[2 * p + 1]) + jnp.log(total)
            a, b, c = split3(lse)
            ext = jnp.where(m64 == 8, -a, jnp.where(m64 == 9, -b, jnp.where(m64 == 10, -c, qm)))
            qx_ref[rows, cols] = ext.astype(jnp.bfloat16)
        return 0
    lax.fori_loop(0, nblk, q_block, 0)


def attn_fwd(lo, hi, q, k, v, qm, km, diag):
    length, width = q.shape
    heads = diag.shape[0]
    pairs = heads // 2
    nblk = length // BLOCK
    smem = pl.BlockSpec(memory_space=pltpu.SMEM)
    vmem = pl.BlockSpec(memory_space=pltpu.VMEM)
    f32, bf16 = jnp.float32, jnp.bfloat16
    return pl.pallas_call(
        functools.partial(attn_fwd_kernel, heads=heads),
        out_shape=(jax.ShapeDtypeStruct((length, width), bf16), jax.ShapeDtypeStruct((length, width), bf16)),
        in_specs=[smem, smem] + [vmem] * 6,
        out_specs=(vmem, vmem),
        scratch_shapes=[
            pltpu.VMEM((pairs, nblk, 2 * BLOCK, 2 * LANES), bf16),
            pltpu.VMEM((pairs, nblk, 2 * BLOCK, 2 * LANES), bf16),
            pltpu.VMEM((heads, NEAR, BLOCK, BLOCK), f32),
            pltpu.VMEM((pairs, nblk, BLOCK, 2 * BLOCK), f32),
            pltpu.VMEM((heads, BLOCK, LANES), f32),
            pltpu.VMEM((pairs, BLOCK, 2 * LANES), f32),
        ],
        compiler_params=pltpu.CompilerParams(vmem_limit_bytes=60 << 20),
        cost_estimate=pl.CostEstimate(flops=4 * length * length * width, bytes_accessed=10 * length * width, transcendentals=length * length * heads),
    )(lo, hi, q, k, v, qm, km, diag)


def attn_bwd_kernel(lo_ref, hi_ref, q_ref, k_ref, v_ref, qx_ref, do_ref, o_ref, km_ref, diag_ref,
                    dq_ref, dk_ref, dv_ref, gsum_ref,
                    qst, dost, bias, gacc, dkacc, dvacc, dqacc, *, heads, scale):
    pairs = heads // 2
    length = q_ref.shape[0]
    nblk = length // BLOCK
    lane = lax.broadcasted_iota(jnp.int32, (1, LANES), 1)
    low = lane < 64
    m64 = lane % 64
    f32, bf16 = jnp.float32, jnp.bfloat16
    for h in range(heads):
        for d in range(NEAR):
            if d in (0, 4):
                col = diag_ref[h : h + 1, 0:1] if d == 0 else diag_ref[h : h + 1, 511:512]
                bias[h, d] = jnp.broadcast_to(col, (BLOCK, BLOCK))
            else:
                base = (3 - d) * BLOCK
                v = jnp.broadcast_to(diag_ref[heads + h : heads + h + 1, base : base + 256], (BLOCK, 256))
                bias[h, d] = pltpu.roll(v, 128, 1, stride=1, stride_axis=0)[:, :BLOCK]
    zero = jnp.zeros((BLOCK, LANES), bf16)
    gacc[...] = jnp.zeros_like(gacc)
    dkacc[...] = jnp.zeros_like(dkacc)
    dvacc[...] = jnp.zeros_like(dvacc)

    def q_block(i, _):
        lo = lo_ref[i]
        hi = hi_ref[i]
        rows = pl.ds(pl.multiple_of(i * BLOCK, BLOCK), BLOCK)
        for p in range(pairs):
            cols = pl.ds(p * LANES, LANES)
            qq = q_ref[rows, cols]
            qx = qx_ref[rows, cols]
            qst[p] = jnp.concatenate([
                jnp.concatenate([jnp.where(low, qq, zero), jnp.where(low, qx, zero)], 1),
                jnp.concatenate([jnp.where(low, zero, qq), jnp.where((lane < 8) | ~low, qx, zero)], 1)], 0)
            dd = do_ref[rows, cols]
            prod = dd.astype(f32) * o_ref[rows, cols].astype(f32)
            in0 = jnp.sum(jnp.where(low, prod, 0.0), 1, keepdims=True)
            in1 = jnp.sum(jnp.where(low, 0.0, prod), 1, keepdims=True)
            inner = jnp.where(low, in0, in1)
            a, b, c = split3(inner)
            ext = jnp.where(m64 == 8, -a, jnp.where(m64 == 9, -b, jnp.where(m64 == 10, -c, zero)))
            dost[p] = jnp.concatenate([
                jnp.concatenate([jnp.where(low, dd, zero), jnp.where(low, ext, zero)], 1),
                jnp.concatenate([jnp.where(low, zero, dd), jnp.where(low, zero, ext)], 1)], 0)
        dqacc[...] = jnp.zeros_like(dqacc)

        def k_block(j, _):
            d = jnp.clip(j - i, -2, 2) + 2
            krows = pl.ds(pl.multiple_of(j * BLOCK, BLOCK), BLOCK)
            km = km_ref[krows, :]
            for p in range(pairs):
                cols = pl.ds(p * LANES, LANES)
                kk = k_ref[krows, cols]
                vv = v_ref[krows, cols]
                qs = qst[p]
                ds_ = dost[p]
                st = dot_nt(jnp.concatenate([kk, km], 1), qs)
                dpt = dot_nt(jnp.concatenate([vv, km], 1), ds_)
                p0 = jnp.exp(st[:, :BLOCK] + bias[2 * p, d])
                p1 = jnp.exp(st[:, BLOCK:] + bias[2 * p + 1, d])
                d0 = p0 * dpt[:, :BLOCK]
                d1 = p1 * dpt[:, BLOCK:]
                gacc[2 * p, d] += d0
                gacc[2 * p + 1, d] += d1
                pb = jnp.concatenate([p0.astype(bf16), p1.astype(bf16)], 1)
                d0b = d0.astype(bf16)
                d1b = d1.astype(bf16)
                db = jnp.concatenate([d0b, d1b], 1)
                dvacc[krows, cols] += dot_nn(pb, ds_[:, :LANES])
                dkacc[krows, cols] += dot_nn(db, qs[:, :LANES])
                dst = jnp.concatenate([d0b.T, d1b.T], 1)
                kz = jnp.concatenate([jnp.where(low, kk, zero), jnp.where(low, zero, kk)], 0)
                dqacc[:, cols] += dot_nn(dst, kz)
            return 0
        lax.fori_loop(lo, hi, k_block, 0)
        dq_ref[rows, :] = (dqacc[...] * scale).astype(bf16)
        return 0
    lax.fori_loop(0, nblk, q_block, 0)
    dk_ref[...] = dkacc[...].astype(bf16)
    dv_ref[...] = dvacc[...].astype(bf16)
    pad = jnp.zeros((BLOCK, LANES), f32)
    sub = lax.broadcasted_iota(jnp.int32, (8, 2 * LANES), 0)
    for h in range(heads):
        for d in range(NEAR):
            t = gacc[h, d]
            if d in (0, 4):
                s = jnp.concatenate([jnp.sum(t, 0, keepdims=True), jnp.zeros((1, LANES), f32)], 1)
            else:
                wide = jnp.concatenate([t, pad], 1)
                s = jnp.zeros((8, 2 * LANES), f32)
                for a in range(BLOCK // 8):
                    s = s + pltpu.roll(wide[8 * a : 8 * a + 8], BLOCK - 8 * a, 1)
                for bit in (1, 2, 4):
                    s = jnp.where((sub & bit) > 0, pltpu.roll(s, 2 * LANES - bit, 1), s)
                s = jnp.sum(s, 0, keepdims=True)
            gsum_ref[h * NEAR + d : h * NEAR + d + 1, :] = s


def attn_bwd(lo, hi, q, k, v, qx, do, o, km, diag, scale):
    length, width = q.shape
    heads = diag.shape[0] // 2
    pairs = heads // 2
    nblk = length // BLOCK
    smem = pl.BlockSpec(memory_space=pltpu.SMEM)
    vmem = pl.BlockSpec(memory_space=pltpu.VMEM)
    f32, bf16 = jnp.float32, jnp.bfloat16
    act = jax.ShapeDtypeStruct((length, width), bf16)
    return pl.pallas_call(
        functools.partial(attn_bwd_kernel, heads=heads, scale=scale),
        out_shape=(act, act, act, jax.ShapeDtypeStruct((heads * NEAR, 256), f32)),
        in_specs=[smem, smem] + [vmem] * 8,
        out_specs=(vmem,) * 4,
        scratch_shapes=[
            pltpu.VMEM((pairs, 2 * BLOCK, 2 * LANES), bf16),
            pltpu.VMEM((pairs, 2 * BLOCK, 2 * LANES), bf16),
            pltpu.VMEM((heads, NEAR, BLOCK, BLOCK), f32),
            pltpu.VMEM((heads, NEAR, BLOCK, BLOCK), f32),
            pltpu.VMEM((length, width), f32),
            pltpu.VMEM((length, width), f32),
            pltpu.VMEM((BLOCK, width), f32),
        ],
        compiler_params=pltpu.CompilerParams(vmem_limit_bytes=60 << 20),
        cost_estimate=pl.CostEstimate(flops=10 * length * length * width, bytes_accessed=20 * length * width, transcendentals=length * length * heads),
    )(lo, hi, q, k, v, qx, do, o, km, diag)


def gelu_parts(v):
    mag = jnp.abs(v)
    t = 1.0 / (1.0 + (0.3275911 * 0.7071067811865476) * mag)
    poly = t * (0.127414796 + t * (-0.142248368 + t * (0.7107068705 + t * (-0.7265760135 + t * 0.5307027145))))
    gauss = jnp.exp(-0.5 * v * v)
    tail = poly * gauss
    phi = jnp.where(v < 0, tail, 1.0 - tail)
    return v * phi, phi + v * gauss * 0.3989422804014327


def flip_bits(index, mask, count):
    out = 0
    bit = 1
    while bit < count:
        a, b = (index // bit) % 2, (mask // bit) % 2
        out = out + bit * (a + b - 2 * a * b)
        bit *= 2
    return out


def ffn_kernel(
    xs, gs, g, win_hbm, wout_hbm,
    home, home_gate, produced, keep, give,
    win, wout, xr, gr, act, pg, gated, igs, ggs, dws, dwr, stage,
    wsem, own_sem, psem, ksem, xsend, xrecv, gsend, grecv, isend, irecv, qsend, qrecv, dsend, drecv,
    *, groups, dp_size, tiles,
):
    f32, bf16 = jnp.float32, jnp.bfloat16
    me = lax.axis_index("expert")
    dp = lax.axis_index("dp")
    core = dp % 2
    sibling = dp + 1 - 2 * core
    rows = xs.shape[1]
    width = xs.shape[2]
    hidden = win.shape[1]
    tile = hidden // tiles
    lanes = gs.shape[2]

    def there(peer):
        return (dp, peer)

    load_in = pltpu.make_async_copy(win_hbm, win, wsem.at[0])
    load_out = pltpu.make_async_copy(wout_hbm, wout, wsem.at[1])
    load_in.start()
    load_out.start()
    load_g = pltpu.make_async_copy(g, gated, wsem.at[2])
    load_g.start()

    barrier = pltpu.get_barrier_semaphore()

    def greet(s, _):
        pl.semaphore_signal(
            barrier, inc=1, device_id=there(flip_bits(me, s, groups)), device_id_type=pl.DeviceIdType.MESH
        )
        return 0
    lax.fori_loop(1, groups, greet, 0)
    pl.semaphore_signal(barrier, inc=1, device_id=(sibling, me), device_id_type=pl.DeviceIdType.MESH)
    pl.semaphore_wait(barrier, groups)

    def x_copy(peer, slot):
        return pltpu.make_async_remote_copy(
            src_ref=xs.at[peer], dst_ref=xr.at[slot], send_sem=xsend.at[peer], recv_sem=xrecv.at[slot],
            device_id=there(peer), device_id_type=pl.DeviceIdType.MESH)

    def g_copy(peer, slot):
        return pltpu.make_async_remote_copy(
            src_ref=gs.at[peer], dst_ref=gr.at[slot], send_sem=gsend.at[peer], recv_sem=grecv.at[slot],
            device_id=there(peer), device_id_type=pl.DeviceIdType.MESH)

    def i_copy(peer, slot):
        return pltpu.make_async_remote_copy(
            src_ref=igs.at[peer], dst_ref=home.at[slot], send_sem=isend.at[peer], recv_sem=irecv.at[slot],
            device_id=there(peer), device_id_type=pl.DeviceIdType.MESH)

    def q_copy(peer, slot):
        return pltpu.make_async_remote_copy(
            src_ref=ggs.at[peer], dst_ref=home_gate.at[slot], send_sem=qsend.at[peer], recv_sem=qrecv.at[slot],
            device_id=there(peer), device_id_type=pl.DeviceIdType.MESH)

    def send(s, _):
        peer = flip_bits(me, s, groups)
        x_copy(peer, me).start()
        g_copy(peer, me).start()
        return 0
    lax.fori_loop(1, groups, send, 0)
    own_x = pltpu.make_async_copy(xs.at[me], xr.at[me], own_sem.at[0])
    own_g = pltpu.make_async_copy(gs.at[me], gr.at[me], own_sem.at[1])
    own_x.start()
    own_g.start()
    load_in.wait()
    load_out.wait()
    load_g.wait()

    spot = (
        lax.broadcasted_iota(jnp.int32, (rows, lanes), 0)
        == lax.broadcasted_iota(jnp.int32, (rows, lanes), 1)
    )

    def work(p):
        x = xr[p]
        place = pl.ds(pl.multiple_of(p * rows, rows), rows)
        gg = gated[place, :]
        gate = jnp.sum(jnp.where(spot, gr[p, 0:1, :], 0.0), 1, keepdims=True)
        gated[place, :] = (gate * gg.astype(f32)).astype(bf16)
        total = jnp.zeros((rows, width), f32)
        gate_grad = jnp.zeros((rows, 1), f32)
        for t in range(tiles):
            cols = slice(t * tile, (t + 1) * tile)
            pre = matmul(x, win[:, cols])
            out_grad = matmul_nt(gg, wout[cols, :])
            value, slope = gelu_parts(pre)
            act[place, cols] = value.astype(bf16)
            gate_grad = gate_grad + jnp.sum(value * out_grad, 1, keepdims=True)
            low = (gate * out_grad * slope).astype(bf16)
            pg[place, cols] = low
            total = total + matmul_nt(low, win[:, cols])
        igs[p] = total.astype(bf16)
        row = jnp.sum(jnp.where(spot, gate_grad, 0.0), 0, keepdims=True)
        ggs[p] = jnp.broadcast_to(row, ggs.shape[1:])

    own_x.wait()
    own_g.wait()
    work(me)
    own_i = pltpu.make_async_copy(igs.at[me], home.at[me], own_sem.at[0])
    own_q = pltpu.make_async_copy(ggs.at[me], home_gate.at[me], own_sem.at[1])
    own_i.start()
    own_q.start()

    def chunk(s, _):
        peer = flip_bits(me, s, groups)
        x_copy(peer, peer).wait_recv()
        g_copy(peer, peer).wait_recv()
        work(peer)
        i_copy(peer, me).start()
        q_copy(peer, me).start()
        return 0
    lax.fori_loop(1, groups, chunk, 0)

    def d_copy(k):
        return pltpu.make_async_remote_copy(
            src_ref=dws.at[k % 2], dst_ref=dwr.at[k], send_sem=dsend.at[k], recv_sem=drecv.at[k],
            device_id=(sibling, me), device_id_type=pl.DeviceIdType.MESH)

    part = hidden // dp_size
    flat = groups * rows
    items = [(which, half) for half in range(dp_size // 2) for which in range(2)]

    def grad(which, quarter):
        span = pl.ds(pl.multiple_of(quarter * part, part), part)
        if which == 0:
            return matmul_tn(xr[...].reshape(flat, width), pg[:, span])
        return matmul_tn(act[:, span], gated[...])

    half_of = dp // 2
    for k, (which, half) in enumerate(items):
        if k >= 2:
            d_copy(k - 2).wait_send()
        dws[k % 2] = grad(which, 2 * half + 1 - core).astype(bf16)
        d_copy(k).start()

    span = stage.shape[1]
    copies = []
    for b in range(flat // span):
        if b >= 2:
            copies[b - 2].wait()
        stage[b % 2] = matmul(act[b * span : (b + 1) * span, :], wout[...]).astype(bf16)
        copy = pltpu.make_async_copy(stage.at[b % 2], produced.at[pl.ds(b * span, span)], psem.at[b % 2])
        copy.start()
        copies.append(copy)
    for copy in copies[-2:]:
        copy.wait()
    for k, (which, half) in enumerate(items):
        local = grad(which, 2 * half + core)
        d_copy(k).wait_recv()
        both = (local + dwr[k].astype(f32)).astype(bf16)
        dwr[k] = both
    outs = []
    for which in range(2):
        outs.append(pltpu.make_async_copy(dwr.at[half_of * 2 + which], keep.at[which], ksem.at[which]))
        outs.append(pltpu.make_async_copy(dwr.at[(1 - half_of) * 2 + which], give.at[which], ksem.at[2 + which]))
    for copy in outs:
        copy.start()
    for copy in outs:
        copy.wait()
    own_i.wait()
    own_q.wait()
    for k in (2, 3):
        d_copy(k).wait_send()

    def finish(s, _):
        peer = flip_bits(me, s, groups)
        x_copy(peer, me).wait_send()
        g_copy(peer, me).wait_send()
        i_copy(peer, me).wait_send()
        q_copy(peer, me).wait_send()
        i_copy(peer, peer).wait_recv()
        q_copy(peer, peer).wait_recv()
        return 0
    lax.fori_loop(1, groups, finish, 0)


def ffn(xs, gs, g, weight_in, weight_out, groups, dp_size, tiles=6):
    f32, bf16 = jnp.float32, jnp.bfloat16
    _, rows, width = xs.shape
    hidden = weight_in.shape[1]
    lanes = gs.shape[2]
    part = hidden // dp_size
    anywhere = pl.BlockSpec(memory_space=pl.ANY)
    sem = pltpu.SemaphoreType.DMA
    flat = groups * rows
    shape = jax.ShapeDtypeStruct
    return pl.pallas_call(
        functools.partial(ffn_kernel, groups=groups, dp_size=dp_size, tiles=tiles),
        out_shape=(
            shape((groups, rows, width), bf16),
            shape((groups, 8, lanes), f32),
            shape((flat, width), bf16),
            shape((2, width, part), bf16),
            shape((2, width, part), bf16),
        ),
        in_specs=[anywhere] * 5,
        out_specs=(anywhere,) * 5,
        scratch_shapes=[
            pltpu.VMEM((width, hidden), bf16),
            pltpu.VMEM((hidden, width), bf16),
            pltpu.VMEM((groups, rows, width), bf16),
            pltpu.VMEM((groups, 8, lanes), f32),
            pltpu.VMEM((flat, hidden), bf16),
            pltpu.VMEM((flat, hidden), bf16),
            pltpu.VMEM((flat, width), bf16),
            pltpu.VMEM((groups, rows, width), bf16),
            pltpu.VMEM((groups, 8, lanes), f32),
            pltpu.VMEM((2, width, part), bf16),
            pltpu.VMEM((4, width, part), bf16),
            pltpu.VMEM((2, flat // 8, width), bf16),
            sem((3,)), sem((2,)), sem((2,)), sem((4,)),
            sem((groups,)), sem((groups,)), sem((groups,)), sem((groups,)),
            sem((groups,)), sem((groups,)), sem((groups,)), sem((groups,)),
            sem((4,)), sem((4,)),
        ],
        compiler_params=pltpu.CompilerParams(
            collective_id=1, has_side_effects=True, vmem_limit_bytes=62 << 20
        ),
        cost_estimate=pl.CostEstimate(
            flops=12 * flat * width * hidden, bytes_accessed=40 << 20, transcendentals=flat * hidden
        ),
    )(xs, gs, g, weight_in, weight_out)


def rms_forward(values, norm_gain):
    inverse = lax.rsqrt(jnp.mean(values * values, -1, keepdims=True) + epsilon)
    return (values * inverse * norm_gain, inverse)


def rms_backward(values, inverse, norm_gain, upstream):
    scaled = upstream * norm_gain
    gain_grad = jnp.sum(upstream * values * inverse, 0)
    input_grad = inverse * (
        scaled - values * inverse * inverse * jnp.mean(scaled * values, -1, keepdims=True)
    )
    return (input_grad, gain_grad)


def matmul(left, right):
    return jnp.dot(left, right, preferred_element_type=jnp.float32)


def matmul_tn(left, right):
    return lax.dot_general(left, right, (((0,), (0,)), ((), ())), preferred_element_type=jnp.float32)


def matmul_nt(left, right):
    return lax.dot_general(left, right, (((1,), (1,)), ((), ())), preferred_element_type=jnp.float32)


def pieces(column):
    return jnp.stack(split3(column), 1)


def attention_operands(segment_row, bias_grid):
    f32 = jnp.float32
    first, last = segment_row[::BLOCK], segment_row[BLOCK - 1 :: BLOCK]
    lo = jnp.sum(segment_row[None, :] < first[:, None], 1) // BLOCK
    hi = (jnp.sum(segment_row[None, :] <= last[:, None], 1) + BLOCK - 1) // BLOCK
    lane = lax.iota(jnp.int32, LANES)[None, :]
    same = segment_row[:, None] == lane
    query_mask = jnp.where(same, masked_score, 0.0).astype(jnp.bfloat16)
    ones = ((lane % 64 >= 8) & (lane % 64 <= 10)).astype(f32)
    key_mask = jnp.where(lane < 8, 1.0 - same.astype(f32), ones).astype(jnp.bfloat16)
    relative = lax.iota(jnp.int32, 512) - 256
    buckets = bucket_of(jnp.concatenate([relative, 256 - lax.iota(jnp.int32, 512)]))
    hot = (lax.iota(jnp.int32, bias_grid.shape[0])[:, None] == buckets[None, :]).astype(f32)
    along = lax.dot_general(
        bias_grid, hot, (((0,), (0,)), ((), ())), precision=precise_setting
    )
    diag = jnp.concatenate([along[:, :512], along[:, 512:]], 0)
    return lo.astype(jnp.int32), hi.astype(jnp.int32), query_mask, key_mask, diag


def bias_grad(sums, heads, bucket_count):
    near = lax.broadcasted_iota(jnp.int32, (NEAR, 2 * LANES), 0)
    place = lax.broadcasted_iota(jnp.int32, (NEAR, 2 * LANES), 1)
    bucket = bucket_of((near - 2) * BLOCK + BLOCK - place)
    bucket = jnp.where(near == 0, 15, jnp.where(near == NEAR - 1, 31, bucket))
    hot = (bucket.reshape(-1)[:, None] == lax.iota(jnp.int32, bucket_count)[None, :]).astype(jnp.float32)
    return jnp.dot(sums.reshape(heads, -1), hot, precision=precise_setting).T


def per_device(
    tokens,
    segments,
    routes,
    cotangent,
    attn_gain,
    ffn_gain,
    query_weight,
    key_weight,
    value_weight,
    output_weight,
    position_bias_grid,
    router_weight,
    expert_in,
    expert_out,
):
    f32, bf16 = jnp.float32, jnp.bfloat16
    token_count, model_width = tokens.shape
    bucket_count, head_count = position_bias_grid.shape
    head_width = model_width // head_count
    score_scale = head_width ** (-0.5)
    experts_all = router_weight.shape[1]
    capacity = (5 * token_count + 4 * experts_all - 1) // (4 * experts_all)
    slot_rows = (capacity + 15) // 16 * 16
    slots = experts_all * slot_rows
    groups = lax.axis_size("expert")
    dp_size = lax.axis_size("dp")

    chosen = routes[:, 0]
    expert_hot = chosen[:, None] == lax.iota(jnp.int32, experts_all)[None, :]
    expert_float = expert_hot.astype(f32)
    before = lax.iota(jnp.int32, token_count)[:, None] > lax.iota(jnp.int32, token_count)[None, :]
    ranks = matmul(before.astype(bf16), expert_hot.astype(bf16))
    slot_rank = jnp.sum(ranks * expert_float, 1).astype(jnp.int32)
    token_slot = jnp.where(slot_rank < capacity, chosen * slot_rows + slot_rank, slots)
    to_slots = (lax.iota(jnp.int32, slots)[:, None] == token_slot[None, :]).astype(bf16)

    inputs = tokens.astype(f32)
    normed, inverse_one = rms_forward(inputs, attn_gain)
    normed_low = normed.astype(bf16)
    queries = (matmul(normed_low, query_weight).astype(bf16) * score_scale).astype(bf16)
    key_rows = matmul(normed_low, key_weight).astype(bf16)
    value_rows = matmul(normed_low, value_weight).astype(bf16)
    lo, hi, query_mask, key_mask, diag = attention_operands(segments[0], position_bias_grid)
    attended, query_extra = attn_fwd(
        lo, hi, queries, key_rows, value_rows, query_mask, key_mask, diag[:head_count]
    )
    middle = inputs + matmul(attended, output_weight)
    hidden_two, inverse_two = rms_forward(middle, ffn_gain)
    logits = jnp.dot(hidden_two, router_weight, precision=precise_setting)
    top_logit = jnp.max(logits, -1, keepdims=True)
    exponents_router = jnp.exp(logits - top_logit)
    router_probs = exponents_router / jnp.sum(exponents_router, -1, keepdims=True)
    gate_values = jnp.sum(router_probs * expert_float, 1)
    upstream = cotangent.astype(f32)

    def exchange(rows):
        rows = rows.reshape(experts_all, slot_rows, model_width)
        return lax.all_to_all(rows, "expert", split_axis=0, concat_axis=0, tiled=True)

    grad_arrived = exchange(matmul(to_slots, cotangent).astype(bf16))
    sent = matmul(to_slots, hidden_two.astype(bf16)).astype(bf16)
    gate_slots = jnp.sum(matmul(to_slots, pieces(gate_values)), 1)
    lanes = (slot_rows + LANES - 1) // LANES * LANES
    gate_slots = jnp.pad(gate_slots.reshape(experts_all, slot_rows), ((0, 0), (0, lanes - slot_rows)))
    gate_slots = jnp.broadcast_to(gate_slots[:, None, :], (experts_all, 8, lanes))
    home_grad, home_gate, produced, keep, give = ffn(
        sent.reshape(experts_all, slot_rows, model_width), gate_slots,
        grad_arrived.reshape(slots, model_width),
        expert_in[0], expert_out[0], groups, dp_size,
    )
    passed = lax.ppermute(give, "dp", [(i, (i + dp_size // 2) % dp_size) for i in range(dp_size)])
    weight_grads = keep.astype(f32) + passed.astype(f32)
    in_weight_grad, out_weight_grad = weight_grads[0], weight_grads[1]
    returned = exchange(produced).reshape(slots, model_width)
    expert_rows = matmul_tn(to_slots, returned)
    mixed = (middle + gate_values[:, None] * expert_rows).astype(bf16)

    gate_grad_slots = home_gate[:, 0, :slot_rows].reshape(slots)
    gate_grad = jnp.sum(matmul_tn(to_slots, pieces(gate_grad_slots)), 1)
    expert_input_grad = matmul_tn(to_slots, home_grad.reshape(slots, model_width))
    logit_grad = router_probs * (
        expert_float * gate_grad[:, None] - (gate_values * gate_grad)[:, None]
    )
    router_grad = jnp.dot(hidden_two.T, logit_grad, precision=precise_setting)
    hidden_grad = expert_input_grad + jnp.dot(
        logit_grad, router_weight.T, precision=precise_setting
    )
    middle_part, ffn_gain_grad = rms_backward(middle, inverse_two, ffn_gain, hidden_grad)
    middle_grad = upstream + middle_part
    branch_grad = middle_grad.astype(bf16)
    output_weight_grad = matmul_tn(attended, branch_grad)
    attended_grad = matmul_nt(branch_grad, output_weight).astype(bf16)
    query_grad, key_grad, value_grad, diag_sums = attn_bwd(
        lo, hi, queries, key_rows, value_rows, query_extra, attended_grad, attended, key_mask,
        diag, score_scale,
    )
    table_grad = bias_grad(diag_sums, head_count, bucket_count)
    query_weight_grad = matmul_tn(normed_low, query_grad)
    key_weight_grad = matmul_tn(normed_low, key_grad)
    value_weight_grad = matmul_tn(normed_low, value_grad)
    normed_grad = (
        matmul_nt(query_grad, query_weight)
        + matmul_nt(key_grad, key_weight)
        + matmul_nt(value_grad, value_weight)
    )
    input_part, attn_gain_grad = rms_backward(inputs, inverse_one, attn_gain, normed_grad)
    token_grad = (middle_grad + input_part).astype(bf16)
    weights = jnp.concatenate(
        [query_weight_grad, key_weight_grad, value_weight_grad, output_weight_grad], 1
    ).astype(bf16)
    weights = lax.psum(weights, ("dp", "expert")).astype(f32)
    weights = [weights[:, i * model_width : (i + 1) * model_width] for i in range(4)]
    small = lax.psum((table_grad, router_grad, attn_gain_grad, ffn_gain_grad), ("dp", "expert"))
    return (
        mixed,
        token_grad,
        small[2],
        small[3],
        *weights,
        small[0],
        small[1],
        in_weight_grad[None],
        out_weight_grad[None],
    )


def solution(mesh):
    rows = P(("dp", "expert"), None)
    return jax.shard_map(
        per_device,
        mesh=mesh,
        in_specs=(rows,) * 4 + (P(),) * 8 + (P("expert", None, None),) * 2,
        out_specs=(rows,) * 2 + (P(),) * 8 + (P("expert", None, "dp"), P("expert", "dp", None)),
        check_vma=False,
    )
```

```python
import functools

import jax
import jax.numpy as jnp
from jax import lax
from jax.experimental import pallas as pl
from jax.experimental.pallas import tpu as pltpu
from jax.sharding import PartitionSpec as P

epsilon = 1e-06
precise_setting = lax.Precision.HIGHEST
bucket_bounds = (12, 16, 23, 32, 46, 64, 91)
masked_score = -1e30
LANES = 128
BLOCK = 128
NEAR = 5


def bucket_of(relative):
    distance = jnp.abs(relative)
    beyond = jnp.zeros_like(distance)
    for threshold in bucket_bounds:
        beyond = beyond + (distance >= threshold).astype(jnp.int32)
    inside = jnp.where(distance < 8, distance, 8 + beyond)
    return inside + 16 * (relative > 0).astype(jnp.int32)


def dot_nt(a, b):
    return lax.dot_general(a, b, (((1,), (1,)), ((), ())), preferred_element_type=jnp.float32)


def dot_nn(a, b):
    return lax.dot_general(a, b, (((1,), (0,)), ((), ())), preferred_element_type=jnp.float32)


def split3(x):
    a = x.astype(jnp.bfloat16)
    r = x - a.astype(jnp.float32)
    b = r.astype(jnp.bfloat16)
    c = (r - b.astype(jnp.float32)).astype(jnp.bfloat16)
    return a, b, c


def attn_fwd_kernel(lo_ref, hi_ref, q_ref, k_ref, v_ref, qm_ref, km_ref, diag_ref, o_ref, qx_ref,
                    kext, vext, bias, sc, mx, acc, *, heads):
    pairs = heads // 2
    length = q_ref.shape[0]
    nblk = length // BLOCK
    lane = lax.broadcasted_iota(jnp.int32, (1, LANES), 1)
    low = lane < 64
    for h in range(heads):
        for d in range(NEAR):
            if d in (0, 4):
                col = diag_ref[h : h + 1, 0:1] if d == 0 else diag_ref[h : h + 1, 511:512]
                bias[h, d] = jnp.broadcast_to(col, (BLOCK, BLOCK))
            else:
                v = jnp.broadcast_to(diag_ref[h : h + 1, (d - 1) * 128 : (d - 1) * 128 + 256], (BLOCK, 256))
                bias[h, d] = pltpu.roll(v, 128, 1, stride=1, stride_axis=0)[:, :BLOCK]
    zero = jnp.zeros((BLOCK, LANES), jnp.bfloat16)

    def build(j, _):
        rows = pl.ds(pl.multiple_of(j * BLOCK, BLOCK), BLOCK)
        km = km_ref[rows, :]
        km0 = jnp.where(low, km, 0).astype(jnp.bfloat16)
        km1 = jnp.where((lane < 8) | (lane >= 64), km, 0).astype(jnp.bfloat16)
        one0 = jnp.broadcast_to(low.astype(jnp.bfloat16), (BLOCK, LANES))
        one1 = jnp.broadcast_to((~low).astype(jnp.bfloat16), (BLOCK, LANES))
        for p in range(pairs):
            cols = pl.ds(p * LANES, LANES)
            kk = k_ref[rows, cols]
            vv = v_ref[rows, cols]
            kext[p, j] = jnp.concatenate([
                jnp.concatenate([jnp.where(low, kk, zero), km0], 1),
                jnp.concatenate([jnp.where(low, zero, kk), km1], 1)], 0)
            vext[p, j] = jnp.concatenate([
                jnp.concatenate([jnp.where(low, vv, zero), one0], 1),
                jnp.concatenate([jnp.where(low, zero, vv), one1], 1)], 0)
        return 0
    lax.fori_loop(0, nblk, build, 0)

    def q_block(i, _):
        lo = lo_ref[i]
        hi = hi_ref[i]
        rows = pl.ds(pl.multiple_of(i * BLOCK, BLOCK), BLOCK)
        qm = qm_ref[rows, :]
        mx[...] = jnp.full(mx.shape, -3e38, jnp.float32)

        def pass1(j, _):
            d = jnp.clip(j - i, -2, 2) + 2
            for p in range(pairs):
                qe = jnp.concatenate([q_ref[rows, pl.ds(p * LANES, LANES)], qm], 1)
                s = dot_nt(qe, kext[p, j])
                s0 = s[:, :BLOCK] + bias[2 * p, d]
                s1 = s[:, BLOCK:] + bias[2 * p + 1, d]
                sc[p, j, :, :BLOCK] = s0
                sc[p, j, :, BLOCK:] = s1
                mx[2 * p] = jnp.maximum(mx[2 * p], s0)
                mx[2 * p + 1] = jnp.maximum(mx[2 * p + 1], s1)
            return 0
        lax.fori_loop(lo, hi, pass1, 0)
        for h in range(heads):
            mx[h] = jnp.broadcast_to(jnp.max(mx[h], 1, keepdims=True), (BLOCK, LANES))
        acc[...] = jnp.zeros_like(acc)

        def pass2(j, _):
            for p in range(pairs):
                p0 = jnp.exp(sc[p, j, :, :BLOCK] - mx[2 * p]).astype(jnp.bfloat16)
                p1 = jnp.exp(sc[p, j, :, BLOCK:] - mx[2 * p + 1]).astype(jnp.bfloat16)
                acc[p] += dot_nn(jnp.concatenate([p0, p1], 1), vext[p, j])
            return 0
        lax.fori_loop(lo, hi, pass2, 0)
        m64 = lane % 64
        for p in range(pairs):
            cols = pl.ds(p * LANES, LANES)
            total = acc[p, :, LANES:]
            o_ref[rows, cols] = (acc[p, :, :LANES] / total).astype(jnp.bfloat16)
            lse = jnp.where(low, mx[2 * p], mx[2 * p + 1]) + jnp.log(total)
            a, b, c = split3(lse)
            ext = jnp.where(m64 == 8, -a, jnp.where(m64 == 9, -b, jnp.where(m64 == 10, -c, qm)))
            qx_ref[rows, cols] = ext.astype(jnp.bfloat16)
        return 0
    lax.fori_loop(0, nblk, q_block, 0)


def attn_fwd(lo, hi, q, k, v, qm, km, diag):
    length, width = q.shape
    heads = diag.shape[0]
    pairs = heads // 2
    nblk = length // BLOCK
    smem = pl.BlockSpec(memory_space=pltpu.SMEM)
    vmem = pl.BlockSpec(memory_space=pltpu.VMEM)
    f32, bf16 = jnp.float32, jnp.bfloat16
    return pl.pallas_call(
        functools.partial(attn_fwd_kernel, heads=heads),
        out_shape=(jax.ShapeDtypeStruct((length, width), bf16), jax.ShapeDtypeStruct((length, width), bf16)),
        in_specs=[smem, smem] + [vmem] * 6,
        out_specs=(vmem, vmem),
        scratch_shapes=[
            pltpu.VMEM((pairs, nblk, 2 * BLOCK, 2 * LANES), bf16),
            pltpu.VMEM((pairs, nblk, 2 * BLOCK, 2 * LANES), bf16),
            pltpu.VMEM((heads, NEAR, BLOCK, BLOCK), f32),
            pltpu.VMEM((pairs, nblk, BLOCK, 2 * BLOCK), f32),
            pltpu.VMEM((heads, BLOCK, LANES), f32),
            pltpu.VMEM((pairs, BLOCK, 2 * LANES), f32),
        ],
        compiler_params=pltpu.CompilerParams(vmem_limit_bytes=60 << 20),
        cost_estimate=pl.CostEstimate(flops=4 * length * length * width, bytes_accessed=10 * length * width, transcendentals=length * length * heads),
    )(lo, hi, q, k, v, qm, km, diag)


def attn_bwd_kernel(lo_ref, hi_ref, q_ref, k_ref, v_ref, qx_ref, do_ref, o_ref, km_ref, diag_ref,
                    dq_ref, dk_ref, dv_ref, gsum_ref,
                    qst, dost, bias, gacc, dkacc, dvacc, dqacc, *, heads, scale):
    pairs = heads // 2
    length = q_ref.shape[0]
    nblk = length // BLOCK
    lane = lax.broadcasted_iota(jnp.int32, (1, LANES), 1)
    low = lane < 64
    m64 = lane % 64
    f32, bf16 = jnp.float32, jnp.bfloat16
    for h in range(heads):
        for d in range(NEAR):
            if d in (0, 4):
                col = diag_ref[h : h + 1, 0:1] if d == 0 else diag_ref[h : h + 1, 511:512]
                bias[h, d] = jnp.broadcast_to(col, (BLOCK, BLOCK))
            else:
                base = (3 - d) * BLOCK
                v = jnp.broadcast_to(diag_ref[heads + h : heads + h + 1, base : base + 256], (BLOCK, 256))
                bias[h, d] = pltpu.roll(v, 128, 1, stride=1, stride_axis=0)[:, :BLOCK]
    zero = jnp.zeros((BLOCK, LANES), bf16)
    gacc[...] = jnp.zeros_like(gacc)
    dkacc[...] = jnp.zeros_like(dkacc)
    dvacc[...] = jnp.zeros_like(dvacc)

    def q_block(i, _):
        lo = lo_ref[i]
        hi = hi_ref[i]
        rows = pl.ds(pl.multiple_of(i * BLOCK, BLOCK), BLOCK)
        for p in range(pairs):
            cols = pl.ds(p * LANES, LANES)
            qq = q_ref[rows, cols]
            qx = qx_ref[rows, cols]
            qst[p] = jnp.concatenate([
                jnp.concatenate([jnp.where(low, qq, zero), jnp.where(low, qx, zero)], 1),
                jnp.concatenate([jnp.where(low, zero, qq), jnp.where((lane < 8) | ~low, qx, zero)], 1)], 0)
            dd = do_ref[rows, cols]
            prod = dd.astype(f32) * o_ref[rows, cols].astype(f32)
            in0 = jnp.sum(jnp.where(low, prod, 0.0), 1, keepdims=True)
            in1 = jnp.sum(jnp.where(low, 0.0, prod), 1, keepdims=True)
            inner = jnp.where(low, in0, in1)
            a, b, c = split3(inner)
            ext = jnp.where(m64 == 8, -a, jnp.where(m64 == 9, -b, jnp.where(m64 == 10, -c, zero)))
            dost[p] = jnp.concatenate([
                jnp.concatenate([jnp.where(low, dd, zero), jnp.where(low, ext, zero)], 1),
                jnp.concatenate([jnp.where(low, zero, dd), jnp.where(low, zero, ext)], 1)], 0)
        dqacc[...] = jnp.zeros_like(dqacc)

        def k_block(j, _):
            d = jnp.clip(j - i, -2, 2) + 2
            krows = pl.ds(pl.multiple_of(j * BLOCK, BLOCK), BLOCK)
            km = km_ref[krows, :]
            for p in range(pairs):
                cols = pl.ds(p * LANES, LANES)
                kk = k_ref[krows, cols]
                vv = v_ref[krows, cols]
                qs = qst[p]
                ds_ = dost[p]
                st = dot_nt(jnp.concatenate([kk, km], 1), qs)
                dpt = dot_nt(jnp.concatenate([vv, km], 1), ds_)
                p0 = jnp.exp(st[:, :BLOCK] + bias[2 * p, d])
                p1 = jnp.exp(st[:, BLOCK:] + bias[2 * p + 1, d])
                d0 = p0 * dpt[:, :BLOCK]
                d1 = p1 * dpt[:, BLOCK:]
                gacc[2 * p, d] += d0
                gacc[2 * p + 1, d] += d1
                pb = jnp.concatenate([p0.astype(bf16), p1.astype(bf16)], 1)
                d0b = d0.astype(bf16)
                d1b = d1.astype(bf16)
                db = jnp.concatenate([d0b, d1b], 1)
                dvacc[krows, cols] += dot_nn(pb, ds_[:, :LANES])
                dkacc[krows, cols] += dot_nn(db, qs[:, :LANES])
                dst = jnp.concatenate([d0b.T, d1b.T], 1)
                kz = jnp.concatenate([jnp.where(low, kk, zero), jnp.where(low, zero, kk)], 0)
                dqacc[:, cols] += dot_nn(dst, kz)
            return 0
        lax.fori_loop(lo, hi, k_block, 0)
        dq_ref[rows, :] = (dqacc[...] * scale).astype(bf16)
        return 0
    lax.fori_loop(0, nblk, q_block, 0)
    dk_ref[...] = dkacc[...].astype(bf16)
    dv_ref[...] = dvacc[...].astype(bf16)
    pad = jnp.zeros((BLOCK, LANES), f32)
    sub = lax.broadcasted_iota(jnp.int32, (8, 2 * LANES), 0)
    for h in range(heads):
        for d in range(NEAR):
            t = gacc[h, d]
            if d in (0, 4):
                s = jnp.concatenate([jnp.sum(t, 0, keepdims=True), jnp.zeros((1, LANES), f32)], 1)
            else:
                wide = jnp.concatenate([t, pad], 1)
                s = jnp.zeros((8, 2 * LANES), f32)
                for a in range(BLOCK // 8):
                    s = s + pltpu.roll(wide[8 * a : 8 * a + 8], BLOCK - 8 * a, 1)
                for bit in (1, 2, 4):
                    s = jnp.where((sub & bit) > 0, pltpu.roll(s, 2 * LANES - bit, 1), s)
                s = jnp.sum(s, 0, keepdims=True)
            gsum_ref[h * NEAR + d : h * NEAR + d + 1, :] = s


def attn_bwd(lo, hi, q, k, v, qx, do, o, km, diag, scale):
    length, width = q.shape
    heads = diag.shape[0] // 2
    pairs = heads // 2
    nblk = length // BLOCK
    smem = pl.BlockSpec(memory_space=pltpu.SMEM)
    vmem = pl.BlockSpec(memory_space=pltpu.VMEM)
    f32, bf16 = jnp.float32, jnp.bfloat16
    act = jax.ShapeDtypeStruct((length, width), bf16)
    return pl.pallas_call(
        functools.partial(attn_bwd_kernel, heads=heads, scale=scale),
        out_shape=(act, act, act, jax.ShapeDtypeStruct((heads * NEAR, 256), f32)),
        in_specs=[smem, smem] + [vmem] * 8,
        out_specs=(vmem,) * 4,
        scratch_shapes=[
            pltpu.VMEM((pairs, 2 * BLOCK, 2 * LANES), bf16),
            pltpu.VMEM((pairs, 2 * BLOCK, 2 * LANES), bf16),
            pltpu.VMEM((heads, NEAR, BLOCK, BLOCK), f32),
            pltpu.VMEM((heads, NEAR, BLOCK, BLOCK), f32),
            pltpu.VMEM((length, width), f32),
            pltpu.VMEM((length, width), f32),
            pltpu.VMEM((BLOCK, width), f32),
        ],
        compiler_params=pltpu.CompilerParams(vmem_limit_bytes=60 << 20),
        cost_estimate=pl.CostEstimate(flops=10 * length * length * width, bytes_accessed=20 * length * width, transcendentals=length * length * heads),
    )(lo, hi, q, k, v, qx, do, o, km, diag)


def gelu_parts(v):
    mag = jnp.abs(v)
    t = 1.0 / (1.0 + (0.3275911 * 0.7071067811865476) * mag)
    poly = t * (0.127414796 + t * (-0.142248368 + t * (0.7107068705 + t * (-0.7265760135 + t * 0.5307027145))))
    gauss = jnp.exp(-0.5 * v * v)
    tail = poly * gauss
    phi = jnp.where(v < 0, tail, 1.0 - tail)
    return v * phi, phi + v * gauss * 0.3989422804014327


def flip_bits(index, mask, count):
    out = 0
    bit = 1
    while bit < count:
        a, b = (index // bit) % 2, (mask // bit) % 2
        out = out + bit * (a + b - 2 * a * b)
        bit *= 2
    return out


def ffn_kernel(
    xs, gs, g, win_hbm, wout_hbm,
    home, home_gate, produced, keep, give,
    win, wout, xr, gr, act, pg, gated, igs, ggs, dws, dwr, stage,
    wsem, own_sem, psem, ksem, xsend, xrecv, gsend, grecv, isend, irecv, qsend, qrecv, dsend, drecv,
    *, groups, dp_size, tiles,
):
    f32, bf16 = jnp.float32, jnp.bfloat16
    me = lax.axis_index("expert")
    dp = lax.axis_index("dp")
    core = dp % 2
    sibling = dp + 1 - 2 * core
    rows = xs.shape[1]
    width = xs.shape[2]
    hidden = win.shape[1]
    tile = hidden // tiles
    lanes = gs.shape[2]

    def there(peer):
        return (dp, peer)

    load_in = pltpu.make_async_copy(win_hbm, win, wsem.at[0])
    load_out = pltpu.make_async_copy(wout_hbm, wout, wsem.at[1])
    load_in.start()
    load_out.start()
    load_g = pltpu.make_async_copy(g, gated, wsem.at[2])
    load_g.start()

    barrier = pltpu.get_barrier_semaphore()

    def greet(s, _):
        pl.semaphore_signal(
            barrier, inc=1, device_id=there(flip_bits(me, s, groups)), device_id_type=pl.DeviceIdType.MESH
        )
        return 0
    lax.fori_loop(1, groups, greet, 0)
    pl.semaphore_signal(barrier, inc=1, device_id=(sibling, me), device_id_type=pl.DeviceIdType.MESH)
    pl.semaphore_wait(barrier, groups)

    def x_copy(peer, slot):
        return pltpu.make_async_remote_copy(
            src_ref=xs.at[peer], dst_ref=xr.at[slot], send_sem=xsend.at[peer], recv_sem=xrecv.at[slot],
            device_id=there(peer), device_id_type=pl.DeviceIdType.MESH)

    def g_copy(peer, slot):
        return pltpu.make_async_remote_copy(
            src_ref=gs.at[peer], dst_ref=gr.at[slot], send_sem=gsend.at[peer], recv_sem=grecv.at[slot],
            device_id=there(peer), device_id_type=pl.DeviceIdType.MESH)

    def i_copy(peer, slot):
        return pltpu.make_async_remote_copy(
            src_ref=igs.at[peer], dst_ref=home.at[slot], send_sem=isend.at[peer], recv_sem=irecv.at[slot],
            device_id=there(peer), device_id_type=pl.DeviceIdType.MESH)

    def q_copy(peer, slot):
        return pltpu.make_async_remote_copy(
            src_ref=ggs.at[peer], dst_ref=home_gate.at[slot], send_sem=qsend.at[peer], recv_sem=qrecv.at[slot],
            device_id=there(peer), device_id_type=pl.DeviceIdType.MESH)

    def send(s, _):
        peer = flip_bits(me, s, groups)
        x_copy(peer, me).start()
        g_copy(peer, me).start()
        return 0
    lax.fori_loop(1, groups, send, 0)
    own_x = pltpu.make_async_copy(xs.at[me], xr.at[me], own_sem.at[0])
    own_g = pltpu.make_async_copy(gs.at[me], gr.at[me], own_sem.at[1])
    own_x.start()
    own_g.start()
    load_in.wait()
    load_out.wait()
    load_g.wait()

    spot = (
        lax.broadcasted_iota(jnp.int32, (rows, lanes), 0)
        == lax.broadcasted_iota(jnp.int32, (rows, lanes), 1)
    )

    def work(p):
        x = xr[p]
        place = pl.ds(pl.multiple_of(p * rows, rows), rows)
        gg = gated[place, :]
        gate = jnp.sum(jnp.where(spot, gr[p, 0:1, :], 0.0), 1, keepdims=True)
        gated[place, :] = (gate * gg.astype(f32)).astype(bf16)
        total = jnp.zeros((rows, width), f32)
        gate_grad = jnp.zeros((rows, 1), f32)
        for t in range(tiles):
            cols = slice(t * tile, (t + 1) * tile)
            pre = matmul(x, win[:, cols])
            out_grad = matmul_nt(gg, wout[cols, :])
            value, slope = gelu_parts(pre)
            act[place, cols] = value.astype(bf16)
            gate_grad = gate_grad + jnp.sum(value * out_grad, 1, keepdims=True)
            low = (gate * out_grad * slope).astype(bf16)
            pg[place, cols] = low
            total = total + matmul_nt(low, win[:, cols])
        igs[p] = total.astype(bf16)
        row = jnp.sum(jnp.where(spot, gate_grad, 0.0), 0, keepdims=True)
        ggs[p] = jnp.broadcast_to(row, ggs.shape[1:])

    own_x.wait()
    own_g.wait()
    work(me)
    own_i = pltpu.make_async_copy(igs.at[me], home.at[me], own_sem.at[0])
    own_q = pltpu.make_async_copy(ggs.at[me], home_gate.at[me], own_sem.at[1])
    own_i.start()
    own_q.start()

    def chunk(s, _):
        peer = flip_bits(me, s, groups)
        x_copy(peer, peer).wait_recv()
        g_copy(peer, peer).wait_recv()
        work(peer)
        i_copy(peer, me).start()
        q_copy(peer, me).start()
        return 0
    lax.fori_loop(1, groups, chunk, 0)

    def d_copy(k):
        return pltpu.make_async_remote_copy(
            src_ref=dws.at[k % 2], dst_ref=dwr.at[k], send_sem=dsend.at[k], recv_sem=drecv.at[k],
            device_id=(sibling, me), device_id_type=pl.DeviceIdType.MESH)

    part = hidden // dp_size
    flat = groups * rows
    items = [(which, half) for half in range(dp_size // 2) for which in range(2)]

    def grad(which, quarter):
        span = pl.ds(pl.multiple_of(quarter * part, part), part)
        if which == 0:
            return matmul_tn(xr[...].reshape(flat, width), pg[:, span])
        return matmul_tn(act[:, span], gated[...])

    half_of = dp // 2
    for k, (which, half) in enumerate(items):
        if k >= 2:
            d_copy(k - 2).wait_send()
        dws[k % 2] = grad(which, 2 * half + 1 - core).astype(bf16)
        d_copy(k).start()

    span = stage.shape[1]
    copies = []
    for b in range(flat // span):
        if b >= 2:
            copies[b - 2].wait()
        stage[b % 2] = matmul(act[b * span : (b + 1) * span, :], wout[...]).astype(bf16)
        copy = pltpu.make_async_copy(stage.at[b % 2], produced.at[pl.ds(b * span, span)], psem.at[b % 2])
        copy.start()
        copies.append(copy)
    for copy in copies[-2:]:
        copy.wait()
    for k, (which, half) in enumerate(items):
        local = grad(which, 2 * half + core)
        d_copy(k).wait_recv()
        both = (local + dwr[k].astype(f32)).astype(bf16)
        dwr[k] = both
    outs = []
    for which in range(2):
        outs.append(pltpu.make_async_copy(dwr.at[half_of * 2 + which], keep.at[which], ksem.at[which]))
        outs.append(pltpu.make_async_copy(dwr.at[(1 - half_of) * 2 + which], give.at[which], ksem.at[2 + which]))
    for copy in outs:
        copy.start()
    for copy in outs:
        copy.wait()
    own_i.wait()
    own_q.wait()
    for k in (2, 3):
        d_copy(k).wait_send()

    def finish(s, _):
        peer = flip_bits(me, s, groups)
        x_copy(peer, me).wait_send()
        g_copy(peer, me).wait_send()
        i_copy(peer, me).wait_send()
        q_copy(peer, me).wait_send()
        i_copy(peer, peer).wait_recv()
        q_copy(peer, peer).wait_recv()
        return 0
    lax.fori_loop(1, groups, finish, 0)


def ffn(xs, gs, g, weight_in, weight_out, groups, dp_size, tiles=6):
    f32, bf16 = jnp.float32, jnp.bfloat16
    _, rows, width = xs.shape
    hidden = weight_in.shape[1]
    lanes = gs.shape[2]
    part = hidden // dp_size
    anywhere = pl.BlockSpec(memory_space=pl.ANY)
    sem = pltpu.SemaphoreType.DMA
    flat = groups * rows
    shape = jax.ShapeDtypeStruct
    return pl.pallas_call(
        functools.partial(ffn_kernel, groups=groups, dp_size=dp_size, tiles=tiles),
        out_shape=(
            shape((groups, rows, width), bf16),
            shape((groups, 8, lanes), f32),
            shape((flat, width), bf16),
            shape((2, width, part), bf16),
            shape((2, width, part), bf16),
        ),
        in_specs=[anywhere] * 5,
        out_specs=(anywhere,) * 5,
        scratch_shapes=[
            pltpu.VMEM((width, hidden), bf16),
            pltpu.VMEM((hidden, width), bf16),
            pltpu.VMEM((groups, rows, width), bf16),
            pltpu.VMEM((groups, 8, lanes), f32),
            pltpu.VMEM((flat, hidden), bf16),
            pltpu.VMEM((flat, hidden), bf16),
            pltpu.VMEM((flat, width), bf16),
            pltpu.VMEM((groups, rows, width), bf16),
            pltpu.VMEM((groups, 8, lanes), f32),
            pltpu.VMEM((2, width, part), bf16),
            pltpu.VMEM((4, width, part), bf16),
            pltpu.VMEM((2, flat // 8, width), bf16),
            sem((3,)), sem((2,)), sem((2,)), sem((4,)),
            sem((groups,)), sem((groups,)), sem((groups,)), sem((groups,)),
            sem((groups,)), sem((groups,)), sem((groups,)), sem((groups,)),
            sem((4,)), sem((4,)),
        ],
        compiler_params=pltpu.CompilerParams(
            collective_id=1, has_side_effects=True, vmem_limit_bytes=62 << 20
        ),
        cost_estimate=pl.CostEstimate(
            flops=12 * flat * width * hidden, bytes_accessed=40 << 20, transcendentals=flat * hidden
        ),
    )(xs, gs, g, weight_in, weight_out)


def fold_steps(rows, cols, bits):
    steps = []
    for bit in bits:
        if rows % 32 == 0:
            rows = rows // 2
            steps.append((bit, "rows", rows, cols))
        elif cols % 256 == 0:
            cols = cols // 2
            steps.append((bit, "cols", rows, cols))
        else:
            steps.append((bit, "whole", rows, cols))
    return steps


def reduce_kernel(
    normed, attended, branch, dq, dk, dv, wq, wk, wv, tokens, middle_grad, inverse, gain, small_in,
    sums, token_grad, small_out,
    acc, outbox, inbox, small_box, small_sent,
    ssend, srecv, tsend, trecv,
    *, dp_bits, expert_bits,
):
    f32, bf16 = jnp.float32, jnp.bfloat16
    dp = lax.axis_index("dp")
    ex = lax.axis_index("expert")
    MESH = pl.DeviceIdType.MESH
    length, width = normed.shape

    def own_bit(bit):
        axis, place = bit
        return (dp // 2 ** place) % 2 if axis == "dp" else (ex // 2 ** place) % 2

    def partner(bit):
        axis, place = bit
        flip = (1 - 2 * own_bit(bit)) * 2 ** place
        return (dp + flip, ex) if axis == "dp" else (dp, ex + flip)

    dpb = [("dp", i) for i in range(dp_bits)]
    exb = [("expert", i) for i in range(expert_bits)]
    orders = [
        [dpb[0], dpb[1], exb[0]] + dpb[2:] + exb[1:],
        [dpb[0], exb[0], dpb[1]] + dpb[2:] + exb[1:],
    ]
    every = dpb + exb
    count = len(every)

    barrier = pltpu.get_barrier_semaphore()
    for bit in every:
        pl.semaphore_signal(barrier, inc=1, device_id=partner(bit), device_id_type=MESH)
    pl.semaphore_wait(barrier, count)

    lefts = (attended, normed, normed, normed)
    rights = (branch, dv, dk, dq)
    streams = []
    for s in range(4):
        steps = fold_steps(width, width, orders[s % 2])
        row, col = 0, 0
        at = 0
        plan = []
        for bit, kind, r, c in steps:
            mine = own_bit(bit)
            if kind == "rows":
                keep_at, send_at = (row + mine * r, col), (row + (1 - mine) * r, col)
            elif kind == "cols":
                keep_at, send_at = (row, col + mine * c), (row, col + (1 - mine) * c)
            else:
                keep_at, send_at = (row, col), (row, col)
            plan.append((bit, kind, r, c, at, keep_at, send_at))
            row, col = keep_at
            at += r
        streams.append(plan)

    def rs_copy(s, k):
        bit, kind, r, c, at, _, _ = streams[s][k]
        return pltpu.make_async_remote_copy(
            src_ref=outbox.at[s, pl.ds(at, r), pl.ds(0, c)],
            dst_ref=inbox.at[s, pl.ds(at, r), pl.ds(0, c)],
            send_sem=ssend.at[s, k], recv_sem=srecv.at[s, k],
            device_id=partner(bit), device_id_type=MESH)

    def block(s, at, r, c):
        row, col = at
        row = pl.multiple_of(row, 16) if not isinstance(row, int) else row
        col = pl.multiple_of(col, 128) if not isinstance(col, int) else col
        return sums.at[s, pl.ds(row, r), pl.ds(col, c)]

    def ag_copy(s, k, incoming):
        bit, kind, r, c, _, keep_at, send_at = streams[s][k]
        ref = block(s, send_at if incoming else keep_at, r, c)
        return pltpu.make_async_remote_copy(
            src_ref=ref, dst_ref=ref,
            send_sem=ssend.at[s, count + k], recv_sem=srecv.at[s, count + k],
            device_id=partner(bit), device_id_type=MESH)

    half = width // 2
    core = own_bit(dpb[0])

    def grad(s, which):
        span = pl.ds(pl.multiple_of(which * half, half), half)
        return matmul_tn(lefts[s][:, span], rights[s][...])

    def local(s, k, at):
        base = streams[s][0][5][0]
        row, col = at
        row = row - base
        row = pl.multiple_of(row, 16) if not isinstance(row, int) else row
        col = pl.multiple_of(col, 128) if not isinstance(col, int) else col
        return row, col

    def phase(s, k):
        plan = streams[s]
        if k == 0:
            outbox[s, 0:half, :] = grad(s, 1 - core).astype(bf16)
            rs_copy(s, 0).start()
            acc[s] = grad(s, core)
            return
        if k <= count:
            bit, kind, r, c, at, keep_at, _ = plan[k - 1]
            rs_copy(s, k - 1).wait_recv()
            row, col = local(s, k - 1, keep_at)
            view = acc.at[s, pl.ds(row, r), pl.ds(col, c)]
            own = outbox[s, at : at + r, 0:c].astype(f32) if kind == "whole" else view[...]
            view[...] = own + inbox[s, at : at + r, 0:c].astype(f32)
            if k < count:
                bit, kind, r, c, at, keep_at, send_at = plan[k]
                row, col = local(s, k, send_at)
                outbox[s, at : at + r, 0:c] = acc[s, pl.ds(row, r), pl.ds(col, c)].astype(bf16)
                rs_copy(s, k).start()
                return
            block(s, keep_at, r, c)[...] = view[...].astype(bf16)
        g = 2 * count - 1 - k
        if k > count:
            prev = g + 1
            if plan[prev][1] != "whole":
                ag_copy(s, prev, True).wait_recv()
        if g >= 0 and plan[g][1] != "whole":
            ag_copy(s, g, False).start()

    gain_row = gain[...]
    rows = 256

    def norm_block(i, gain_grad):
        span = pl.ds(pl.multiple_of(i * rows, rows), rows)
        grads = (
            matmul_nt(dq[span, :], wq[...]) + matmul_nt(dk[span, :], wk[...]) + matmul_nt(dv[span, :], wv[...])
        )
        x = tokens[span, :].astype(f32)
        inv = inverse[span, :]
        scaled = grads * gain_row
        mean = jnp.sum(scaled * x, 1, keepdims=True) * (1.0 / width)
        part = inv * (scaled - x * (inv * inv * mean))
        token_grad[span, :] = (middle_grad[span, :] + part).astype(bf16)
        return gain_grad + jnp.sum(grads * (x * inv), 0, keepdims=True)

    def small_copy(k):
        return pltpu.make_async_remote_copy(
            src_ref=small_sent.at[k], dst_ref=small_box.at[k],
            send_sem=tsend.at[k], recv_sem=trecv.at[k],
            device_id=partner(every[k]), device_id_type=MESH)

    def small_phase(k):
        if k == 0:
            gain_grad = lax.fori_loop(0, length // rows, norm_block, jnp.zeros((1, width), f32))
            small_out[...] = small_in[...]
            for i in range(width // LANES):
                small_out[i : i + 1, :] = gain_grad[:, i * LANES : (i + 1) * LANES]
        else:
            small_copy(k - 1).wait_recv()
            small_out[...] = small_out[...] + small_box[k - 1]
        if k < count:
            small_sent[k] = small_out[...]
            small_copy(k).start()

    last = 2 * count
    for t in range(last + 4):
        for s in range(4):
            if 0 <= t - s <= last:
                phase(s, t - s)
        if 4 <= t and t - 4 <= count:
            small_phase(t - 4)
    for s in range(4):
        for k in range(count):
            rs_copy(s, k).wait_send()
            if streams[s][k][1] != "whole":
                ag_copy(s, k, False).wait_send()
    for k in range(count):
        small_copy(k).wait_send()


def reduce_grads(normed, attended, branch, dq, dk, dv, wq, wk, wv, tokens, middle_grad, inverse, gain, small, dp_size, groups):
    f32, bf16 = jnp.float32, jnp.bfloat16
    length, width = normed.shape
    dp_bits, expert_bits = dp_size.bit_length() - 1, groups.bit_length() - 1
    count = dp_bits + expert_bits
    box = sum(step[2] for step in fold_steps(width, width, range(count)))
    vmem = pl.BlockSpec(memory_space=pltpu.VMEM)
    sem = pltpu.SemaphoreType.DMA
    shape = jax.ShapeDtypeStruct
    return pl.pallas_call(
        functools.partial(reduce_kernel, dp_bits=dp_bits, expert_bits=expert_bits),
        out_shape=(shape((4, width, width), bf16), shape((length, width), bf16), shape(small.shape, f32)),
        in_specs=[vmem] * 14,
        out_specs=(vmem,) * 3,
        scratch_shapes=[
            pltpu.VMEM((4, width // 2, width), f32),
            pltpu.VMEM((4, box, width), bf16),
            pltpu.VMEM((4, box, width), bf16),
            pltpu.VMEM((count,) + small.shape, f32),
            pltpu.VMEM((count,) + small.shape, f32),
            sem((4, 2 * count)), sem((4, 2 * count)), sem((count,)), sem((count,)),
        ],
        compiler_params=pltpu.CompilerParams(
            collective_id=2, has_side_effects=True, vmem_limit_bytes=62 << 20
        ),
        cost_estimate=pl.CostEstimate(
            flops=14 * length * width * width, bytes_accessed=30 << 20, transcendentals=0
        ),
    )(normed, attended, branch, dq, dk, dv, wq, wk, wv, tokens, middle_grad, inverse, gain, small)


def rms_forward(values, norm_gain):
    inverse = lax.rsqrt(jnp.mean(values * values, -1, keepdims=True) + epsilon)
    return (values * inverse * norm_gain, inverse)


def rms_backward(values, inverse, norm_gain, upstream):
    scaled = upstream * norm_gain
    gain_grad = jnp.sum(upstream * values * inverse, 0)
    input_grad = inverse * (
        scaled - values * inverse * inverse * jnp.mean(scaled * values, -1, keepdims=True)
    )
    return (input_grad, gain_grad)


def matmul(left, right):
    return jnp.dot(left, right, preferred_element_type=jnp.float32)


def matmul_tn(left, right):
    return lax.dot_general(left, right, (((0,), (0,)), ((), ())), preferred_element_type=jnp.float32)


def matmul_nt(left, right):
    return lax.dot_general(left, right, (((1,), (1,)), ((), ())), preferred_element_type=jnp.float32)


def pieces(column):
    return jnp.stack(split3(column), 1)


def attention_operands(segment_row, bias_grid):
    f32 = jnp.float32
    first, last = segment_row[::BLOCK], segment_row[BLOCK - 1 :: BLOCK]
    lo = jnp.sum(segment_row[None, :] < first[:, None], 1) // BLOCK
    hi = (jnp.sum(segment_row[None, :] <= last[:, None], 1) + BLOCK - 1) // BLOCK
    lane = lax.iota(jnp.int32, LANES)[None, :]
    same = segment_row[:, None] == lane
    query_mask = jnp.where(same, masked_score, 0.0).astype(jnp.bfloat16)
    ones = ((lane % 64 >= 8) & (lane % 64 <= 10)).astype(f32)
    key_mask = jnp.where(lane < 8, 1.0 - same.astype(f32), ones).astype(jnp.bfloat16)
    relative = lax.iota(jnp.int32, 512) - 256
    buckets = bucket_of(jnp.concatenate([relative, 256 - lax.iota(jnp.int32, 512)]))
    hot = (lax.iota(jnp.int32, bias_grid.shape[0])[:, None] == buckets[None, :]).astype(f32)
    along = lax.dot_general(
        bias_grid, hot, (((0,), (0,)), ((), ())), precision=precise_setting
    )
    diag = jnp.concatenate([along[:, :512], along[:, 512:]], 0)
    return lo.astype(jnp.int32), hi.astype(jnp.int32), query_mask, key_mask, diag


def bias_grad(sums, heads, bucket_count):
    near = lax.broadcasted_iota(jnp.int32, (NEAR, 2 * LANES), 0)
    place = lax.broadcasted_iota(jnp.int32, (NEAR, 2 * LANES), 1)
    bucket = bucket_of((near - 2) * BLOCK + BLOCK - place)
    bucket = jnp.where(near == 0, 15, jnp.where(near == NEAR - 1, 31, bucket))
    hot = (bucket.reshape(-1)[:, None] == lax.iota(jnp.int32, bucket_count)[None, :]).astype(jnp.float32)
    return jnp.dot(sums.reshape(heads, -1), hot, precision=precise_setting).T


def per_device(
    tokens,
    segments,
    routes,
    cotangent,
    attn_gain,
    ffn_gain,
    query_weight,
    key_weight,
    value_weight,
    output_weight,
    position_bias_grid,
    router_weight,
    expert_in,
    expert_out,
):
    f32, bf16 = jnp.float32, jnp.bfloat16
    token_count, model_width = tokens.shape
    bucket_count, head_count = position_bias_grid.shape
    head_width = model_width // head_count
    score_scale = head_width ** (-0.5)
    experts_all = router_weight.shape[1]
    capacity = (5 * token_count + 4 * experts_all - 1) // (4 * experts_all)
    slot_rows = (capacity + 15) // 16 * 16
    slots = experts_all * slot_rows
    groups = lax.axis_size("expert")
    dp_size = lax.axis_size("dp")

    chosen = routes[:, 0]
    expert_hot = chosen[:, None] == lax.iota(jnp.int32, experts_all)[None, :]
    expert_float = expert_hot.astype(f32)
    before = lax.iota(jnp.int32, token_count)[:, None] > lax.iota(jnp.int32, token_count)[None, :]
    ranks = matmul(before.astype(bf16), expert_hot.astype(bf16))
    slot_rank = jnp.sum(ranks * expert_float, 1).astype(jnp.int32)
    token_slot = jnp.where(slot_rank < capacity, chosen * slot_rows + slot_rank, slots)
    to_slots = (lax.iota(jnp.int32, slots)[:, None] == token_slot[None, :]).astype(bf16)

    inputs = tokens.astype(f32)
    normed, inverse_one = rms_forward(inputs, attn_gain)
    normed_low = normed.astype(bf16)
    queries = (matmul(normed_low, query_weight).astype(bf16) * score_scale).astype(bf16)
    key_rows = matmul(normed_low, key_weight).astype(bf16)
    value_rows = matmul(normed_low, value_weight).astype(bf16)
    lo, hi, query_mask, key_mask, diag = attention_operands(segments[0], position_bias_grid)
    attended, query_extra = attn_fwd(
        lo, hi, queries, key_rows, value_rows, query_mask, key_mask, diag[:head_count]
    )
    middle = inputs + matmul(attended, output_weight)
    hidden_two, inverse_two = rms_forward(middle, ffn_gain)
    logits = jnp.dot(hidden_two, router_weight, precision=precise_setting)
    top_logit = jnp.max(logits, -1, keepdims=True)
    exponents_router = jnp.exp(logits - top_logit)
    router_probs = exponents_router / jnp.sum(exponents_router, -1, keepdims=True)
    gate_values = jnp.sum(router_probs * expert_float, 1)
    upstream = cotangent.astype(f32)

    def exchange(rows):
        rows = rows.reshape(experts_all, slot_rows, model_width)
        return lax.all_to_all(rows, "expert", split_axis=0, concat_axis=0, tiled=True)

    grad_arrived = exchange(matmul(to_slots, cotangent).astype(bf16))
    sent = matmul(to_slots, hidden_two.astype(bf16)).astype(bf16)
    gate_slots = jnp.sum(matmul(to_slots, pieces(gate_values)), 1)
    lanes = (slot_rows + LANES - 1) // LANES * LANES
    gate_slots = jnp.pad(gate_slots.reshape(experts_all, slot_rows), ((0, 0), (0, lanes - slot_rows)))
    gate_slots = jnp.broadcast_to(gate_slots[:, None, :], (experts_all, 8, lanes))
    home_grad, home_gate, produced, keep, give = ffn(
        sent.reshape(experts_all, slot_rows, model_width), gate_slots,
        grad_arrived.reshape(slots, model_width),
        expert_in[0], expert_out[0], groups, dp_size,
    )
    passed = lax.ppermute(give, "dp", [(i, (i + dp_size // 2) % dp_size) for i in range(dp_size)])
    weight_grads = keep.astype(f32) + passed.astype(f32)
    in_weight_grad, out_weight_grad = weight_grads[0], weight_grads[1]
    returned = exchange(produced).reshape(slots, model_width)
    expert_rows = matmul_tn(to_slots, returned)
    mixed = (middle + gate_values[:, None] * expert_rows).astype(bf16)

    gate_grad_slots = home_gate[:, 0, :slot_rows].reshape(slots)
    gate_grad = jnp.sum(matmul_tn(to_slots, pieces(gate_grad_slots)), 1)
    expert_input_grad = matmul_tn(to_slots, home_grad.reshape(slots, model_width))
    logit_grad = router_probs * (
        expert_float * gate_grad[:, None] - (gate_values * gate_grad)[:, None]
    )
    router_grad = jnp.dot(hidden_two.T, logit_grad, precision=precise_setting)
    hidden_grad = expert_input_grad + jnp.dot(
        logit_grad, router_weight.T, precision=precise_setting
    )
    middle_part, ffn_gain_grad = rms_backward(middle, inverse_two, ffn_gain, hidden_grad)
    middle_grad = upstream + middle_part
    branch_grad = middle_grad.astype(bf16)
    attended_grad = matmul_nt(branch_grad, output_weight).astype(bf16)
    query_grad, key_grad, value_grad, diag_sums = attn_bwd(
        lo, hi, queries, key_rows, value_rows, query_extra, attended_grad, attended, key_mask,
        diag, score_scale,
    )
    table_grad = bias_grad(diag_sums, head_count, bucket_count)
    flat = jnp.concatenate(
        [jnp.zeros((model_width,), f32), ffn_gain_grad, table_grad.reshape(-1), router_grad.reshape(-1)]
    )
    small_rows = -(-flat.shape[0] // (8 * LANES)) * 8
    small = jnp.pad(flat, (0, small_rows * LANES - flat.shape[0])).reshape(small_rows, LANES)
    weights, token_grad, small = reduce_grads(
        normed_low, attended, branch_grad, query_grad, key_grad, value_grad,
        query_weight, key_weight, value_weight, tokens, middle_grad, inverse_one,
        attn_gain[None, :], small, dp_size, groups,
    )
    weights = weights.astype(f32)
    flat = small.reshape(-1)
    ends = [model_width, 2 * model_width]
    ends.append(ends[-1] + table_grad.size)
    ends.append(ends[-1] + router_grad.size)
    return (
        mixed,
        token_grad,
        flat[: ends[0]],
        flat[ends[0] : ends[1]],
        weights[3],
        weights[2],
        weights[1],
        weights[0],
        flat[ends[1] : ends[2]].reshape(table_grad.shape),
        flat[ends[2] : ends[3]].reshape(router_grad.shape),
        in_weight_grad[None],
        out_weight_grad[None],
    )


def solution(mesh):
    rows = P(("dp", "expert"), None)
    return jax.shard_map(
        per_device,
        mesh=mesh,
        in_specs=(rows,) * 4 + (P(),) * 8 + (P("expert", None, None),) * 2,
        out_specs=(rows,) * 2 + (P(),) * 8 + (P("expert", None, "dp"), P("expert", "dp", None)),
        check_vma=False,
    )
```

```python
import functools

import jax
import jax.numpy as jnp
from jax import lax
from jax.experimental import pallas as pl
from jax.experimental.pallas import tpu as pltpu
from jax.sharding import PartitionSpec as P

epsilon = 1e-06
precise_setting = lax.Precision.HIGHEST
def matmul(left, right):
    return jnp.dot(left, right, preferred_element_type=jnp.float32)


def matmul_tn(left, right):
    return lax.dot_general(left, right, (((0,), (0,)), ((), ())), preferred_element_type=jnp.float32)


def matmul_nt(left, right):
    return lax.dot_general(left, right, (((1,), (1,)), ((), ())), preferred_element_type=jnp.float32)


bucket_bounds = (12, 16, 23, 32, 46, 64, 91)
masked_score = -1e30
LANES = 128
BLOCK = 128
NEAR = 5
UF = 6
UB = 6


def bucket_of(relative):
    distance = jnp.abs(relative)
    beyond = jnp.zeros_like(distance)
    for threshold in bucket_bounds:
        beyond = beyond + (distance >= threshold).astype(jnp.int32)
    inside = jnp.where(distance < 8, distance, 8 + beyond)
    return inside + 16 * (relative > 0).astype(jnp.int32)


def dot_nt(a, b):
    return lax.dot_general(a, b, (((1,), (1,)), ((), ())), preferred_element_type=jnp.float32)


def dot_nn(a, b):
    return lax.dot_general(a, b, (((1,), (0,)), ((), ())), preferred_element_type=jnp.float32)


def split3(x):
    a = x.astype(jnp.bfloat16)
    r = x - a.astype(jnp.float32)
    b = r.astype(jnp.bfloat16)
    c = (r - b.astype(jnp.float32)).astype(jnp.bfloat16)
    return a, b, c


def fill_bias(diag_ref, bias, pairs):
    for p in range(pairs):
        for d in range(NEAR):
            tiles = []
            for h in (2 * p, 2 * p + 1):
                row = diag_ref[h : h + 1, :]
                if d in (0, NEAR - 1):
                    col = row[:, 511:512] if d == 0 else row[:, 0:1]
                    tiles.append(jnp.broadcast_to(col, (BLOCK, BLOCK)))
                else:
                    base = (3 - d) * BLOCK
                    wide = jnp.broadcast_to(row[:, base : base + 2 * BLOCK], (BLOCK, 2 * BLOCK))
                    tiles.append(pltpu.roll(wide, BLOCK, 1, stride=1, stride_axis=0)[:, :BLOCK])
            bias[p, d] = jnp.concatenate(tiles, 1)


def heads_apart(block, low, extra=None):
    zero = jnp.zeros_like(block)
    first, second = jnp.where(low, block, zero), jnp.where(low, zero, block)
    if extra is not None:
        first, second = jnp.concatenate([first, extra], 1), jnp.concatenate([second, extra], 1)
    return jnp.concatenate([first, second], 0)


def by_count(lo, hi, most, body):
    for n in range(1, most + 1):
        pl.when(hi - lo == n)(functools.partial(body, n))


def own_heads(wide):
    return jnp.concatenate([wide[:64, :LANES], wide[64:128, LANES:]], 0)


def attend(lo_ref, hi_ref, q_ref, k_ref, vt_ref, qm_ref, km_ref, bias, o_ref, lse_ref):
    pairs = q_ref.shape[1] // LANES
    length = q_ref.shape[0]
    nblk = length // BLOCK
    f32, bf16 = jnp.float32, jnp.bfloat16
    low = lax.broadcasted_iota(jnp.int32, (1, LANES), 1) < 64

    def q_block(i, _):
        lo, hi = lo_ref[i], hi_ref[i]
        rows = pl.ds(pl.multiple_of(i * BLOCK, BLOCK), BLOCK)
        start = pl.multiple_of(lo * BLOCK, BLOCK)
        qm = qm_ref[rows, :]

        def body(n):
            span = pl.ds(start, n * BLOCK)
            km = km_ref[span, :]

            def lanes_of(p):
                return pl.ds(pl.multiple_of(p * LANES, LANES), LANES)

            def scores(p):
                qs = heads_apart(q_ref[rows, lanes_of(p)], low, qm)
                return dot_nt(jnp.concatenate([k_ref[span, lanes_of(p)], km], 1), qs)

            def soften(p, st):
                parts = []
                top = None
                for b in range(n):
                    d = jnp.clip(lo + b - i, -2, 2) + 2
                    s = st[b * BLOCK : (b + 1) * BLOCK] + bias[p, d]
                    parts.append(s)
                    top = s if top is None else jnp.maximum(top, s)
                top = jnp.max(top, 0, keepdims=True)
                return jnp.concatenate([jnp.exp(s - top).astype(bf16) for s in parts], 0), top

            def mix(p, probs):
                values = jnp.concatenate([vt_ref[lanes_of(p), span], jnp.ones((16, n * BLOCK), bf16)], 0)
                return dot_nn(values, probs)

            def finish(p, acc, top):
                total = acc[LANES : LANES + 1]
                inv = 1.0 / total
                ot = own_heads(acc)
                ot = jnp.concatenate([ot[:64] * inv[:, :LANES], ot[64:] * inv[:, LANES:]], 0)
                o_ref[rows, lanes_of(p)] = ot.T.astype(bf16)
                lse_ref[i, pl.ds(p, 1), :] = top + jnp.log(total)

            def some(g, _):
                ps = [g * UF + u for u in range(UF)]
                sts = [scores(p) for p in ps]
                soft = [soften(p, st) for p, st in zip(ps, sts)]
                accs = [mix(p, x[0]) for p, x in zip(ps, soft)]
                for p, acc, x in zip(ps, accs, soft):
                    finish(p, acc, x[1])
                return 0
            lax.fori_loop(0, pairs // UF, some, 0)

        by_count(lo, hi, nblk, body)
        return 0
    lax.fori_loop(0, nblk, q_block, 0)


def attend_back(
    lo_ref, hi_ref, q_ref, k_ref, kt_ref, v_ref, lse_ref, do_ref, o_ref, qm_ref, km_ref, bias,
    dq_ref, dk_ref, dv_ref, gsum_ref, gacc, dkacc, dvacc, scale,
):
    length, width = q_ref.shape
    pairs = width // LANES
    nblk = length // BLOCK
    f32, bf16 = jnp.float32, jnp.bfloat16
    low = lax.broadcasted_iota(jnp.int32, (1, LANES), 1) < 64
    pick = (
        lax.broadcasted_iota(jnp.int32, (16, LANES), 0) == lax.broadcasted_iota(jnp.int32, (16, LANES), 1) // 64
    ).astype(f32).astype(bf16)
    gacc[...] = jnp.zeros_like(gacc)
    dkacc[...] = jnp.zeros_like(dkacc)
    dvacc[...] = jnp.zeros_like(dvacc)

    def q_block(i, _):
        lo, hi = lo_ref[i], hi_ref[i]
        rows = pl.ds(pl.multiple_of(i * BLOCK, BLOCK), BLOCK)
        start = pl.multiple_of(lo * BLOCK, BLOCK)
        qm = qm_ref[rows, :]

        def body(n):
            span = pl.ds(start, n * BLOCK)
            km = km_ref[span, :]

            def lanes_of(p):
                return pl.ds(pl.multiple_of(p * LANES, LANES), LANES)

            def products(p):
                cols = lanes_of(p)
                qs = heads_apart(q_ref[rows, cols], low, qm)
                dd = do_ref[rows, cols]
                dos = heads_apart(dd, low)
                prod = dd.astype(f32) * o_ref[rows, cols].astype(f32)
                prod_hi = prod.astype(bf16)
                prod_lo = (prod - prod_hi.astype(f32)).astype(bf16)
                inner = dot_nt(pick, prod_hi) + dot_nt(pick, prod_lo)
                inner = jnp.concatenate([inner[0:1], inner[1:2]], 1)
                st = dot_nt(jnp.concatenate([k_ref[span, cols], km], 1), qs)
                dpt = dot_nt(v_ref[span, cols], dos)
                return qs, dos, inner, st, dpt

            def pointwise(p, inner, st, dpt):
                lse = lse_ref[i, pl.ds(p, 1), :]
                probs, grads = [], []
                for b in range(n):
                    d = jnp.clip(lo + b - i, -2, 2) + 2
                    part = slice(b * BLOCK, (b + 1) * BLOCK)
                    prob = jnp.exp(st[part] + bias[p, d] - lse)
                    grad = prob * (dpt[part] - inner)
                    gacc[p, d] += grad
                    probs.append(prob.astype(bf16))
                    grads.append(grad.astype(bf16))
                return jnp.concatenate(probs, 0), jnp.concatenate(grads, 0)

            def back(p, qs, dos, probs, grads):
                cols = lanes_of(p)
                return (
                    dot_nn(probs, dos), dot_nn(grads, qs[:, :LANES]), dot_nn(kt_ref[cols, span], grads)
                )

            def finish(p, dv, dk, dqt):
                cols = lanes_of(p)
                dvacc[span, cols] += dv
                dkacc[span, cols] += dk
                dq_ref[rows, cols] = (own_heads(dqt).T * scale).astype(bf16)

            def some(g, _):
                ps = [g * UB + u for u in range(UB)]
                first = [products(p) for p in ps]
                points = [pointwise(p, *x[2:]) for p, x in zip(ps, first)]
                last = [back(p, *x[:2], *y) for p, x, y in zip(ps, first, points)]
                for p, x in zip(ps, last):
                    finish(p, *x)
                return 0
            lax.fori_loop(0, pairs // UB, some, 0)

        by_count(lo, hi, nblk, body)
        return 0
    lax.fori_loop(0, nblk, q_block, 0)
    dk_ref[...] = dkacc[...].astype(bf16)
    dv_ref[...] = dvacc[...].astype(bf16)
    turn = (
        lax.broadcasted_iota(jnp.int32, (BLOCK, BLOCK), 0) + lax.broadcasted_iota(jnp.int32, (BLOCK, BLOCK), 1)
        == BLOCK - 1
    ).astype(f32).astype(bf16)
    for p in range(pairs):
        for d in range(NEAR):
            t = gacc[p, d]
            if 0 < d < NEAR - 1:
                hi = t.astype(bf16)
                t = dot_nn(turn, hi) + dot_nn(turn, (t - hi.astype(f32)).astype(bf16))
            for u in range(2):
                s = jnp.concatenate([t[:, u * LANES : (u + 1) * LANES], jnp.zeros((BLOCK, LANES), f32)], 1)
                if 0 < d < NEAR - 1:
                    s = pltpu.roll(s, 0, 1, stride=1, stride_axis=0)
                at = (2 * p + u) * NEAR + d
                gsum_ref[at : at + 1, :] = jnp.sum(s, 0, keepdims=True)


def two(x):
    a = x.astype(jnp.bfloat16)
    return a, (x - a.astype(jnp.float32)).astype(jnp.bfloat16)


def row_pieces(row):
    place = lax.broadcasted_iota(jnp.int32, (16, row.shape[1]), 0)
    a, b, c = [x.astype(jnp.float32) for x in split3(row)]
    return jnp.where(place == 0, a, jnp.where(place == 1, b, jnp.where(place == 2, c, 0.0))).astype(jnp.bfloat16)


def each(count, body):
    if count <= 8:
        for e in range(count):
            body(e)
    else:
        def step(e, _):
            body(e)
            return 0
        lax.fori_loop(0, count, step, 0)


def slot_hot(slot_row, e, slot_rows):
    place = lax.broadcasted_iota(jnp.int32, (slot_rows, slot_row.shape[1]), 0) + e * slot_rows
    return (place == slot_row).astype(jnp.float32).astype(jnp.bfloat16)


def slots_kernel(routes_ref, rows_ref, slot_ref, out_ref, *, experts, capacity, slot_rows):
    f32, bf16 = jnp.float32, jnp.bfloat16
    tokens = routes_ref.shape[1]
    routes = routes_ref[...]
    pad = max(experts, 16)
    hot = (lax.broadcasted_iota(jnp.int32, (pad, tokens), 0) == routes).astype(f32)
    earlier = (
        lax.broadcasted_iota(jnp.int32, (tokens, tokens), 0) < lax.broadcasted_iota(jnp.int32, (tokens, tokens), 1)
    ).astype(f32).astype(bf16)
    ranks = dot_nn(hot.astype(bf16), earlier)
    rank = jnp.sum(ranks * hot, 0, keepdims=True).astype(jnp.int32)
    slot = jnp.where(rank < capacity, routes * slot_rows + rank, -1)
    slot_ref[...] = jnp.broadcast_to(slot, slot_ref.shape)

    def one(e):
        out_ref[e] = dot_nn(slot_hot(slot, e, slot_rows), rows_ref[...]).astype(bf16)
    each(experts, one)


def first_slots(routes_row, rows, experts, capacity, slot_rows):
    tokens, width = rows.shape
    vmem = pl.BlockSpec(memory_space=pltpu.VMEM)
    return pl.pallas_call(
        functools.partial(slots_kernel, experts=experts, capacity=capacity, slot_rows=slot_rows),
        out_shape=(
            jax.ShapeDtypeStruct((8, tokens), jnp.int32),
            jax.ShapeDtypeStruct((experts, slot_rows, width), jnp.bfloat16),
        ),
        in_specs=[vmem] * 2,
        out_specs=(vmem,) * 2,
        compiler_params=pltpu.CompilerParams(vmem_limit_bytes=60 << 20),
        cost_estimate=pl.CostEstimate(
            flops=2 * experts * slot_rows * tokens * width, bytes_accessed=4 << 20, transcendentals=0
        ),
    )(routes_row, rows)


def fill_masks(segment_row, qm, km):
    f32, bf16 = jnp.float32, jnp.bfloat16
    lane = lax.broadcasted_iota(jnp.int32, (1, LANES), 1)
    for b in range(qm.shape[0] // BLOCK):
        span = slice(b * BLOCK, (b + 1) * BLOCK)
        hot = (lax.broadcasted_iota(jnp.int32, (LANES, BLOCK), 0) == segment_row[:, span]).astype(f32).T
        qm[span, :] = (hot * masked_score).astype(bf16)
        km[span, :] = jnp.where(lane < 8, 1.0 - hot, 0.0).astype(bf16)


def fill_diag(grid_ref, diag, heads):
    bf16 = jnp.bfloat16
    buckets = grid_ref.shape[0]
    relative = 256 - lax.broadcasted_iota(jnp.int32, (buckets, 4 * LANES), 1)
    hot = (lax.broadcasted_iota(jnp.int32, (buckets, 4 * LANES), 0) == bucket_of(relative))
    hot = hot.astype(jnp.float32).astype(bf16)
    grid = jnp.concatenate(
        [grid_ref[...], jnp.zeros((buckets, LANES - heads), jnp.float32)], 1
    ).T[:16]
    total = None
    for piece in split3(grid):
        term = dot_nn(piece, hot)
        total = term if total is None else total + term
    diag[...] = total


def front_kernel(
    lo_ref, hi_ref, tokens, segment_row, slot_ref, routes_ref, gain_one, gain_two, wq, wk, wv, wo, grid_ref, router_t,
    q_ref, k_ref, kt_ref, v_ref, o_ref, lse_ref, middle_ref, probs_ref, xs_ref, gs_ref,
    vt_ref, qm_ref, km_ref, diag, bias, hidden, *, experts, slot_rows, scale,
):
    f32, bf16 = jnp.float32, jnp.bfloat16
    length, width = tokens.shape
    pairs = width // LANES
    nblk = length // BLOCK
    heads = grid_ref.shape[1]
    low = lax.broadcasted_iota(jnp.int32, (1, LANES), 1) < 64
    step = 256

    for b in range(length // step):
        span = slice(b * step, (b + 1) * step)
        x = tokens[span, :].astype(f32)
        inverse = lax.rsqrt(jnp.mean(x * x, 1, keepdims=True) + epsilon)
        normed = (x * inverse * gain_one[...]).astype(bf16)
        q_ref[span, :] = (dot_nn(normed, wq[...]).astype(bf16).astype(f32) * scale).astype(bf16)
        k = dot_nn(normed, wk[...]).astype(bf16)
        k_ref[span, :] = k
        kt_ref[:, span] = k.T
        v = dot_nn(normed, wv[...]).astype(bf16)
        v_ref[span, :] = v
        vt_ref[:, span] = v.T
    fill_masks(segment_row[...], qm_ref, km_ref)
    fill_diag(grid_ref, diag, heads)
    fill_bias(diag, bias, pairs)
    attend(lo_ref, hi_ref, q_ref, k_ref, vt_ref, qm_ref, km_ref, bias, o_ref, lse_ref)

    rw = two(router_t[...])
    routes = routes_ref[...]
    pad = router_t.shape[0]
    place = lax.broadcasted_iota(jnp.int32, (pad, step), 0)
    gates = []
    for b in range(length // step):
        span = slice(b * step, (b + 1) * step)
        middle = tokens[span, :].astype(f32) + dot_nn(o_ref[span, :], wo[...])
        middle_ref[span, :] = middle
        inverse = lax.rsqrt(jnp.mean(middle * middle, 1, keepdims=True) + epsilon)
        parts = two(middle * inverse * gain_two[...])
        hidden[span, :] = parts[0]
        logits = dot_nt(rw[0], parts[0]) + dot_nt(rw[0], parts[1]) + dot_nt(rw[1], parts[0])
        logits = jnp.where(place < experts, logits, -1e30)
        powers = jnp.exp(logits - jnp.max(logits, 0, keepdims=True))
        probs = powers / jnp.sum(powers, 0, keepdims=True)
        probs_ref[:, span] = probs
        gates.append(jnp.sum(jnp.where(place == routes[:, span], probs, 0.0), 0, keepdims=True))
    gates = row_pieces(jnp.concatenate(gates, 1))
    slot = slot_ref[0:1, :]
    lanes = gs_ref.shape[2]

    def one(e):
        hot = slot_hot(slot, e, slot_rows)
        xs_ref[e] = dot_nn(hot, hidden[...]).astype(bf16)
        if lanes > slot_rows:
            hot = jnp.concatenate([hot, jnp.zeros((lanes - slot_rows, length), bf16)], 0)
        row = jnp.sum(dot_nt(gates, hot), 0, keepdims=True)
        gs_ref[e] = jnp.broadcast_to(row, gs_ref.shape[1:])
    each(experts, one)


def front(lo, hi, tokens, segments, slot, routes_row, gain_one, gain_two, wq, wk, wv, wo, grid, router_t, experts, slot_rows, scale):
    length, width = tokens.shape
    heads = grid.shape[1]
    pairs = width // LANES
    nblk = length // BLOCK
    lanes = (slot_rows + LANES - 1) // LANES * LANES
    smem = pl.BlockSpec(memory_space=pltpu.SMEM)
    vmem = pl.BlockSpec(memory_space=pltpu.VMEM)
    f32, bf16 = jnp.float32, jnp.bfloat16
    shape = jax.ShapeDtypeStruct
    act = shape((length, width), bf16)
    return pl.pallas_call(
        functools.partial(front_kernel, experts=experts, slot_rows=slot_rows, scale=scale),
        out_shape=(
            act, act, shape((width, length), bf16), act, act,
            shape((nblk, 8, 2 * LANES), f32), shape((length, width), f32),
            shape((router_t.shape[0], length), f32),
            shape((experts, slot_rows, width), bf16), shape((experts, 8, lanes), f32),
        ),
        in_specs=[smem] * 2 + [vmem] * 12,
        out_specs=(vmem,) * 10,
        scratch_shapes=[
            pltpu.VMEM((width, length), bf16),
            pltpu.VMEM((length, LANES), bf16),
            pltpu.VMEM((length, LANES), bf16),
            pltpu.VMEM((16, 4 * LANES), f32),
            pltpu.VMEM((pairs, NEAR, BLOCK, 2 * LANES), f32),
            pltpu.VMEM((length, width), bf16),
        ],
        compiler_params=pltpu.CompilerParams(vmem_limit_bytes=60 << 20),
        cost_estimate=pl.CostEstimate(
            flops=4 * length * length * width + 12 * length * width * width, bytes_accessed=20 << 20,
            transcendentals=length * length * heads,
        ),
    )(lo, hi, tokens, segments, slot, routes_row, gain_one, gain_two, wq, wk, wv, wo, grid, router_t)


def back_kernel(
    lo_ref, hi_ref, home, home_gate, slot_ref, routes_ref, probs_ref, middle_ref, cotangent, segment_row, gain_two,
    wo, router_t, grid_ref, q_ref, k_ref, kt_ref, v_ref, lse_ref, o_ref,
    dq_ref, dk_ref, dv_ref, gsum_ref, middle_grad, router_grad, gain_grad,
    do_ref, qm_ref, km_ref, diag, bias, gacc, dkacc, dvacc, logit, *, experts, slot_rows, scale,
):
    f32, bf16 = jnp.float32, jnp.bfloat16
    length, width = middle_ref.shape
    pairs = width // LANES
    pad = router_t.shape[0]
    heads = grid_ref.shape[1]
    slot = slot_ref[0:1, :]
    lanes = home_gate.shape[2]

    gate_grad = [jnp.zeros((16, length), f32)]
    if experts <= 8:
        total = jnp.zeros((16, length), f32)
        for e in range(experts):
            total = total + dot_nn(row_pieces(home_gate[e, 0:1, :])[:, :slot_rows], slot_hot(slot, e, slot_rows))
    else:
        def add(e, total):
            return total + dot_nn(row_pieces(home_gate[e, 0:1, :])[:, :slot_rows], slot_hot(slot, e, slot_rows))
        total = lax.fori_loop(0, experts, add, jnp.zeros((16, length), f32))
    gate_grad = jnp.sum(total, 0, keepdims=True)
    place = lax.broadcasted_iota(jnp.int32, (pad, length), 0)
    hot = place == routes_ref[...]
    probs = probs_ref[...]
    gate = jnp.sum(jnp.where(hot, probs, 0.0), 0, keepdims=True)
    logit[...] = probs * (jnp.where(hot, gate_grad, 0.0) - gate * gate_grad)
    rw = two(router_t[...])
    slots = experts * slot_rows
    router_sum = jnp.zeros((pad, width), f32)
    gain_sum = jnp.zeros((1, width), f32)
    step = 256
    for b in range(length // step):
        span = slice(b * step, (b + 1) * step)
        hots = []
        for c in range(b * step, (b + 1) * step, BLOCK):
            column = jnp.broadcast_to(slot[:, c : c + BLOCK].astype(f32), (BLOCK, BLOCK)).T
            first = lax.broadcasted_iota(jnp.int32, (BLOCK, LANES), 1).astype(f32)
            hots.append(jnp.concatenate(
                [(column == first + float(s)).astype(f32).astype(bf16) for s in range(0, slots, LANES)], 1))
        spread = jnp.concatenate(hots, 0)
        hidden_grad = dot_nn(spread, home[...].reshape(slots, width))
        lg = two(logit[:, span])
        hidden_grad = hidden_grad + (
            matmul_tn(lg[0], rw[0]) + matmul_tn(lg[0], rw[1]) + matmul_tn(lg[1], rw[0])
        )
        middle = middle_ref[span, :]
        inverse = lax.rsqrt(jnp.mean(middle * middle, 1, keepdims=True) + epsilon)
        unit = middle * inverse
        hidden = two(unit * gain_two[...])
        router_sum = router_sum + (dot_nn(lg[0], hidden[0]) + dot_nn(lg[0], hidden[1]) + dot_nn(lg[1], hidden[0]))
        gain_sum = gain_sum + jnp.sum(hidden_grad * unit, 0, keepdims=True)
        scaled = hidden_grad * gain_two[...]
        mean = jnp.mean(scaled * middle, 1, keepdims=True)
        grad = cotangent[span, :].astype(f32) + inverse * (scaled - unit * (inverse * mean))
        middle_grad[span, :] = grad
        do_ref[span, :] = matmul_nt(grad.astype(bf16), wo[...]).astype(bf16)
    router_grad[...] = router_sum
    gain_grad[...] = gain_sum

    fill_masks(segment_row[...], qm_ref, km_ref)
    fill_diag(grid_ref, diag, heads)
    fill_bias(diag, bias, pairs)
    attend_back(
        lo_ref, hi_ref, q_ref, k_ref, kt_ref, v_ref, lse_ref, do_ref, o_ref, qm_ref, km_ref, bias,
        dq_ref, dk_ref, dv_ref, gsum_ref, gacc, dkacc, dvacc, scale,
    )


def back(lo, hi, home, home_gate, slot, routes_row, probs, middle, cotangent, segments, gain_two, wo, router_t, grid,
         q, k, kt, v, lse, o, experts, slot_rows, scale):
    length, width = middle.shape
    heads = grid.shape[1]
    pairs = width // LANES
    smem = pl.BlockSpec(memory_space=pltpu.SMEM)
    vmem = pl.BlockSpec(memory_space=pltpu.VMEM)
    f32, bf16 = jnp.float32, jnp.bfloat16
    shape = jax.ShapeDtypeStruct
    act = shape((length, width), bf16)
    return pl.pallas_call(
        functools.partial(back_kernel, experts=experts, slot_rows=slot_rows, scale=scale),
        out_shape=(
            act, act, act, shape((heads * NEAR, 2 * LANES), f32), shape((length, width), f32),
            shape((router_t.shape[0], width), f32), shape((1, width), f32),
        ),
        in_specs=[smem] * 2 + [vmem] * 18,
        out_specs=(vmem,) * 7,
        scratch_shapes=[
            pltpu.VMEM((length, width), bf16),
            pltpu.VMEM((length, LANES), bf16),
            pltpu.VMEM((length, LANES), bf16),
            pltpu.VMEM((16, 4 * LANES), f32),
            pltpu.VMEM((pairs, NEAR, BLOCK, 2 * LANES), f32),
            pltpu.VMEM((pairs, NEAR, BLOCK, 2 * LANES), f32),
            pltpu.VMEM((length, width), f32),
            pltpu.VMEM((length, width), f32),
            pltpu.VMEM((router_t.shape[0], length), f32),
        ],
        compiler_params=pltpu.CompilerParams(vmem_limit_bytes=60 << 20),
        cost_estimate=pl.CostEstimate(
            flops=10 * length * length * width + 6 * length * width * width, bytes_accessed=30 << 20,
            transcendentals=length * length * heads,
        ),
    )(lo, hi, home, home_gate, slot, routes_row, probs, middle, cotangent, segments, gain_two, wo, router_t, grid,
      q, k, kt, v, lse, o)


def gelu_parts(v):
    mag = jnp.abs(v)
    t = 1.0 / (1.0 + (0.3275911 * 0.7071067811865476) * mag)
    poly = t * (0.127414796 + t * (-0.142248368 + t * (0.7107068705 + t * (-0.7265760135 + t * 0.5307027145))))
    gauss = jnp.exp(-0.5 * v * v)
    tail = poly * gauss
    phi = jnp.where(v < 0, tail, 1.0 - tail)
    return v * phi, phi + v * gauss * 0.3989422804014327


def flip_bits(index, mask, count):
    out = 0
    bit = 1
    while bit < count:
        a, b = (index // bit) % 2, (mask // bit) % 2
        out = out + bit * (a + b - 2 * a * b)
        bit *= 2
    return out


def ffn_kernel(
    xs, gs, g, win_hbm, wout_hbm,
    home, home_gate, produced, keep, give,
    win, wout, xr, gr, act, pg, gated, igs, ggs, dws, dwr, stage,
    wsem, own_sem, psem, ksem, xsend, xrecv, gsend, grecv, isend, irecv, qsend, qrecv, dsend, drecv,
    *, groups, dp_size, tiles,
):
    f32, bf16 = jnp.float32, jnp.bfloat16
    me = lax.axis_index("expert")
    dp = lax.axis_index("dp")
    core = dp % 2
    sibling = dp + 1 - 2 * core
    rows = xs.shape[1]
    width = xs.shape[2]
    hidden = win.shape[1]
    tile = hidden // tiles
    lanes = gs.shape[2]

    def there(peer):
        return (dp, peer)

    load_in = pltpu.make_async_copy(win_hbm, win, wsem.at[0])
    load_out = pltpu.make_async_copy(wout_hbm, wout, wsem.at[1])
    load_in.start()
    load_out.start()
    load_g = pltpu.make_async_copy(g, gated, wsem.at[2])
    load_g.start()

    barrier = pltpu.get_barrier_semaphore()

    def greet(s, _):
        pl.semaphore_signal(
            barrier, inc=1, device_id=there(flip_bits(me, s, groups)), device_id_type=pl.DeviceIdType.MESH
        )
        return 0
    lax.fori_loop(1, groups, greet, 0)
    pl.semaphore_signal(barrier, inc=1, device_id=(sibling, me), device_id_type=pl.DeviceIdType.MESH)
    pl.semaphore_wait(barrier, groups)

    def x_copy(peer, slot):
        return pltpu.make_async_remote_copy(
            src_ref=xs.at[peer], dst_ref=xr.at[slot], send_sem=xsend.at[peer], recv_sem=xrecv.at[slot],
            device_id=there(peer), device_id_type=pl.DeviceIdType.MESH)

    def g_copy(peer, slot):
        return pltpu.make_async_remote_copy(
            src_ref=gs.at[peer], dst_ref=gr.at[slot], send_sem=gsend.at[peer], recv_sem=grecv.at[slot],
            device_id=there(peer), device_id_type=pl.DeviceIdType.MESH)

    def i_copy(peer, slot):
        return pltpu.make_async_remote_copy(
            src_ref=igs.at[peer], dst_ref=home.at[slot], send_sem=isend.at[peer], recv_sem=irecv.at[slot],
            device_id=there(peer), device_id_type=pl.DeviceIdType.MESH)

    def q_copy(peer, slot):
        return pltpu.make_async_remote_copy(
            src_ref=ggs.at[peer], dst_ref=home_gate.at[slot], send_sem=qsend.at[peer], recv_sem=qrecv.at[slot],
            device_id=there(peer), device_id_type=pl.DeviceIdType.MESH)

    def send(s, _):
        peer = flip_bits(me, s, groups)
        x_copy(peer, me).start()
        g_copy(peer, me).start()
        return 0
    lax.fori_loop(1, groups, send, 0)
    own_x = pltpu.make_async_copy(xs.at[me], xr.at[me], own_sem.at[0])
    own_g = pltpu.make_async_copy(gs.at[me], gr.at[me], own_sem.at[1])
    own_x.start()
    own_g.start()
    load_in.wait()
    load_out.wait()
    load_g.wait()

    spot = (
        lax.broadcasted_iota(jnp.int32, (rows, lanes), 0)
        == lax.broadcasted_iota(jnp.int32, (rows, lanes), 1)
    )

    def work(p):
        x = xr[p]
        place = pl.ds(pl.multiple_of(p * rows, rows), rows)
        gg = gated[place, :]
        gate = jnp.sum(jnp.where(spot, gr[p, 0:1, :], 0.0), 1, keepdims=True)
        gated[place, :] = (gate * gg.astype(f32)).astype(bf16)
        total = jnp.zeros((rows, width), f32)
        gate_grad = jnp.zeros((rows, 1), f32)
        for t in range(tiles):
            cols = slice(t * tile, (t + 1) * tile)
            pre = matmul(x, win[:, cols])
            out_grad = matmul_nt(gg, wout[cols, :])
            value, slope = gelu_parts(pre)
            act[place, cols] = value.astype(bf16)
            gate_grad = gate_grad + jnp.sum(value * out_grad, 1, keepdims=True)
            low = (gate * out_grad * slope).astype(bf16)
            pg[place, cols] = low
            total = total + matmul_nt(low, win[:, cols])
        igs[p] = total.astype(bf16)
        row = jnp.sum(jnp.where(spot, gate_grad, 0.0), 0, keepdims=True)
        ggs[p] = jnp.broadcast_to(row, ggs.shape[1:])

    own_x.wait()
    own_g.wait()
    work(me)
    own_i = pltpu.make_async_copy(igs.at[me], home.at[me], own_sem.at[0])
    own_q = pltpu.make_async_copy(ggs.at[me], home_gate.at[me], own_sem.at[1])
    own_i.start()
    own_q.start()

    def chunk(s, _):
        peer = flip_bits(me, s, groups)
        x_copy(peer, peer).wait_recv()
        g_copy(peer, peer).wait_recv()
        work(peer)
        i_copy(peer, me).start()
        q_copy(peer, me).start()
        return 0
    lax.fori_loop(1, groups, chunk, 0)

    def d_copy(k):
        return pltpu.make_async_remote_copy(
            src_ref=dws.at[k % 2], dst_ref=dwr.at[k], send_sem=dsend.at[k], recv_sem=drecv.at[k],
            device_id=(sibling, me), device_id_type=pl.DeviceIdType.MESH)

    part = hidden // dp_size
    flat = groups * rows
    items = [(which, half) for half in range(dp_size // 2) for which in range(2)]

    def grad(which, quarter):
        span = pl.ds(pl.multiple_of(quarter * part, part), part)
        if which == 0:
            return matmul_tn(xr[...].reshape(flat, width), pg[:, span])
        return matmul_tn(act[:, span], gated[...])

    half_of = dp // 2
    for k, (which, half) in enumerate(items):
        if k >= 2:
            d_copy(k - 2).wait_send()
        dws[k % 2] = grad(which, 2 * half + 1 - core).astype(bf16)
        d_copy(k).start()

    span = stage.shape[1]
    copies = []
    for b in range(flat // span):
        if b >= 2:
            copies[b - 2].wait()
        stage[b % 2] = matmul(act[b * span : (b + 1) * span, :], wout[...]).astype(bf16)
        copy = pltpu.make_async_copy(stage.at[b % 2], produced.at[pl.ds(b * span, span)], psem.at[b % 2])
        copy.start()
        copies.append(copy)
    for copy in copies[-2:]:
        copy.wait()
    for k, (which, half) in enumerate(items):
        local = grad(which, 2 * half + core)
        d_copy(k).wait_recv()
        both = (local + dwr[k].astype(f32)).astype(bf16)
        dwr[k] = both
    outs = []
    for which in range(2):
        outs.append(pltpu.make_async_copy(dwr.at[half_of * 2 + which], keep.at[which], ksem.at[which]))
        outs.append(pltpu.make_async_copy(dwr.at[(1 - half_of) * 2 + which], give.at[which], ksem.at[2 + which]))
    for copy in outs:
        copy.start()
    for copy in outs:
        copy.wait()
    own_i.wait()
    own_q.wait()
    for k in (2, 3):
        d_copy(k).wait_send()

    def finish(s, _):
        peer = flip_bits(me, s, groups)
        x_copy(peer, me).wait_send()
        g_copy(peer, me).wait_send()
        i_copy(peer, me).wait_send()
        q_copy(peer, me).wait_send()
        i_copy(peer, peer).wait_recv()
        q_copy(peer, peer).wait_recv()
        return 0
    lax.fori_loop(1, groups, finish, 0)


def ffn(xs, gs, g, weight_in, weight_out, groups, dp_size, tiles=6):
    f32, bf16 = jnp.float32, jnp.bfloat16
    _, rows, width = xs.shape
    hidden = weight_in.shape[1]
    lanes = gs.shape[2]
    part = hidden // dp_size
    anywhere = pl.BlockSpec(memory_space=pl.ANY)
    sem = pltpu.SemaphoreType.DMA
    flat = groups * rows
    shape = jax.ShapeDtypeStruct
    return pl.pallas_call(
        functools.partial(ffn_kernel, groups=groups, dp_size=dp_size, tiles=tiles),
        out_shape=(
            shape((groups, rows, width), bf16),
            shape((groups, 8, lanes), f32),
            shape((flat, width), bf16),
            shape((2, width, part), bf16),
            shape((2, width, part), bf16),
        ),
        in_specs=[anywhere] * 5,
        out_specs=(anywhere,) * 5,
        scratch_shapes=[
            pltpu.VMEM((width, hidden), bf16),
            pltpu.VMEM((hidden, width), bf16),
            pltpu.VMEM((groups, rows, width), bf16),
            pltpu.VMEM((groups, 8, lanes), f32),
            pltpu.VMEM((flat, hidden), bf16),
            pltpu.VMEM((flat, hidden), bf16),
            pltpu.VMEM((flat, width), bf16),
            pltpu.VMEM((groups, rows, width), bf16),
            pltpu.VMEM((groups, 8, lanes), f32),
            pltpu.VMEM((2, width, part), bf16),
            pltpu.VMEM((4, width, part), bf16),
            pltpu.VMEM((2, flat // 8, width), bf16),
            sem((3,)), sem((2,)), sem((2,)), sem((4,)),
            sem((groups,)), sem((groups,)), sem((groups,)), sem((groups,)),
            sem((groups,)), sem((groups,)), sem((groups,)), sem((groups,)),
            sem((4,)), sem((4,)),
        ],
        compiler_params=pltpu.CompilerParams(
            collective_id=1, has_side_effects=True, vmem_limit_bytes=62 << 20
        ),
        cost_estimate=pl.CostEstimate(
            flops=12 * flat * width * hidden, bytes_accessed=40 << 20, transcendentals=flat * hidden
        ),
    )(xs, gs, g, weight_in, weight_out)


def fold_steps(rows, cols, bits):
    steps = []
    for bit in bits:
        if rows % 32 == 0:
            rows = rows // 2
            steps.append((bit, "rows", rows, cols))
        elif cols % 256 == 0:
            cols = cols // 2
            steps.append((bit, "cols", rows, cols))
        else:
            steps.append((bit, "whole", rows, cols))
    return steps


def reduce_kernel(
    tokens, attended, middle_grad, dq, dk, dv, wq, wk, wv, gain, small_in,
    returned, slot_ref, routes_ref, probs_ref, middle,
    sums, token_grad, small_out, mixed,
    normed, branch, acc, outbox, inbox, small_box, small_sent,
    ssend, srecv, tsend, trecv,
    *, dp_bits, expert_bits,
):
    f32, bf16 = jnp.float32, jnp.bfloat16
    dp = lax.axis_index("dp")
    ex = lax.axis_index("expert")
    MESH = pl.DeviceIdType.MESH
    length, width = tokens.shape

    def own_bit(bit):
        axis, place = bit
        return (dp // 2 ** place) % 2 if axis == "dp" else (ex // 2 ** place) % 2

    def partner(bit):
        axis, place = bit
        flip = (1 - 2 * own_bit(bit)) * 2 ** place
        return (dp + flip, ex) if axis == "dp" else (dp, ex + flip)

    dpb = [("dp", i) for i in range(dp_bits)]
    exb = [("expert", i) for i in range(expert_bits)]
    orders = [
        [dpb[0], dpb[1], exb[0]] + dpb[2:] + exb[1:],
        [dpb[0], exb[0], dpb[1]] + dpb[2:] + exb[1:],
    ]
    every = dpb + exb
    count = len(every)

    barrier = pltpu.get_barrier_semaphore()
    for bit in every:
        pl.semaphore_signal(barrier, inc=1, device_id=partner(bit), device_id_type=MESH)
    pl.semaphore_wait(barrier, count)

    def prepare(i, _):
        span = pl.ds(pl.multiple_of(i * 256, 256), 256)
        x = tokens[span, :].astype(f32)
        inv = lax.rsqrt(jnp.mean(x * x, 1, keepdims=True) + epsilon)
        normed[span, :] = (x * inv * gain[...]).astype(bf16)
        branch[span, :] = middle_grad[span, :].astype(bf16)
        return 0
    lax.fori_loop(0, length // 256, prepare, 0)

    lefts = (attended, normed, normed, normed)
    rights = (branch, dv, dk, dq)
    streams = []
    for s in range(4):
        steps = fold_steps(width, width, orders[s % 2])
        row, col = 0, 0
        at = 0
        plan = []
        for bit, kind, r, c in steps:
            mine = own_bit(bit)
            if kind == "rows":
                keep_at, send_at = (row + mine * r, col), (row + (1 - mine) * r, col)
            elif kind == "cols":
                keep_at, send_at = (row, col + mine * c), (row, col + (1 - mine) * c)
            else:
                keep_at, send_at = (row, col), (row, col)
            plan.append((bit, kind, r, c, at, keep_at, send_at))
            row, col = keep_at
            at += r
        streams.append(plan)

    def rs_copy(s, k):
        bit, kind, r, c, at, _, _ = streams[s][k]
        return pltpu.make_async_remote_copy(
            src_ref=outbox.at[s, pl.ds(at, r), pl.ds(0, c)],
            dst_ref=inbox.at[s, pl.ds(at, r), pl.ds(0, c)],
            send_sem=ssend.at[s, k], recv_sem=srecv.at[s, k],
            device_id=partner(bit), device_id_type=MESH)

    def block(s, at, r, c):
        row, col = at
        row = pl.multiple_of(row, 16) if not isinstance(row, int) else row
        col = pl.multiple_of(col, 128) if not isinstance(col, int) else col
        return sums.at[s, pl.ds(row, r), pl.ds(col, c)]

    def ag_copy(s, k, incoming):
        bit, kind, r, c, _, keep_at, send_at = streams[s][k]
        ref = block(s, send_at if incoming else keep_at, r, c)
        return pltpu.make_async_remote_copy(
            src_ref=ref, dst_ref=ref,
            send_sem=ssend.at[s, count + k], recv_sem=srecv.at[s, count + k],
            device_id=partner(bit), device_id_type=MESH)

    half = width // 2
    core = own_bit(dpb[0])

    def grad(s, which):
        span = pl.ds(pl.multiple_of(which * half, half), half)
        return matmul_tn(lefts[s][:, span], rights[s][...])

    def local(s, k, at):
        base = streams[s][0][5][0]
        row, col = at
        row = row - base
        row = pl.multiple_of(row, 16) if not isinstance(row, int) else row
        col = pl.multiple_of(col, 128) if not isinstance(col, int) else col
        return row, col

    def phase(s, k):
        plan = streams[s]
        if k == 0:
            outbox[s, 0:half, :] = grad(s, 1 - core).astype(bf16)
            rs_copy(s, 0).start()
            acc[s] = grad(s, core)
            return
        if k <= count:
            bit, kind, r, c, at, keep_at, _ = plan[k - 1]
            rs_copy(s, k - 1).wait_recv()
            row, col = local(s, k - 1, keep_at)
            view = acc.at[s, pl.ds(row, r), pl.ds(col, c)]
            own = outbox[s, at : at + r, 0:c].astype(f32) if kind == "whole" else view[...]
            view[...] = own + inbox[s, at : at + r, 0:c].astype(f32)
            if k < count:
                bit, kind, r, c, at, keep_at, send_at = plan[k]
                row, col = local(s, k, send_at)
                outbox[s, at : at + r, 0:c] = acc[s, pl.ds(row, r), pl.ds(col, c)].astype(bf16)
                rs_copy(s, k).start()
                return
            block(s, keep_at, r, c)[...] = view[...].astype(bf16)
        g = 2 * count - 1 - k
        if k > count:
            prev = g + 1
            if plan[prev][1] != "whole":
                ag_copy(s, prev, True).wait_recv()
        if g >= 0 and plan[g][1] != "whole":
            ag_copy(s, g, False).start()

    gain_row = gain[...]
    rows = 256

    def norm_block(i, gain_grad):
        span = pl.ds(pl.multiple_of(i * rows, rows), rows)
        grads = (
            matmul_nt(dq[span, :], wq[...]) + matmul_nt(dk[span, :], wk[...]) + matmul_nt(dv[span, :], wv[...])
        )
        x = tokens[span, :].astype(f32)
        inv = lax.rsqrt(jnp.mean(x * x, 1, keepdims=True) + epsilon)
        scaled = grads * gain_row
        mean = jnp.sum(scaled * x, 1, keepdims=True) * (1.0 / width)
        part = inv * (scaled - x * (inv * inv * mean))
        token_grad[span, :] = (middle_grad[span, :] + part).astype(bf16)
        return gain_grad + jnp.sum(grads * (x * inv), 0, keepdims=True)

    slots = returned.shape[0]
    routes = routes_ref[...]
    pad = probs_ref.shape[0]
    hot = lax.broadcasted_iota(jnp.int32, (pad, length), 0) == routes
    gate_row = jnp.sum(jnp.where(hot, probs_ref[...], 0.0), 0, keepdims=True)

    def mix(c):
        at = slice(c, c + BLOCK)
        column = jnp.broadcast_to(slot_ref[0:1, at].astype(f32), (BLOCK, BLOCK)).T
        first = lax.broadcasted_iota(jnp.int32, (BLOCK, LANES), 1).astype(f32)
        spread = jnp.concatenate(
            [(column == first + float(s)).astype(f32).astype(bf16) for s in range(0, slots, LANES)], 1)
        rows_back = dot_nn(spread, returned[...])
        gate = jnp.broadcast_to(gate_row[:, at], (BLOCK, BLOCK)).T
        gate = jnp.concatenate([gate] * (width // LANES), 1)
        mixed[at, :] = (middle[at, :] + gate * rows_back).astype(bf16)

    def small_copy(k):
        return pltpu.make_async_remote_copy(
            src_ref=small_sent.at[k], dst_ref=small_box.at[k],
            send_sem=tsend.at[k], recv_sem=trecv.at[k],
            device_id=partner(every[k]), device_id_type=MESH)

    def small_phase(k):
        if k == 0:
            gain_grad = lax.fori_loop(0, length // rows, norm_block, jnp.zeros((1, width), f32))
            small_out[...] = small_in[...]
            for i in range(width // LANES):
                small_out[i : i + 1, :] = gain_grad[:, i * LANES : (i + 1) * LANES]
        else:
            small_copy(k - 1).wait_recv()
            small_out[...] = small_out[...] + small_box[k - 1]
        if k < count:
            small_sent[k] = small_out[...]
            small_copy(k).start()

    last = 2 * count
    for t in range(last + 4):
        for s in range(4):
            if 0 <= t - s <= last:
                phase(s, t - s)
        if 4 <= t and t - 4 <= count:
            small_phase(t - 4)
        if 5 <= t and t - 5 < length // BLOCK:
            mix((t - 5) * BLOCK)
    for s in range(4):
        for k in range(count):
            rs_copy(s, k).wait_send()
            if streams[s][k][1] != "whole":
                ag_copy(s, k, False).wait_send()
    for k in range(count):
        small_copy(k).wait_send()


def reduce_grads(tokens, attended, middle_grad, dq, dk, dv, wq, wk, wv, gain, small,
                 returned, slot, routes_row, probs, middle, dp_size, groups):
    f32, bf16 = jnp.float32, jnp.bfloat16
    length, width = tokens.shape
    dp_bits, expert_bits = dp_size.bit_length() - 1, groups.bit_length() - 1
    count = dp_bits + expert_bits
    box = sum(step[2] for step in fold_steps(width, width, range(count)))
    vmem = pl.BlockSpec(memory_space=pltpu.VMEM)
    sem = pltpu.SemaphoreType.DMA
    shape = jax.ShapeDtypeStruct
    return pl.pallas_call(
        functools.partial(reduce_kernel, dp_bits=dp_bits, expert_bits=expert_bits),
        out_shape=(shape((4, width, width), bf16), shape((length, width), bf16), shape(small.shape, f32),
                   shape((length, width), bf16)),
        in_specs=[vmem] * 16,
        out_specs=(vmem,) * 4,
        scratch_shapes=[
            pltpu.VMEM((length, width), bf16),
            pltpu.VMEM((length, width), bf16),
            pltpu.VMEM((4, width // 2, width), f32),
            pltpu.VMEM((4, box, width), bf16),
            pltpu.VMEM((4, box, width), bf16),
            pltpu.VMEM((count,) + small.shape, f32),
            pltpu.VMEM((count,) + small.shape, f32),
            sem((4, 2 * count)), sem((4, 2 * count)), sem((count,)), sem((count,)),
        ],
        compiler_params=pltpu.CompilerParams(
            collective_id=2, has_side_effects=True, vmem_limit_bytes=62 << 20
        ),
        cost_estimate=pl.CostEstimate(
            flops=14 * length * width * width, bytes_accessed=30 << 20, transcendentals=0
        ),
    )(tokens, attended, middle_grad, dq, dk, dv, wq, wk, wv, gain, small, returned, slot, routes_row, probs, middle)


def key_ranges(segment_row):
    first, last = segment_row[::BLOCK], segment_row[BLOCK - 1 :: BLOCK]
    lo = jnp.sum(segment_row[None, :] < first[:, None], 1) // BLOCK
    hi = (jnp.sum(segment_row[None, :] <= last[:, None], 1) + BLOCK - 1) // BLOCK
    return lo.astype(jnp.int32), hi.astype(jnp.int32)


def bias_grad(sums, heads, bucket_count):
    near = lax.broadcasted_iota(jnp.int32, (NEAR, 2 * LANES), 0)
    place = lax.broadcasted_iota(jnp.int32, (NEAR, 2 * LANES), 1)
    bucket = bucket_of((near - 2) * BLOCK + BLOCK - 1 - place)
    bucket = jnp.where(near == 0, 15, jnp.where(near == NEAR - 1, 31, bucket))
    hot = (bucket.reshape(-1)[:, None] == lax.iota(jnp.int32, bucket_count)[None, :]).astype(jnp.float32)
    return jnp.dot(sums.reshape(heads, -1), hot, precision=precise_setting).T


def per_device(
    tokens,
    segments,
    routes,
    cotangent,
    attn_gain,
    ffn_gain,
    query_weight,
    key_weight,
    value_weight,
    output_weight,
    position_bias_grid,
    router_weight,
    expert_in,
    expert_out,
):
    f32, bf16 = jnp.float32, jnp.bfloat16
    token_count, model_width = tokens.shape
    bucket_count, head_count = position_bias_grid.shape
    score_scale = (model_width // head_count) ** (-0.5)
    experts_all = router_weight.shape[1]
    capacity = (5 * token_count + 4 * experts_all - 1) // (4 * experts_all)
    slot_rows = (capacity + 15) // 16 * 16
    slots = experts_all * slot_rows
    groups = lax.axis_size("expert")
    dp_size = lax.axis_size("dp")

    def exchange(rows):
        return lax.all_to_all(rows, "expert", split_axis=0, concat_axis=0, tiled=True)

    routes_row = routes.reshape(1, token_count)
    token_slot, grad_slots = first_slots(routes_row, cotangent, experts_all, capacity, slot_rows)
    grad_arrived = exchange(grad_slots)
    lo, hi = key_ranges(segments[0])
    router_pad = max(experts_all, 16)
    router_t = jnp.pad(router_weight.T, ((0, router_pad - experts_all), (0, 0)))
    gain_one, gain_two = attn_gain[None, :], ffn_gain[None, :]
    queries, key_rows, keys_t, value_rows, attended, log_sums, middle, router_probs, sent, gate_slots = front(
        lo, hi, tokens, segments, token_slot, routes_row, gain_one, gain_two,
        query_weight, key_weight, value_weight, output_weight, position_bias_grid, router_t,
        experts_all, slot_rows, score_scale,
    )
    home_grad, home_gate, produced, keep, give = ffn(
        sent, gate_slots, grad_arrived.reshape(slots, model_width), expert_in[0], expert_out[0], groups, dp_size,
    )
    passed = lax.ppermute(give, "dp", [(i, (i + dp_size // 2) % dp_size) for i in range(dp_size)])
    weight_grads = keep.astype(f32) + passed.astype(f32)
    in_weight_grad, out_weight_grad = weight_grads[0], weight_grads[1]
    returned = exchange(produced.reshape(experts_all, slot_rows, model_width)).reshape(slots, model_width)
    query_grad, key_grad, value_grad, diag_sums, middle_grad, router_grad, ffn_gain_grad = back(
        lo, hi, home_grad, home_gate, token_slot, routes_row, router_probs, middle, cotangent, segments, gain_two,
        output_weight, router_t, position_bias_grid, queries, key_rows, keys_t, value_rows, log_sums, attended,
        experts_all, slot_rows, score_scale,
    )
    table_grad = bias_grad(diag_sums, head_count, bucket_count)
    router_grad = router_grad[:experts_all]
    flat = jnp.concatenate(
        [jnp.zeros((model_width,), f32), ffn_gain_grad.reshape(-1), router_grad.reshape(-1), table_grad.reshape(-1)]
    )
    small_rows = -(-flat.shape[0] // (8 * LANES)) * 8
    small = jnp.pad(flat, (0, small_rows * LANES - flat.shape[0])).reshape(small_rows, LANES)
    weights, token_grad, small, mixed = reduce_grads(
        tokens, attended, middle_grad, query_grad, key_grad, value_grad,
        query_weight, key_weight, value_weight, gain_one, small,
        returned, token_slot, routes_row, router_probs, middle, dp_size, groups,
    )
    weights = weights.astype(f32)
    flat = small.reshape(-1)
    ends = [model_width, 2 * model_width]
    ends.append(ends[-1] + router_grad.size)
    ends.append(ends[-1] + table_grad.size)
    return (
        mixed,
        token_grad,
        flat[: ends[0]],
        flat[ends[0] : ends[1]],
        weights[3],
        weights[2],
        weights[1],
        weights[0],
        flat[ends[2] : ends[3]].reshape(table_grad.shape),
        flat[ends[1] : ends[2]].reshape(experts_all, model_width).T,
        in_weight_grad[None],
        out_weight_grad[None],
    )


def solution(mesh):
    rows = P(("dp", "expert"), None)
    return jax.shard_map(
        per_device,
        mesh=mesh,
        in_specs=(rows,) * 4 + (P(),) * 8 + (P("expert", None, None),) * 2,
        out_specs=(rows,) * 2 + (P(),) * 8 + (P("expert", None, "dp"), P("expert", "dp", None)),
        check_vma=False,
    )
```

```python
import functools

import jax
import jax.numpy as jnp
from jax import lax
from jax.experimental import pallas as pl
from jax.experimental.pallas import tpu as pltpu
from jax.sharding import PartitionSpec as P

epsilon = 1e-06
precise_setting = lax.Precision.HIGHEST
def matmul(left, right):
    return jnp.dot(left, right, preferred_element_type=jnp.float32)


def matmul_tn(left, right):
    return lax.dot_general(left, right, (((0,), (0,)), ((), ())), preferred_element_type=jnp.float32)


def matmul_nt(left, right):
    return lax.dot_general(left, right, (((1,), (1,)), ((), ())), preferred_element_type=jnp.float32)


bucket_bounds = (12, 16, 23, 32, 46, 64, 91)
masked_score = -1e30
LANES = 128
BLOCK = 128
NEAR = 5
UF = 6
UB = 6


def bucket_of(relative):
    distance = jnp.abs(relative)
    beyond = jnp.zeros_like(distance)
    for threshold in bucket_bounds:
        beyond = beyond + (distance >= threshold).astype(jnp.int32)
    inside = jnp.where(distance < 8, distance, 8 + beyond)
    return inside + 16 * (relative > 0).astype(jnp.int32)


def dot_nt(a, b):
    return lax.dot_general(a, b, (((1,), (1,)), ((), ())), preferred_element_type=jnp.float32)


def dot_nn(a, b):
    return lax.dot_general(a, b, (((1,), (0,)), ((), ())), preferred_element_type=jnp.float32)


def split3(x):
    a = x.astype(jnp.bfloat16)
    r = x - a.astype(jnp.float32)
    b = r.astype(jnp.bfloat16)
    c = (r - b.astype(jnp.float32)).astype(jnp.bfloat16)
    return a, b, c


def fill_bias(diag_ref, bias, pairs):
    for p in range(pairs):
        for d in range(NEAR):
            tiles = []
            for h in (2 * p, 2 * p + 1):
                row = diag_ref[h : h + 1, :]
                if d in (0, NEAR - 1):
                    col = row[:, 511:512] if d == 0 else row[:, 0:1]
                    tiles.append(jnp.broadcast_to(col, (BLOCK, BLOCK)))
                else:
                    base = (3 - d) * BLOCK
                    wide = jnp.broadcast_to(row[:, base : base + 2 * BLOCK], (BLOCK, 2 * BLOCK))
                    tiles.append(pltpu.roll(wide, BLOCK, 1, stride=1, stride_axis=0)[:, :BLOCK])
            bias[p, d] = jnp.concatenate(tiles, 1)


def heads_apart(block, low, extra=None):
    zero = jnp.zeros_like(block)
    first, second = jnp.where(low, block, zero), jnp.where(low, zero, block)
    if extra is not None:
        first, second = jnp.concatenate([first, extra], 1), jnp.concatenate([second, extra], 1)
    return jnp.concatenate([first, second], 0)


def by_count(lo, hi, most, body):
    for n in range(1, most + 1):
        pl.when(hi - lo == n)(functools.partial(body, n))


def own_heads(wide):
    return jnp.concatenate([wide[:64, :LANES], wide[64:128, LANES:]], 0)


def attend(lo_ref, hi_ref, q_ref, k_ref, vt_ref, qm_ref, km_ref, bias, o_ref, lse_ref):
    pairs = q_ref.shape[1] // LANES
    length = q_ref.shape[0]
    nblk = length // BLOCK
    f32, bf16 = jnp.float32, jnp.bfloat16
    low = lax.broadcasted_iota(jnp.int32, (1, LANES), 1) < 64

    def q_block(i, _):
        lo, hi = lo_ref[i], hi_ref[i]
        rows = pl.ds(pl.multiple_of(i * BLOCK, BLOCK), BLOCK)
        start = pl.multiple_of(lo * BLOCK, BLOCK)
        qm = qm_ref[rows, :]

        def body(n):
            span = pl.ds(start, n * BLOCK)
            km = km_ref[span, :]

            def lanes_of(p):
                return pl.ds(pl.multiple_of(p * LANES, LANES), LANES)

            def scores(p):
                qs = heads_apart(q_ref[rows, lanes_of(p)], low, qm)
                return dot_nt(jnp.concatenate([k_ref[span, lanes_of(p)], km], 1), qs)

            def soften(p, st):
                parts = []
                top = None
                for b in range(n):
                    d = jnp.clip(lo + b - i, -2, 2) + 2
                    s = st[b * BLOCK : (b + 1) * BLOCK] + bias[p, d]
                    parts.append(s)
                    top = s if top is None else jnp.maximum(top, s)
                top = jnp.max(top, 0, keepdims=True)
                return jnp.concatenate([jnp.exp(s - top).astype(bf16) for s in parts], 0), top

            def mix(p, probs):
                values = jnp.concatenate([vt_ref[lanes_of(p), span], jnp.ones((16, n * BLOCK), bf16)], 0)
                return dot_nn(values, probs)

            def finish(p, acc, top):
                total = acc[LANES : LANES + 1]
                inv = 1.0 / total
                ot = own_heads(acc)
                ot = jnp.concatenate([ot[:64] * inv[:, :LANES], ot[64:] * inv[:, LANES:]], 0)
                o_ref[rows, lanes_of(p)] = ot.T.astype(bf16)
                lse_ref[i, pl.ds(p, 1), :] = top + jnp.log(total)

            def some(g, _):
                ps = [g * UF + u for u in range(UF)]
                sts = [scores(p) for p in ps]
                soft = [soften(p, st) for p, st in zip(ps, sts)]
                accs = [mix(p, x[0]) for p, x in zip(ps, soft)]
                for p, acc, x in zip(ps, accs, soft):
                    finish(p, acc, x[1])
                return 0
            lax.fori_loop(0, pairs // UF, some, 0)

        by_count(lo, hi, nblk, body)
        return 0
    lax.fori_loop(0, nblk, q_block, 0)


def attend_back(
    lo_ref, hi_ref, q_ref, k_ref, kt_ref, v_ref, lse_ref, do_ref, o_ref, qm_ref, km_ref, bias,
    dq_ref, dk_ref, dv_ref, gsum_ref, gacc, dkacc, dvacc, scale,
):
    length, width = q_ref.shape
    pairs = width // LANES
    nblk = length // BLOCK
    f32, bf16 = jnp.float32, jnp.bfloat16
    low = lax.broadcasted_iota(jnp.int32, (1, LANES), 1) < 64
    pick = (
        lax.broadcasted_iota(jnp.int32, (16, LANES), 0) == lax.broadcasted_iota(jnp.int32, (16, LANES), 1) // 64
    ).astype(f32).astype(bf16)
    gacc[...] = jnp.zeros_like(gacc)
    dkacc[...] = jnp.zeros_like(dkacc)
    dvacc[...] = jnp.zeros_like(dvacc)

    def q_block(i, _):
        lo, hi = lo_ref[i], hi_ref[i]
        rows = pl.ds(pl.multiple_of(i * BLOCK, BLOCK), BLOCK)
        start = pl.multiple_of(lo * BLOCK, BLOCK)
        qm = qm_ref[rows, :]

        def body(n):
            span = pl.ds(start, n * BLOCK)
            km = km_ref[span, :]

            def lanes_of(p):
                return pl.ds(pl.multiple_of(p * LANES, LANES), LANES)

            def products(p):
                cols = lanes_of(p)
                qs = heads_apart(q_ref[rows, cols], low, qm)
                dd = do_ref[rows, cols]
                dos = heads_apart(dd, low)
                prod = dd.astype(f32) * o_ref[rows, cols].astype(f32)
                prod_hi = prod.astype(bf16)
                prod_lo = (prod - prod_hi.astype(f32)).astype(bf16)
                inner = dot_nt(pick, prod_hi) + dot_nt(pick, prod_lo)
                inner = jnp.concatenate([inner[0:1], inner[1:2]], 1)
                st = dot_nt(jnp.concatenate([k_ref[span, cols], km], 1), qs)
                dpt = dot_nt(v_ref[span, cols], dos)
                return qs, dos, inner, st, dpt

            def pointwise(p, inner, st, dpt):
                lse = lse_ref[i, pl.ds(p, 1), :]
                probs, grads = [], []
                for b in range(n):
                    d = jnp.clip(lo + b - i, -2, 2) + 2
                    part = slice(b * BLOCK, (b + 1) * BLOCK)
                    prob = jnp.exp(st[part] + bias[p, d] - lse)
                    grad = prob * (dpt[part] - inner)
                    gacc[p, d] += grad
                    probs.append(prob.astype(bf16))
                    grads.append(grad.astype(bf16))
                return jnp.concatenate(probs, 0), jnp.concatenate(grads, 0)

            def back(p, qs, dos, probs, grads):
                cols = lanes_of(p)
                return (
                    dot_nn(probs, dos), dot_nn(grads, qs[:, :LANES]), dot_nn(kt_ref[cols, span], grads)
                )

            def finish(p, dv, dk, dqt):
                cols = lanes_of(p)
                dvacc[span, cols] += dv
                dkacc[span, cols] += dk
                dq_ref[rows, cols] = (own_heads(dqt).T * scale).astype(bf16)

            def some(g, _):
                ps = [g * UB + u for u in range(UB)]
                first = [products(p) for p in ps]
                points = [pointwise(p, *x[2:]) for p, x in zip(ps, first)]
                last = [back(p, *x[:2], *y) for p, x, y in zip(ps, first, points)]
                for p, x in zip(ps, last):
                    finish(p, *x)
                return 0
            lax.fori_loop(0, pairs // UB, some, 0)

        by_count(lo, hi, nblk, body)
        return 0
    lax.fori_loop(0, nblk, q_block, 0)
    dk_ref[...] = dkacc[...].astype(bf16)
    dv_ref[...] = dvacc[...].astype(bf16)
    turn = (
        lax.broadcasted_iota(jnp.int32, (BLOCK, BLOCK), 0) + lax.broadcasted_iota(jnp.int32, (BLOCK, BLOCK), 1)
        == BLOCK - 1
    ).astype(f32).astype(bf16)
    for p in range(pairs):
        for d in range(NEAR):
            t = gacc[p, d]
            if 0 < d < NEAR - 1:
                hi = t.astype(bf16)
                t = dot_nn(turn, hi) + dot_nn(turn, (t - hi.astype(f32)).astype(bf16))
            for u in range(2):
                s = jnp.concatenate([t[:, u * LANES : (u + 1) * LANES], jnp.zeros((BLOCK, LANES), f32)], 1)
                if 0 < d < NEAR - 1:
                    s = pltpu.roll(s, 0, 1, stride=1, stride_axis=0)
                at = (2 * p + u) * NEAR + d
                gsum_ref[at : at + 1, :] = jnp.sum(s, 0, keepdims=True)


def two(x):
    a = x.astype(jnp.bfloat16)
    return a, (x - a.astype(jnp.float32)).astype(jnp.bfloat16)


def row_pieces(row):
    place = lax.broadcasted_iota(jnp.int32, (16, row.shape[1]), 0)
    a, b, c = [x.astype(jnp.float32) for x in split3(row)]
    return jnp.where(place == 0, a, jnp.where(place == 1, b, jnp.where(place == 2, c, 0.0))).astype(jnp.bfloat16)


def each(count, body):
    if count <= 8:
        for e in range(count):
            body(e)
    else:
        def step(e, _):
            body(e)
            return 0
        lax.fori_loop(0, count, step, 0)


def slot_hot(slot_row, e, slot_rows):
    place = lax.broadcasted_iota(jnp.int32, (slot_rows, slot_row.shape[1]), 0) + e * slot_rows
    return (place == slot_row).astype(jnp.float32).astype(jnp.bfloat16)


def slots_kernel(routes_ref, rows_ref, slot_ref, out_ref, *, experts, capacity, slot_rows):
    f32, bf16 = jnp.float32, jnp.bfloat16
    tokens = routes_ref.shape[1]
    routes = routes_ref[...]
    pad = max(experts, 16)
    hot = (lax.broadcasted_iota(jnp.int32, (pad, tokens), 0) == routes).astype(f32)
    earlier = (
        lax.broadcasted_iota(jnp.int32, (tokens, tokens), 0) < lax.broadcasted_iota(jnp.int32, (tokens, tokens), 1)
    ).astype(f32).astype(bf16)
    ranks = dot_nn(hot.astype(bf16), earlier)
    rank = jnp.sum(ranks * hot, 0, keepdims=True).astype(jnp.int32)
    slot = jnp.where(rank < capacity, routes * slot_rows + rank, -1)
    slot_ref[...] = jnp.broadcast_to(slot, slot_ref.shape)

    def one(e):
        out_ref[e] = dot_nn(slot_hot(slot, e, slot_rows), rows_ref[...]).astype(bf16)
    each(experts, one)


def first_slots(routes_row, rows, experts, capacity, slot_rows):
    tokens, width = rows.shape
    vmem = pl.BlockSpec(memory_space=pltpu.VMEM)
    return pl.pallas_call(
        functools.partial(slots_kernel, experts=experts, capacity=capacity, slot_rows=slot_rows),
        out_shape=(
            jax.ShapeDtypeStruct((8, tokens), jnp.int32),
            jax.ShapeDtypeStruct((experts, slot_rows, width), jnp.bfloat16),
        ),
        in_specs=[vmem] * 2,
        out_specs=(vmem,) * 2,
        compiler_params=pltpu.CompilerParams(vmem_limit_bytes=60 << 20),
        cost_estimate=pl.CostEstimate(
            flops=2 * experts * slot_rows * tokens * width, bytes_accessed=4 << 20, transcendentals=0
        ),
    )(routes_row, rows)


def fill_masks(segment_row, qm, km):
    f32, bf16 = jnp.float32, jnp.bfloat16
    lane = lax.broadcasted_iota(jnp.int32, (1, LANES), 1)
    for b in range(qm.shape[0] // BLOCK):
        span = slice(b * BLOCK, (b + 1) * BLOCK)
        hot = (lax.broadcasted_iota(jnp.int32, (LANES, BLOCK), 0) == segment_row[:, span]).astype(f32).T
        qm[span, :] = (hot * masked_score).astype(bf16)
        km[span, :] = jnp.where(lane < 8, 1.0 - hot, 0.0).astype(bf16)


def fill_diag(grid_ref, diag, heads):
    bf16 = jnp.bfloat16
    buckets = grid_ref.shape[0]
    relative = 256 - lax.broadcasted_iota(jnp.int32, (buckets, 4 * LANES), 1)
    hot = (lax.broadcasted_iota(jnp.int32, (buckets, 4 * LANES), 0) == bucket_of(relative))
    hot = hot.astype(jnp.float32).astype(bf16)
    grid = jnp.concatenate(
        [grid_ref[...], jnp.zeros((buckets, LANES - heads), jnp.float32)], 1
    ).T[:16]
    total = None
    for piece in split3(grid):
        term = dot_nn(piece, hot)
        total = term if total is None else total + term
    diag[...] = total


def front_kernel(
    lo_ref, hi_ref, tokens, segment_row, slot_ref, routes_ref, gain_one, gain_two, wq, wk, wv, wo, grid_ref, router_t,
    q_ref, k_ref, kt_ref, v_ref, o_ref, lse_ref, middle_ref, probs_ref, xs_ref, gs_ref,
    vt_ref, qm_ref, km_ref, diag, bias, hidden, *, experts, slot_rows, scale,
):
    f32, bf16 = jnp.float32, jnp.bfloat16
    length, width = tokens.shape
    pairs = width // LANES
    nblk = length // BLOCK
    heads = grid_ref.shape[1]
    low = lax.broadcasted_iota(jnp.int32, (1, LANES), 1) < 64
    step = 256

    for b in range(length // step):
        span = slice(b * step, (b + 1) * step)
        x = tokens[span, :].astype(f32)
        inverse = lax.rsqrt(jnp.mean(x * x, 1, keepdims=True) + epsilon)
        normed = (x * inverse * gain_one[...]).astype(bf16)
        q_ref[span, :] = (dot_nn(normed, wq[...]).astype(bf16).astype(f32) * scale).astype(bf16)
        k = dot_nn(normed, wk[...]).astype(bf16)
        k_ref[span, :] = k
        kt_ref[:, span] = k.T
        v = dot_nn(normed, wv[...]).astype(bf16)
        v_ref[span, :] = v
        vt_ref[:, span] = v.T
    fill_masks(segment_row[...], qm_ref, km_ref)
    fill_diag(grid_ref, diag, heads)
    fill_bias(diag, bias, pairs)
    attend(lo_ref, hi_ref, q_ref, k_ref, vt_ref, qm_ref, km_ref, bias, o_ref, lse_ref)

    rw = two(router_t[...])
    routes = routes_ref[...]
    pad = router_t.shape[0]
    place = lax.broadcasted_iota(jnp.int32, (pad, step), 0)
    gates = []
    for b in range(length // step):
        span = slice(b * step, (b + 1) * step)
        middle = tokens[span, :].astype(f32) + dot_nn(o_ref[span, :], wo[...])
        middle_ref[span, :] = middle
        inverse = lax.rsqrt(jnp.mean(middle * middle, 1, keepdims=True) + epsilon)
        parts = two(middle * inverse * gain_two[...])
        hidden[span, :] = parts[0]
        logits = dot_nt(rw[0], parts[0]) + dot_nt(rw[0], parts[1]) + dot_nt(rw[1], parts[0])
        logits = jnp.where(place < experts, logits, -1e30)
        powers = jnp.exp(logits - jnp.max(logits, 0, keepdims=True))
        probs = powers / jnp.sum(powers, 0, keepdims=True)
        probs_ref[:, span] = probs
        gates.append(jnp.sum(jnp.where(place == routes[:, span], probs, 0.0), 0, keepdims=True))
    gates = row_pieces(jnp.concatenate(gates, 1))
    slot = slot_ref[0:1, :]
    lanes = gs_ref.shape[2]

    def one(e):
        hot = slot_hot(slot, e, slot_rows)
        xs_ref[e] = dot_nn(hot, hidden[...]).astype(bf16)
        if lanes > slot_rows:
            hot = jnp.concatenate([hot, jnp.zeros((lanes - slot_rows, length), bf16)], 0)
        row = jnp.sum(dot_nt(gates, hot), 0, keepdims=True)
        gs_ref[e] = jnp.broadcast_to(row, gs_ref.shape[1:])
    each(experts, one)


def front(lo, hi, tokens, segments, slot, routes_row, gain_one, gain_two, wq, wk, wv, wo, grid, router_t, experts, slot_rows, scale):
    length, width = tokens.shape
    heads = grid.shape[1]
    pairs = width // LANES
    nblk = length // BLOCK
    lanes = (slot_rows + LANES - 1) // LANES * LANES
    smem = pl.BlockSpec(memory_space=pltpu.SMEM)
    vmem = pl.BlockSpec(memory_space=pltpu.VMEM)
    f32, bf16 = jnp.float32, jnp.bfloat16
    shape = jax.ShapeDtypeStruct
    act = shape((length, width), bf16)
    return pl.pallas_call(
        functools.partial(front_kernel, experts=experts, slot_rows=slot_rows, scale=scale),
        out_shape=(
            act, act, shape((width, length), bf16), act, act,
            shape((nblk, 8, 2 * LANES), f32), shape((length, width), f32),
            shape((router_t.shape[0], length), f32),
            shape((experts, slot_rows, width), bf16), shape((experts, 8, lanes), f32),
        ),
        in_specs=[smem] * 2 + [vmem] * 12,
        out_specs=(vmem,) * 10,
        scratch_shapes=[
            pltpu.VMEM((width, length), bf16),
            pltpu.VMEM((length, LANES), bf16),
            pltpu.VMEM((length, LANES), bf16),
            pltpu.VMEM((16, 4 * LANES), f32),
            pltpu.VMEM((pairs, NEAR, BLOCK, 2 * LANES), f32),
            pltpu.VMEM((length, width), bf16),
        ],
        compiler_params=pltpu.CompilerParams(vmem_limit_bytes=60 << 20),
        cost_estimate=pl.CostEstimate(
            flops=4 * length * length * width + 12 * length * width * width, bytes_accessed=20 << 20,
            transcendentals=length * length * heads,
        ),
    )(lo, hi, tokens, segments, slot, routes_row, gain_one, gain_two, wq, wk, wv, wo, grid, router_t)


def back_kernel(
    lo_ref, hi_ref, home, home_gate, slot_ref, routes_ref, probs_ref, middle_ref, cotangent, segment_row, gain_two,
    wo, router_t, grid_ref, q_ref, k_ref, kt_ref, v_ref, lse_ref, o_ref,
    dq_ref, dk_ref, dv_ref, gsum_ref, middle_grad, router_grad, gain_grad,
    do_ref, qm_ref, km_ref, diag, bias, gacc, dkacc, dvacc, logit, *, experts, slot_rows, scale,
):
    f32, bf16 = jnp.float32, jnp.bfloat16
    length, width = middle_ref.shape
    pairs = width // LANES
    pad = router_t.shape[0]
    heads = grid_ref.shape[1]
    slot = slot_ref[0:1, :]
    lanes = home_gate.shape[2]

    gate_grad = [jnp.zeros((16, length), f32)]
    if experts <= 8:
        total = jnp.zeros((16, length), f32)
        for e in range(experts):
            total = total + dot_nn(row_pieces(home_gate[e, 0:1, :])[:, :slot_rows], slot_hot(slot, e, slot_rows))
    else:
        def add(e, total):
            return total + dot_nn(row_pieces(home_gate[e, 0:1, :])[:, :slot_rows], slot_hot(slot, e, slot_rows))
        total = lax.fori_loop(0, experts, add, jnp.zeros((16, length), f32))
    gate_grad = jnp.sum(total, 0, keepdims=True)
    place = lax.broadcasted_iota(jnp.int32, (pad, length), 0)
    hot = place == routes_ref[...]
    probs = probs_ref[...]
    gate = jnp.sum(jnp.where(hot, probs, 0.0), 0, keepdims=True)
    logit[...] = probs * (jnp.where(hot, gate_grad, 0.0) - gate * gate_grad)
    rw = two(router_t[...])
    slots = experts * slot_rows
    router_sum = jnp.zeros((pad, width), f32)
    gain_sum = jnp.zeros((1, width), f32)
    step = 256
    for b in range(length // step):
        span = slice(b * step, (b + 1) * step)
        hots = []
        for c in range(b * step, (b + 1) * step, BLOCK):
            column = jnp.broadcast_to(slot[:, c : c + BLOCK].astype(f32), (BLOCK, BLOCK)).T
            first = lax.broadcasted_iota(jnp.int32, (BLOCK, LANES), 1).astype(f32)
            hots.append(jnp.concatenate(
                [(column == first + float(s)).astype(f32).astype(bf16) for s in range(0, slots, LANES)], 1))
        spread = jnp.concatenate(hots, 0)
        hidden_grad = dot_nn(spread, home[...].reshape(slots, width))
        lg = two(logit[:, span])
        hidden_grad = hidden_grad + (
            matmul_tn(lg[0], rw[0]) + matmul_tn(lg[0], rw[1]) + matmul_tn(lg[1], rw[0])
        )
        middle = middle_ref[span, :]
        inverse = lax.rsqrt(jnp.mean(middle * middle, 1, keepdims=True) + epsilon)
        unit = middle * inverse
        hidden = two(unit * gain_two[...])
        router_sum = router_sum + (dot_nn(lg[0], hidden[0]) + dot_nn(lg[0], hidden[1]) + dot_nn(lg[1], hidden[0]))
        gain_sum = gain_sum + jnp.sum(hidden_grad * unit, 0, keepdims=True)
        scaled = hidden_grad * gain_two[...]
        mean = jnp.mean(scaled * middle, 1, keepdims=True)
        grad = cotangent[span, :].astype(f32) + inverse * (scaled - unit * (inverse * mean))
        middle_grad[span, :] = grad
        do_ref[span, :] = matmul_nt(grad.astype(bf16), wo[...]).astype(bf16)
    router_grad[...] = router_sum
    gain_grad[...] = gain_sum

    fill_masks(segment_row[...], qm_ref, km_ref)
    fill_diag(grid_ref, diag, heads)
    fill_bias(diag, bias, pairs)
    attend_back(
        lo_ref, hi_ref, q_ref, k_ref, kt_ref, v_ref, lse_ref, do_ref, o_ref, qm_ref, km_ref, bias,
        dq_ref, dk_ref, dv_ref, gsum_ref, gacc, dkacc, dvacc, scale,
    )


def back(lo, hi, home, home_gate, slot, routes_row, probs, middle, cotangent, segments, gain_two, wo, router_t, grid,
         q, k, kt, v, lse, o, experts, slot_rows, scale):
    length, width = middle.shape
    heads = grid.shape[1]
    pairs = width // LANES
    smem = pl.BlockSpec(memory_space=pltpu.SMEM)
    vmem = pl.BlockSpec(memory_space=pltpu.VMEM)
    f32, bf16 = jnp.float32, jnp.bfloat16
    shape = jax.ShapeDtypeStruct
    act = shape((length, width), bf16)
    return pl.pallas_call(
        functools.partial(back_kernel, experts=experts, slot_rows=slot_rows, scale=scale),
        out_shape=(
            act, act, act, shape((heads * NEAR, 2 * LANES), f32), shape((length, width), f32),
            shape((router_t.shape[0], width), f32), shape((1, width), f32),
        ),
        in_specs=[smem] * 2 + [vmem] * 18,
        out_specs=(vmem,) * 7,
        scratch_shapes=[
            pltpu.VMEM((length, width), bf16),
            pltpu.VMEM((length, LANES), bf16),
            pltpu.VMEM((length, LANES), bf16),
            pltpu.VMEM((16, 4 * LANES), f32),
            pltpu.VMEM((pairs, NEAR, BLOCK, 2 * LANES), f32),
            pltpu.VMEM((pairs, NEAR, BLOCK, 2 * LANES), f32),
            pltpu.VMEM((length, width), f32),
            pltpu.VMEM((length, width), f32),
            pltpu.VMEM((router_t.shape[0], length), f32),
        ],
        compiler_params=pltpu.CompilerParams(vmem_limit_bytes=60 << 20),
        cost_estimate=pl.CostEstimate(
            flops=10 * length * length * width + 6 * length * width * width, bytes_accessed=30 << 20,
            transcendentals=length * length * heads,
        ),
    )(lo, hi, home, home_gate, slot, routes_row, probs, middle, cotangent, segments, gain_two, wo, router_t, grid,
      q, k, kt, v, lse, o)


def gelu_parts(v):
    mag = jnp.abs(v)
    t = 1.0 / (1.0 + (0.3275911 * 0.7071067811865476) * mag)
    poly = t * (0.127414796 + t * (-0.142248368 + t * (0.7107068705 + t * (-0.7265760135 + t * 0.5307027145))))
    gauss = jnp.exp(-0.5 * v * v)
    tail = poly * gauss
    phi = jnp.where(v < 0, tail, 1.0 - tail)
    return v * phi, phi + v * gauss * 0.3989422804014327


def flip_bits(index, mask, count):
    out = 0
    bit = 1
    while bit < count:
        a, b = (index // bit) % 2, (mask // bit) % 2
        out = out + bit * (a + b - 2 * a * b)
        bit *= 2
    return out


def ffn_kernel(
    xs, gs, g, win_hbm, wout_hbm,
    home, home_gate, produced, keep, give,
    win, wout, xr, gr, act, pg, gated, igs, ggs, dws, dwr, stage,
    wsem, own_sem, psem, ksem, xsend, xrecv, gsend, grecv, isend, irecv, qsend, qrecv, dsend, drecv,
    *, groups, dp_size, tiles,
):
    f32, bf16 = jnp.float32, jnp.bfloat16
    me = lax.axis_index("expert")
    dp = lax.axis_index("dp")
    core = dp % 2
    sibling = dp + 1 - 2 * core
    rows = xs.shape[1]
    width = xs.shape[2]
    hidden = win.shape[1]
    tile = hidden // tiles
    lanes = gs.shape[2]

    def there(peer):
        return (dp, peer)

    load_in = pltpu.make_async_copy(win_hbm, win, wsem.at[0])
    load_out = pltpu.make_async_copy(wout_hbm, wout, wsem.at[1])
    load_in.start()
    load_out.start()
    load_g = pltpu.make_async_copy(g, gated, wsem.at[2])
    load_g.start()

    barrier = pltpu.get_barrier_semaphore()

    def greet(s, _):
        pl.semaphore_signal(
            barrier, inc=1, device_id=there(flip_bits(me, s, groups)), device_id_type=pl.DeviceIdType.MESH
        )
        return 0
    lax.fori_loop(1, groups, greet, 0)
    pl.semaphore_signal(barrier, inc=1, device_id=(sibling, me), device_id_type=pl.DeviceIdType.MESH)
    pl.semaphore_wait(barrier, groups)

    def x_copy(peer, slot):
        return pltpu.make_async_remote_copy(
            src_ref=xs.at[peer], dst_ref=xr.at[slot], send_sem=xsend.at[peer], recv_sem=xrecv.at[slot],
            device_id=there(peer), device_id_type=pl.DeviceIdType.MESH)

    def g_copy(peer, slot):
        return pltpu.make_async_remote_copy(
            src_ref=gs.at[peer], dst_ref=gr.at[slot], send_sem=gsend.at[peer], recv_sem=grecv.at[slot],
            device_id=there(peer), device_id_type=pl.DeviceIdType.MESH)

    def i_copy(peer, slot):
        return pltpu.make_async_remote_copy(
            src_ref=igs.at[peer], dst_ref=home.at[slot], send_sem=isend.at[peer], recv_sem=irecv.at[slot],
            device_id=there(peer), device_id_type=pl.DeviceIdType.MESH)

    def q_copy(peer, slot):
        return pltpu.make_async_remote_copy(
            src_ref=ggs.at[peer], dst_ref=home_gate.at[slot], send_sem=qsend.at[peer], recv_sem=qrecv.at[slot],
            device_id=there(peer), device_id_type=pl.DeviceIdType.MESH)

    def send(i, _):
        s = groups - i
        peer = flip_bits(me, s, groups)
        x_copy(peer, me).start()
        g_copy(peer, me).start()
        return 0
    lax.fori_loop(1, groups, send, 0)
    own_x = pltpu.make_async_copy(xs.at[me], xr.at[me], own_sem.at[0])
    own_g = pltpu.make_async_copy(gs.at[me], gr.at[me], own_sem.at[1])
    own_x.start()
    own_g.start()
    load_in.wait()
    load_out.wait()
    load_g.wait()

    spot = (
        lax.broadcasted_iota(jnp.int32, (rows, lanes), 0)
        == lax.broadcasted_iota(jnp.int32, (rows, lanes), 1)
    )

    def work(base):
        both = pl.ds(base, 2)
        x = xr[both].reshape(2 * rows, width)
        place = pl.ds(pl.multiple_of(base * rows, rows), 2 * rows)
        gg = gated[place, :]
        gate = jnp.concatenate(
            [jnp.sum(jnp.where(spot, gr[base + u, 0:1, :], 0.0), 1, keepdims=True) for u in range(2)], 0
        )
        gated[place, :] = (gate * gg.astype(f32)).astype(bf16)
        total = jnp.zeros((2 * rows, width), f32)
        gate_grad = jnp.zeros((2 * rows, 1), f32)

        def columns(t):
            return slice(t * tile, (t + 1) * tile)

        def products(t):
            return matmul(x, win[:, columns(t)]), matmul_nt(gg, wout[columns(t), :])

        ahead = products(0)
        for t in range(tiles):
            pre, out_grad = ahead
            if t + 1 < tiles:
                ahead = products(t + 1)
            value, slope = gelu_parts(pre)
            act[place, columns(t)] = value.astype(bf16)
            gate_grad = gate_grad + jnp.sum(value * out_grad, 1, keepdims=True)
            low = (gate * out_grad * slope).astype(bf16)
            pg[place, columns(t)] = low
            total = total + matmul_nt(low, win[:, columns(t)])
        igs[both] = total.astype(bf16).reshape(2, rows, width)
        for u in range(2):
            row = jnp.sum(jnp.where(spot, gate_grad[u * rows : (u + 1) * rows], 0.0), 0, keepdims=True)
            ggs[base + u] = jnp.broadcast_to(row, ggs.shape[1:])

    def arrive(peer):
        x_copy(peer, peer).wait_recv()
        g_copy(peer, peer).wait_recv()

    def back(peer):
        i_copy(peer, me).start()
        q_copy(peer, me).start()

    own_x.wait()
    own_g.wait()
    arrive(flip_bits(me, 1, groups))
    work(me - me % 2)
    own_i = pltpu.make_async_copy(igs.at[me], home.at[me], own_sem.at[0])
    own_q = pltpu.make_async_copy(ggs.at[me], home_gate.at[me], own_sem.at[1])
    own_i.start()
    own_q.start()
    back(flip_bits(me, 1, groups))

    def chunk(j, _):
        peer = flip_bits(me, 2 * j, groups)
        other = flip_bits(me, 2 * j + 1, groups)
        arrive(peer)
        arrive(other)
        work(peer - peer % 2)
        back(peer)
        back(other)
        return 0
    lax.fori_loop(1, groups // 2, chunk, 0)

    def d_copy(k):
        return pltpu.make_async_remote_copy(
            src_ref=dws.at[k % 2], dst_ref=dwr.at[k], send_sem=dsend.at[k], recv_sem=drecv.at[k],
            device_id=(sibling, me), device_id_type=pl.DeviceIdType.MESH)

    part = hidden // dp_size
    flat = groups * rows
    items = [(which, half) for half in range(dp_size // 2) for which in range(2)]

    def grad(which, quarter):
        span = pl.ds(pl.multiple_of(quarter * part, part), part)
        if which == 0:
            return matmul_tn(xr[...].reshape(flat, width), pg[:, span])
        return matmul_tn(act[:, span], gated[...])

    half_of = dp // 2
    for k, (which, half) in enumerate(items):
        if k >= 2:
            d_copy(k - 2).wait_send()
        dws[k % 2] = grad(which, 2 * half + 1 - core).astype(bf16)
        d_copy(k).start()

    span = stage.shape[1]
    copies = []
    for b in range(flat // span):
        if b >= 2:
            copies[b - 2].wait()
        stage[b % 2] = matmul(act[b * span : (b + 1) * span, :], wout[...]).astype(bf16)
        copy = pltpu.make_async_copy(stage.at[b % 2], produced.at[pl.ds(b * span, span)], psem.at[b % 2])
        copy.start()
        copies.append(copy)
    for copy in copies[-2:]:
        copy.wait()
    for k, (which, half) in enumerate(items):
        local = grad(which, 2 * half + core)
        d_copy(k).wait_recv()
        both = (local + dwr[k].astype(f32)).astype(bf16)
        dwr[k] = both
    outs = []
    for which in range(2):
        outs.append(pltpu.make_async_copy(dwr.at[half_of * 2 + which], keep.at[which], ksem.at[which]))
        outs.append(pltpu.make_async_copy(dwr.at[(1 - half_of) * 2 + which], give.at[which], ksem.at[2 + which]))
    for copy in outs:
        copy.start()
    for copy in outs:
        copy.wait()
    own_i.wait()
    own_q.wait()
    for k in (2, 3):
        d_copy(k).wait_send()

    def finish(s, _):
        peer = flip_bits(me, s, groups)
        x_copy(peer, me).wait_send()
        g_copy(peer, me).wait_send()
        i_copy(peer, me).wait_send()
        q_copy(peer, me).wait_send()
        i_copy(peer, peer).wait_recv()
        q_copy(peer, peer).wait_recv()
        return 0
    lax.fori_loop(1, groups, finish, 0)


def ffn(xs, gs, g, weight_in, weight_out, groups, dp_size, tiles=6):
    f32, bf16 = jnp.float32, jnp.bfloat16
    _, rows, width = xs.shape
    hidden = weight_in.shape[1]
    lanes = gs.shape[2]
    part = hidden // dp_size
    anywhere = pl.BlockSpec(memory_space=pl.ANY)
    sem = pltpu.SemaphoreType.DMA
    flat = groups * rows
    shape = jax.ShapeDtypeStruct
    return pl.pallas_call(
        functools.partial(ffn_kernel, groups=groups, dp_size=dp_size, tiles=tiles),
        out_shape=(
            shape((groups, rows, width), bf16),
            shape((groups, 8, lanes), f32),
            shape((flat, width), bf16),
            shape((2, width, part), bf16),
            shape((2, width, part), bf16),
        ),
        in_specs=[anywhere] * 5,
        out_specs=(anywhere,) * 5,
        scratch_shapes=[
            pltpu.VMEM((width, hidden), bf16),
            pltpu.VMEM((hidden, width), bf16),
            pltpu.VMEM((groups, rows, width), bf16),
            pltpu.VMEM((groups, 8, lanes), f32),
            pltpu.VMEM((flat, hidden), bf16),
            pltpu.VMEM((flat, hidden), bf16),
            pltpu.VMEM((flat, width), bf16),
            pltpu.VMEM((groups, rows, width), bf16),
            pltpu.VMEM((groups, 8, lanes), f32),
            pltpu.VMEM((2, width, part), bf16),
            pltpu.VMEM((4, width, part), bf16),
            pltpu.VMEM((2, flat // 8, width), bf16),
            sem((3,)), sem((2,)), sem((2,)), sem((4,)),
            sem((groups,)), sem((groups,)), sem((groups,)), sem((groups,)),
            sem((groups,)), sem((groups,)), sem((groups,)), sem((groups,)),
            sem((4,)), sem((4,)),
        ],
        compiler_params=pltpu.CompilerParams(
            collective_id=1, has_side_effects=True, vmem_limit_bytes=62 << 20
        ),
        cost_estimate=pl.CostEstimate(
            flops=12 * flat * width * hidden, bytes_accessed=40 << 20, transcendentals=flat * hidden
        ),
    )(xs, gs, g, weight_in, weight_out)


def fold_steps(rows, cols, bits):
    steps = []
    for bit in bits:
        if rows % 32 == 0:
            rows = rows // 2
            steps.append((bit, "rows", rows, cols))
        elif cols % 256 == 0:
            cols = cols // 2
            steps.append((bit, "cols", rows, cols))
        else:
            steps.append((bit, "whole", rows, cols))
    return steps


def reduce_kernel(
    attended_hbm, middle_grad_hbm, tokens_hbm, dv_hbm, dk_hbm, dq_hbm, wq_hbm, wk_hbm, wv_hbm, returned_hbm, middle_hbm,
    gain, small_in, slot_ref, routes_ref, probs_ref,
    sum_o, sum_v, sum_k, sum_q, token_grad_hbm, small_out, mixed_hbm,
    attended, middle_grad, tokens, dv, dk, dq, wq, wk, wv, returned, middle,
    token_grad, mixed, sums, normed, branch, acc, outbox, inbox, small_box, small_sent, load_sem, store_sem,
    ssend, srecv, tsend, trecv,
    *, dp_bits, expert_bits,
):
    f32, bf16 = jnp.float32, jnp.bfloat16
    dp = lax.axis_index("dp")
    ex = lax.axis_index("expert")
    MESH = pl.DeviceIdType.MESH
    length, width = tokens.shape
    held = (attended, middle_grad, tokens, dv, dk, dq, wq, wk, wv, returned, middle)
    loads = [
        pltpu.make_async_copy(there, here, load_sem.at[i])
        for i, (there, here) in enumerate(zip(
            (attended_hbm, middle_grad_hbm, tokens_hbm, dv_hbm, dk_hbm, dq_hbm, wq_hbm, wk_hbm, wv_hbm,
             returned_hbm, middle_hbm), held))
    ]
    for load in loads:
        load.start()

    def own_bit(bit):
        axis, place = bit
        return (dp // 2 ** place) % 2 if axis == "dp" else (ex // 2 ** place) % 2

    def partner(bit):
        axis, place = bit
        flip = (1 - 2 * own_bit(bit)) * 2 ** place
        return (dp + flip, ex) if axis == "dp" else (dp, ex + flip)

    dpb = [("dp", i) for i in range(dp_bits)]
    exb = [("expert", i) for i in range(expert_bits)]
    orders = [
        [dpb[0], dpb[1], exb[0]] + dpb[2:] + exb[1:],
        [dpb[0], exb[0], dpb[1]] + dpb[2:] + exb[1:],
    ]
    every = dpb + exb
    count = len(every)

    barrier = pltpu.get_barrier_semaphore()
    for bit in every:
        pl.semaphore_signal(barrier, inc=1, device_id=partner(bit), device_id_type=MESH)
    pl.semaphore_wait(barrier, count)

    def prepare(i, _):
        span = pl.ds(pl.multiple_of(i * 256, 256), 256)
        x = tokens[span, :].astype(f32)
        inv = lax.rsqrt(jnp.mean(x * x, 1, keepdims=True) + epsilon)
        normed[span, :] = (x * inv * gain[...]).astype(bf16)
        branch[span, :] = middle_grad[span, :].astype(bf16)
        return 0
    for load in loads[:3]:
        load.wait()
    lax.fori_loop(0, length // 256, prepare, 0)

    lefts = (attended, normed, normed, normed)
    rights = (branch, dv, dk, dq)
    streams = []
    for s in range(4):
        steps = fold_steps(width, width, orders[s % 2])
        row, col = 0, 0
        at = 0
        plan = []
        for bit, kind, r, c in steps:
            mine = own_bit(bit)
            if kind == "rows":
                keep_at, send_at = (row + mine * r, col), (row + (1 - mine) * r, col)
            elif kind == "cols":
                keep_at, send_at = (row, col + mine * c), (row, col + (1 - mine) * c)
            else:
                keep_at, send_at = (row, col), (row, col)
            plan.append((bit, kind, r, c, at, keep_at, send_at))
            row, col = keep_at
            at += r
        streams.append(plan)

    def rs_copy(s, k):
        bit, kind, r, c, at, _, _ = streams[s][k]
        return pltpu.make_async_remote_copy(
            src_ref=outbox.at[s, pl.ds(at, r), pl.ds(0, c)],
            dst_ref=inbox.at[s, pl.ds(at, r), pl.ds(0, c)],
            send_sem=ssend.at[s, k], recv_sem=srecv.at[s, k],
            device_id=partner(bit), device_id_type=MESH)

    def block(s, at, r, c):
        row, col = at
        row = pl.multiple_of(row, 16) if not isinstance(row, int) else row
        col = pl.multiple_of(col, 128) if not isinstance(col, int) else col
        return sums.at[s, pl.ds(row, r), pl.ds(col, c)]

    def ag_copy(s, k, incoming):
        bit, kind, r, c, _, keep_at, send_at = streams[s][k]
        ref = block(s, send_at if incoming else keep_at, r, c)
        return pltpu.make_async_remote_copy(
            src_ref=ref, dst_ref=ref,
            send_sem=ssend.at[s, count + k], recv_sem=srecv.at[s, count + k],
            device_id=partner(bit), device_id_type=MESH)

    half = width // 2
    core = own_bit(dpb[0])

    def grad(s, which):
        span = pl.ds(pl.multiple_of(which * half, half), half)
        return matmul_tn(lefts[s][:, span], rights[s][...])

    def local(s, k, at):
        base = streams[s][0][5][0]
        row, col = at
        row = row - base
        row = pl.multiple_of(row, 16) if not isinstance(row, int) else row
        col = pl.multiple_of(col, 128) if not isinstance(col, int) else col
        return row, col

    def phase(s, k):
        plan = streams[s]
        if k == 0:
            if s > 0:
                loads[2 + s].wait()
            outbox[s, 0:half, :] = grad(s, 1 - core).astype(bf16)
            rs_copy(s, 0).start()
            acc[s] = grad(s, core)
            return
        if k <= count:
            bit, kind, r, c, at, keep_at, _ = plan[k - 1]
            rs_copy(s, k - 1).wait_recv()
            row, col = local(s, k - 1, keep_at)
            view = acc.at[s, pl.ds(row, r), pl.ds(col, c)]
            own = outbox[s, at : at + r, 0:c].astype(f32) if kind == "whole" else view[...]
            view[...] = own + inbox[s, at : at + r, 0:c].astype(f32)
            if k < count:
                bit, kind, r, c, at, keep_at, send_at = plan[k]
                row, col = local(s, k, send_at)
                outbox[s, at : at + r, 0:c] = acc[s, pl.ds(row, r), pl.ds(col, c)].astype(bf16)
                rs_copy(s, k).start()
                return
            block(s, keep_at, r, c)[...] = view[...].astype(bf16)
        g = 2 * count - 1 - k
        if k > count:
            prev = g + 1
            if plan[prev][1] != "whole":
                ag_copy(s, prev, True).wait_recv()
        if g >= 0 and plan[g][1] != "whole":
            ag_copy(s, g, False).start()

    gain_row = gain[...]
    rows = 256

    def norm_block(i, gain_grad):
        span = pl.ds(pl.multiple_of(i * rows, rows), rows)
        grads = (
            matmul_nt(dq[span, :], wq[...]) + matmul_nt(dk[span, :], wk[...]) + matmul_nt(dv[span, :], wv[...])
        )
        x = tokens[span, :].astype(f32)
        inv = lax.rsqrt(jnp.mean(x * x, 1, keepdims=True) + epsilon)
        scaled = grads * gain_row
        mean = jnp.sum(scaled * x, 1, keepdims=True) * (1.0 / width)
        part = inv * (scaled - x * (inv * inv * mean))
        token_grad[span, :] = (middle_grad[span, :] + part).astype(bf16)
        return gain_grad + jnp.sum(grads * (x * inv), 0, keepdims=True)

    slots = returned.shape[0]
    routes = routes_ref[...]
    pad = probs_ref.shape[0]
    hot = lax.broadcasted_iota(jnp.int32, (pad, length), 0) == routes
    gate_row = jnp.sum(jnp.where(hot, probs_ref[...], 0.0), 0, keepdims=True)

    def mix(c):
        at = slice(c, c + BLOCK)
        column = jnp.broadcast_to(slot_ref[0:1, at].astype(f32), (BLOCK, BLOCK)).T
        first = lax.broadcasted_iota(jnp.int32, (BLOCK, LANES), 1).astype(f32)
        spread = jnp.concatenate(
            [(column == first + float(s)).astype(f32).astype(bf16) for s in range(0, slots, LANES)], 1)
        rows_back = dot_nn(spread, returned[...])
        gate = jnp.broadcast_to(gate_row[:, at], (BLOCK, BLOCK)).T
        gate = jnp.concatenate([gate] * (width // LANES), 1)
        mixed[at, :] = (middle[at, :] + gate * rows_back).astype(bf16)

    def small_copy(k):
        return pltpu.make_async_remote_copy(
            src_ref=small_sent.at[k], dst_ref=small_box.at[k],
            send_sem=tsend.at[k], recv_sem=trecv.at[k],
            device_id=partner(every[k]), device_id_type=MESH)

    def small_phase(k):
        if k == 0:
            gain_grad = lax.fori_loop(0, length // rows, norm_block, jnp.zeros((1, width), f32))
            small_out[...] = small_in[...]
            for i in range(width // LANES):
                small_out[i : i + 1, :] = gain_grad[:, i * LANES : (i + 1) * LANES]
        else:
            small_copy(k - 1).wait_recv()
            small_out[...] = small_out[...] + small_box[k - 1]
        if k < count:
            small_sent[k] = small_out[...]
            small_copy(k).start()

    last = 2 * count
    starts = (0, 0, 2, 2)
    stores = [
        pltpu.make_async_copy(sums.at[s], out, store_sem.at[s]) for s, out in enumerate((sum_o, sum_v, sum_k, sum_q))
    ]
    stores.append(pltpu.make_async_copy(token_grad, token_grad_hbm, store_sem.at[4]))
    stores.append(pltpu.make_async_copy(mixed, mixed_hbm, store_sem.at[5]))
    mixes = length // BLOCK
    for t in range(max(last + starts[-1], count + 4, mixes + 5) + 1):
        for s in range(4):
            if 0 <= t - starts[s] <= last:
                phase(s, t - starts[s])
                if t - starts[s] == last:
                    stores[s].start()
        if t == 3:
            for load in loads[6:9]:
                load.wait()
        if 0 <= t - 3 <= count:
            small_phase(t - 3)
            if t == 3:
                stores[4].start()
        if t == 4:
            for load in loads[9:]:
                load.wait()
        if 0 <= t - 4 < mixes:
            mix((t - 4) * BLOCK)
            if t - 4 == mixes - 1:
                stores[5].start()
    for store in stores:
        store.wait()
    for s in range(4):
        for k in range(count):
            rs_copy(s, k).wait_send()
            if streams[s][k][1] != "whole":
                ag_copy(s, k, False).wait_send()
    for k in range(count):
        small_copy(k).wait_send()


def reduce_grads(tokens, attended, middle_grad, dq, dk, dv, wq, wk, wv, gain, small,
                 returned, slot, routes_row, probs, middle, dp_size, groups):
    f32, bf16 = jnp.float32, jnp.bfloat16
    length, width = tokens.shape
    dp_bits, expert_bits = dp_size.bit_length() - 1, groups.bit_length() - 1
    count = dp_bits + expert_bits
    box = sum(step[2] for step in fold_steps(width, width, range(count)))
    vmem = pl.BlockSpec(memory_space=pltpu.VMEM)
    anywhere = pl.BlockSpec(memory_space=pl.ANY)
    sem = pltpu.SemaphoreType.DMA
    shape = jax.ShapeDtypeStruct
    act, square = shape((length, width), bf16), shape((width, width), bf16)
    big = (attended, middle_grad, tokens, dv, dk, dq, wq, wk, wv, returned, middle)
    return pl.pallas_call(
        functools.partial(reduce_kernel, dp_bits=dp_bits, expert_bits=expert_bits),
        out_shape=(square, square, square, square, act, shape(small.shape, f32), act),
        in_specs=[anywhere] * len(big) + [vmem] * 5,
        out_specs=(anywhere,) * 5 + (vmem, anywhere),
        scratch_shapes=[pltpu.VMEM(x.shape, x.dtype) for x in big] + [
            pltpu.VMEM((length, width), bf16),
            pltpu.VMEM((length, width), bf16),
            pltpu.VMEM((4, width, width), bf16),
            pltpu.VMEM((length, width), bf16),
            pltpu.VMEM((length, width), bf16),
            pltpu.VMEM((4, width // 2, width), f32),
            pltpu.VMEM((4, box, width), bf16),
            pltpu.VMEM((4, box, width), bf16),
            pltpu.VMEM((count,) + small.shape, f32),
            pltpu.VMEM((count,) + small.shape, f32),
            sem((len(big),)), sem((6,)),
            sem((4, 2 * count)), sem((4, 2 * count)), sem((count,)), sem((count,)),
        ],
        compiler_params=pltpu.CompilerParams(
            collective_id=2, has_side_effects=True, vmem_limit_bytes=62 << 20
        ),
        cost_estimate=pl.CostEstimate(
            flops=14 * length * width * width, bytes_accessed=30 << 20, transcendentals=0
        ),
    )(*big, gain, small, slot, routes_row, probs)


def key_ranges(segment_row):
    first, last = segment_row[::BLOCK], segment_row[BLOCK - 1 :: BLOCK]
    lo = jnp.sum(segment_row[None, :] < first[:, None], 1) // BLOCK
    hi = (jnp.sum(segment_row[None, :] <= last[:, None], 1) + BLOCK - 1) // BLOCK
    return lo.astype(jnp.int32), hi.astype(jnp.int32)


def bias_grad(sums, heads, bucket_count):
    near = lax.broadcasted_iota(jnp.int32, (NEAR, 2 * LANES), 0)
    place = lax.broadcasted_iota(jnp.int32, (NEAR, 2 * LANES), 1)
    bucket = bucket_of((near - 2) * BLOCK + BLOCK - 1 - place)
    bucket = jnp.where(near == 0, 15, jnp.where(near == NEAR - 1, 31, bucket))
    hot = (bucket.reshape(-1)[:, None] == lax.iota(jnp.int32, bucket_count)[None, :]).astype(jnp.float32)
    return jnp.dot(sums.reshape(heads, -1), hot, precision=precise_setting).T


def per_device(
    tokens,
    segments,
    routes,
    cotangent,
    attn_gain,
    ffn_gain,
    query_weight,
    key_weight,
    value_weight,
    output_weight,
    position_bias_grid,
    router_weight,
    expert_in,
    expert_out,
):
    f32, bf16 = jnp.float32, jnp.bfloat16
    token_count, model_width = tokens.shape
    bucket_count, head_count = position_bias_grid.shape
    score_scale = (model_width // head_count) ** (-0.5)
    experts_all = router_weight.shape[1]
    capacity = (5 * token_count + 4 * experts_all - 1) // (4 * experts_all)
    slot_rows = (capacity + 15) // 16 * 16
    slots = experts_all * slot_rows
    groups = lax.axis_size("expert")
    dp_size = lax.axis_size("dp")

    def exchange(rows):
        return lax.all_to_all(rows, "expert", split_axis=0, concat_axis=0, tiled=True)

    routes_row = routes.reshape(1, token_count)
    token_slot, grad_slots = first_slots(routes_row, cotangent, experts_all, capacity, slot_rows)
    grad_arrived = exchange(grad_slots)
    lo, hi = key_ranges(segments[0])
    router_pad = max(experts_all, 16)
    router_t = jnp.pad(router_weight.T, ((0, router_pad - experts_all), (0, 0)))
    gain_one, gain_two = attn_gain[None, :], ffn_gain[None, :]
    queries, key_rows, keys_t, value_rows, attended, log_sums, middle, router_probs, sent, gate_slots = front(
        lo, hi, tokens, segments, token_slot, routes_row, gain_one, gain_two,
        query_weight, key_weight, value_weight, output_weight, position_bias_grid, router_t,
        experts_all, slot_rows, score_scale,
    )
    home_grad, home_gate, produced, keep, give = ffn(
        sent, gate_slots, grad_arrived.reshape(slots, model_width), expert_in[0], expert_out[0], groups, dp_size,
    )
    passed = lax.ppermute(give, "dp", [(i, (i + dp_size // 2) % dp_size) for i in range(dp_size)])
    in_weight_grad = keep[0].astype(f32) + passed[0].astype(f32)
    out_weight_grad = keep[1].astype(f32) + passed[1].astype(f32)
    returned = exchange(produced.reshape(experts_all, slot_rows, model_width)).reshape(slots, model_width)
    query_grad, key_grad, value_grad, diag_sums, middle_grad, router_grad, ffn_gain_grad = back(
        lo, hi, home_grad, home_gate, token_slot, routes_row, router_probs, middle, cotangent, segments, gain_two,
        output_weight, router_t, position_bias_grid, queries, key_rows, keys_t, value_rows, log_sums, attended,
        experts_all, slot_rows, score_scale,
    )
    table_grad = bias_grad(diag_sums, head_count, bucket_count)
    router_grad = router_grad[:experts_all]
    flat = jnp.concatenate(
        [jnp.zeros((model_width,), f32), ffn_gain_grad.reshape(-1), router_grad.reshape(-1), table_grad.reshape(-1)]
    )
    small_rows = -(-flat.shape[0] // (8 * LANES)) * 8
    small = jnp.pad(flat, (0, small_rows * LANES - flat.shape[0])).reshape(small_rows, LANES)
    *weights, token_grad, small, mixed = reduce_grads(
        tokens, attended, middle_grad, query_grad, key_grad, value_grad,
        query_weight, key_weight, value_weight, gain_one, small,
        returned, token_slot, routes_row, router_probs, middle, dp_size, groups,
    )
    weights = [weight.astype(f32) for weight in weights]
    flat = small.reshape(-1)
    ends = [model_width, 2 * model_width]
    ends.append(ends[-1] + router_grad.size)
    ends.append(ends[-1] + table_grad.size)
    return (
        mixed,
        token_grad,
        flat[: ends[0]],
        flat[ends[0] : ends[1]],
        weights[3],
        weights[2],
        weights[1],
        weights[0],
        flat[ends[2] : ends[3]].reshape(table_grad.shape),
        flat[ends[1] : ends[2]].reshape(experts_all, model_width).T,
        in_weight_grad[None],
        out_weight_grad[None],
    )


def solution(mesh):
    rows = P(("dp", "expert"), None)
    return jax.shard_map(
        per_device,
        mesh=mesh,
        in_specs=(rows,) * 4 + (P(),) * 8 + (P("expert", None, None),) * 2,
        out_specs=(rows,) * 2 + (P(),) * 8 + (P("expert", None, "dp"), P("expert", "dp", None)),
        check_vma=False,
    )
```

```python
import functools

import jax
import jax.numpy as jnp
from jax import lax
from jax.experimental import pallas as pl
from jax.experimental.pallas import tpu as pltpu
from jax.sharding import PartitionSpec as P

epsilon = 1e-06
precise_setting = lax.Precision.HIGHEST
def matmul(left, right):
    return jnp.dot(left, right, preferred_element_type=jnp.float32)


def matmul_tn(left, right):
    return lax.dot_general(left, right, (((0,), (0,)), ((), ())), preferred_element_type=jnp.float32)


def matmul_nt(left, right):
    return lax.dot_general(left, right, (((1,), (1,)), ((), ())), preferred_element_type=jnp.float32)


bucket_bounds = (12, 16, 23, 32, 46, 64, 91)
masked_score = -1e30
LANES = 128
BLOCK = 128
NEAR = 5
UF = 6
UB = 6


def bucket_of(relative):
    distance = jnp.abs(relative)
    beyond = jnp.zeros_like(distance)
    for threshold in bucket_bounds:
        beyond = beyond + (distance >= threshold).astype(jnp.int32)
    inside = jnp.where(distance < 8, distance, 8 + beyond)
    return inside + 16 * (relative > 0).astype(jnp.int32)


def dot_nt(a, b):
    return lax.dot_general(a, b, (((1,), (1,)), ((), ())), preferred_element_type=jnp.float32)


def dot_nn(a, b):
    return lax.dot_general(a, b, (((1,), (0,)), ((), ())), preferred_element_type=jnp.float32)


def split3(x):
    a = x.astype(jnp.bfloat16)
    r = x - a.astype(jnp.float32)
    b = r.astype(jnp.bfloat16)
    c = (r - b.astype(jnp.float32)).astype(jnp.bfloat16)
    return a, b, c


def fill_bias(diag_ref, bias, pairs):
    for p in range(pairs):
        for d in range(NEAR):
            tiles = []
            for h in (2 * p, 2 * p + 1):
                row = diag_ref[h : h + 1, :]
                if d in (0, NEAR - 1):
                    col = row[:, 511:512] if d == 0 else row[:, 0:1]
                    tiles.append(jnp.broadcast_to(col, (BLOCK, BLOCK)))
                else:
                    base = (3 - d) * BLOCK
                    wide = jnp.broadcast_to(row[:, base : base + 2 * BLOCK], (BLOCK, 2 * BLOCK))
                    tiles.append(pltpu.roll(wide, BLOCK, 1, stride=1, stride_axis=0)[:, :BLOCK])
            bias[p, d] = jnp.concatenate(tiles, 1)


def heads_apart(block, low, extra=None):
    zero = jnp.zeros_like(block)
    first, second = jnp.where(low, block, zero), jnp.where(low, zero, block)
    if extra is not None:
        first, second = jnp.concatenate([first, extra], 1), jnp.concatenate([second, extra], 1)
    return jnp.concatenate([first, second], 0)


def by_count(lo, hi, most, body):
    for n in range(1, most + 1):
        pl.when(hi - lo == n)(functools.partial(body, n))


def own_heads(wide):
    return jnp.concatenate([wide[:64, :LANES], wide[64:128, LANES:]], 0)


def attend(lo_ref, hi_ref, q_ref, k_ref, vt_ref, qm_ref, km_ref, bias, o_ref, lse_ref):
    pairs = q_ref.shape[1] // LANES
    length = q_ref.shape[0]
    nblk = length // BLOCK
    f32, bf16 = jnp.float32, jnp.bfloat16
    low = lax.broadcasted_iota(jnp.int32, (1, LANES), 1) < 64

    def q_block(i, _):
        lo, hi = lo_ref[i], hi_ref[i]
        rows = pl.ds(pl.multiple_of(i * BLOCK, BLOCK), BLOCK)
        start = pl.multiple_of(lo * BLOCK, BLOCK)
        qm = qm_ref[rows, :]

        def body(n):
            span = pl.ds(start, n * BLOCK)
            km = km_ref[span, :]

            def lanes_of(p):
                return pl.ds(pl.multiple_of(p * LANES, LANES), LANES)

            def scores(p):
                qs = heads_apart(q_ref[rows, lanes_of(p)], low, qm)
                return dot_nt(jnp.concatenate([k_ref[span, lanes_of(p)], km], 1), qs)

            def soften(p, st):
                parts = []
                top = None
                for b in range(n):
                    d = jnp.clip(lo + b - i, -2, 2) + 2
                    s = st[b * BLOCK : (b + 1) * BLOCK] + bias[p, d]
                    parts.append(s)
                    top = s if top is None else jnp.maximum(top, s)
                top = jnp.max(top, 0, keepdims=True)
                return jnp.concatenate([jnp.exp(s - top).astype(bf16) for s in parts], 0), top

            def mix(p, probs):
                values = jnp.concatenate([vt_ref[lanes_of(p), span], jnp.ones((16, n * BLOCK), bf16)], 0)
                return dot_nn(values, probs)

            def finish(p, acc, top):
                total = acc[LANES : LANES + 1]
                inv = 1.0 / total
                ot = own_heads(acc)
                ot = jnp.concatenate([ot[:64] * inv[:, :LANES], ot[64:] * inv[:, LANES:]], 0)
                o_ref[rows, lanes_of(p)] = ot.T.astype(bf16)
                lse_ref[i, pl.ds(p, 1), :] = top + jnp.log(total)

            def some(g, _):
                ps = [g * UF + u for u in range(UF)]
                sts = [scores(p) for p in ps]
                soft = [soften(p, st) for p, st in zip(ps, sts)]
                accs = [mix(p, x[0]) for p, x in zip(ps, soft)]
                for p, acc, x in zip(ps, accs, soft):
                    finish(p, acc, x[1])
                return 0
            lax.fori_loop(0, pairs // UF, some, 0)

        by_count(lo, hi, nblk, body)
        return 0
    lax.fori_loop(0, nblk, q_block, 0)


def attend_back(
    lo_ref, hi_ref, q_ref, k_ref, kt_ref, v_ref, lse_ref, do_ref, o_ref, qm_ref, km_ref, bias,
    dq_ref, dk_ref, dv_ref, gsum_ref, gacc, dkacc, dvacc, scale,
):
    length, width = q_ref.shape
    pairs = width // LANES
    nblk = length // BLOCK
    f32, bf16 = jnp.float32, jnp.bfloat16
    low = lax.broadcasted_iota(jnp.int32, (1, LANES), 1) < 64
    pick = (
        lax.broadcasted_iota(jnp.int32, (16, LANES), 0) == lax.broadcasted_iota(jnp.int32, (16, LANES), 1) // 64
    ).astype(f32).astype(bf16)
    gacc[...] = jnp.zeros_like(gacc)
    gsum_ref[...] = jnp.zeros_like(gsum_ref)
    dkacc[...] = jnp.zeros_like(dkacc)
    dvacc[...] = jnp.zeros_like(dvacc)

    def q_block(i, _):
        lo, hi = lo_ref[i], hi_ref[i]
        rows = pl.ds(pl.multiple_of(i * BLOCK, BLOCK), BLOCK)
        start = pl.multiple_of(lo * BLOCK, BLOCK)
        qm = qm_ref[rows, :]

        def body(n):
            span = pl.ds(start, n * BLOCK)
            km = km_ref[span, :]

            def lanes_of(p):
                return pl.ds(pl.multiple_of(p * LANES, LANES), LANES)

            def products(p):
                cols = lanes_of(p)
                qs = heads_apart(q_ref[rows, cols], low, qm)
                dd = do_ref[rows, cols]
                dos = heads_apart(dd, low)
                prod = dd.astype(f32) * o_ref[rows, cols].astype(f32)
                prod_hi = prod.astype(bf16)
                prod_lo = (prod - prod_hi.astype(f32)).astype(bf16)
                inner = dot_nt(pick, prod_hi) + dot_nt(pick, prod_lo)
                inner = jnp.concatenate([inner[0:1], inner[1:2]], 1)
                st = dot_nt(jnp.concatenate([k_ref[span, cols], km], 1), qs)
                dpt = dot_nt(v_ref[span, cols], dos)
                return qs, dos, inner, st, dpt

            def pointwise(p, inner, st, dpt):
                lse = lse_ref[i, pl.ds(p, 1), :]
                probs, grads = [], []
                for b in range(n):
                    d = jnp.clip(lo + b - i, -2, 2) + 2
                    part = slice(b * BLOCK, (b + 1) * BLOCK)
                    prob = jnp.exp(st[part] + bias[p, d] - lse)
                    grad = prob * (dpt[part] - inner)
                    gacc[p, d] += grad
                    probs.append(prob.astype(bf16))
                    grads.append(grad.astype(bf16))
                return jnp.concatenate(probs, 0), jnp.concatenate(grads, 0)

            def back(p, qs, dos, probs, grads):
                cols = lanes_of(p)
                return (
                    dot_nn(probs, dos), dot_nn(grads, qs[:, :LANES]), dot_nn(kt_ref[cols, span], grads)
                )

            def finish(p, dv, dk, dqt):
                cols = lanes_of(p)
                dvacc[span, cols] += dv
                dkacc[span, cols] += dk
                dq_ref[rows, cols] = (own_heads(dqt).T * scale).astype(bf16)

            def some(g, _):
                ps = [g * UB + u for u in range(UB)]
                first = [products(p) for p in ps]
                points = [pointwise(p, *x[2:]) for p, x in zip(ps, first)]
                last = [back(p, *x[:2], *y) for p, x, y in zip(ps, first, points)]
                for p, x in zip(ps, last):
                    finish(p, *x)
                return 0
            lax.fori_loop(0, pairs // UB, some, 0)

        by_count(lo, hi, nblk, body)
        return 0
    lax.fori_loop(0, nblk, q_block, 0)
    dk_ref[...] = dkacc[...].astype(bf16)
    dv_ref[...] = dvacc[...].astype(bf16)
    turn = (
        lax.broadcasted_iota(jnp.int32, (BLOCK, BLOCK), 0) + lax.broadcasted_iota(jnp.int32, (BLOCK, BLOCK), 1)
        == BLOCK - 1
    ).astype(f32).astype(bf16)
    for p in range(pairs):
        for d in range(NEAR):
            t = gacc[p, d]
            if 0 < d < NEAR - 1:
                hi = t.astype(bf16)
                t = dot_nn(turn, hi) + dot_nn(turn, (t - hi.astype(f32)).astype(bf16))
            for u in range(2):
                s = jnp.concatenate([t[:, u * LANES : (u + 1) * LANES], jnp.zeros((BLOCK, LANES), f32)], 1)
                if 0 < d < NEAR - 1:
                    s = pltpu.roll(s, 0, 1, stride=1, stride_axis=0)
                at = d * 16 + 2 * p + u
                gsum_ref[at : at + 1, :] = jnp.sum(s, 0, keepdims=True)


def two(x):
    a = x.astype(jnp.bfloat16)
    return a, (x - a.astype(jnp.float32)).astype(jnp.bfloat16)


def row_pieces(row):
    place = lax.broadcasted_iota(jnp.int32, (16, row.shape[1]), 0)
    a, b, c = [x.astype(jnp.float32) for x in split3(row)]
    return jnp.where(place == 0, a, jnp.where(place == 1, b, jnp.where(place == 2, c, 0.0))).astype(jnp.bfloat16)


def each(count, body):
    if count <= 8:
        for e in range(count):
            body(e)
    else:
        def step(e, _):
            body(e)
            return 0
        lax.fori_loop(0, count, step, 0)


def slot_hot(slot_row, e, slot_rows):
    place = lax.broadcasted_iota(jnp.int32, (slot_rows, slot_row.shape[1]), 0) + e * slot_rows
    return (place == slot_row).astype(jnp.float32).astype(jnp.bfloat16)


def slots_kernel(routes_ref, rows_ref, slot_ref, out_ref, *, experts, capacity, slot_rows):
    f32, bf16 = jnp.float32, jnp.bfloat16
    tokens = routes_ref.shape[1]
    routes = routes_ref[...]
    pad = max(experts, 16)
    hot = (lax.broadcasted_iota(jnp.int32, (pad, tokens), 0) == routes).astype(f32)
    earlier = (
        lax.broadcasted_iota(jnp.int32, (tokens, tokens), 0) < lax.broadcasted_iota(jnp.int32, (tokens, tokens), 1)
    ).astype(f32).astype(bf16)
    ranks = dot_nn(hot.astype(bf16), earlier)
    rank = jnp.sum(ranks * hot, 0, keepdims=True).astype(jnp.int32)
    slot = jnp.where(rank < capacity, routes * slot_rows + rank, -1)
    slot_ref[...] = jnp.broadcast_to(slot, slot_ref.shape)

    def pair(e):
        rows = dot_nn(slot_hot(slot, e, 2 * slot_rows), rows_ref[...]).astype(bf16)
        out_ref[pl.ds(2 * e, 2)] = rows.reshape(2, slot_rows, rows.shape[1])
    each(experts // 2, pair)


def first_slots(routes_row, rows, experts, capacity, slot_rows):
    tokens, width = rows.shape
    vmem = pl.BlockSpec(memory_space=pltpu.VMEM)
    return pl.pallas_call(
        functools.partial(slots_kernel, experts=experts, capacity=capacity, slot_rows=slot_rows),
        out_shape=(
            jax.ShapeDtypeStruct((8, tokens), jnp.int32),
            jax.ShapeDtypeStruct((experts, slot_rows, width), jnp.bfloat16),
        ),
        in_specs=[vmem] * 2,
        out_specs=(vmem,) * 2,
        compiler_params=pltpu.CompilerParams(vmem_limit_bytes=60 << 20),
        cost_estimate=pl.CostEstimate(
            flops=2 * experts * slot_rows * tokens * width, bytes_accessed=4 << 20, transcendentals=0
        ),
    )(routes_row, rows)


def fill_masks(segment_row, qm, km):
    f32, bf16 = jnp.float32, jnp.bfloat16
    lane = lax.broadcasted_iota(jnp.int32, (1, LANES), 1)
    for b in range(qm.shape[0] // BLOCK):
        span = slice(b * BLOCK, (b + 1) * BLOCK)
        hot = (lax.broadcasted_iota(jnp.int32, (LANES, BLOCK), 0) == segment_row[:, span]).astype(f32).T
        qm[span, :] = (hot * masked_score).astype(bf16)
        km[span, :] = jnp.where(lane < 8, 1.0 - hot, 0.0).astype(bf16)


def fill_diag(grid_ref, diag, heads):
    bf16 = jnp.bfloat16
    buckets = grid_ref.shape[0]
    relative = 256 - lax.broadcasted_iota(jnp.int32, (buckets, 4 * LANES), 1)
    hot = (lax.broadcasted_iota(jnp.int32, (buckets, 4 * LANES), 0) == bucket_of(relative))
    hot = hot.astype(jnp.float32).astype(bf16)
    grid = jnp.concatenate(
        [grid_ref[...], jnp.zeros((buckets, LANES - heads), jnp.float32)], 1
    ).T[:16]
    total = None
    for piece in split3(grid):
        term = dot_nn(piece, hot)
        total = term if total is None else total + term
    diag[...] = total


def front_kernel(
    lo_ref, hi_ref, tokens, segment_row, slot_ref, routes_ref, gain_one, gain_two, wq, wk, wv, wo, grid_ref, router_t,
    q_ref, k_ref, kt_ref, v_ref, o_ref, lse_ref, middle_ref, probs_ref, xs_ref, gs_ref,
    vt_ref, qm_ref, km_ref, diag, bias, hidden, *, experts, slot_rows, scale,
):
    f32, bf16 = jnp.float32, jnp.bfloat16
    length, width = tokens.shape
    pairs = width // LANES
    nblk = length // BLOCK
    heads = grid_ref.shape[1]
    low = lax.broadcasted_iota(jnp.int32, (1, LANES), 1) < 64
    step = 256

    for b in range(length // step):
        span = slice(b * step, (b + 1) * step)
        x = tokens[span, :].astype(f32)
        inverse = lax.rsqrt(jnp.mean(x * x, 1, keepdims=True) + epsilon)
        normed = (x * inverse * gain_one[...]).astype(bf16)
        q_ref[span, :] = (dot_nn(normed, wq[...]).astype(bf16).astype(f32) * scale).astype(bf16)
        k = dot_nn(normed, wk[...]).astype(bf16)
        k_ref[span, :] = k
        kt_ref[:, span] = k.T
        v = dot_nn(normed, wv[...]).astype(bf16)
        v_ref[span, :] = v
        vt_ref[:, span] = v.T
    fill_masks(segment_row[...], qm_ref, km_ref)
    fill_diag(grid_ref, diag, heads)
    fill_bias(diag, bias, pairs)
    attend(lo_ref, hi_ref, q_ref, k_ref, vt_ref, qm_ref, km_ref, bias, o_ref, lse_ref)

    rw = two(router_t[...])
    routes = routes_ref[...]
    pad = router_t.shape[0]
    place = lax.broadcasted_iota(jnp.int32, (pad, step), 0)
    gates = []
    for b in range(length // step):
        span = slice(b * step, (b + 1) * step)
        middle = tokens[span, :].astype(f32) + dot_nn(o_ref[span, :], wo[...])
        middle_ref[span, :] = middle
        inverse = lax.rsqrt(jnp.mean(middle * middle, 1, keepdims=True) + epsilon)
        parts = two(middle * inverse * gain_two[...])
        hidden[span, :] = parts[0]
        logits = dot_nt(rw[0], parts[0]) + dot_nt(rw[0], parts[1]) + dot_nt(rw[1], parts[0])
        logits = jnp.where(place < experts, logits, -1e30)
        powers = jnp.exp(logits - jnp.max(logits, 0, keepdims=True))
        probs = powers / jnp.sum(powers, 0, keepdims=True)
        probs_ref[:, span] = probs
        gates.append(jnp.sum(jnp.where(place == routes[:, span], probs, 0.0), 0, keepdims=True))
    gates = row_pieces(jnp.concatenate(gates, 1))
    slot = slot_ref[0:1, :]
    lanes = gs_ref.shape[2]

    def one(e):
        hot = slot_hot(slot, e, slot_rows)
        xs_ref[e] = dot_nn(hot, hidden[...]).astype(bf16)
        if lanes > slot_rows:
            hot = jnp.concatenate([hot, jnp.zeros((lanes - slot_rows, length), bf16)], 0)
        row = jnp.sum(dot_nt(gates, hot), 0, keepdims=True)
        gs_ref[e] = jnp.broadcast_to(row, gs_ref.shape[1:])
    each(experts, one)


def front(lo, hi, tokens, segments, slot, routes_row, gain_one, gain_two, wq, wk, wv, wo, grid, router_t, experts, slot_rows, scale):
    length, width = tokens.shape
    heads = grid.shape[1]
    pairs = width // LANES
    nblk = length // BLOCK
    lanes = (slot_rows + LANES - 1) // LANES * LANES
    smem = pl.BlockSpec(memory_space=pltpu.SMEM)
    vmem = pl.BlockSpec(memory_space=pltpu.VMEM)
    f32, bf16 = jnp.float32, jnp.bfloat16
    shape = jax.ShapeDtypeStruct
    act = shape((length, width), bf16)
    return pl.pallas_call(
        functools.partial(front_kernel, experts=experts, slot_rows=slot_rows, scale=scale),
        out_shape=(
            act, act, shape((width, length), bf16), act, act,
            shape((nblk, 8, 2 * LANES), f32), shape((length, width), f32),
            shape((router_t.shape[0], length), f32),
            shape((experts, slot_rows, width), bf16), shape((experts, 8, lanes), f32),
        ),
        in_specs=[smem] * 2 + [vmem] * 12,
        out_specs=(vmem,) * 10,
        scratch_shapes=[
            pltpu.VMEM((width, length), bf16),
            pltpu.VMEM((length, LANES), bf16),
            pltpu.VMEM((length, LANES), bf16),
            pltpu.VMEM((16, 4 * LANES), f32),
            pltpu.VMEM((pairs, NEAR, BLOCK, 2 * LANES), f32),
            pltpu.VMEM((length, width), bf16),
        ],
        compiler_params=pltpu.CompilerParams(vmem_limit_bytes=60 << 20),
        cost_estimate=pl.CostEstimate(
            flops=4 * length * length * width + 12 * length * width * width, bytes_accessed=20 << 20,
            transcendentals=length * length * heads,
        ),
    )(lo, hi, tokens, segments, slot, routes_row, gain_one, gain_two, wq, wk, wv, wo, grid, router_t)


def bucket_sums(gsum_ref):
    bf16 = jnp.bfloat16
    total = jnp.zeros((16, LANES), jnp.float32)
    lane = lax.broadcasted_iota(jnp.int32, (2 * LANES, LANES), 1)
    for d in range(NEAR):
        relative = (d - 2) * BLOCK + BLOCK - 1 - lax.broadcasted_iota(jnp.int32, (2 * LANES, LANES), 0)
        bucket = 15 if d == 0 else 31 if d == NEAR - 1 else bucket_of(relative)
        hot = (lane == bucket).astype(jnp.float32).astype(bf16)
        for piece in split3(gsum_ref[d * 16 : (d + 1) * 16, :]):
            total = total + dot_nn(piece, hot)
    return total


def small_shape(width, experts):
    return (16 + width // LANES * experts + 16, LANES)


def back_kernel(
    lo_ref, hi_ref, home, home_gate, slot_ref, routes_ref, probs_ref, middle_ref, cotangent, segment_row, gain_two,
    wo, router_t, grid_ref, lse_ref, q_hbm, k_hbm, kt_hbm, v_hbm, o_hbm,
    dq_ref, dk_ref, dv_ref, middle_grad_hbm, small,
    q_ref, k_ref, kt_ref, v_ref, o_ref, middle_grad,
    do_ref, qm_ref, km_ref, diag, bias, gacc, dkacc, dvacc, logit, gsum_ref, sems,
    *, experts, slot_rows, scale,
):
    f32, bf16 = jnp.float32, jnp.bfloat16
    length, width = middle_ref.shape
    pairs = width // LANES
    pad = router_t.shape[0]
    heads = grid_ref.shape[1]
    slot = slot_ref[0:1, :]
    loads = [
        pltpu.make_async_copy(there, here, sems.at[i])
        for i, (there, here) in enumerate(zip(
            (q_hbm, k_hbm, kt_hbm, v_hbm, o_hbm), (q_ref, k_ref, kt_ref, v_ref, o_ref)))
    ]
    for load in loads:
        load.start()

    if experts <= 8:
        total = jnp.zeros((16, length), f32)
        for e in range(experts):
            total = total + dot_nn(row_pieces(home_gate[e, 0:1, :])[:, :slot_rows], slot_hot(slot, e, slot_rows))
    else:
        def add(e, total):
            return total + dot_nn(row_pieces(home_gate[e, 0:1, :])[:, :slot_rows], slot_hot(slot, e, slot_rows))
        total = lax.fori_loop(0, experts, add, jnp.zeros((16, length), f32))
    gate_grad = jnp.sum(total, 0, keepdims=True)
    place = lax.broadcasted_iota(jnp.int32, (pad, length), 0)
    hot = place == routes_ref[...]
    probs = probs_ref[...]
    gate = jnp.sum(jnp.where(hot, probs, 0.0), 0, keepdims=True)
    logit[...] = probs * (jnp.where(hot, gate_grad, 0.0) - gate * gate_grad)
    rw = two(router_t[...])
    slots = experts * slot_rows
    router_sum = jnp.zeros((pad, width), f32)
    gain_sum = jnp.zeros((1, width), f32)
    step = 256
    for b in range(length // step):
        span = slice(b * step, (b + 1) * step)
        hots = []
        for c in range(b * step, (b + 1) * step, BLOCK):
            column = jnp.broadcast_to(slot[:, c : c + BLOCK].astype(f32), (BLOCK, BLOCK)).T
            first = lax.broadcasted_iota(jnp.int32, (BLOCK, LANES), 1).astype(f32)
            hots.append(jnp.concatenate(
                [(column == first + float(s)).astype(f32).astype(bf16) for s in range(0, slots, LANES)], 1))
        spread = jnp.concatenate(hots, 0)
        hidden_grad = dot_nn(spread, home[...].reshape(slots, width))
        lg = two(logit[:, span])
        hidden_grad = hidden_grad + (
            matmul_tn(lg[0], rw[0]) + matmul_tn(lg[0], rw[1]) + matmul_tn(lg[1], rw[0])
        )
        middle = middle_ref[span, :]
        inverse = lax.rsqrt(jnp.mean(middle * middle, 1, keepdims=True) + epsilon)
        unit = middle * inverse
        hidden = two(unit * gain_two[...])
        router_sum = router_sum + (dot_nn(lg[0], hidden[0]) + dot_nn(lg[0], hidden[1]) + dot_nn(lg[1], hidden[0]))
        gain_sum = gain_sum + jnp.sum(hidden_grad * unit, 0, keepdims=True)
        scaled = hidden_grad * gain_two[...]
        mean = jnp.mean(scaled * middle, 1, keepdims=True)
        grad = cotangent[span, :].astype(f32) + inverse * (scaled - unit * (inverse * mean))
        middle_grad[span, :] = grad
        do_ref[span, :] = matmul_nt(grad.astype(bf16), wo[...]).astype(bf16)
    store = pltpu.make_async_copy(middle_grad, middle_grad_hbm, sems.at[5])
    store.start()
    small[...] = jnp.zeros_like(small)
    chunks = width // LANES
    for c in range(chunks):
        cols = slice(c * LANES, (c + 1) * LANES)
        small[8 + c : 9 + c, :] = gain_sum[:, cols]
        small[16 + c * experts : 16 + (c + 1) * experts, :] = router_sum[:experts, cols]

    fill_masks(segment_row[...], qm_ref, km_ref)
    fill_diag(grid_ref, diag, heads)
    fill_bias(diag, bias, pairs)
    for load in loads:
        load.wait()
    attend_back(
        lo_ref, hi_ref, q_ref, k_ref, kt_ref, v_ref, lse_ref, do_ref, o_ref, qm_ref, km_ref, bias,
        dq_ref, dk_ref, dv_ref, gsum_ref, gacc, dkacc, dvacc, scale,
    )
    at = 16 + chunks * experts
    small[at : at + 16, :] = bucket_sums(gsum_ref)
    store.wait()


def back(lo, hi, home, home_gate, slot, routes_row, probs, middle, cotangent, segments, gain_two, wo, router_t, grid,
         q, k, kt, v, lse, o, experts, slot_rows, scale):
    length, width = middle.shape
    heads = grid.shape[1]
    pairs = width // LANES
    smem = pl.BlockSpec(memory_space=pltpu.SMEM)
    vmem = pl.BlockSpec(memory_space=pltpu.VMEM)
    f32, bf16 = jnp.float32, jnp.bfloat16
    shape = jax.ShapeDtypeStruct
    act = shape((length, width), bf16)
    anywhere = pl.BlockSpec(memory_space=pl.ANY)
    return pl.pallas_call(
        functools.partial(back_kernel, experts=experts, slot_rows=slot_rows, scale=scale),
        out_shape=(act, act, act, shape((length, width), f32), shape(small_shape(width, experts), f32)),
        in_specs=[smem] * 2 + [vmem] * 13 + [anywhere] * 5,
        out_specs=(vmem, vmem, vmem, anywhere, vmem),
        scratch_shapes=[
            pltpu.VMEM((length, width), bf16),
            pltpu.VMEM((length, width), bf16),
            pltpu.VMEM((width, length), bf16),
            pltpu.VMEM((length, width), bf16),
            pltpu.VMEM((length, width), bf16),
            pltpu.VMEM((length, width), f32),
            pltpu.VMEM((length, width), bf16),
            pltpu.VMEM((length, LANES), bf16),
            pltpu.VMEM((length, LANES), bf16),
            pltpu.VMEM((16, 4 * LANES), f32),
            pltpu.VMEM((pairs, NEAR, BLOCK, 2 * LANES), f32),
            pltpu.VMEM((pairs, NEAR, BLOCK, 2 * LANES), f32),
            pltpu.VMEM((length, width), f32),
            pltpu.VMEM((length, width), f32),
            pltpu.VMEM((router_t.shape[0], length), f32),
            pltpu.VMEM((NEAR * 16, 2 * LANES), f32),
            pltpu.SemaphoreType.DMA((6,)),
        ],
        compiler_params=pltpu.CompilerParams(vmem_limit_bytes=62 << 20),
        cost_estimate=pl.CostEstimate(
            flops=10 * length * length * width + 6 * length * width * width, bytes_accessed=30 << 20,
            transcendentals=length * length * heads,
        ),
    )(lo, hi, home, home_gate, slot, routes_row, probs, middle, cotangent, segments, gain_two, wo, router_t, grid,
      lse, q, k, kt, v, o)


def finish_kernel(
    sum_q, sum_k, sum_v, sum_o, keep, passed, small,
    gain_one, gain_two, grad_q, grad_k, grad_v, grad_o, table, router, grad_in, grad_out,
    low, wide, load_sem, store_sem, *, experts,
):
    f32 = jnp.float32
    sources = (sum_q, sum_k, sum_v, sum_o, keep.at[0], keep.at[1], passed.at[0], passed.at[1])
    targets = (grad_q, grad_k, grad_v, grad_o, grad_in, grad_out)
    loads = [pltpu.make_async_copy(x, low.at[i], load_sem.at[i]) for i, x in enumerate(sources)]
    stores = [pltpu.make_async_copy(wide.at[i], x, store_sem.at[i]) for i, x in enumerate(targets)]
    for load in loads:
        load.start()
    width = gain_one.shape[1]
    chunks = width // LANES
    gain_one[...] = jnp.concatenate([small[c : c + 1, :] for c in range(chunks)], 1)
    gain_two[...] = jnp.concatenate([small[8 + c : 9 + c, :] for c in range(chunks)], 1)
    for c in range(chunks):
        block = small[16 + c * experts : 16 + (c + 1) * experts, :]
        block = jnp.concatenate([block, jnp.zeros((LANES - experts, LANES), f32)], 0).T
        router[c * LANES : (c + 1) * LANES, :] = block[:, :experts]
    at = 16 + chunks * experts
    buckets, heads = table.shape
    block = jnp.concatenate([small[at : at + 16, :], jnp.zeros((LANES - 16, LANES), f32)], 0).T
    table[...] = block[:buckets, :heads]
    for i in range(4):
        loads[i].wait()
        wide[i] = low[i].astype(f32)
        stores[i].start()
    for i in range(2):
        loads[4 + i].wait()
        loads[6 + i].wait()
        wide[4 + i] = low[4 + i].astype(f32) + low[6 + i].astype(f32)
        stores[4 + i].start()
    for store in stores:
        store.wait()


def finish(sums, keep, passed, small, grid_shape, experts):
    f32, bf16 = jnp.float32, jnp.bfloat16
    width = sums[0].shape[0]
    vmem = pl.BlockSpec(memory_space=pltpu.VMEM)
    anywhere = pl.BlockSpec(memory_space=pl.ANY)
    shape = jax.ShapeDtypeStruct
    square, row = shape((width, width), f32), shape((1, width), f32)
    return pl.pallas_call(
        functools.partial(finish_kernel, experts=experts),
        out_shape=(row, row, square, square, square, square, shape(grid_shape, f32),
                   shape((width, experts), f32), square, square),
        in_specs=[anywhere] * 6 + [vmem],
        out_specs=(vmem, vmem) + (anywhere,) * 4 + (vmem, vmem) + (anywhere,) * 2,
        scratch_shapes=[
            pltpu.VMEM((8, width, width), bf16), pltpu.VMEM((6, width, width), f32),
            pltpu.SemaphoreType.DMA((8,)), pltpu.SemaphoreType.DMA((6,)),
        ],
        compiler_params=pltpu.CompilerParams(vmem_limit_bytes=60 << 20),
        cost_estimate=pl.CostEstimate(flops=0, bytes_accessed=24 << 20, transcendentals=0),
    )(*sums, keep, passed, small)


def gelu_parts(v):
    mag = jnp.abs(v)
    t = 1.0 / (1.0 + (0.3275911 * 0.7071067811865476) * mag)
    poly = t * (0.127414796 + t * (-0.142248368 + t * (0.7107068705 + t * (-0.7265760135 + t * 0.5307027145))))
    gauss = jnp.exp(-0.5 * v * v)
    tail = poly * gauss
    phi = jnp.where(v < 0, tail, 1.0 - tail)
    return v * phi, phi + v * gauss * 0.3989422804014327


def flip_bits(index, mask, count):
    out = 0
    bit = 1
    while bit < count:
        a, b = (index // bit) % 2, (mask // bit) % 2
        out = out + bit * (a + b - 2 * a * b)
        bit *= 2
    return out


def ffn_kernel(
    xs, gs, g, win_hbm, wout_hbm,
    home, home_gate, produced, keep, give,
    win, wout, xr, gr, act, pg, gated, igs, ggs, dws, dwr, stage,
    wsem, own_sem, psem, ksem, xsend, xrecv, gsend, grecv, isend, irecv, qsend, qrecv, dsend, drecv,
    *, groups, dp_size, tiles,
):
    f32, bf16 = jnp.float32, jnp.bfloat16
    me = lax.axis_index("expert")
    dp = lax.axis_index("dp")
    core = dp % 2
    sibling = dp + 1 - 2 * core
    half_of = dp // 2
    rows = xs.shape[1]
    width = xs.shape[2]
    hidden = win.shape[1]
    tile = hidden // tiles
    lanes = gs.shape[2]

    def there(peer):
        return (dp, peer)

    load_in = pltpu.make_async_copy(win_hbm, win, wsem.at[0])
    load_out = pltpu.make_async_copy(wout_hbm, wout, wsem.at[1])
    load_in.start()
    load_out.start()
    load_g = pltpu.make_async_copy(g, gated, wsem.at[2])
    load_g.start()

    barrier = pltpu.get_barrier_semaphore()

    def greet(s, _):
        pl.semaphore_signal(
            barrier, inc=1, device_id=there(flip_bits(me, s, groups)), device_id_type=pl.DeviceIdType.MESH
        )
        return 0
    lax.fori_loop(1, groups, greet, 0)
    pl.semaphore_signal(barrier, inc=1, device_id=(sibling, me), device_id_type=pl.DeviceIdType.MESH)
    pl.semaphore_wait(barrier, groups)

    def x_copy(peer, slot):
        return pltpu.make_async_remote_copy(
            src_ref=xs.at[peer], dst_ref=xr.at[slot], send_sem=xsend.at[peer], recv_sem=xrecv.at[slot],
            device_id=there(peer), device_id_type=pl.DeviceIdType.MESH)

    def g_copy(peer, slot):
        return pltpu.make_async_remote_copy(
            src_ref=gs.at[peer], dst_ref=gr.at[slot], send_sem=gsend.at[peer], recv_sem=grecv.at[slot],
            device_id=there(peer), device_id_type=pl.DeviceIdType.MESH)

    def i_copy(peer, slot):
        return pltpu.make_async_remote_copy(
            src_ref=igs.at[peer], dst_ref=home.at[slot], send_sem=isend.at[peer], recv_sem=irecv.at[slot],
            device_id=there(peer), device_id_type=pl.DeviceIdType.MESH)

    def q_copy(peer, slot):
        return pltpu.make_async_remote_copy(
            src_ref=ggs.at[peer], dst_ref=home_gate.at[slot], send_sem=qsend.at[peer], recv_sem=qrecv.at[slot],
            device_id=there(peer), device_id_type=pl.DeviceIdType.MESH)

    def send(i, _):
        s = groups - i
        peer = flip_bits(me, s, groups)
        x_copy(peer, me).start()
        g_copy(peer, me).start()
        return 0
    lax.fori_loop(1, groups, send, 0)
    own_x = pltpu.make_async_copy(xs.at[me], xr.at[me], own_sem.at[0])
    own_g = pltpu.make_async_copy(gs.at[me], gr.at[me], own_sem.at[1])
    own_x.start()
    own_g.start()
    load_in.wait()
    load_out.wait()
    load_g.wait()

    spot = (
        lax.broadcasted_iota(jnp.int32, (rows, lanes), 0)
        == lax.broadcasted_iota(jnp.int32, (rows, lanes), 1)
    )

    def work(base):
        both = pl.ds(base, 2)
        x = xr[both].reshape(2 * rows, width)
        place = pl.ds(pl.multiple_of(base * rows, rows), 2 * rows)
        gg = gated[place, :]
        gate = jnp.concatenate(
            [jnp.sum(jnp.where(spot, gr[base + u, 0:1, :], 0.0), 1, keepdims=True) for u in range(2)], 0
        )
        gated[place, :] = (gate * gg.astype(f32)).astype(bf16)
        total = jnp.zeros((2 * rows, width), f32)
        gate_grad = jnp.zeros((2 * rows, 1), f32)

        def columns(t):
            return slice(t * tile, (t + 1) * tile)

        def products(t):
            return matmul(x, win[:, columns(t)]), matmul_nt(gg, wout[columns(t), :])

        ahead = products(0)
        for t in range(tiles):
            pre, out_grad = ahead
            if t + 1 < tiles:
                ahead = products(t + 1)
            value, slope = gelu_parts(pre)
            act[place, columns(t)] = value.astype(bf16)
            gate_grad = gate_grad + jnp.sum(value * out_grad, 1, keepdims=True)
            low = (gate * out_grad * slope).astype(bf16)
            pg[place, columns(t)] = low
            total = total + matmul_nt(low, win[:, columns(t)])
        igs[both] = total.astype(bf16).reshape(2, rows, width)
        for u in range(2):
            row = jnp.sum(jnp.where(spot, gate_grad[u * rows : (u + 1) * rows], 0.0), 0, keepdims=True)
            ggs[base + u] = jnp.broadcast_to(row, ggs.shape[1:])

    def arrive(peer):
        x_copy(peer, peer).wait_recv()
        g_copy(peer, peer).wait_recv()

    def back(peer):
        i_copy(peer, me).start()
        q_copy(peer, me).start()

    own_x.wait()
    own_g.wait()
    arrive(flip_bits(me, 1, groups))
    work(me - me % 2)
    own_i = pltpu.make_async_copy(igs.at[me], home.at[me], own_sem.at[0])
    own_q = pltpu.make_async_copy(ggs.at[me], home_gate.at[me], own_sem.at[1])
    own_i.start()
    own_q.start()
    back(flip_bits(me, 1, groups))

    def chunk(j, _):
        peer = flip_bits(me, 2 * j, groups)
        other = flip_bits(me, 2 * j + 1, groups)
        arrive(peer)
        arrive(other)
        work(peer - peer % 2)
        back(peer)
        back(other)
        return 0
    lax.fori_loop(1, groups // 2, chunk, 0)

    def d_copy(k):
        return pltpu.make_async_remote_copy(
            src_ref=dws.at[k % 2], dst_ref=dwr.at[k], send_sem=dsend.at[k], recv_sem=drecv.at[k],
            device_id=(sibling, me), device_id_type=pl.DeviceIdType.MESH)

    part = hidden // dp_size
    flat = groups * rows
    items = [(which, half) for half in (1 - half_of, half_of) for which in range(2)]

    def grad(which, quarter):
        span = pl.ds(pl.multiple_of(quarter * part, part), part)
        if which == 0:
            return matmul_tn(xr[...].reshape(flat, width), pg[:, span])
        return matmul_tn(act[:, span], gated[...])

    for k, (which, half) in enumerate(items):
        if k >= 2:
            d_copy(k - 2).wait_send()
        dws[k % 2] = grad(which, 2 * half + 1 - core).astype(bf16)
        d_copy(k).start()
    outs = [
        pltpu.make_async_copy(dwr.at[0], give.at[0], ksem.at[0]),
        pltpu.make_async_copy(dwr.at[1], give.at[1], ksem.at[1]),
        pltpu.make_async_copy(dwr.at[2], keep.at[0], ksem.at[2]),
        pltpu.make_async_copy(dwr.at[3], keep.at[1], ksem.at[3]),
    ]
    for k, (which, half) in enumerate(items):
        local = grad(which, 2 * half + core)
        d_copy(k).wait_recv()
        dwr[k] = (local + dwr[k].astype(f32)).astype(bf16)
        outs[k].start()

    span = stage.shape[1]
    copies = []
    for b in range(flat // span):
        if b >= 2:
            copies[b - 2].wait()
        stage[b % 2] = matmul(act[b * span : (b + 1) * span, :], wout[...]).astype(bf16)
        copy = pltpu.make_async_copy(stage.at[b % 2], produced.at[pl.ds(b * span, span)], psem.at[b % 2])
        copy.start()
        copies.append(copy)
    for copy in copies[-2:] + outs:
        copy.wait()
    own_i.wait()
    own_q.wait()
    for k in (2, 3):
        d_copy(k).wait_send()

    def finish(s, _):
        peer = flip_bits(me, s, groups)
        x_copy(peer, me).wait_send()
        g_copy(peer, me).wait_send()
        i_copy(peer, me).wait_send()
        q_copy(peer, me).wait_send()
        i_copy(peer, peer).wait_recv()
        q_copy(peer, peer).wait_recv()
        return 0
    lax.fori_loop(1, groups, finish, 0)


def ffn(xs, gs, g, weight_in, weight_out, groups, dp_size, tiles=6):
    f32, bf16 = jnp.float32, jnp.bfloat16
    _, rows, width = xs.shape
    hidden = weight_in.shape[1]
    lanes = gs.shape[2]
    part = hidden // dp_size
    anywhere = pl.BlockSpec(memory_space=pl.ANY)
    sem = pltpu.SemaphoreType.DMA
    flat = groups * rows
    shape = jax.ShapeDtypeStruct
    return pl.pallas_call(
        functools.partial(ffn_kernel, groups=groups, dp_size=dp_size, tiles=tiles),
        out_shape=(
            shape((groups, rows, width), bf16),
            shape((groups, 8, lanes), f32),
            shape((flat, width), bf16),
            shape((2, width, part), bf16),
            shape((2, width, part), bf16),
        ),
        in_specs=[anywhere] * 5,
        out_specs=(anywhere,) * 5,
        scratch_shapes=[
            pltpu.VMEM((width, hidden), bf16),
            pltpu.VMEM((hidden, width), bf16),
            pltpu.VMEM((groups, rows, width), bf16),
            pltpu.VMEM((groups, 8, lanes), f32),
            pltpu.VMEM((flat, hidden), bf16),
            pltpu.VMEM((flat, hidden), bf16),
            pltpu.VMEM((flat, width), bf16),
            pltpu.VMEM((groups, rows, width), bf16),
            pltpu.VMEM((groups, 8, lanes), f32),
            pltpu.VMEM((2, width, part), bf16),
            pltpu.VMEM((4, width, part), bf16),
            pltpu.VMEM((2, flat // 8, width), bf16),
            sem((3,)), sem((2,)), sem((2,)), sem((4,)),
            sem((groups,)), sem((groups,)), sem((groups,)), sem((groups,)),
            sem((groups,)), sem((groups,)), sem((groups,)), sem((groups,)),
            sem((4,)), sem((4,)),
        ],
        compiler_params=pltpu.CompilerParams(
            collective_id=1, has_side_effects=True, vmem_limit_bytes=62 << 20
        ),
        cost_estimate=pl.CostEstimate(
            flops=12 * flat * width * hidden, bytes_accessed=40 << 20, transcendentals=flat * hidden
        ),
    )(xs, gs, g, weight_in, weight_out)


def fold_steps(rows, cols, bits):
    steps = []
    for bit in bits[:3]:
        rows = rows // 2
        steps.append(((bit,), "half", rows, cols))
    rows, cols = rows // 2, cols // 2
    steps.append((tuple(bits[3:5]), "quad", rows, cols))
    for bit in bits[5:]:
        steps.append(((bit,), "whole", rows, cols))
    return steps


def reduce_kernel(
    attended_hbm, middle_grad_hbm, tokens_hbm, dv_hbm, dk_hbm, dq_hbm, wq_hbm, wk_hbm, wv_hbm, returned_hbm, middle_hbm,
    gain, small_in, slot_ref, routes_ref, probs_ref,
    sum_o, sum_v, sum_k, sum_q, token_grad_hbm, small_out, mixed_hbm,
    attended, middle_grad, tokens, dv, dk, dq, wq, wk, wv, returned, middle,
    token_grad, mixed, sums, normed, branch, acc, outbox, inbox, small_box, small_sent, load_sem, store_sem,
    ssend, srecv, tsend, trecv,
    *, dp_bits, expert_bits,
):
    f32, bf16 = jnp.float32, jnp.bfloat16
    dp = lax.axis_index("dp")
    ex = lax.axis_index("expert")
    MESH = pl.DeviceIdType.MESH
    length, width = tokens.shape
    held = (attended, middle_grad, tokens, dv, dk, dq, wq, wk, wv, returned, middle)
    loads = [
        pltpu.make_async_copy(there, here, load_sem.at[i])
        for i, (there, here) in enumerate(zip(
            (attended_hbm, middle_grad_hbm, tokens_hbm, dv_hbm, dk_hbm, dq_hbm, wq_hbm, wk_hbm, wv_hbm,
             returned_hbm, middle_hbm), held))
    ]
    for load in loads:
        load.start()

    def own_bit(bit):
        axis, place = bit
        return (dp // 2 ** place) % 2 if axis == "dp" else (ex // 2 ** place) % 2

    def partner(bits):
        there = [dp, ex]
        for bit in bits:
            there[bit[0] == "expert"] = there[bit[0] == "expert"] + (1 - 2 * own_bit(bit)) * 2 ** bit[1]
        return tuple(there)

    dpb = [("dp", i) for i in range(dp_bits)]
    exb = [("expert", i) for i in range(expert_bits)]
    orders = [
        [dpb[0], dpb[1], exb[0]] + dpb[2:] + exb[1:],
        [dpb[0], exb[0], dpb[1]] + dpb[2:] + exb[1:],
    ]
    every = dpb + exb
    small_count = len(every)

    barrier = pltpu.get_barrier_semaphore()
    greeted = [(bit,) for bit in every] + [tuple(orders[0][3:5])]
    for bits in greeted:
        pl.semaphore_signal(barrier, inc=1, device_id=partner(bits), device_id_type=MESH)
    pl.semaphore_wait(barrier, len(greeted))

    def prepare(i, _):
        span = pl.ds(pl.multiple_of(i * 256, 256), 256)
        x = tokens[span, :].astype(f32)
        inv = lax.rsqrt(jnp.mean(x * x, 1, keepdims=True) + epsilon)
        normed[span, :] = (x * inv * gain[...]).astype(bf16)
        branch[span, :] = middle_grad[span, :].astype(bf16)
        return 0
    for load in loads[:3]:
        load.wait()
    lax.fori_loop(0, length // 256, prepare, 0)

    lefts = (attended, normed, normed, normed)
    rights = (branch, dv, dk, dq)
    streams = []
    for s in range(4):
        row, col, at, sem_at = 0, 0, 0, 0
        plan = []
        for bits, kind, r, c in fold_steps(width, width, orders[s % 2]):
            mine = [own_bit(bit) for bit in bits]
            if kind == "half":
                peers = [bits]
                keep_at = (row + mine[0] * r, col)
                theirs = [(row + (1 - mine[0]) * r, col)]
            elif kind == "quad":
                peers = [bits[:1], bits[1:], bits]
                keep_at = (row + mine[0] * r, col + mine[1] * c)
                theirs = [
                    (row + (1 - mine[0]) * r, col + mine[1] * c),
                    (row + mine[0] * r, col + (1 - mine[1]) * c),
                    (row + (1 - mine[0]) * r, col + (1 - mine[1]) * c),
                ]
            else:
                peers, keep_at, theirs = [bits], (row, col), [(row, col)]
            plan.append((peers, kind, r, c, at, keep_at, theirs, sem_at))
            row, col = keep_at
            at += r * len(peers)
            sem_at += len(peers)
        streams.append(plan)
    count = len(streams[0])
    sems = ssend.shape[1] // 2

    def rs_copy(s, k, i):
        peers, kind, r, c, at, _, _, sem_at = streams[s][k]
        box = pl.ds(at + i * r, r)
        return pltpu.make_async_remote_copy(
            src_ref=outbox.at[s, box, pl.ds(0, c)], dst_ref=inbox.at[s, box, pl.ds(0, c)],
            send_sem=ssend.at[s, sem_at + i], recv_sem=srecv.at[s, sem_at + i],
            device_id=partner(peers[i]), device_id_type=MESH)

    def aligned(at):
        row, col = at
        row = pl.multiple_of(row, 16) if not isinstance(row, int) else row
        col = pl.multiple_of(col, 128) if not isinstance(col, int) else col
        return row, col

    def block(s, at, r, c):
        row, col = aligned(at)
        return sums.at[s, pl.ds(row, r), pl.ds(col, c)]

    def ag_copy(s, k, i, incoming):
        peers, kind, r, c, _, keep_at, theirs, sem_at = streams[s][k]
        ref = block(s, theirs[i] if incoming else keep_at, r, c)
        return pltpu.make_async_remote_copy(
            src_ref=ref, dst_ref=ref,
            send_sem=ssend.at[s, sems + sem_at + i], recv_sem=srecv.at[s, sems + sem_at + i],
            device_id=partner(peers[i]), device_id_type=MESH)

    half = width // 2
    core = own_bit(dpb[0])

    def grad(s, which):
        span = pl.ds(pl.multiple_of(which * half, half), half)
        return matmul_tn(lefts[s][:, span], rights[s][...])

    def local(s, at, r, c):
        row, col = aligned((at[0] - streams[s][0][5][0], at[1]))
        return acc.at[s, pl.ds(row, r), pl.ds(col, c)]

    def phase(s, k):
        plan = streams[s]
        if k == 0:
            if s > 0:
                loads[2 + s].wait()
            outbox[s, 0:half, :] = grad(s, 1 - core).astype(bf16)
            rs_copy(s, 0, 0).start()
            acc[s] = grad(s, core)
            return
        if k <= count:
            peers, kind, r, c, at, keep_at, _, _ = plan[k - 1]
            view = local(s, keep_at, r, c)
            total = outbox[s, at : at + r, 0:c].astype(f32) if kind == "whole" else view[...]
            for i in range(len(peers)):
                rs_copy(s, k - 1, i).wait_recv()
                total = total + inbox[s, at + i * r : at + (i + 1) * r, 0:c].astype(f32)
            if k < count:
                view[...] = total
                peers, kind, r, c, at, _, theirs, _ = plan[k]
                for i in range(len(peers)):
                    outbox[s, at + i * r : at + (i + 1) * r, 0:c] = local(s, theirs[i], r, c)[...].astype(bf16)
                    rs_copy(s, k, i).start()
                return
            block(s, keep_at, r, c)[...] = total.astype(bf16)
        g = 2 * count - 1 - k
        if k > count and plan[g + 1][1] != "whole":
            for i in range(len(plan[g + 1][0])):
                ag_copy(s, g + 1, i, True).wait_recv()
        if g >= 0 and plan[g][1] != "whole":
            for i in range(len(plan[g][0])):
                ag_copy(s, g, i, False).start()

    gain_row = gain[...]
    rows = 256

    def norm_block(i, gain_grad):
        span = pl.ds(pl.multiple_of(i * rows, rows), rows)
        grads = (
            matmul_nt(dq[span, :], wq[...]) + matmul_nt(dk[span, :], wk[...]) + matmul_nt(dv[span, :], wv[...])
        )
        x = tokens[span, :].astype(f32)
        inv = lax.rsqrt(jnp.mean(x * x, 1, keepdims=True) + epsilon)
        scaled = grads * gain_row
        mean = jnp.sum(scaled * x, 1, keepdims=True) * (1.0 / width)
        part = inv * (scaled - x * (inv * inv * mean))
        token_grad[span, :] = (middle_grad[span, :] + part).astype(bf16)
        return gain_grad + jnp.sum(grads * (x * inv), 0, keepdims=True)

    slots = returned.shape[0]
    routes = routes_ref[...]
    pad = probs_ref.shape[0]
    hot = lax.broadcasted_iota(jnp.int32, (pad, length), 0) == routes
    gate_row = jnp.sum(jnp.where(hot, probs_ref[...], 0.0), 0, keepdims=True)

    def mix(c):
        at = slice(c, c + BLOCK)
        column = jnp.broadcast_to(slot_ref[0:1, at].astype(f32), (BLOCK, BLOCK)).T
        first = lax.broadcasted_iota(jnp.int32, (BLOCK, LANES), 1).astype(f32)
        spread = jnp.concatenate(
            [(column == first + float(s)).astype(f32).astype(bf16) for s in range(0, slots, LANES)], 1)
        rows_back = dot_nn(spread, returned[...])
        gate = jnp.broadcast_to(gate_row[:, at], (BLOCK, BLOCK)).T
        gate = jnp.concatenate([gate] * (width // LANES), 1)
        mixed[at, :] = (middle[at, :] + gate * rows_back).astype(bf16)

    def small_copy(k):
        return pltpu.make_async_remote_copy(
            src_ref=small_sent.at[k], dst_ref=small_box.at[k],
            send_sem=tsend.at[k], recv_sem=trecv.at[k],
            device_id=partner((every[k],)), device_id_type=MESH)

    def small_phase(k):
        if k == 0:
            gain_grad = lax.fori_loop(0, length // rows, norm_block, jnp.zeros((1, width), f32))
            small_out[...] = small_in[...]
            for i in range(width // LANES):
                small_out[i : i + 1, :] = gain_grad[:, i * LANES : (i + 1) * LANES]
        else:
            small_copy(k - 1).wait_recv()
            small_out[...] = small_out[...] + small_box[k - 1]
        if k < small_count:
            small_sent[k] = small_out[...]
            small_copy(k).start()

    last = 2 * count
    starts = (0, 0, 2, 2)
    stores = [
        pltpu.make_async_copy(sums.at[s], out, store_sem.at[s]) for s, out in enumerate((sum_o, sum_v, sum_k, sum_q))
    ]
    stores.append(pltpu.make_async_copy(token_grad, token_grad_hbm, store_sem.at[4]))
    stores.append(pltpu.make_async_copy(mixed, mixed_hbm, store_sem.at[5]))
    mixes = length // BLOCK
    for t in range(max(last + starts[-1], small_count + 4, mixes + 5) + 1):
        for s in range(4):
            if 0 <= t - starts[s] <= last:
                phase(s, t - starts[s])
                if t - starts[s] == last:
                    stores[s].start()
        if t == 3:
            for load in loads[6:9]:
                load.wait()
        if 0 <= t - 3 <= small_count:
            small_phase(t - 3)
            if t == 3:
                stores[4].start()
        if t == 4:
            for load in loads[9:]:
                load.wait()
        if 0 <= t - 4 < mixes:
            mix((t - 4) * BLOCK)
            if t - 4 == mixes - 1:
                stores[5].start()
    for store in stores:
        store.wait()
    for s in range(4):
        for k in range(count):
            for i in range(len(streams[s][k][0])):
                rs_copy(s, k, i).wait_send()
                if streams[s][k][1] != "whole":
                    ag_copy(s, k, i, False).wait_send()
    for k in range(small_count):
        small_copy(k).wait_send()


def reduce_grads(tokens, attended, middle_grad, dq, dk, dv, wq, wk, wv, gain, small,
                 returned, slot, routes_row, probs, middle, dp_size, groups):
    f32, bf16 = jnp.float32, jnp.bfloat16
    length, width = tokens.shape
    dp_bits, expert_bits = dp_size.bit_length() - 1, groups.bit_length() - 1
    count = dp_bits + expert_bits
    steps = fold_steps(width, width, list(range(count)))
    box = sum(step[2] * (3 if step[1] == "quad" else 1) for step in steps)
    messages = sum(3 if step[1] == "quad" else 1 for step in steps)
    vmem = pl.BlockSpec(memory_space=pltpu.VMEM)
    anywhere = pl.BlockSpec(memory_space=pl.ANY)
    sem = pltpu.SemaphoreType.DMA
    shape = jax.ShapeDtypeStruct
    act, square = shape((length, width), bf16), shape((width, width), bf16)
    big = (attended, middle_grad, tokens, dv, dk, dq, wq, wk, wv, returned, middle)
    return pl.pallas_call(
        functools.partial(reduce_kernel, dp_bits=dp_bits, expert_bits=expert_bits),
        out_shape=(square, square, square, square, act, shape(small.shape, f32), act),
        in_specs=[anywhere] * len(big) + [vmem] * 5,
        out_specs=(anywhere,) * 5 + (vmem, anywhere),
        scratch_shapes=[pltpu.VMEM(x.shape, x.dtype) for x in big] + [
            pltpu.VMEM((length, width), bf16),
            pltpu.VMEM((length, width), bf16),
            pltpu.VMEM((4, width, width), bf16),
            pltpu.VMEM((length, width), bf16),
            pltpu.VMEM((length, width), bf16),
            pltpu.VMEM((4, width // 2, width), f32),
            pltpu.VMEM((4, box, width), bf16),
            pltpu.VMEM((4, box, width), bf16),
            pltpu.VMEM((count,) + small.shape, f32),
            pltpu.VMEM((count,) + small.shape, f32),
            sem((len(big),)), sem((6,)),
            sem((4, 2 * messages)), sem((4, 2 * messages)), sem((count,)), sem((count,)),
        ],
        compiler_params=pltpu.CompilerParams(
            collective_id=2, has_side_effects=True, vmem_limit_bytes=62 << 20
        ),
        cost_estimate=pl.CostEstimate(
            flops=14 * length * width * width, bytes_accessed=30 << 20, transcendentals=0
        ),
    )(*big, gain, small, slot, routes_row, probs)


def key_ranges(segment_row):
    first, last = segment_row[::BLOCK], segment_row[BLOCK - 1 :: BLOCK]
    lo = jnp.sum(segment_row[None, :] < first[:, None], 1) // BLOCK
    hi = (jnp.sum(segment_row[None, :] <= last[:, None], 1) + BLOCK - 1) // BLOCK
    return lo.astype(jnp.int32), hi.astype(jnp.int32)


def per_device(
    tokens,
    segments,
    routes,
    cotangent,
    attn_gain,
    ffn_gain,
    query_weight,
    key_weight,
    value_weight,
    output_weight,
    position_bias_grid,
    router_weight,
    expert_in,
    expert_out,
):
    f32, bf16 = jnp.float32, jnp.bfloat16
    token_count, model_width = tokens.shape
    head_count = position_bias_grid.shape[1]
    score_scale = (model_width // head_count) ** (-0.5)
    experts_all = router_weight.shape[1]
    capacity = (5 * token_count + 4 * experts_all - 1) // (4 * experts_all)
    slot_rows = (capacity + 15) // 16 * 16
    slots = experts_all * slot_rows
    groups = lax.axis_size("expert")
    dp_size = lax.axis_size("dp")

    def exchange(rows):
        return lax.all_to_all(rows, "expert", split_axis=0, concat_axis=0, tiled=True)

    routes_row = routes.reshape(1, token_count)
    token_slot, grad_slots = first_slots(routes_row, cotangent, experts_all, capacity, slot_rows)
    grad_arrived = exchange(grad_slots)
    lo, hi = key_ranges(segments[0])
    router_pad = max(experts_all, 16)
    router_t = jnp.pad(router_weight.T, ((0, router_pad - experts_all), (0, 0)))
    gain_one, gain_two = attn_gain[None, :], ffn_gain[None, :]
    queries, key_rows, keys_t, value_rows, attended, log_sums, middle, router_probs, sent, gate_slots = front(
        lo, hi, tokens, segments, token_slot, routes_row, gain_one, gain_two,
        query_weight, key_weight, value_weight, output_weight, position_bias_grid, router_t,
        experts_all, slot_rows, score_scale,
    )
    home_grad, home_gate, produced, keep, give = ffn(
        sent, gate_slots, grad_arrived.reshape(slots, model_width), expert_in[0], expert_out[0], groups, dp_size,
    )
    passed = lax.ppermute(give, "dp", [(i, (i + dp_size // 2) % dp_size) for i in range(dp_size)])
    returned = exchange(produced.reshape(experts_all, slot_rows, model_width)).reshape(slots, model_width)
    query_grad, key_grad, value_grad, middle_grad, small = back(
        lo, hi, home_grad, home_gate, token_slot, routes_row, router_probs, middle, cotangent, segments, gain_two,
        output_weight, router_t, position_bias_grid, queries, key_rows, keys_t, value_rows, log_sums, attended,
        experts_all, slot_rows, score_scale,
    )
    sum_o, sum_v, sum_k, sum_q, token_grad, small, mixed = reduce_grads(
        tokens, attended, middle_grad, query_grad, key_grad, value_grad,
        query_weight, key_weight, value_weight, gain_one, small,
        returned, token_slot, routes_row, router_probs, middle, dp_size, groups,
    )
    attn_gain_grad, ffn_gain_grad, grad_q, grad_k, grad_v, grad_o, table_grad, router_grad, grad_in, grad_out = finish(
        (sum_q, sum_k, sum_v, sum_o), keep, passed, small, position_bias_grid.shape, experts_all
    )
    return (
        mixed,
        token_grad,
        attn_gain_grad.reshape(model_width),
        ffn_gain_grad.reshape(model_width),
        grad_q,
        grad_k,
        grad_v,
        grad_o,
        table_grad,
        router_grad,
        grad_in[None],
        grad_out[None],
    )


def solution(mesh):
    rows = P(("dp", "expert"), None)
    return jax.shard_map(
        per_device,
        mesh=mesh,
        in_specs=(rows,) * 4 + (P(),) * 8 + (P("expert", None, None),) * 2,
        out_specs=(rows,) * 2 + (P(),) * 8 + (P("expert", None, "dp"), P("expert", "dp", None)),
        check_vma=False,
    )
```

```python
import functools

import jax
import jax.numpy as jnp
from jax import lax
from jax.experimental import pallas as pl
from jax.experimental.pallas import tpu as pltpu
from jax.sharding import PartitionSpec as P

epsilon = 1e-06
precise_setting = lax.Precision.HIGHEST
def matmul(left, right):
    return jnp.dot(left, right, preferred_element_type=jnp.float32)


def matmul_tn(left, right):
    return lax.dot_general(left, right, (((0,), (0,)), ((), ())), preferred_element_type=jnp.float32)


def matmul_nt(left, right):
    return lax.dot_general(left, right, (((1,), (1,)), ((), ())), preferred_element_type=jnp.float32)


bucket_bounds = (12, 16, 23, 32, 46, 64, 91)
masked_score = -1e30
LANES = 128
BLOCK = 128
NEAR = 5
UF = 6
UB = 6


def bucket_of(relative):
    distance = jnp.abs(relative)
    beyond = jnp.zeros_like(distance)
    for threshold in bucket_bounds:
        beyond = beyond + (distance >= threshold).astype(jnp.int32)
    inside = jnp.where(distance < 8, distance, 8 + beyond)
    return inside + 16 * (relative > 0).astype(jnp.int32)


def dot_nt(a, b):
    return lax.dot_general(a, b, (((1,), (1,)), ((), ())), preferred_element_type=jnp.float32)


def dot_nn(a, b):
    return lax.dot_general(a, b, (((1,), (0,)), ((), ())), preferred_element_type=jnp.float32)


def split3(x):
    a = x.astype(jnp.bfloat16)
    r = x - a.astype(jnp.float32)
    b = r.astype(jnp.bfloat16)
    c = (r - b.astype(jnp.float32)).astype(jnp.bfloat16)
    return a, b, c


def fill_bias(diag_ref, bias, pairs):
    for p in range(pairs):
        for d in range(NEAR):
            tiles = []
            for h in (2 * p, 2 * p + 1):
                row = diag_ref[h : h + 1, :]
                if d in (0, NEAR - 1):
                    col = row[:, 511:512] if d == 0 else row[:, 0:1]
                    tiles.append(jnp.broadcast_to(col, (BLOCK, BLOCK)))
                else:
                    base = (3 - d) * BLOCK
                    wide = jnp.broadcast_to(row[:, base : base + 2 * BLOCK], (BLOCK, 2 * BLOCK))
                    tiles.append(pltpu.roll(wide, BLOCK, 1, stride=1, stride_axis=0)[:, :BLOCK])
            bias[p, d] = jnp.concatenate(tiles, 1)


def heads_apart(block, low, extra=None):
    zero = jnp.zeros_like(block)
    first, second = jnp.where(low, block, zero), jnp.where(low, zero, block)
    if extra is not None:
        first, second = jnp.concatenate([first, extra], 1), jnp.concatenate([second, extra], 1)
    return jnp.concatenate([first, second], 0)


def by_count(lo, hi, most, body):
    for n in range(1, most + 1):
        pl.when(hi - lo == n)(functools.partial(body, n))


def own_heads(wide):
    return jnp.concatenate([wide[:64, :LANES], wide[64:128, LANES:]], 0)


def attend(lo_ref, hi_ref, q_ref, k_ref, vt_ref, qm_ref, km_ref, bias, o_ref, lse_ref):
    pairs = q_ref.shape[1] // LANES
    length = q_ref.shape[0]
    nblk = length // BLOCK
    f32, bf16 = jnp.float32, jnp.bfloat16
    low = lax.broadcasted_iota(jnp.int32, (1, LANES), 1) < 64

    def q_block(i, _):
        lo, hi = lo_ref[i], hi_ref[i]
        rows = pl.ds(pl.multiple_of(i * BLOCK, BLOCK), BLOCK)
        start = pl.multiple_of(lo * BLOCK, BLOCK)
        qm = qm_ref[rows, :]

        def body(n):
            span = pl.ds(start, n * BLOCK)
            km = km_ref[span, :]

            def lanes_of(p):
                return pl.ds(pl.multiple_of(p * LANES, LANES), LANES)

            def scores(p):
                qs = heads_apart(q_ref[rows, lanes_of(p)], low, qm)
                return dot_nt(jnp.concatenate([k_ref[span, lanes_of(p)], km], 1), qs)

            def soften(p, st):
                parts = []
                top = None
                for b in range(n):
                    d = jnp.clip(lo + b - i, -2, 2) + 2
                    s = st[b * BLOCK : (b + 1) * BLOCK] + bias[p, d]
                    parts.append(s)
                    top = s if top is None else jnp.maximum(top, s)
                top = jnp.max(top, 0, keepdims=True)
                return jnp.concatenate([jnp.exp(s - top).astype(bf16) for s in parts], 0), top

            def mix(p, probs):
                values = jnp.concatenate([vt_ref[lanes_of(p), span], jnp.ones((16, n * BLOCK), bf16)], 0)
                return dot_nn(values, probs)

            def finish(p, acc, top):
                total = acc[LANES : LANES + 1]
                inv = 1.0 / total
                ot = own_heads(acc)
                ot = jnp.concatenate([ot[:64] * inv[:, :LANES], ot[64:] * inv[:, LANES:]], 0)
                o_ref[rows, lanes_of(p)] = ot.T.astype(bf16)
                lse_ref[i, pl.ds(p, 1), :] = top + jnp.log(total)

            def some(g, _):
                ps = [g * UF + u for u in range(UF)]
                sts = [scores(p) for p in ps]
                soft = [soften(p, st) for p, st in zip(ps, sts)]
                accs = [mix(p, x[0]) for p, x in zip(ps, soft)]
                for p, acc, x in zip(ps, accs, soft):
                    finish(p, acc, x[1])
                return 0
            lax.fori_loop(0, pairs // UF, some, 0)

        by_count(lo, hi, nblk, body)
        return 0
    lax.fori_loop(0, nblk, q_block, 0)


def attend_back(
    lo_ref, hi_ref, q_ref, k_ref, kt_ref, v_ref, lse_ref, do_ref, o_ref, qm_ref, km_ref, bias,
    dq_ref, dk_ref, dv_ref, gsum_ref, gacc, dkacc, dvacc, scale,
):
    length, width = q_ref.shape
    pairs = width // LANES
    nblk = length // BLOCK
    f32, bf16 = jnp.float32, jnp.bfloat16
    low = lax.broadcasted_iota(jnp.int32, (1, LANES), 1) < 64
    pick = (
        lax.broadcasted_iota(jnp.int32, (16, LANES), 0) == lax.broadcasted_iota(jnp.int32, (16, LANES), 1) // 64
    ).astype(f32).astype(bf16)
    gacc[...] = jnp.zeros_like(gacc)
    gsum_ref[...] = jnp.zeros_like(gsum_ref)
    dkacc[...] = jnp.zeros_like(dkacc)
    dvacc[...] = jnp.zeros_like(dvacc)

    def q_block(i, _):
        lo, hi = lo_ref[i], hi_ref[i]
        rows = pl.ds(pl.multiple_of(i * BLOCK, BLOCK), BLOCK)
        start = pl.multiple_of(lo * BLOCK, BLOCK)
        qm = qm_ref[rows, :]

        def body(n):
            span = pl.ds(start, n * BLOCK)
            km = km_ref[span, :]

            def lanes_of(p):
                return pl.ds(pl.multiple_of(p * LANES, LANES), LANES)

            def products(p):
                cols = lanes_of(p)
                qs = heads_apart(q_ref[rows, cols], low, qm)
                dd = do_ref[rows, cols]
                dos = heads_apart(dd, low)
                prod = dd.astype(f32) * o_ref[rows, cols].astype(f32)
                prod_hi = prod.astype(bf16)
                prod_lo = (prod - prod_hi.astype(f32)).astype(bf16)
                inner = dot_nt(pick, prod_hi) + dot_nt(pick, prod_lo)
                inner = jnp.concatenate([inner[0:1], inner[1:2]], 1)
                st = dot_nt(jnp.concatenate([k_ref[span, cols], km], 1), qs)
                dpt = dot_nt(v_ref[span, cols], dos)
                return qs, dos, inner, st, dpt

            def pointwise(p, inner, st, dpt):
                lse = lse_ref[i, pl.ds(p, 1), :]
                probs, grads = [], []
                for b in range(n):
                    d = jnp.clip(lo + b - i, -2, 2) + 2
                    part = slice(b * BLOCK, (b + 1) * BLOCK)
                    prob = jnp.exp(st[part] + bias[p, d] - lse)
                    grad = prob * (dpt[part] - inner)
                    gacc[p, d] += grad
                    probs.append(prob.astype(bf16))
                    grads.append(grad.astype(bf16))
                return jnp.concatenate(probs, 0), jnp.concatenate(grads, 0)

            def back(p, qs, dos, probs, grads):
                cols = lanes_of(p)
                return (
                    dot_nn(probs, dos), dot_nn(grads, qs[:, :LANES]), dot_nn(kt_ref[cols, span], grads)
                )

            def finish(p, dv, dk, dqt):
                cols = lanes_of(p)
                dvacc[span, cols] += dv
                dkacc[span, cols] += dk
                dq_ref[rows, cols] = (own_heads(dqt).T * scale).astype(bf16)

            def some(g, _):
                ps = [g * UB + u for u in range(UB)]
                first = [products(p) for p in ps]
                points = [pointwise(p, *x[2:]) for p, x in zip(ps, first)]
                last = [back(p, *x[:2], *y) for p, x, y in zip(ps, first, points)]
                for p, x in zip(ps, last):
                    finish(p, *x)
                return 0
            lax.fori_loop(0, pairs // UB, some, 0)

        by_count(lo, hi, nblk, body)
        return 0
    lax.fori_loop(0, nblk, q_block, 0)
    dk_ref[...] = dkacc[...].astype(bf16)
    dv_ref[...] = dvacc[...].astype(bf16)
    turn = (
        lax.broadcasted_iota(jnp.int32, (BLOCK, BLOCK), 0) + lax.broadcasted_iota(jnp.int32, (BLOCK, BLOCK), 1)
        == BLOCK - 1
    ).astype(f32).astype(bf16)
    for p in range(pairs):
        for d in range(NEAR):
            t = gacc[p, d]
            if 0 < d < NEAR - 1:
                hi = t.astype(bf16)
                t = dot_nn(turn, hi) + dot_nn(turn, (t - hi.astype(f32)).astype(bf16))
            for u in range(2):
                s = jnp.concatenate([t[:, u * LANES : (u + 1) * LANES], jnp.zeros((BLOCK, LANES), f32)], 1)
                if 0 < d < NEAR - 1:
                    s = pltpu.roll(s, 0, 1, stride=1, stride_axis=0)
                at = d * 16 + 2 * p + u
                gsum_ref[at : at + 1, :] = jnp.sum(s, 0, keepdims=True)


def two(x):
    a = x.astype(jnp.bfloat16)
    return a, (x - a.astype(jnp.float32)).astype(jnp.bfloat16)


def row_pieces(row):
    place = lax.broadcasted_iota(jnp.int32, (16, row.shape[1]), 0)
    a, b, c = [x.astype(jnp.float32) for x in split3(row)]
    return jnp.where(place == 0, a, jnp.where(place == 1, b, jnp.where(place == 2, c, 0.0))).astype(jnp.bfloat16)


def each(count, body):
    if count <= 8:
        for e in range(count):
            body(e)
    else:
        def step(e, _):
            body(e)
            return 0
        lax.fori_loop(0, count, step, 0)


def slot_hot(slot_row, e, slot_rows):
    place = lax.broadcasted_iota(jnp.int32, (slot_rows, slot_row.shape[1]), 0) + e * slot_rows
    return (place == slot_row).astype(jnp.float32).astype(jnp.bfloat16)


def slots_kernel(routes_ref, rows_ref, slot_ref, out_ref, *, experts, capacity, slot_rows):
    f32, bf16 = jnp.float32, jnp.bfloat16
    tokens = routes_ref.shape[1]
    routes = routes_ref[...]
    pad = max(experts, 16)
    hot = (lax.broadcasted_iota(jnp.int32, (pad, tokens), 0) == routes).astype(f32)
    earlier = (
        lax.broadcasted_iota(jnp.int32, (BLOCK, BLOCK), 0) < lax.broadcasted_iota(jnp.int32, (BLOCK, BLOCK), 1)
    ).astype(f32).astype(bf16)
    seen = jnp.zeros((pad, 1), f32)
    ranks = []
    for c in range(0, tokens, BLOCK):
        part = hot[:, c : c + BLOCK]
        ranks.append(jnp.sum((dot_nn(part.astype(bf16), earlier) + seen) * part, 0, keepdims=True))
        seen = seen + jnp.sum(part, 1, keepdims=True)
    rank = jnp.concatenate(ranks, 1).astype(jnp.int32)
    slot = jnp.where(rank < capacity, routes * slot_rows + rank, -1)
    slot_ref[...] = jnp.broadcast_to(slot, slot_ref.shape)

    def pair(e):
        rows = dot_nn(slot_hot(slot, e, 2 * slot_rows), rows_ref[...]).astype(bf16)
        out_ref[pl.ds(2 * e, 2)] = rows.reshape(2, slot_rows, rows.shape[1])
    each(experts // 2, pair)


def first_slots(routes_row, rows, experts, capacity, slot_rows):
    tokens, width = rows.shape
    vmem = pl.BlockSpec(memory_space=pltpu.VMEM)
    return pl.pallas_call(
        functools.partial(slots_kernel, experts=experts, capacity=capacity, slot_rows=slot_rows),
        out_shape=(
            jax.ShapeDtypeStruct((8, tokens), jnp.int32),
            jax.ShapeDtypeStruct((experts, slot_rows, width), jnp.bfloat16),
        ),
        in_specs=[vmem] * 2,
        out_specs=(vmem,) * 2,
        compiler_params=pltpu.CompilerParams(vmem_limit_bytes=60 << 20),
        cost_estimate=pl.CostEstimate(
            flops=2 * experts * slot_rows * tokens * width, bytes_accessed=4 << 20, transcendentals=0
        ),
    )(routes_row, rows)


def fill_masks(segment_row, qm, km):
    f32, bf16 = jnp.float32, jnp.bfloat16
    lane = lax.broadcasted_iota(jnp.int32, (1, LANES), 1)
    for b in range(qm.shape[0] // BLOCK):
        span = slice(b * BLOCK, (b + 1) * BLOCK)
        hot = (lax.broadcasted_iota(jnp.int32, (LANES, BLOCK), 0) == segment_row[:, span]).astype(f32).T
        qm[span, :] = (hot * masked_score).astype(bf16)
        km[span, :] = jnp.where(lane < 8, 1.0 - hot, 0.0).astype(bf16)


def fill_diag(grid_ref, diag, heads):
    bf16 = jnp.bfloat16
    buckets = grid_ref.shape[0]
    relative = 256 - lax.broadcasted_iota(jnp.int32, (buckets, 4 * LANES), 1)
    hot = (lax.broadcasted_iota(jnp.int32, (buckets, 4 * LANES), 0) == bucket_of(relative))
    hot = hot.astype(jnp.float32).astype(bf16)
    grid = jnp.concatenate(
        [grid_ref[...], jnp.zeros((buckets, LANES - heads), jnp.float32)], 1
    ).T[:16]
    total = None
    for piece in split3(grid):
        term = dot_nn(piece, hot)
        total = term if total is None else total + term
    diag[...] = total


def front_kernel(
    lo_ref, hi_ref, tokens, segment_row, slot_ref, routes_ref, gain_one, gain_two, wq, wk, wv, wo, grid_ref, router_t,
    q_ref, k_ref, kt_ref, v_ref, o_ref, lse_ref, middle_ref, probs_ref, xs_ref, gs_ref,
    vt_ref, qm_ref, km_ref, diag, bias, hidden, *, experts, slot_rows, scale,
):
    f32, bf16 = jnp.float32, jnp.bfloat16
    length, width = tokens.shape
    pairs = width // LANES
    nblk = length // BLOCK
    heads = grid_ref.shape[1]
    low = lax.broadcasted_iota(jnp.int32, (1, LANES), 1) < 64
    step = 256

    for b in range(length // step):
        span = slice(b * step, (b + 1) * step)
        x = tokens[span, :].astype(f32)
        inverse = lax.rsqrt(jnp.mean(x * x, 1, keepdims=True) + epsilon)
        normed = (x * inverse * gain_one[...]).astype(bf16)
        q_ref[span, :] = (dot_nn(normed, wq[...]).astype(bf16).astype(f32) * scale).astype(bf16)
        k = dot_nn(normed, wk[...]).astype(bf16)
        k_ref[span, :] = k
        kt_ref[:, span] = k.T
        v = dot_nn(normed, wv[...]).astype(bf16)
        v_ref[span, :] = v
        vt_ref[:, span] = v.T
    fill_masks(segment_row[...], qm_ref, km_ref)
    fill_diag(grid_ref, diag, heads)
    fill_bias(diag, bias, pairs)
    attend(lo_ref, hi_ref, q_ref, k_ref, vt_ref, qm_ref, km_ref, bias, o_ref, lse_ref)

    rw = two(router_t[...])
    routes = routes_ref[...]
    pad = router_t.shape[0]
    place = lax.broadcasted_iota(jnp.int32, (pad, step), 0)
    gates = []
    for b in range(length // step):
        span = slice(b * step, (b + 1) * step)
        middle = tokens[span, :].astype(f32) + dot_nn(o_ref[span, :], wo[...])
        middle_ref[span, :] = middle
        inverse = lax.rsqrt(jnp.mean(middle * middle, 1, keepdims=True) + epsilon)
        parts = two(middle * inverse * gain_two[...])
        hidden[span, :] = parts[0]
        logits = dot_nt(rw[0], parts[0]) + dot_nt(rw[0], parts[1]) + dot_nt(rw[1], parts[0])
        logits = jnp.where(place < experts, logits, -1e30)
        powers = jnp.exp(logits - jnp.max(logits, 0, keepdims=True))
        probs = powers / jnp.sum(powers, 0, keepdims=True)
        probs_ref[:, span] = probs
        gates.append(jnp.sum(jnp.where(place == routes[:, span], probs, 0.0), 0, keepdims=True))
    gates = row_pieces(jnp.concatenate(gates, 1))
    slot = slot_ref[0:1, :]
    lanes = gs_ref.shape[2]

    def one(e):
        hot = slot_hot(slot, e, slot_rows)
        xs_ref[e] = dot_nn(hot, hidden[...]).astype(bf16)
        if lanes > slot_rows:
            hot = jnp.concatenate([hot, jnp.zeros((lanes - slot_rows, length), bf16)], 0)
        row = jnp.sum(dot_nt(gates, hot), 0, keepdims=True)
        gs_ref[e] = jnp.broadcast_to(row, gs_ref.shape[1:])
    each(experts, one)


def front(lo, hi, tokens, segments, slot, routes_row, gain_one, gain_two, wq, wk, wv, wo, grid, router_t, experts, slot_rows, scale):
    length, width = tokens.shape
    heads = grid.shape[1]
    pairs = width // LANES
    nblk = length // BLOCK
    lanes = (slot_rows + LANES - 1) // LANES * LANES
    smem = pl.BlockSpec(memory_space=pltpu.SMEM)
    vmem = pl.BlockSpec(memory_space=pltpu.VMEM)
    f32, bf16 = jnp.float32, jnp.bfloat16
    shape = jax.ShapeDtypeStruct
    act = shape((length, width), bf16)
    return pl.pallas_call(
        functools.partial(front_kernel, experts=experts, slot_rows=slot_rows, scale=scale),
        out_shape=(
            act, act, shape((width, length), bf16), act, act,
            shape((nblk, 8, 2 * LANES), f32), shape((length, width), f32),
            shape((router_t.shape[0], length), f32),
            shape((experts, slot_rows, width), bf16), shape((experts, 8, lanes), f32),
        ),
        in_specs=[smem] * 2 + [vmem] * 12,
        out_specs=(vmem,) * 10,
        scratch_shapes=[
            pltpu.VMEM((width, length), bf16),
            pltpu.VMEM((length, LANES), bf16),
            pltpu.VMEM((length, LANES), bf16),
            pltpu.VMEM((16, 4 * LANES), f32),
            pltpu.VMEM((pairs, NEAR, BLOCK, 2 * LANES), f32),
            pltpu.VMEM((length, width), bf16),
        ],
        compiler_params=pltpu.CompilerParams(vmem_limit_bytes=60 << 20),
        cost_estimate=pl.CostEstimate(
            flops=4 * length * length * width + 12 * length * width * width, bytes_accessed=20 << 20,
            transcendentals=length * length * heads,
        ),
    )(lo, hi, tokens, segments, slot, routes_row, gain_one, gain_two, wq, wk, wv, wo, grid, router_t)


def bucket_sums(gsum_ref):
    bf16 = jnp.bfloat16
    total = jnp.zeros((16, LANES), jnp.float32)
    lane = lax.broadcasted_iota(jnp.int32, (2 * LANES, LANES), 1)
    for d in range(NEAR):
        relative = (d - 2) * BLOCK + BLOCK - 1 - lax.broadcasted_iota(jnp.int32, (2 * LANES, LANES), 0)
        bucket = 15 if d == 0 else 31 if d == NEAR - 1 else bucket_of(relative)
        hot = (lane == bucket).astype(jnp.float32).astype(bf16)
        for piece in split3(gsum_ref[d * 16 : (d + 1) * 16, :]):
            total = total + dot_nn(piece, hot)
    return total


def small_shape(width, experts):
    return (16 + width // LANES * experts + 16, LANES)


def back_kernel(
    lo_ref, hi_ref, home, home_gate, slot_ref, routes_ref, probs_ref, middle_ref, cotangent, segment_row, gain_two,
    wo, router_t, grid_ref, lse_ref, q_hbm, k_hbm, kt_hbm, v_hbm, o_hbm,
    dq_ref, dk_ref, dv_ref, middle_grad_hbm, small,
    q_ref, k_ref, kt_ref, v_ref, o_ref, middle_grad,
    do_ref, qm_ref, km_ref, diag, bias, gacc, dkacc, dvacc, logit, gsum_ref, sems,
    *, experts, slot_rows, scale,
):
    f32, bf16 = jnp.float32, jnp.bfloat16
    length, width = middle_ref.shape
    pairs = width // LANES
    pad = router_t.shape[0]
    heads = grid_ref.shape[1]
    slot = slot_ref[0:1, :]
    loads = [
        pltpu.make_async_copy(there, here, sems.at[i])
        for i, (there, here) in enumerate(zip(
            (q_hbm, k_hbm, kt_hbm, v_hbm, o_hbm), (q_ref, k_ref, kt_ref, v_ref, o_ref)))
    ]
    for load in loads:
        load.start()

    if experts <= 8:
        total = jnp.zeros((16, length), f32)
        for e in range(experts):
            total = total + dot_nn(row_pieces(home_gate[e, 0:1, :])[:, :slot_rows], slot_hot(slot, e, slot_rows))
    else:
        def add(e, total):
            return total + dot_nn(row_pieces(home_gate[e, 0:1, :])[:, :slot_rows], slot_hot(slot, e, slot_rows))
        total = lax.fori_loop(0, experts, add, jnp.zeros((16, length), f32))
    gate_grad = jnp.sum(total, 0, keepdims=True)
    place = lax.broadcasted_iota(jnp.int32, (pad, length), 0)
    hot = place == routes_ref[...]
    probs = probs_ref[...]
    gate = jnp.sum(jnp.where(hot, probs, 0.0), 0, keepdims=True)
    logit[...] = probs * (jnp.where(hot, gate_grad, 0.0) - gate * gate_grad)
    rw = two(router_t[...])
    slots = experts * slot_rows
    router_sum = jnp.zeros((pad, width), f32)
    gain_sum = jnp.zeros((1, width), f32)
    step = 256
    for b in range(length // step):
        span = slice(b * step, (b + 1) * step)
        hots = []
        for c in range(b * step, (b + 1) * step, BLOCK):
            column = jnp.broadcast_to(slot[:, c : c + BLOCK].astype(f32), (BLOCK, BLOCK)).T
            first = lax.broadcasted_iota(jnp.int32, (BLOCK, LANES), 1).astype(f32)
            hots.append(jnp.concatenate(
                [(column == first + float(s)).astype(f32).astype(bf16) for s in range(0, slots, LANES)], 1))
        spread = jnp.concatenate(hots, 0)
        hidden_grad = dot_nn(spread, home[...].reshape(slots, width))
        lg = two(logit[:, span])
        hidden_grad = hidden_grad + (
            matmul_tn(lg[0], rw[0]) + matmul_tn(lg[0], rw[1]) + matmul_tn(lg[1], rw[0])
        )
        middle = middle_ref[span, :]
        inverse = lax.rsqrt(jnp.mean(middle * middle, 1, keepdims=True) + epsilon)
        unit = middle * inverse
        hidden = two(unit * gain_two[...])
        router_sum = router_sum + (dot_nn(lg[0], hidden[0]) + dot_nn(lg[0], hidden[1]) + dot_nn(lg[1], hidden[0]))
        gain_sum = gain_sum + jnp.sum(hidden_grad * unit, 0, keepdims=True)
        scaled = hidden_grad * gain_two[...]
        mean = jnp.mean(scaled * middle, 1, keepdims=True)
        grad = cotangent[span, :].astype(f32) + inverse * (scaled - unit * (inverse * mean))
        middle_grad[span, :] = grad
        do_ref[span, :] = matmul_nt(grad.astype(bf16), wo[...]).astype(bf16)
    store = pltpu.make_async_copy(middle_grad, middle_grad_hbm, sems.at[5])
    store.start()
    small[...] = jnp.zeros_like(small)
    chunks = width // LANES
    for c in range(chunks):
        cols = slice(c * LANES, (c + 1) * LANES)
        small[8 + c : 9 + c, :] = gain_sum[:, cols]
        small[16 + c * experts : 16 + (c + 1) * experts, :] = router_sum[:experts, cols]

    fill_masks(segment_row[...], qm_ref, km_ref)
    fill_diag(grid_ref, diag, heads)
    fill_bias(diag, bias, pairs)
    for load in loads:
        load.wait()
    attend_back(
        lo_ref, hi_ref, q_ref, k_ref, kt_ref, v_ref, lse_ref, do_ref, o_ref, qm_ref, km_ref, bias,
        dq_ref, dk_ref, dv_ref, gsum_ref, gacc, dkacc, dvacc, scale,
    )
    at = 16 + chunks * experts
    small[at : at + 16, :] = bucket_sums(gsum_ref)
    store.wait()


def back(lo, hi, home, home_gate, slot, routes_row, probs, middle, cotangent, segments, gain_two, wo, router_t, grid,
         q, k, kt, v, lse, o, experts, slot_rows, scale):
    length, width = middle.shape
    heads = grid.shape[1]
    pairs = width // LANES
    smem = pl.BlockSpec(memory_space=pltpu.SMEM)
    vmem = pl.BlockSpec(memory_space=pltpu.VMEM)
    f32, bf16 = jnp.float32, jnp.bfloat16
    shape = jax.ShapeDtypeStruct
    act = shape((length, width), bf16)
    anywhere = pl.BlockSpec(memory_space=pl.ANY)
    return pl.pallas_call(
        functools.partial(back_kernel, experts=experts, slot_rows=slot_rows, scale=scale),
        out_shape=(act, act, act, shape((length, width), f32), shape(small_shape(width, experts), f32)),
        in_specs=[smem] * 2 + [vmem] * 13 + [anywhere] * 5,
        out_specs=(vmem, vmem, vmem, anywhere, vmem),
        scratch_shapes=[
            pltpu.VMEM((length, width), bf16),
            pltpu.VMEM((length, width), bf16),
            pltpu.VMEM((width, length), bf16),
            pltpu.VMEM((length, width), bf16),
            pltpu.VMEM((length, width), bf16),
            pltpu.VMEM((length, width), f32),
            pltpu.VMEM((length, width), bf16),
            pltpu.VMEM((length, LANES), bf16),
            pltpu.VMEM((length, LANES), bf16),
            pltpu.VMEM((16, 4 * LANES), f32),
            pltpu.VMEM((pairs, NEAR, BLOCK, 2 * LANES), f32),
            pltpu.VMEM((pairs, NEAR, BLOCK, 2 * LANES), f32),
            pltpu.VMEM((length, width), f32),
            pltpu.VMEM((length, width), f32),
            pltpu.VMEM((router_t.shape[0], length), f32),
            pltpu.VMEM((NEAR * 16, 2 * LANES), f32),
            pltpu.SemaphoreType.DMA((6,)),
        ],
        compiler_params=pltpu.CompilerParams(vmem_limit_bytes=62 << 20),
        cost_estimate=pl.CostEstimate(
            flops=10 * length * length * width + 6 * length * width * width, bytes_accessed=30 << 20,
            transcendentals=length * length * heads,
        ),
    )(lo, hi, home, home_gate, slot, routes_row, probs, middle, cotangent, segments, gain_two, wo, router_t, grid,
      lse, q, k, kt, v, o)


def finish_kernel(
    sum_q, sum_k, sum_v, sum_o, keep, passed, mixed_in, token_in, small,
    mixed_out, token_out, gain_one, gain_two, grad_q, grad_k, grad_v, grad_o, table_t, router_t, grad_in, grad_out,
    low, wide, load_sem, store_sem, copy_sem, *, experts,
):
    f32 = jnp.float32
    sources = (sum_o, sum_v, sum_k, sum_q, keep.at[0], keep.at[1], passed.at[0], passed.at[1])
    targets = (grad_o, grad_v, grad_k, grad_q, grad_in, grad_out)
    width = sum_q.shape[0]
    rows = 256
    spans = [pl.ds(r, rows) for r in range(0, width, rows)]
    copies = [
        pltpu.make_async_copy(mixed_in, mixed_out, copy_sem.at[0]),
        pltpu.make_async_copy(token_in, token_out, copy_sem.at[1]),
    ]
    loads = [
        [pltpu.make_async_copy(x.at[span], low.at[i, span], load_sem.at[i, j]) for j, span in enumerate(spans)]
        for i, x in enumerate(sources)
    ]
    stores = [
        [pltpu.make_async_copy(wide.at[i, span], x.at[span], store_sem.at[i, j]) for j, span in enumerate(spans)]
        for i, x in enumerate(targets)
    ]
    for i in range(8):
        for load in loads[i]:
            load.start()
    for copy in copies:
        copy.start()
    chunks = width // LANES
    gain_one[...] = jnp.concatenate([small[c : c + 1, :] for c in range(chunks)], 1).reshape(width)
    gain_two[...] = jnp.concatenate([small[8 + c : 9 + c, :] for c in range(chunks)], 1).reshape(width)
    for c in range(chunks):
        router_t[:, c * LANES : (c + 1) * LANES] = small[16 + c * experts : 16 + (c + 1) * experts, :]
    at = 16 + chunks * experts
    heads, buckets = table_t.shape
    table_t[...] = small[at : at + heads, :buckets]
    for i in range(4):
        for j, span in enumerate(spans):
            loads[i][j].wait()
            wide[i, span, :] = low[i, span, :].astype(f32)
            stores[i][j].start()
    for i in (4, 5):
        for j, span in enumerate(spans):
            loads[i][j].wait()
            loads[i + 2][j].wait()
            wide[i, span, :] = low[i, span, :].astype(f32) + low[i + 2, span, :].astype(f32)
            stores[i][j].start()
    for i in range(6):
        for store in stores[i]:
            store.wait()
    for copy in copies:
        copy.wait()


def finish(sums, keep, passed, mixed, token_grad, small, grid_shape, experts):
    f32, bf16 = jnp.float32, jnp.bfloat16
    width = sums[0].shape[0]
    vmem = pl.BlockSpec(memory_space=pltpu.VMEM)
    anywhere = pl.BlockSpec(memory_space=pl.ANY)
    shape = jax.ShapeDtypeStruct
    act = shape(mixed.shape, bf16)
    square, row = shape((width, width), f32), shape((width,), f32)
    blocks = width // 256
    return pl.pallas_call(
        functools.partial(finish_kernel, experts=experts),
        out_shape=(act, act, row, row, square, square, square, square, shape(grid_shape[::-1], f32),
                   shape((experts, width), f32), square, square),
        in_specs=[anywhere] * 8 + [vmem],
        out_specs=(anywhere,) * 2 + (vmem, vmem) + (anywhere,) * 4 + (vmem, vmem) + (anywhere,) * 2,
        scratch_shapes=[
            pltpu.VMEM((8, width, width), bf16), pltpu.VMEM((6, width, width), f32),
            pltpu.SemaphoreType.DMA((8, blocks)), pltpu.SemaphoreType.DMA((6, blocks)),
            pltpu.SemaphoreType.DMA((2,)),
        ],
        compiler_params=pltpu.CompilerParams(vmem_limit_bytes=40 << 20),
        cost_estimate=pl.CostEstimate(flops=0, bytes_accessed=30 << 20, transcendentals=0),
    )(*sums, keep, passed, mixed, token_grad, small)


def gelu_parts(v):
    mag = jnp.abs(v)
    t = 1.0 / (1.0 + (0.3275911 * 0.7071067811865476) * mag)
    poly = t * (0.127414796 + t * (-0.142248368 + t * (0.7107068705 + t * (-0.7265760135 + t * 0.5307027145))))
    gauss = jnp.exp(-0.5 * v * v)
    tail = poly * gauss
    phi = jnp.where(v < 0, tail, 1.0 - tail)
    return v * phi, phi + v * gauss * 0.3989422804014327


def flip_bits(index, mask, count):
    out = 0
    bit = 1
    while bit < count:
        a, b = (index // bit) % 2, (mask // bit) % 2
        out = out + bit * (a + b - 2 * a * b)
        bit *= 2
    return out


def ffn_kernel(
    xs, gs, g, win_hbm, wout_hbm,
    home, home_gate, produced, keep, give,
    win, wout, xr, gr, act, pg, gated, igs, ggs, dws, dwr, stage,
    wsem, own_sem, psem, ksem, xsend, xrecv, gsend, grecv, isend, irecv, qsend, qrecv, dsend, drecv,
    *, groups, dp_size, tiles,
):
    f32, bf16 = jnp.float32, jnp.bfloat16
    me = lax.axis_index("expert")
    dp = lax.axis_index("dp")
    core = dp % 2
    sibling = dp + 1 - 2 * core
    half_of = dp // 2
    rows = xs.shape[1]
    width = xs.shape[2]
    hidden = win.shape[1]
    tile = hidden // tiles
    lanes = gs.shape[2]

    def there(peer):
        return (dp, peer)

    load_in = pltpu.make_async_copy(win_hbm, win, wsem.at[0])
    load_out = pltpu.make_async_copy(wout_hbm, wout, wsem.at[1])
    load_in.start()
    load_out.start()
    load_g = pltpu.make_async_copy(g, gated, wsem.at[2])
    load_g.start()

    barrier = pltpu.get_barrier_semaphore()

    def greet(s, _):
        pl.semaphore_signal(
            barrier, inc=1, device_id=there(flip_bits(me, s, groups)), device_id_type=pl.DeviceIdType.MESH
        )
        return 0
    lax.fori_loop(1, groups, greet, 0)
    pl.semaphore_signal(barrier, inc=1, device_id=(sibling, me), device_id_type=pl.DeviceIdType.MESH)
    pl.semaphore_wait(barrier, groups)

    def x_copy(peer, slot):
        return pltpu.make_async_remote_copy(
            src_ref=xs.at[peer], dst_ref=xr.at[slot], send_sem=xsend.at[peer], recv_sem=xrecv.at[slot],
            device_id=there(peer), device_id_type=pl.DeviceIdType.MESH)

    def g_copy(peer, slot):
        return pltpu.make_async_remote_copy(
            src_ref=gs.at[peer], dst_ref=gr.at[slot], send_sem=gsend.at[peer], recv_sem=grecv.at[slot],
            device_id=there(peer), device_id_type=pl.DeviceIdType.MESH)

    def i_copy(peer, slot):
        return pltpu.make_async_remote_copy(
            src_ref=igs.at[peer], dst_ref=home.at[slot], send_sem=isend.at[peer], recv_sem=irecv.at[slot],
            device_id=there(peer), device_id_type=pl.DeviceIdType.MESH)

    def q_copy(peer, slot):
        return pltpu.make_async_remote_copy(
            src_ref=ggs.at[peer], dst_ref=home_gate.at[slot], send_sem=qsend.at[peer], recv_sem=qrecv.at[slot],
            device_id=there(peer), device_id_type=pl.DeviceIdType.MESH)

    def send(i, _):
        odd = (i - 1) % 2
        s = (1 - odd) * (groups - 1 - (i - 1) // 2) + odd * (i // 2)
        peer = flip_bits(me, s, groups)
        x_copy(peer, me).start()
        g_copy(peer, me).start()
        return 0
    lax.fori_loop(1, groups, send, 0)
    own_x = pltpu.make_async_copy(xs.at[me], xr.at[me], own_sem.at[0])
    own_g = pltpu.make_async_copy(gs.at[me], gr.at[me], own_sem.at[1])
    own_x.start()
    own_g.start()
    load_in.wait()
    load_out.wait()
    load_g.wait()

    spot = (
        lax.broadcasted_iota(jnp.int32, (rows, lanes), 0)
        == lax.broadcasted_iota(jnp.int32, (rows, lanes), 1)
    )

    def work(base):
        both = pl.ds(base, 2)
        x = xr[both].reshape(2 * rows, width)
        place = pl.ds(pl.multiple_of(base * rows, rows), 2 * rows)
        gg = gated[place, :]
        gate = jnp.concatenate(
            [jnp.sum(jnp.where(spot, gr[base + u, 0:1, :], 0.0), 1, keepdims=True) for u in range(2)], 0
        )
        gated[place, :] = (gate * gg.astype(f32)).astype(bf16)
        total = jnp.zeros((2 * rows, width), f32)
        gate_grad = jnp.zeros((2 * rows, 1), f32)

        def columns(t):
            return slice(t * tile, (t + 1) * tile)

        def products(t):
            return matmul(x, win[:, columns(t)]), matmul_nt(gg, wout[columns(t), :])

        ahead = products(0)
        for t in range(tiles):
            pre, out_grad = ahead
            if t + 1 < tiles:
                ahead = products(t + 1)
            value, slope = gelu_parts(pre)
            act[place, columns(t)] = value.astype(bf16)
            gate_grad = gate_grad + jnp.sum(value * out_grad, 1, keepdims=True)
            low = (gate * out_grad * slope).astype(bf16)
            pg[place, columns(t)] = low
            total = total + matmul_nt(low, win[:, columns(t)])
        igs[both] = total.astype(bf16).reshape(2, rows, width)
        for u in range(2):
            row = jnp.sum(jnp.where(spot, gate_grad[u * rows : (u + 1) * rows], 0.0), 0, keepdims=True)
            ggs[base + u] = jnp.broadcast_to(row, ggs.shape[1:])

    def arrive(peer):
        x_copy(peer, peer).wait_recv()
        g_copy(peer, peer).wait_recv()

    def back(peer):
        i_copy(peer, me).start()
        q_copy(peer, me).start()

    own_x.wait()
    own_g.wait()
    arrive(flip_bits(me, 1, groups))
    work(me - me % 2)
    own_i = pltpu.make_async_copy(igs.at[me], home.at[me], own_sem.at[0])
    own_q = pltpu.make_async_copy(ggs.at[me], home_gate.at[me], own_sem.at[1])
    own_i.start()
    own_q.start()
    back(flip_bits(me, 1, groups))

    def chunk(j, _):
        peer = flip_bits(me, 2 * j, groups)
        other = flip_bits(me, 2 * j + 1, groups)
        arrive(peer)
        arrive(other)
        work(peer - peer % 2)
        back(peer)
        back(other)
        return 0
    lax.fori_loop(1, groups // 2, chunk, 0)

    def d_copy(k):
        return pltpu.make_async_remote_copy(
            src_ref=dws.at[k % 2], dst_ref=dwr.at[k], send_sem=dsend.at[k], recv_sem=drecv.at[k],
            device_id=(sibling, me), device_id_type=pl.DeviceIdType.MESH)

    part = hidden // dp_size
    flat = groups * rows
    items = [(which, half) for half in (1 - half_of, half_of) for which in range(2)]

    def grad(which, quarter):
        span = pl.ds(pl.multiple_of(quarter * part, part), part)
        if which == 0:
            return matmul_tn(xr[...].reshape(flat, width), pg[:, span])
        return matmul_tn(act[:, span], gated[...])

    for k, (which, half) in enumerate(items):
        if k >= 2:
            d_copy(k - 2).wait_send()
        dws[k % 2] = grad(which, 2 * half + 1 - core).astype(bf16)
        d_copy(k).start()
    outs = [
        pltpu.make_async_copy(dwr.at[0], give.at[0], ksem.at[0]),
        pltpu.make_async_copy(dwr.at[1], give.at[1], ksem.at[1]),
        pltpu.make_async_copy(dwr.at[2], keep.at[0], ksem.at[2]),
        pltpu.make_async_copy(dwr.at[3], keep.at[1], ksem.at[3]),
    ]
    for k, (which, half) in enumerate(items):
        local = grad(which, 2 * half + core)
        d_copy(k).wait_recv()
        dwr[k] = (local + dwr[k].astype(f32)).astype(bf16)
        outs[k].start()

    span = stage.shape[1]
    copies = []
    for b in range(flat // span):
        if b >= 2:
            copies[b - 2].wait()
        stage[b % 2] = matmul(act[b * span : (b + 1) * span, :], wout[...]).astype(bf16)
        copy = pltpu.make_async_copy(stage.at[b % 2], produced.at[pl.ds(b * span, span)], psem.at[b % 2])
        copy.start()
        copies.append(copy)
    for copy in copies[-2:] + outs:
        copy.wait()
    own_i.wait()
    own_q.wait()
    for k in (2, 3):
        d_copy(k).wait_send()

    def finish(s, _):
        peer = flip_bits(me, s, groups)
        x_copy(peer, me).wait_send()
        g_copy(peer, me).wait_send()
        i_copy(peer, me).wait_send()
        q_copy(peer, me).wait_send()
        i_copy(peer, peer).wait_recv()
        q_copy(peer, peer).wait_recv()
        return 0
    lax.fori_loop(1, groups, finish, 0)


def ffn(xs, gs, g, weight_in, weight_out, groups, dp_size, tiles=6):
    f32, bf16 = jnp.float32, jnp.bfloat16
    _, rows, width = xs.shape
    hidden = weight_in.shape[1]
    lanes = gs.shape[2]
    part = hidden // dp_size
    anywhere = pl.BlockSpec(memory_space=pl.ANY)
    sem = pltpu.SemaphoreType.DMA
    flat = groups * rows
    shape = jax.ShapeDtypeStruct
    scratch = 2 * (2 * width * hidden + flat * (3 * width + 2 * hidden) + 6 * width * part + flat // 4 * width)
    return pl.pallas_call(
        functools.partial(ffn_kernel, groups=groups, dp_size=dp_size, tiles=tiles),
        out_shape=(
            shape((groups, rows, width), bf16),
            shape((groups, 8, lanes), f32),
            shape((flat, width), bf16),
            shape((2, width, part), bf16),
            shape((2, width, part), bf16),
        ),
        in_specs=[anywhere] * 5,
        out_specs=(anywhere,) * 5,
        scratch_shapes=[
            pltpu.VMEM((width, hidden), bf16),
            pltpu.VMEM((hidden, width), bf16),
            pltpu.VMEM((groups, rows, width), bf16),
            pltpu.VMEM((groups, 8, lanes), f32),
            pltpu.VMEM((flat, hidden), bf16),
            pltpu.VMEM((flat, hidden), bf16),
            pltpu.VMEM((flat, width), bf16),
            pltpu.VMEM((groups, rows, width), bf16),
            pltpu.VMEM((groups, 8, lanes), f32),
            pltpu.VMEM((2, width, part), bf16),
            pltpu.VMEM((4, width, part), bf16),
            pltpu.VMEM((2, flat // 8, width), bf16),
            sem((3,)), sem((2,)), sem((2,)), sem((4,)),
            sem((groups,)), sem((groups,)), sem((groups,)), sem((groups,)),
            sem((groups,)), sem((groups,)), sem((groups,)), sem((groups,)),
            sem((4,)), sem((4,)),
        ],
        compiler_params=pltpu.CompilerParams(
            collective_id=1, has_side_effects=True, vmem_limit_bytes=min(62 << 20, scratch + (12 << 20))
        ),
        cost_estimate=pl.CostEstimate(
            flops=12 * flat * width * hidden, bytes_accessed=40 << 20, transcendentals=flat * hidden
        ),
    )(xs, gs, g, weight_in, weight_out)


def fold_steps(rows, cols, bits):
    steps = []
    for bit in bits[:3]:
        rows = rows // 2
        steps.append(((bit,), "half", rows, cols))
    rows, cols = rows // 2, cols // 2
    steps.append((tuple(bits[3:5]), "quad", rows, cols))
    for bit in bits[5:]:
        steps.append(((bit,), "whole", rows, cols))
    return steps


def reduce_kernel(
    attended_hbm, middle_grad_hbm, tokens_hbm, dv_hbm, dk_hbm, dq_hbm, wq_hbm, wk_hbm, wv_hbm, returned_hbm, middle_hbm,
    gain, small_in, slot_ref, routes_ref, probs_ref,
    sum_o, sum_v, sum_k, sum_q, token_grad_hbm, small_out, mixed_hbm,
    attended, middle_grad, tokens, dv, dk, dq, wq, wk, wv, returned, middle,
    token_grad, mixed, sums, normed, branch, acc, outbox, inbox, small_box, small_sent, load_sem, store_sem,
    ssend, srecv, tsend, trecv,
    *, dp_bits, expert_bits,
):
    f32, bf16 = jnp.float32, jnp.bfloat16
    dp = lax.axis_index("dp")
    ex = lax.axis_index("expert")
    MESH = pl.DeviceIdType.MESH
    length, width = tokens.shape
    held = (attended, middle_grad, tokens, dv, dk, dq, wq, wk, wv, returned, middle)
    loads = [
        pltpu.make_async_copy(there, here, load_sem.at[i])
        for i, (there, here) in enumerate(zip(
            (attended_hbm, middle_grad_hbm, tokens_hbm, dv_hbm, dk_hbm, dq_hbm, wq_hbm, wk_hbm, wv_hbm,
             returned_hbm, middle_hbm), held))
    ]
    for load in loads:
        load.start()

    def own_bit(bit):
        axis, place = bit
        return (dp // 2 ** place) % 2 if axis == "dp" else (ex // 2 ** place) % 2

    def partner(bits):
        there = [dp, ex]
        for bit in bits:
            there[bit[0] == "expert"] = there[bit[0] == "expert"] + (1 - 2 * own_bit(bit)) * 2 ** bit[1]
        return tuple(there)

    dpb = [("dp", i) for i in range(dp_bits)]
    exb = [("expert", i) for i in range(expert_bits)]
    orders = [
        [dpb[0], dpb[1], exb[0]] + dpb[2:] + exb[1:],
        [dpb[0], exb[0], dpb[1]] + dpb[2:] + exb[1:],
    ]
    every = dpb + exb
    small_count = len(every)

    barrier = pltpu.get_barrier_semaphore()
    greeted = [(bit,) for bit in every] + [tuple(orders[0][3:5])]
    for bits in greeted:
        pl.semaphore_signal(barrier, inc=1, device_id=partner(bits), device_id_type=MESH)
    pl.semaphore_wait(barrier, len(greeted))

    def prepare(i, _):
        span = pl.ds(pl.multiple_of(i * 256, 256), 256)
        x = tokens[span, :].astype(f32)
        inv = lax.rsqrt(jnp.mean(x * x, 1, keepdims=True) + epsilon)
        normed[span, :] = (x * inv * gain[...]).astype(bf16)
        branch[span, :] = middle_grad[span, :].astype(bf16)
        return 0
    for load in loads[:3]:
        load.wait()
    lax.fori_loop(0, length // 256, prepare, 0)

    lefts = (attended, normed, normed, normed)
    rights = (branch, dv, dk, dq)
    streams = []
    for s in range(4):
        row, col, at, sem_at = 0, 0, 0, 0
        plan = []
        for bits, kind, r, c in fold_steps(width, width, orders[s % 2]):
            mine = [own_bit(bit) for bit in bits]
            if kind == "half":
                peers = [bits]
                keep_at = (row + mine[0] * r, col)
                theirs = [(row + (1 - mine[0]) * r, col)]
            elif kind == "quad":
                peers = [bits[:1], bits[1:], bits]
                keep_at = (row + mine[0] * r, col + mine[1] * c)
                theirs = [
                    (row + (1 - mine[0]) * r, col + mine[1] * c),
                    (row + mine[0] * r, col + (1 - mine[1]) * c),
                    (row + (1 - mine[0]) * r, col + (1 - mine[1]) * c),
                ]
            else:
                peers, keep_at, theirs = [bits], (row, col), [(row, col)]
            plan.append((peers, kind, r, c, at, keep_at, theirs, sem_at))
            row, col = keep_at
            at += r * len(peers)
            sem_at += len(peers)
        streams.append(plan)
    count = len(streams[0])
    sems = ssend.shape[1] // 2

    def rs_copy(s, k, i):
        peers, kind, r, c, at, _, _, sem_at = streams[s][k]
        box = pl.ds(at + i * r, r)
        return pltpu.make_async_remote_copy(
            src_ref=outbox.at[s, box, pl.ds(0, c)], dst_ref=inbox.at[s, box, pl.ds(0, c)],
            send_sem=ssend.at[s, sem_at + i], recv_sem=srecv.at[s, sem_at + i],
            device_id=partner(peers[i]), device_id_type=MESH)

    def aligned(at):
        row, col = at
        row = pl.multiple_of(row, 16) if not isinstance(row, int) else row
        col = pl.multiple_of(col, 128) if not isinstance(col, int) else col
        return row, col

    def block(s, at, r, c):
        row, col = aligned(at)
        return sums.at[s, pl.ds(row, r), pl.ds(col, c)]

    def ag_copy(s, k, i, incoming):
        peers, kind, r, c, _, keep_at, theirs, sem_at = streams[s][k]
        ref = block(s, theirs[i] if incoming else keep_at, r, c)
        return pltpu.make_async_remote_copy(
            src_ref=ref, dst_ref=ref,
            send_sem=ssend.at[s, sems + sem_at + i], recv_sem=srecv.at[s, sems + sem_at + i],
            device_id=partner(peers[i]), device_id_type=MESH)

    half = width // 2
    core = own_bit(dpb[0])

    def grad(s, which):
        span = pl.ds(pl.multiple_of(which * half, half), half)
        return matmul_tn(lefts[s][:, span], rights[s][...])

    def local(s, at, r, c):
        row, col = aligned((at[0] - streams[s][0][5][0], at[1]))
        return acc.at[s, pl.ds(row, r), pl.ds(col, c)]

    def phase(s, k):
        plan = streams[s]
        if k == 0:
            if s > 0:
                loads[2 + s].wait()
            outbox[s, 0:half, :] = grad(s, 1 - core).astype(bf16)
            rs_copy(s, 0, 0).start()
            acc[s] = grad(s, core)
            return
        if k <= count:
            peers, kind, r, c, at, keep_at, _, _ = plan[k - 1]
            view = local(s, keep_at, r, c)
            total = outbox[s, at : at + r, 0:c].astype(f32) if kind == "whole" else view[...]
            for i in range(len(peers)):
                rs_copy(s, k - 1, i).wait_recv()
                total = total + inbox[s, at + i * r : at + (i + 1) * r, 0:c].astype(f32)
            if k < count:
                view[...] = total
                peers, kind, r, c, at, _, theirs, _ = plan[k]
                for i in range(len(peers)):
                    outbox[s, at + i * r : at + (i + 1) * r, 0:c] = local(s, theirs[i], r, c)[...].astype(bf16)
                    rs_copy(s, k, i).start()
                return
            block(s, keep_at, r, c)[...] = total.astype(bf16)
        g = 2 * count - 1 - k
        if k > count and plan[g + 1][1] != "whole":
            for i in range(len(plan[g + 1][0])):
                ag_copy(s, g + 1, i, True).wait_recv()
        if g >= 0 and plan[g][1] != "whole":
            for i in range(len(plan[g][0])):
                ag_copy(s, g, i, False).start()

    gain_row = gain[...]
    rows = 256

    def norm_block(i, gain_grad):
        span = pl.ds(pl.multiple_of(i * rows, rows), rows)
        grads = (
            matmul_nt(dq[span, :], wq[...]) + matmul_nt(dk[span, :], wk[...]) + matmul_nt(dv[span, :], wv[...])
        )
        x = tokens[span, :].astype(f32)
        inv = lax.rsqrt(jnp.mean(x * x, 1, keepdims=True) + epsilon)
        scaled = grads * gain_row
        mean = jnp.sum(scaled * x, 1, keepdims=True) * (1.0 / width)
        part = inv * (scaled - x * (inv * inv * mean))
        token_grad[span, :] = (middle_grad[span, :] + part).astype(bf16)
        return gain_grad + jnp.sum(grads * (x * inv), 0, keepdims=True)

    slots = returned.shape[0]
    routes = routes_ref[...]
    pad = probs_ref.shape[0]
    hot = lax.broadcasted_iota(jnp.int32, (pad, length), 0) == routes
    gate_row = jnp.sum(jnp.where(hot, probs_ref[...], 0.0), 0, keepdims=True)

    def mix(c):
        at = slice(c, c + BLOCK)
        column = jnp.broadcast_to(slot_ref[0:1, at].astype(f32), (BLOCK, BLOCK)).T
        first = lax.broadcasted_iota(jnp.int32, (BLOCK, LANES), 1).astype(f32)
        spread = jnp.concatenate(
            [(column == first + float(s)).astype(f32).astype(bf16) for s in range(0, slots, LANES)], 1)
        rows_back = dot_nn(spread, returned[...])
        gate = jnp.broadcast_to(gate_row[:, at], (BLOCK, BLOCK)).T
        gate = jnp.concatenate([gate] * (width // LANES), 1)
        mixed[at, :] = (middle[at, :] + gate * rows_back).astype(bf16)

    def small_copy(k):
        return pltpu.make_async_remote_copy(
            src_ref=small_sent.at[k], dst_ref=small_box.at[k],
            send_sem=tsend.at[k], recv_sem=trecv.at[k],
            device_id=partner((every[k],)), device_id_type=MESH)

    def small_phase(k):
        if k == 0:
            gain_grad = lax.fori_loop(0, length // rows, norm_block, jnp.zeros((1, width), f32))
            small_out[...] = small_in[...]
            for i in range(width // LANES):
                small_out[i : i + 1, :] = gain_grad[:, i * LANES : (i + 1) * LANES]
        else:
            small_copy(k - 1).wait_recv()
            small_out[...] = small_out[...] + small_box[k - 1]
        if k < small_count:
            small_sent[k] = small_out[...]
            small_copy(k).start()

    last = 2 * count
    starts = (0, 0, 2, 2)
    stores = [
        pltpu.make_async_copy(sums.at[s], out, store_sem.at[s]) for s, out in enumerate((sum_o, sum_v, sum_k, sum_q))
    ]
    stores.append(pltpu.make_async_copy(token_grad, token_grad_hbm, store_sem.at[4]))
    stores.append(pltpu.make_async_copy(mixed, mixed_hbm, store_sem.at[5]))
    mixes = length // BLOCK
    for t in range(max(last + starts[-1], small_count + 4, mixes + 5) + 1):
        for s in range(4):
            if 0 <= t - starts[s] <= last:
                phase(s, t - starts[s])
                if t - starts[s] == last:
                    stores[s].start()
        if t == 3:
            for load in loads[6:9]:
                load.wait()
        if 0 <= t - 3 <= small_count:
            small_phase(t - 3)
            if t == 3:
                stores[4].start()
        if t == 4:
            for load in loads[9:]:
                load.wait()
        if 0 <= t - 4 < mixes:
            mix((t - 4) * BLOCK)
            if t - 4 == mixes - 1:
                stores[5].start()
    for store in stores:
        store.wait()
    for s in range(4):
        for k in range(count):
            for i in range(len(streams[s][k][0])):
                rs_copy(s, k, i).wait_send()
                if streams[s][k][1] != "whole":
                    ag_copy(s, k, i, False).wait_send()
    for k in range(small_count):
        small_copy(k).wait_send()


def reduce_grads(tokens, attended, middle_grad, dq, dk, dv, wq, wk, wv, gain, small,
                 returned, slot, routes_row, probs, middle, dp_size, groups):
    f32, bf16 = jnp.float32, jnp.bfloat16
    length, width = tokens.shape
    dp_bits, expert_bits = dp_size.bit_length() - 1, groups.bit_length() - 1
    count = dp_bits + expert_bits
    steps = fold_steps(width, width, list(range(count)))
    box = sum(step[2] * (3 if step[1] == "quad" else 1) for step in steps)
    messages = sum(3 if step[1] == "quad" else 1 for step in steps)
    vmem = pl.BlockSpec(memory_space=pltpu.VMEM)
    anywhere = pl.BlockSpec(memory_space=pl.ANY)
    sem = pltpu.SemaphoreType.DMA
    shape = jax.ShapeDtypeStruct
    act, square = shape((length, width), bf16), shape((width, width), bf16)
    big = (attended, middle_grad, tokens, dv, dk, dq, wq, wk, wv, returned, middle)
    return pl.pallas_call(
        functools.partial(reduce_kernel, dp_bits=dp_bits, expert_bits=expert_bits),
        out_shape=(square, square, square, square, act, shape(small.shape, f32), act),
        in_specs=[anywhere] * len(big) + [vmem] * 5,
        out_specs=(anywhere,) * 5 + (vmem, anywhere),
        scratch_shapes=[pltpu.VMEM(x.shape, x.dtype) for x in big] + [
            pltpu.VMEM((length, width), bf16),
            pltpu.VMEM((length, width), bf16),
            pltpu.VMEM((4, width, width), bf16),
            pltpu.VMEM((length, width), bf16),
            pltpu.VMEM((length, width), bf16),
            pltpu.VMEM((4, width // 2, width), f32),
            pltpu.VMEM((4, box, width), bf16),
            pltpu.VMEM((4, box, width), bf16),
            pltpu.VMEM((count,) + small.shape, f32),
            pltpu.VMEM((count,) + small.shape, f32),
            sem((len(big),)), sem((6,)),
            sem((4, 2 * messages)), sem((4, 2 * messages)), sem((count,)), sem((count,)),
        ],
        compiler_params=pltpu.CompilerParams(
            collective_id=2, has_side_effects=True, vmem_limit_bytes=56 << 20
        ),
        cost_estimate=pl.CostEstimate(
            flops=14 * length * width * width, bytes_accessed=30 << 20, transcendentals=0
        ),
    )(*big, gain, small, slot, routes_row, probs)


def key_ranges(segment_row):
    first, last = segment_row[::BLOCK], segment_row[BLOCK - 1 :: BLOCK]
    lo = jnp.sum(segment_row[None, :] < first[:, None], 1) // BLOCK
    hi = (jnp.sum(segment_row[None, :] <= last[:, None], 1) + BLOCK - 1) // BLOCK
    return lo.astype(jnp.int32), hi.astype(jnp.int32)


def per_device(
    tokens,
    segments,
    routes,
    cotangent,
    attn_gain,
    ffn_gain,
    query_weight,
    key_weight,
    value_weight,
    output_weight,
    position_bias_grid,
    router_weight,
    expert_in,
    expert_out,
):
    f32, bf16 = jnp.float32, jnp.bfloat16
    token_count, model_width = tokens.shape
    head_count = position_bias_grid.shape[1]
    score_scale = (model_width // head_count) ** (-0.5)
    experts_all = router_weight.shape[1]
    capacity = (5 * token_count + 4 * experts_all - 1) // (4 * experts_all)
    slot_rows = (capacity + 15) // 16 * 16
    slots = experts_all * slot_rows
    groups = lax.axis_size("expert")
    dp_size = lax.axis_size("dp")

    def exchange(rows):
        return lax.all_to_all(rows, "expert", split_axis=0, concat_axis=0, tiled=True)

    routes_row = routes.reshape(1, token_count)
    token_slot, grad_slots = first_slots(routes_row, cotangent, experts_all, capacity, slot_rows)
    grad_arrived = exchange(grad_slots)
    lo, hi = key_ranges(segments[0])
    router_pad = max(experts_all, 16)
    router_t = jnp.pad(router_weight.T, ((0, router_pad - experts_all), (0, 0)))
    gain_one, gain_two = attn_gain[None, :], ffn_gain[None, :]
    queries, key_rows, keys_t, value_rows, attended, log_sums, middle, router_probs, sent, gate_slots = front(
        lo, hi, tokens, segments, token_slot, routes_row, gain_one, gain_two,
        query_weight, key_weight, value_weight, output_weight, position_bias_grid, router_t,
        experts_all, slot_rows, score_scale,
    )
    home_grad, home_gate, produced, keep, give = ffn(
        sent, gate_slots, grad_arrived.reshape(slots, model_width), expert_in[0], expert_out[0], groups, dp_size,
    )
    passed = lax.ppermute(give, "dp", [(i, (i + dp_size // 2) % dp_size) for i in range(dp_size)])
    returned = exchange(produced.reshape(experts_all, slot_rows, model_width)).reshape(slots, model_width)
    query_grad, key_grad, value_grad, middle_grad, small = back(
        lo, hi, home_grad, home_gate, token_slot, routes_row, router_probs, middle, cotangent, segments, gain_two,
        output_weight, router_t, position_bias_grid, queries, key_rows, keys_t, value_rows, log_sums, attended,
        experts_all, slot_rows, score_scale,
    )
    sum_o, sum_v, sum_k, sum_q, token_grad, small, mixed = reduce_grads(
        tokens, attended, middle_grad, query_grad, key_grad, value_grad,
        query_weight, key_weight, value_weight, gain_one, small,
        returned, token_slot, routes_row, router_probs, middle, dp_size, groups,
    )
    (mixed, token_grad, attn_gain_grad, ffn_gain_grad, grad_q, grad_k, grad_v, grad_o, table_grad, router_grad,
     grad_in, grad_out) = finish(
        (sum_q, sum_k, sum_v, sum_o), keep, passed, mixed, token_grad, small, position_bias_grid.shape, experts_all
    )
    return (
        mixed,
        token_grad,
        attn_gain_grad,
        ffn_gain_grad,
        grad_q,
        grad_k,
        grad_v,
        grad_o,
        table_grad.T,
        router_grad.T,
        grad_in[None],
        grad_out[None],
    )


def solution(mesh):
    rows = P(("dp", "expert"), None)
    return jax.shard_map(
        per_device,
        mesh=mesh,
        in_specs=(rows,) * 4 + (P(),) * 8 + (P("expert", None, None),) * 2,
        out_specs=(rows,) * 2 + (P(),) * 8 + (P("expert", None, "dp"), P("expert", "dp", None)),
        check_vma=False,
    )
```

```python
import functools

import jax
import jax.numpy as jnp
from jax import lax
from jax.experimental import pallas as pl
from jax.experimental.pallas import tpu as pltpu
from jax.sharding import PartitionSpec as P

epsilon = 1e-06
precise_setting = lax.Precision.HIGHEST
def matmul(left, right):
    return jnp.dot(left, right, preferred_element_type=jnp.float32)


def matmul_tn(left, right):
    return lax.dot_general(left, right, (((0,), (0,)), ((), ())), preferred_element_type=jnp.float32)


def matmul_nt(left, right):
    return lax.dot_general(left, right, (((1,), (1,)), ((), ())), preferred_element_type=jnp.float32)


bucket_bounds = (12, 16, 23, 32, 46, 64, 91)
masked_score = -1e30
LANES = 128
BLOCK = 128
NEAR = 5
UF = 6
UB = 6


def bucket_of(relative):
    distance = jnp.abs(relative)
    beyond = jnp.zeros_like(distance)
    for threshold in bucket_bounds:
        beyond = beyond + (distance >= threshold).astype(jnp.int32)
    inside = jnp.where(distance < 8, distance, 8 + beyond)
    return inside + 16 * (relative > 0).astype(jnp.int32)


def dot_nt(a, b):
    return lax.dot_general(a, b, (((1,), (1,)), ((), ())), preferred_element_type=jnp.float32)


def dot_nn(a, b):
    return lax.dot_general(a, b, (((1,), (0,)), ((), ())), preferred_element_type=jnp.float32)


def split3(x):
    a = x.astype(jnp.bfloat16)
    r = x - a.astype(jnp.float32)
    b = r.astype(jnp.bfloat16)
    c = (r - b.astype(jnp.float32)).astype(jnp.bfloat16)
    return a, b, c


def fill_bias(diag_ref, bias, pairs):
    for p in range(pairs):
        for d in range(NEAR):
            tiles = []
            for h in (2 * p, 2 * p + 1):
                row = diag_ref[h : h + 1, :]
                if d in (0, NEAR - 1):
                    col = row[:, 511:512] if d == 0 else row[:, 0:1]
                    tiles.append(jnp.broadcast_to(col, (BLOCK, BLOCK)))
                else:
                    base = (3 - d) * BLOCK
                    wide = jnp.broadcast_to(row[:, base : base + 2 * BLOCK], (BLOCK, 2 * BLOCK))
                    tiles.append(pltpu.roll(wide, BLOCK, 1, stride=1, stride_axis=0)[:, :BLOCK])
            bias[p, d] = jnp.concatenate(tiles, 1)


def heads_apart(block, low, extra=None):
    zero = jnp.zeros_like(block)
    first, second = jnp.where(low, block, zero), jnp.where(low, zero, block)
    if extra is not None:
        first, second = jnp.concatenate([first, extra], 1), jnp.concatenate([second, extra], 1)
    return jnp.concatenate([first, second], 0)


def by_count(lo, hi, most, body):
    for n in range(1, most + 1):
        pl.when(hi - lo == n)(functools.partial(body, n))


def own_heads(wide):
    return jnp.concatenate([wide[:64, :LANES], wide[64:128, LANES:]], 0)


def attend(lo_ref, hi_ref, q_ref, k_ref, vt_ref, qm_ref, km_ref, bias, o_ref, lse_ref):
    pairs = q_ref.shape[1] // LANES
    length = q_ref.shape[0]
    nblk = length // BLOCK
    f32, bf16 = jnp.float32, jnp.bfloat16
    low = lax.broadcasted_iota(jnp.int32, (1, LANES), 1) < 64

    def q_block(i, _):
        lo, hi = lo_ref[i], hi_ref[i]
        rows = pl.ds(pl.multiple_of(i * BLOCK, BLOCK), BLOCK)
        start = pl.multiple_of(lo * BLOCK, BLOCK)
        qm = qm_ref[rows, :]

        def body(n):
            span = pl.ds(start, n * BLOCK)
            km = km_ref[span, :]

            def lanes_of(p):
                return pl.ds(pl.multiple_of(p * LANES, LANES), LANES)

            def scores(p):
                qs = heads_apart(q_ref[rows, lanes_of(p)], low, qm)
                return dot_nt(jnp.concatenate([k_ref[span, lanes_of(p)], km], 1), qs)

            def soften(p, st):
                parts = []
                top = None
                for b in range(n):
                    d = jnp.clip(lo + b - i, -2, 2) + 2
                    s = st[b * BLOCK : (b + 1) * BLOCK] + bias[p, d]
                    parts.append(s)
                    top = s if top is None else jnp.maximum(top, s)
                top = jnp.max(top, 0, keepdims=True)
                return jnp.concatenate([jnp.exp(s - top).astype(bf16) for s in parts], 0), top

            def mix(p, probs):
                values = jnp.concatenate([vt_ref[lanes_of(p), span], jnp.ones((16, n * BLOCK), bf16)], 0)
                return dot_nn(values, probs)

            def finish(p, acc, top):
                total = acc[LANES : LANES + 1]
                inv = 1.0 / total
                ot = own_heads(acc)
                ot = jnp.concatenate([ot[:64] * inv[:, :LANES], ot[64:] * inv[:, LANES:]], 0)
                o_ref[rows, lanes_of(p)] = ot.T.astype(bf16)
                lse_ref[i, pl.ds(p, 1), :] = top + jnp.log(total)

            def some(g, _):
                ps = [g * UF + u for u in range(UF)]
                sts = [scores(p) for p in ps]
                soft = [soften(p, st) for p, st in zip(ps, sts)]
                accs = [mix(p, x[0]) for p, x in zip(ps, soft)]
                for p, acc, x in zip(ps, accs, soft):
                    finish(p, acc, x[1])
                return 0
            lax.fori_loop(0, pairs // UF, some, 0)

        by_count(lo, hi, nblk, body)
        return 0
    lax.fori_loop(0, nblk, q_block, 0)


def attend_back(
    lo_ref, hi_ref, q_ref, k_ref, kt_ref, v_ref, lse_ref, do_ref, o_ref, qm_ref, km_ref, bias,
    dq_ref, dk_ref, dv_ref, gsum_ref, gacc, dkacc, dvacc, scale,
):
    length, width = q_ref.shape
    pairs = width // LANES
    nblk = length // BLOCK
    f32, bf16 = jnp.float32, jnp.bfloat16
    low = lax.broadcasted_iota(jnp.int32, (1, LANES), 1) < 64
    pick = (
        lax.broadcasted_iota(jnp.int32, (16, LANES), 0) == lax.broadcasted_iota(jnp.int32, (16, LANES), 1) // 64
    ).astype(f32).astype(bf16)
    gacc[...] = jnp.zeros_like(gacc)
    gsum_ref[...] = jnp.zeros_like(gsum_ref)
    dkacc[...] = jnp.zeros_like(dkacc)
    dvacc[...] = jnp.zeros_like(dvacc)

    def q_block(i, _):
        lo, hi = lo_ref[i], hi_ref[i]
        rows = pl.ds(pl.multiple_of(i * BLOCK, BLOCK), BLOCK)
        start = pl.multiple_of(lo * BLOCK, BLOCK)
        qm = qm_ref[rows, :]

        def body(n):
            span = pl.ds(start, n * BLOCK)
            km = km_ref[span, :]

            def lanes_of(p):
                return pl.ds(pl.multiple_of(p * LANES, LANES), LANES)

            def products(p):
                cols = lanes_of(p)
                qs = heads_apart(q_ref[rows, cols], low, qm)
                dd = do_ref[rows, cols]
                dos = heads_apart(dd, low)
                prod = dd.astype(f32) * o_ref[rows, cols].astype(f32)
                prod_hi = prod.astype(bf16)
                prod_lo = (prod - prod_hi.astype(f32)).astype(bf16)
                inner = dot_nt(pick, prod_hi) + dot_nt(pick, prod_lo)
                inner = jnp.concatenate([inner[0:1], inner[1:2]], 1)
                st = dot_nt(jnp.concatenate([k_ref[span, cols], km], 1), qs)
                dpt = dot_nt(v_ref[span, cols], dos)
                return qs, dos, inner, st, dpt

            def pointwise(p, inner, st, dpt):
                lse = lse_ref[i, pl.ds(p, 1), :]
                probs, grads = [], []
                for b in range(n):
                    d = jnp.clip(lo + b - i, -2, 2) + 2
                    part = slice(b * BLOCK, (b + 1) * BLOCK)
                    prob = jnp.exp(st[part] + bias[p, d] - lse)
                    grad = prob * (dpt[part] - inner)
                    gacc[p, d] += grad
                    probs.append(prob.astype(bf16))
                    grads.append(grad.astype(bf16))
                return jnp.concatenate(probs, 0), jnp.concatenate(grads, 0)

            def back(p, qs, dos, probs, grads):
                cols = lanes_of(p)
                return (
                    dot_nn(probs, dos), dot_nn(grads, qs[:, :LANES]), dot_nn(kt_ref[cols, span], grads)
                )

            def finish(p, dv, dk, dqt):
                cols = lanes_of(p)
                dvacc[span, cols] += dv
                dkacc[span, cols] += dk
                dq_ref[rows, cols] = (own_heads(dqt).T * scale).astype(bf16)

            def some(g, _):
                ps = [g * UB + u for u in range(UB)]
                first = [products(p) for p in ps]
                points = [pointwise(p, *x[2:]) for p, x in zip(ps, first)]
                last = [back(p, *x[:2], *y) for p, x, y in zip(ps, first, points)]
                for p, x in zip(ps, last):
                    finish(p, *x)
                return 0
            lax.fori_loop(0, pairs // UB, some, 0)

        by_count(lo, hi, nblk, body)
        return 0
    lax.fori_loop(0, nblk, q_block, 0)
    dk_ref[...] = dkacc[...].astype(bf16)
    dv_ref[...] = dvacc[...].astype(bf16)
    turn = (
        lax.broadcasted_iota(jnp.int32, (BLOCK, BLOCK), 0) + lax.broadcasted_iota(jnp.int32, (BLOCK, BLOCK), 1)
        == BLOCK - 1
    ).astype(f32).astype(bf16)
    for p in range(pairs):
        for d in range(NEAR):
            t = gacc[p, d]
            if 0 < d < NEAR - 1:
                hi = t.astype(bf16)
                t = dot_nn(turn, hi) + dot_nn(turn, (t - hi.astype(f32)).astype(bf16))
            for u in range(2):
                s = jnp.concatenate([t[:, u * LANES : (u + 1) * LANES], jnp.zeros((BLOCK, LANES), f32)], 1)
                if 0 < d < NEAR - 1:
                    s = pltpu.roll(s, 0, 1, stride=1, stride_axis=0)
                at = d * 16 + 2 * p + u
                gsum_ref[at : at + 1, :] = jnp.sum(s, 0, keepdims=True)


def two(x):
    a = x.astype(jnp.bfloat16)
    return a, (x - a.astype(jnp.float32)).astype(jnp.bfloat16)


def row_pieces(row):
    place = lax.broadcasted_iota(jnp.int32, (16, row.shape[1]), 0)
    a, b, c = [x.astype(jnp.float32) for x in split3(row)]
    return jnp.where(place == 0, a, jnp.where(place == 1, b, jnp.where(place == 2, c, 0.0))).astype(jnp.bfloat16)


def each(count, body):
    if count <= 8:
        for e in range(count):
            body(e)
    else:
        def step(e, _):
            body(e)
            return 0
        lax.fori_loop(0, count, step, 0)


def slot_hot(slot_row, e, slot_rows):
    place = lax.broadcasted_iota(jnp.int32, (slot_rows, slot_row.shape[1]), 0) + e * slot_rows
    return (place == slot_row).astype(jnp.float32).astype(jnp.bfloat16)


def slots_kernel(routes_ref, rows_ref, slot_ref, out_ref, *, experts, capacity, slot_rows):
    f32, bf16 = jnp.float32, jnp.bfloat16
    tokens = routes_ref.shape[1]
    routes = routes_ref[...]
    pad = max(experts, 16)
    hot = (lax.broadcasted_iota(jnp.int32, (pad, tokens), 0) == routes).astype(f32)
    earlier = (
        lax.broadcasted_iota(jnp.int32, (BLOCK, BLOCK), 0) < lax.broadcasted_iota(jnp.int32, (BLOCK, BLOCK), 1)
    ).astype(f32).astype(bf16)
    seen = jnp.zeros((pad, 1), f32)
    ranks = []
    for c in range(0, tokens, BLOCK):
        part = hot[:, c : c + BLOCK]
        ranks.append(jnp.sum((dot_nn(part.astype(bf16), earlier) + seen) * part, 0, keepdims=True))
        seen = seen + jnp.sum(part, 1, keepdims=True)
    rank = jnp.concatenate(ranks, 1).astype(jnp.int32)
    slot = jnp.where(rank < capacity, routes * slot_rows + rank, -1)
    slot_ref[...] = jnp.broadcast_to(slot, slot_ref.shape)

    def pair(e):
        rows = dot_nn(slot_hot(slot, e, 2 * slot_rows), rows_ref[...]).astype(bf16)
        out_ref[pl.ds(2 * e, 2)] = rows.reshape(2, slot_rows, rows.shape[1])
    each(experts // 2, pair)


def first_slots(routes_row, rows, experts, capacity, slot_rows):
    tokens, width = rows.shape
    vmem = pl.BlockSpec(memory_space=pltpu.VMEM)
    return pl.pallas_call(
        functools.partial(slots_kernel, experts=experts, capacity=capacity, slot_rows=slot_rows),
        out_shape=(
            jax.ShapeDtypeStruct((8, tokens), jnp.int32),
            jax.ShapeDtypeStruct((experts, slot_rows, width), jnp.bfloat16),
        ),
        in_specs=[vmem] * 2,
        out_specs=(vmem,) * 2,
        compiler_params=pltpu.CompilerParams(vmem_limit_bytes=63 << 20),
        cost_estimate=pl.CostEstimate(
            flops=2 * experts * slot_rows * tokens * width, bytes_accessed=4 << 20, transcendentals=0
        ),
    )(routes_row, rows)


def fill_masks(segment_row, qm, km):
    f32, bf16 = jnp.float32, jnp.bfloat16
    lane = lax.broadcasted_iota(jnp.int32, (1, LANES), 1)
    for b in range(qm.shape[0] // BLOCK):
        span = slice(b * BLOCK, (b + 1) * BLOCK)
        hot = (lax.broadcasted_iota(jnp.int32, (LANES, BLOCK), 0) == segment_row[:, span]).astype(f32).T
        qm[span, :] = (hot * masked_score).astype(bf16)
        km[span, :] = jnp.where(lane < 8, 1.0 - hot, 0.0).astype(bf16)


def fill_diag(grid_ref, diag, heads):
    bf16 = jnp.bfloat16
    buckets = grid_ref.shape[0]
    relative = 256 - lax.broadcasted_iota(jnp.int32, (buckets, 4 * LANES), 1)
    hot = (lax.broadcasted_iota(jnp.int32, (buckets, 4 * LANES), 0) == bucket_of(relative))
    hot = hot.astype(jnp.float32).astype(bf16)
    grid = jnp.concatenate(
        [grid_ref[...], jnp.zeros((buckets, LANES - heads), jnp.float32)], 1
    ).T[:16]
    total = None
    for piece in split3(grid):
        term = dot_nn(piece, hot)
        total = term if total is None else total + term
    diag[...] = total


def front_kernel(
    lo_ref, hi_ref, tokens, segment_row, slot_ref, routes_ref, gain_one, gain_two, wq, wk, wv, wo, grid_ref, router_t,
    q_ref, k_ref, kt_ref, v_ref, o_ref, lse_ref, middle_ref, probs_ref, xs_ref, gs_ref,
    vt_ref, qm_ref, km_ref, diag, bias, hidden, *, experts, slot_rows, scale,
):
    f32, bf16 = jnp.float32, jnp.bfloat16
    length, width = tokens.shape
    pairs = width // LANES
    nblk = length // BLOCK
    heads = grid_ref.shape[1]
    low = lax.broadcasted_iota(jnp.int32, (1, LANES), 1) < 64
    step = 256

    for b in range(length // step):
        span = slice(b * step, (b + 1) * step)
        x = tokens[span, :].astype(f32)
        inverse = lax.rsqrt(jnp.mean(x * x, 1, keepdims=True) + epsilon)
        normed = (x * inverse * gain_one[...]).astype(bf16)
        q_ref[span, :] = (dot_nn(normed, wq[...]).astype(bf16).astype(f32) * scale).astype(bf16)
        k = dot_nn(normed, wk[...]).astype(bf16)
        k_ref[span, :] = k
        kt_ref[:, span] = k.T
        v = dot_nn(normed, wv[...]).astype(bf16)
        v_ref[span, :] = v
        vt_ref[:, span] = v.T
    fill_masks(segment_row[...], qm_ref, km_ref)
    fill_diag(grid_ref, diag, heads)
    fill_bias(diag, bias, pairs)
    attend(lo_ref, hi_ref, q_ref, k_ref, vt_ref, qm_ref, km_ref, bias, o_ref, lse_ref)

    rw = two(router_t[...])
    routes = routes_ref[...]
    pad = router_t.shape[0]
    place = lax.broadcasted_iota(jnp.int32, (pad, step), 0)
    gates = []
    for b in range(length // step):
        span = slice(b * step, (b + 1) * step)
        middle = tokens[span, :].astype(f32) + dot_nn(o_ref[span, :], wo[...])
        middle_ref[span, :] = middle
        inverse = lax.rsqrt(jnp.mean(middle * middle, 1, keepdims=True) + epsilon)
        parts = two(middle * inverse * gain_two[...])
        hidden[span, :] = parts[0]
        logits = dot_nt(rw[0], parts[0]) + dot_nt(rw[0], parts[1]) + dot_nt(rw[1], parts[0])
        logits = jnp.where(place < experts, logits, -1e30)
        powers = jnp.exp(logits - jnp.max(logits, 0, keepdims=True))
        probs = powers / jnp.sum(powers, 0, keepdims=True)
        probs_ref[:, span] = probs
        gates.append(jnp.sum(jnp.where(place == routes[:, span], probs, 0.0), 0, keepdims=True))
    gates = row_pieces(jnp.concatenate(gates, 1))
    slot = slot_ref[0:1, :]
    lanes = gs_ref.shape[2]

    def one(e):
        hot = slot_hot(slot, e, slot_rows)
        xs_ref[e] = dot_nn(hot, hidden[...]).astype(bf16)
        if lanes > slot_rows:
            hot = jnp.concatenate([hot, jnp.zeros((lanes - slot_rows, length), bf16)], 0)
        row = jnp.sum(dot_nt(gates, hot), 0, keepdims=True)
        gs_ref[e] = jnp.broadcast_to(row, gs_ref.shape[1:])
    each(experts, one)


def front(lo, hi, tokens, segments, slot, routes_row, gain_one, gain_two, wq, wk, wv, wo, grid, router_t, experts, slot_rows, scale):
    length, width = tokens.shape
    heads = grid.shape[1]
    pairs = width // LANES
    nblk = length // BLOCK
    lanes = (slot_rows + LANES - 1) // LANES * LANES
    smem = pl.BlockSpec(memory_space=pltpu.SMEM)
    vmem = pl.BlockSpec(memory_space=pltpu.VMEM)
    f32, bf16 = jnp.float32, jnp.bfloat16
    shape = jax.ShapeDtypeStruct
    act = shape((length, width), bf16)
    return pl.pallas_call(
        functools.partial(front_kernel, experts=experts, slot_rows=slot_rows, scale=scale),
        out_shape=(
            act, act, shape((width, length), bf16), act, act,
            shape((nblk, 8, 2 * LANES), f32), shape((length, width), f32),
            shape((router_t.shape[0], length), f32),
            shape((experts, slot_rows, width), bf16), shape((experts, 8, lanes), f32),
        ),
        in_specs=[smem] * 2 + [vmem] * 12,
        out_specs=(vmem,) * 10,
        scratch_shapes=[
            pltpu.VMEM((width, length), bf16),
            pltpu.VMEM((length, LANES), bf16),
            pltpu.VMEM((length, LANES), bf16),
            pltpu.VMEM((16, 4 * LANES), f32),
            pltpu.VMEM((pairs, NEAR, BLOCK, 2 * LANES), f32),
            pltpu.VMEM((length, width), bf16),
        ],
        compiler_params=pltpu.CompilerParams(vmem_limit_bytes=63 << 20),
        cost_estimate=pl.CostEstimate(
            flops=4 * length * length * width + 12 * length * width * width, bytes_accessed=20 << 20,
            transcendentals=length * length * heads,
        ),
    )(lo, hi, tokens, segments, slot, routes_row, gain_one, gain_two, wq, wk, wv, wo, grid, router_t)


def bucket_sums(gsum_ref):
    bf16 = jnp.bfloat16
    total = jnp.zeros((16, LANES), jnp.float32)
    lane = lax.broadcasted_iota(jnp.int32, (2 * LANES, LANES), 1)
    for d in range(NEAR):
        relative = (d - 2) * BLOCK + BLOCK - 1 - lax.broadcasted_iota(jnp.int32, (2 * LANES, LANES), 0)
        bucket = 15 if d == 0 else 31 if d == NEAR - 1 else bucket_of(relative)
        hot = (lane == bucket).astype(jnp.float32).astype(bf16)
        for piece in split3(gsum_ref[d * 16 : (d + 1) * 16, :]):
            total = total + dot_nn(piece, hot)
    return total


def small_shape(width, experts):
    return (16 + width // LANES * experts + 16, LANES)


def back_kernel(
    lo_ref, hi_ref, home, home_gate, slot_ref, routes_ref, probs_ref, middle_ref, cotangent, segment_row, gain_two,
    wo, router_t, grid_ref, lse_ref, q_hbm, k_hbm, kt_hbm, v_hbm, o_hbm,
    dq_ref, dk_ref, dv_ref, middle_grad_hbm, small,
    q_ref, k_ref, kt_ref, v_ref, o_ref, middle_grad,
    do_ref, qm_ref, km_ref, diag, bias, gacc, dkacc, dvacc, logit, gsum_ref, sems,
    *, experts, slot_rows, scale,
):
    f32, bf16 = jnp.float32, jnp.bfloat16
    length, width = middle_ref.shape
    pairs = width // LANES
    pad = router_t.shape[0]
    heads = grid_ref.shape[1]
    slot = slot_ref[0:1, :]
    loads = [
        pltpu.make_async_copy(there, here, sems.at[i])
        for i, (there, here) in enumerate(zip(
            (q_hbm, k_hbm, kt_hbm, v_hbm, o_hbm), (q_ref, k_ref, kt_ref, v_ref, o_ref)))
    ]
    for load in loads:
        load.start()

    if experts <= 8:
        total = jnp.zeros((16, length), f32)
        for e in range(experts):
            total = total + dot_nn(row_pieces(home_gate[e, 0:1, :])[:, :slot_rows], slot_hot(slot, e, slot_rows))
    else:
        def add(e, total):
            return total + dot_nn(row_pieces(home_gate[e, 0:1, :])[:, :slot_rows], slot_hot(slot, e, slot_rows))
        total = lax.fori_loop(0, experts, add, jnp.zeros((16, length), f32))
    gate_grad = jnp.sum(total, 0, keepdims=True)
    place = lax.broadcasted_iota(jnp.int32, (pad, length), 0)
    hot = place == routes_ref[...]
    probs = probs_ref[...]
    gate = jnp.sum(jnp.where(hot, probs, 0.0), 0, keepdims=True)
    logit[...] = probs * (jnp.where(hot, gate_grad, 0.0) - gate * gate_grad)
    rw = two(router_t[...])
    slots = experts * slot_rows
    router_sum = jnp.zeros((pad, width), f32)
    gain_sum = jnp.zeros((1, width), f32)
    step = 256
    for b in range(length // step):
        span = slice(b * step, (b + 1) * step)
        hots = []
        for c in range(b * step, (b + 1) * step, BLOCK):
            column = jnp.broadcast_to(slot[:, c : c + BLOCK].astype(f32), (BLOCK, BLOCK)).T
            first = lax.broadcasted_iota(jnp.int32, (BLOCK, LANES), 1).astype(f32)
            hots.append(jnp.concatenate(
                [(column == first + float(s)).astype(f32).astype(bf16) for s in range(0, slots, LANES)], 1))
        spread = jnp.concatenate(hots, 0)
        hidden_grad = dot_nn(spread, home[...].reshape(slots, width))
        lg = two(logit[:, span])
        hidden_grad = hidden_grad + (
            matmul_tn(lg[0], rw[0]) + matmul_tn(lg[0], rw[1]) + matmul_tn(lg[1], rw[0])
        )
        middle = middle_ref[span, :]
        inverse = lax.rsqrt(jnp.mean(middle * middle, 1, keepdims=True) + epsilon)
        unit = middle * inverse
        hidden = two(unit * gain_two[...])
        router_sum = router_sum + (dot_nn(lg[0], hidden[0]) + dot_nn(lg[0], hidden[1]) + dot_nn(lg[1], hidden[0]))
        gain_sum = gain_sum + jnp.sum(hidden_grad * unit, 0, keepdims=True)
        scaled = hidden_grad * gain_two[...]
        mean = jnp.mean(scaled * middle, 1, keepdims=True)
        grad = cotangent[span, :].astype(f32) + inverse * (scaled - unit * (inverse * mean))
        middle_grad[span, :] = grad
        do_ref[span, :] = matmul_nt(grad.astype(bf16), wo[...]).astype(bf16)
    store = pltpu.make_async_copy(middle_grad, middle_grad_hbm, sems.at[5])
    store.start()
    small[...] = jnp.zeros_like(small)
    chunks = width // LANES
    for c in range(chunks):
        cols = slice(c * LANES, (c + 1) * LANES)
        small[8 + c : 9 + c, :] = gain_sum[:, cols]
        small[16 + c * experts : 16 + (c + 1) * experts, :] = router_sum[:experts, cols]

    fill_masks(segment_row[...], qm_ref, km_ref)
    fill_diag(grid_ref, diag, heads)
    fill_bias(diag, bias, pairs)
    for load in loads:
        load.wait()
    attend_back(
        lo_ref, hi_ref, q_ref, k_ref, kt_ref, v_ref, lse_ref, do_ref, o_ref, qm_ref, km_ref, bias,
        dq_ref, dk_ref, dv_ref, gsum_ref, gacc, dkacc, dvacc, scale,
    )
    at = 16 + chunks * experts
    small[at : at + 16, :] = bucket_sums(gsum_ref)
    store.wait()


def back(lo, hi, home, home_gate, slot, routes_row, probs, middle, cotangent, segments, gain_two, wo, router_t, grid,
         q, k, kt, v, lse, o, experts, slot_rows, scale):
    length, width = middle.shape
    heads = grid.shape[1]
    pairs = width // LANES
    smem = pl.BlockSpec(memory_space=pltpu.SMEM)
    vmem = pl.BlockSpec(memory_space=pltpu.VMEM)
    f32, bf16 = jnp.float32, jnp.bfloat16
    shape = jax.ShapeDtypeStruct
    act = shape((length, width), bf16)
    anywhere = pl.BlockSpec(memory_space=pl.ANY)
    return pl.pallas_call(
        functools.partial(back_kernel, experts=experts, slot_rows=slot_rows, scale=scale),
        out_shape=(act, act, act, shape((length, width), f32), shape(small_shape(width, experts), f32)),
        in_specs=[smem] * 2 + [vmem] * 13 + [anywhere] * 5,
        out_specs=(vmem, vmem, vmem, anywhere, vmem),
        scratch_shapes=[
            pltpu.VMEM((length, width), bf16),
            pltpu.VMEM((length, width), bf16),
            pltpu.VMEM((width, length), bf16),
            pltpu.VMEM((length, width), bf16),
            pltpu.VMEM((length, width), bf16),
            pltpu.VMEM((length, width), f32),
            pltpu.VMEM((length, width), bf16),
            pltpu.VMEM((length, LANES), bf16),
            pltpu.VMEM((length, LANES), bf16),
            pltpu.VMEM((16, 4 * LANES), f32),
            pltpu.VMEM((pairs, NEAR, BLOCK, 2 * LANES), f32),
            pltpu.VMEM((pairs, NEAR, BLOCK, 2 * LANES), f32),
            pltpu.VMEM((length, width), f32),
            pltpu.VMEM((length, width), f32),
            pltpu.VMEM((router_t.shape[0], length), f32),
            pltpu.VMEM((NEAR * 16, 2 * LANES), f32),
            pltpu.SemaphoreType.DMA((6,)),
        ],
        compiler_params=pltpu.CompilerParams(vmem_limit_bytes=63 << 20),
        cost_estimate=pl.CostEstimate(
            flops=10 * length * length * width + 6 * length * width * width, bytes_accessed=30 << 20,
            transcendentals=length * length * heads,
        ),
    )(lo, hi, home, home_gate, slot, routes_row, probs, middle, cotangent, segments, gain_two, wo, router_t, grid,
      lse, q, k, kt, v, o)


def finish_kernel(
    sum_q, sum_k, sum_v, sum_o, keep, passed, mixed_in, token_in, small,
    mixed_out, token_out, gain_one, gain_two, grad_q, grad_k, grad_v, grad_o, table_t, router_t, grad_in, grad_out,
    low, wide, load_sem, store_sem, copy_sem, *, experts,
):
    f32 = jnp.float32
    sources = (sum_o, sum_v, sum_k, sum_q, keep.at[0], keep.at[1], passed.at[0], passed.at[1])
    targets = (grad_o, grad_v, grad_k, grad_q, grad_in, grad_out)
    width = sum_q.shape[0]
    rows = 256
    spans = [pl.ds(r, rows) for r in range(0, width, rows)]
    copies = [
        pltpu.make_async_copy(mixed_in, mixed_out, copy_sem.at[0]),
        pltpu.make_async_copy(token_in, token_out, copy_sem.at[1]),
    ]
    loads = [
        [pltpu.make_async_copy(x.at[span], low.at[i, span], load_sem.at[i, j]) for j, span in enumerate(spans)]
        for i, x in enumerate(sources)
    ]
    stores = [
        [pltpu.make_async_copy(wide.at[i, span], x.at[span], store_sem.at[i, j]) for j, span in enumerate(spans)]
        for i, x in enumerate(targets)
    ]
    for i in range(8):
        for load in loads[i]:
            load.start()
    for copy in copies:
        copy.start()
    chunks = width // LANES
    gain_one[...] = jnp.concatenate([small[c : c + 1, :] for c in range(chunks)], 1).reshape(width)
    gain_two[...] = jnp.concatenate([small[8 + c : 9 + c, :] for c in range(chunks)], 1).reshape(width)
    for c in range(chunks):
        router_t[:, c * LANES : (c + 1) * LANES] = small[16 + c * experts : 16 + (c + 1) * experts, :]
    at = 16 + chunks * experts
    heads, buckets = table_t.shape
    table_t[...] = small[at : at + heads, :buckets]
    for i in range(4):
        for j, span in enumerate(spans):
            loads[i][j].wait()
            wide[i, span, :] = low[i, span, :].astype(f32)
            stores[i][j].start()
    for i in (4, 5):
        for j, span in enumerate(spans):
            loads[i][j].wait()
            loads[i + 2][j].wait()
            wide[i, span, :] = low[i, span, :].astype(f32) + low[i + 2, span, :].astype(f32)
            stores[i][j].start()
    for i in range(6):
        for store in stores[i]:
            store.wait()
    for copy in copies:
        copy.wait()


def finish(sums, keep, passed, mixed, token_grad, small, grid_shape, experts):
    f32, bf16 = jnp.float32, jnp.bfloat16
    width = sums[0].shape[0]
    vmem = pl.BlockSpec(memory_space=pltpu.VMEM)
    anywhere = pl.BlockSpec(memory_space=pl.ANY)
    shape = jax.ShapeDtypeStruct
    act = shape(mixed.shape, bf16)
    square, row = shape((width, width), f32), shape((width,), f32)
    blocks = width // 256
    return pl.pallas_call(
        functools.partial(finish_kernel, experts=experts),
        out_shape=(act, act, row, row, square, square, square, square, shape(grid_shape[::-1], f32),
                   shape((experts, width), f32), square, square),
        in_specs=[anywhere] * 8 + [vmem],
        out_specs=(anywhere,) * 2 + (vmem, vmem) + (anywhere,) * 4 + (vmem, vmem) + (anywhere,) * 2,
        scratch_shapes=[
            pltpu.VMEM((8, width, width), bf16), pltpu.VMEM((6, width, width), f32),
            pltpu.SemaphoreType.DMA((8, blocks)), pltpu.SemaphoreType.DMA((6, blocks)),
            pltpu.SemaphoreType.DMA((2,)),
        ],
        compiler_params=pltpu.CompilerParams(vmem_limit_bytes=63 << 20),
        cost_estimate=pl.CostEstimate(flops=0, bytes_accessed=30 << 20, transcendentals=0),
    )(*sums, keep, passed, mixed, token_grad, small)


def gelu_parts(v):
    mag = jnp.abs(v)
    t = 1.0 / (1.0 + (0.3275911 * 0.7071067811865476) * mag)
    poly = t * (0.127414796 + t * (-0.142248368 + t * (0.7107068705 + t * (-0.7265760135 + t * 0.5307027145))))
    gauss = jnp.exp(-0.5 * v * v)
    tail = poly * gauss
    phi = jnp.where(v < 0, tail, 1.0 - tail)
    return v * phi, phi + v * gauss * 0.3989422804014327


def flip_bits(index, mask, count):
    out = 0
    bit = 1
    while bit < count:
        a, b = (index // bit) % 2, (mask // bit) % 2
        out = out + bit * (a + b - 2 * a * b)
        bit *= 2
    return out


def ffn_kernel(
    xs, gs, g, win_hbm, wout_hbm,
    home, home_gate, produced, keep, give,
    win, wout, xr, gr, act, pg, gated, igs, ggs, dws, dwr, stage,
    wsem, own_sem, psem, ksem, xsend, xrecv, gsend, grecv, isend, irecv, qsend, qrecv, dsend, drecv,
    *, groups, dp_size, tiles,
):
    f32, bf16 = jnp.float32, jnp.bfloat16
    me = lax.axis_index("expert")
    dp = lax.axis_index("dp")
    core = dp % 2
    sibling = dp + 1 - 2 * core
    half_of = dp // 2
    rows = xs.shape[1]
    width = xs.shape[2]
    hidden = win.shape[1]
    tile = hidden // tiles
    lanes = gs.shape[2]

    def there(peer):
        return (dp, peer)

    load_in = pltpu.make_async_copy(win_hbm, win, wsem.at[0])
    load_out = pltpu.make_async_copy(wout_hbm, wout, wsem.at[1])
    load_in.start()
    load_out.start()
    load_g = pltpu.make_async_copy(g, gated, wsem.at[2])
    load_g.start()

    barrier = pltpu.get_barrier_semaphore()

    def greet(s, _):
        pl.semaphore_signal(
            barrier, inc=1, device_id=there(flip_bits(me, s, groups)), device_id_type=pl.DeviceIdType.MESH
        )
        return 0
    lax.fori_loop(1, groups, greet, 0)
    pl.semaphore_signal(barrier, inc=1, device_id=(sibling, me), device_id_type=pl.DeviceIdType.MESH)
    pl.semaphore_wait(barrier, groups)

    def x_copy(peer, slot):
        return pltpu.make_async_remote_copy(
            src_ref=xs.at[peer], dst_ref=xr.at[slot], send_sem=xsend.at[peer], recv_sem=xrecv.at[slot],
            device_id=there(peer), device_id_type=pl.DeviceIdType.MESH)

    def g_copy(peer, slot):
        return pltpu.make_async_remote_copy(
            src_ref=gs.at[peer], dst_ref=gr.at[slot], send_sem=gsend.at[peer], recv_sem=grecv.at[slot],
            device_id=there(peer), device_id_type=pl.DeviceIdType.MESH)

    def i_copy(peer, slot):
        return pltpu.make_async_remote_copy(
            src_ref=igs.at[peer], dst_ref=home.at[slot], send_sem=isend.at[peer], recv_sem=irecv.at[slot],
            device_id=there(peer), device_id_type=pl.DeviceIdType.MESH)

    def q_copy(peer, slot):
        return pltpu.make_async_remote_copy(
            src_ref=ggs.at[peer], dst_ref=home_gate.at[slot], send_sem=qsend.at[peer], recv_sem=qrecv.at[slot],
            device_id=there(peer), device_id_type=pl.DeviceIdType.MESH)

    def send(i, _):
        odd = (i - 1) % 2
        s = (1 - odd) * (groups - 1 - (i - 1) // 2) + odd * (i // 2)
        peer = flip_bits(me, s, groups)
        x_copy(peer, me).start()
        g_copy(peer, me).start()
        return 0
    lax.fori_loop(1, groups, send, 0)
    own_x = pltpu.make_async_copy(xs.at[me], xr.at[me], own_sem.at[0])
    own_g = pltpu.make_async_copy(gs.at[me], gr.at[me], own_sem.at[1])
    own_x.start()
    own_g.start()
    load_in.wait()
    load_out.wait()
    load_g.wait()

    spot = (
        lax.broadcasted_iota(jnp.int32, (rows, lanes), 0)
        == lax.broadcasted_iota(jnp.int32, (rows, lanes), 1)
    )

    def work(base):
        both = pl.ds(base, 2)
        x = xr[both].reshape(2 * rows, width)
        place = pl.ds(pl.multiple_of(base * rows, rows), 2 * rows)
        gg = gated[place, :]
        gate = jnp.concatenate(
            [jnp.sum(jnp.where(spot, gr[base + u, 0:1, :], 0.0), 1, keepdims=True) for u in range(2)], 0
        )
        gated[place, :] = (gate * gg.astype(f32)).astype(bf16)
        total = jnp.zeros((2 * rows, width), f32)
        gate_grad = jnp.zeros((2 * rows, 1), f32)

        def columns(t):
            return slice(t * tile, (t + 1) * tile)

        def products(t):
            return matmul(x, win[:, columns(t)]), matmul_nt(gg, wout[columns(t), :])

        ahead = products(0)
        for t in range(tiles):
            pre, out_grad = ahead
            if t + 1 < tiles:
                ahead = products(t + 1)
            value, slope = gelu_parts(pre)
            act[place, columns(t)] = value.astype(bf16)
            gate_grad = gate_grad + jnp.sum(value * out_grad, 1, keepdims=True)
            low = (gate * out_grad * slope).astype(bf16)
            pg[place, columns(t)] = low
            total = total + matmul_nt(low, win[:, columns(t)])
        igs[both] = total.astype(bf16).reshape(2, rows, width)
        for u in range(2):
            row = jnp.sum(jnp.where(spot, gate_grad[u * rows : (u + 1) * rows], 0.0), 0, keepdims=True)
            ggs[base + u] = jnp.broadcast_to(row, ggs.shape[1:])

    def arrive(peer):
        x_copy(peer, peer).wait_recv()
        g_copy(peer, peer).wait_recv()

    def back(peer):
        i_copy(peer, me).start()
        q_copy(peer, me).start()

    own_x.wait()
    own_g.wait()
    arrive(flip_bits(me, 1, groups))
    work(me - me % 2)
    own_i = pltpu.make_async_copy(igs.at[me], home.at[me], own_sem.at[0])
    own_q = pltpu.make_async_copy(ggs.at[me], home_gate.at[me], own_sem.at[1])
    own_i.start()
    own_q.start()
    back(flip_bits(me, 1, groups))

    def chunk(j, _):
        peer = flip_bits(me, 2 * j, groups)
        other = flip_bits(me, 2 * j + 1, groups)
        arrive(peer)
        arrive(other)
        work(peer - peer % 2)
        back(peer)
        back(other)
        return 0
    lax.fori_loop(1, groups // 2, chunk, 0)

    def d_copy(k):
        return pltpu.make_async_remote_copy(
            src_ref=dws.at[k % 2], dst_ref=dwr.at[k], send_sem=dsend.at[k], recv_sem=drecv.at[k],
            device_id=(sibling, me), device_id_type=pl.DeviceIdType.MESH)

    part = hidden // dp_size
    flat = groups * rows
    items = [(which, half) for half in (1 - half_of, half_of) for which in range(2)]

    def grad(which, quarter):
        span = pl.ds(pl.multiple_of(quarter * part, part), part)
        if which == 0:
            return matmul_tn(xr[...].reshape(flat, width), pg[:, span])
        return matmul_tn(act[:, span], gated[...])

    for k, (which, half) in enumerate(items):
        if k >= 2:
            d_copy(k - 2).wait_send()
        dws[k % 2] = grad(which, 2 * half + 1 - core).astype(bf16)
        d_copy(k).start()
    outs = [
        pltpu.make_async_copy(dwr.at[0], give.at[0], ksem.at[0]),
        pltpu.make_async_copy(dwr.at[1], give.at[1], ksem.at[1]),
        pltpu.make_async_copy(dwr.at[2], keep.at[0], ksem.at[2]),
        pltpu.make_async_copy(dwr.at[3], keep.at[1], ksem.at[3]),
    ]
    for k, (which, half) in enumerate(items):
        local = grad(which, 2 * half + core)
        d_copy(k).wait_recv()
        dwr[k] = (local + dwr[k].astype(f32)).astype(bf16)
        outs[k].start()

    span = stage.shape[1]
    copies = []
    for b in range(flat // span):
        if b >= 2:
            copies[b - 2].wait()
        stage[b % 2] = matmul(act[b * span : (b + 1) * span, :], wout[...]).astype(bf16)
        copy = pltpu.make_async_copy(stage.at[b % 2], produced.at[pl.ds(b * span, span)], psem.at[b % 2])
        copy.start()
        copies.append(copy)
    for copy in copies[-2:] + outs:
        copy.wait()
    own_i.wait()
    own_q.wait()
    for k in (2, 3):
        d_copy(k).wait_send()

    def finish(s, _):
        peer = flip_bits(me, s, groups)
        x_copy(peer, me).wait_send()
        g_copy(peer, me).wait_send()
        i_copy(peer, me).wait_send()
        q_copy(peer, me).wait_send()
        i_copy(peer, peer).wait_recv()
        q_copy(peer, peer).wait_recv()
        return 0
    lax.fori_loop(1, groups, finish, 0)


def ffn(xs, gs, g, weight_in, weight_out, groups, dp_size, tiles=6):
    f32, bf16 = jnp.float32, jnp.bfloat16
    _, rows, width = xs.shape
    hidden = weight_in.shape[1]
    lanes = gs.shape[2]
    part = hidden // dp_size
    anywhere = pl.BlockSpec(memory_space=pl.ANY)
    sem = pltpu.SemaphoreType.DMA
    flat = groups * rows
    shape = jax.ShapeDtypeStruct
    return pl.pallas_call(
        functools.partial(ffn_kernel, groups=groups, dp_size=dp_size, tiles=tiles),
        out_shape=(
            shape((groups, rows, width), bf16),
            shape((groups, 8, lanes), f32),
            shape((flat, width), bf16),
            shape((2, width, part), bf16),
            shape((2, width, part), bf16),
        ),
        in_specs=[anywhere] * 5,
        out_specs=(anywhere,) * 5,
        scratch_shapes=[
            pltpu.VMEM((width, hidden), bf16),
            pltpu.VMEM((hidden, width), bf16),
            pltpu.VMEM((groups, rows, width), bf16),
            pltpu.VMEM((groups, 8, lanes), f32),
            pltpu.VMEM((flat, hidden), bf16),
            pltpu.VMEM((flat, hidden), bf16),
            pltpu.VMEM((flat, width), bf16),
            pltpu.VMEM((groups, rows, width), bf16),
            pltpu.VMEM((groups, 8, lanes), f32),
            pltpu.VMEM((2, width, part), bf16),
            pltpu.VMEM((4, width, part), bf16),
            pltpu.VMEM((2, flat // 8, width), bf16),
            sem((3,)), sem((2,)), sem((2,)), sem((4,)),
            sem((groups,)), sem((groups,)), sem((groups,)), sem((groups,)),
            sem((groups,)), sem((groups,)), sem((groups,)), sem((groups,)),
            sem((4,)), sem((4,)),
        ],
        compiler_params=pltpu.CompilerParams(
            collective_id=1, has_side_effects=True, vmem_limit_bytes=62 << 20
        ),
        cost_estimate=pl.CostEstimate(
            flops=12 * flat * width * hidden, bytes_accessed=40 << 20, transcendentals=flat * hidden
        ),
    )(xs, gs, g, weight_in, weight_out)


def fold_steps(rows, cols, bits):
    steps = []
    for bit in bits[:3]:
        rows = rows // 2
        steps.append(((bit,), "half", rows, cols))
    rows, cols = rows // 2, cols // 2
    steps.append((tuple(bits[3:5]), "quad", rows, cols))
    for bit in bits[5:]:
        steps.append(((bit,), "whole", rows, cols))
    return steps


def reduce_kernel(
    attended_hbm, middle_grad_hbm, tokens_hbm, dv_hbm, dk_hbm, dq_hbm, wq_hbm, wk_hbm, wv_hbm, returned_hbm, middle_hbm,
    gain, small_in, slot_ref, routes_ref, probs_ref,
    sum_o, sum_v, sum_k, sum_q, token_grad_hbm, small_out, mixed_hbm,
    attended, middle_grad, tokens, dv, dk, dq, wq, wk, wv, returned, middle,
    token_grad, mixed, sums, normed, branch, acc, outbox, inbox, small_box, small_sent, load_sem, store_sem,
    ssend, srecv, tsend, trecv,
    *, dp_bits, expert_bits,
):
    f32, bf16 = jnp.float32, jnp.bfloat16
    dp = lax.axis_index("dp")
    ex = lax.axis_index("expert")
    MESH = pl.DeviceIdType.MESH
    length, width = tokens.shape
    held = (attended, middle_grad, tokens, dv, dk, dq, wq, wk, wv, returned, middle)
    loads = [
        pltpu.make_async_copy(there, here, load_sem.at[i])
        for i, (there, here) in enumerate(zip(
            (attended_hbm, middle_grad_hbm, tokens_hbm, dv_hbm, dk_hbm, dq_hbm, wq_hbm, wk_hbm, wv_hbm,
             returned_hbm, middle_hbm), held))
    ]
    first = 4
    for load in loads[:first]:
        load.start()

    def own_bit(bit):
        axis, place = bit
        return (dp // 2 ** place) % 2 if axis == "dp" else (ex // 2 ** place) % 2

    def partner(bits):
        there = [dp, ex]
        for bit in bits:
            there[bit[0] == "expert"] = there[bit[0] == "expert"] + (1 - 2 * own_bit(bit)) * 2 ** bit[1]
        return tuple(there)

    dpb = [("dp", i) for i in range(dp_bits)]
    exb = [("expert", i) for i in range(expert_bits)]
    orders = [
        [dpb[0], dpb[1], exb[0]] + dpb[2:] + exb[1:],
        [dpb[0], exb[0], dpb[1]] + dpb[2:] + exb[1:],
    ]
    every = dpb + exb
    small_count = len(every)

    barrier = pltpu.get_barrier_semaphore()
    greeted = [(bit,) for bit in every] + [tuple(orders[0][3:5])]
    for bits in greeted:
        pl.semaphore_signal(barrier, inc=1, device_id=partner(bits), device_id_type=MESH)
    pl.semaphore_wait(barrier, len(greeted))

    def prepare(i, _):
        span = pl.ds(pl.multiple_of(i * 256, 256), 256)
        x = tokens[span, :].astype(f32)
        inv = lax.rsqrt(jnp.mean(x * x, 1, keepdims=True) + epsilon)
        normed[span, :] = (x * inv * gain[...]).astype(bf16)
        branch[span, :] = middle_grad[span, :].astype(bf16)
        return 0
    for load in loads[:3]:
        load.wait()
    for load in loads[first:]:
        load.start()
    lax.fori_loop(0, length // 256, prepare, 0)

    lefts = (attended, normed, normed, normed)
    rights = (branch, dv, dk, dq)
    streams = []
    for s in range(4):
        row, col, at, sem_at = 0, 0, 0, 0
        plan = []
        for bits, kind, r, c in fold_steps(width, width, orders[s % 2]):
            mine = [own_bit(bit) for bit in bits]
            if kind == "half":
                peers = [bits]
                keep_at = (row + mine[0] * r, col)
                theirs = [(row + (1 - mine[0]) * r, col)]
            elif kind == "quad":
                peers = [bits[:1], bits[1:], bits]
                keep_at = (row + mine[0] * r, col + mine[1] * c)
                theirs = [
                    (row + (1 - mine[0]) * r, col + mine[1] * c),
                    (row + mine[0] * r, col + (1 - mine[1]) * c),
                    (row + (1 - mine[0]) * r, col + (1 - mine[1]) * c),
                ]
            else:
                peers, keep_at, theirs = [bits], (row, col), [(row, col)]
            plan.append((peers, kind, r, c, at, keep_at, theirs, sem_at))
            row, col = keep_at
            at += r * len(peers)
            sem_at += len(peers)
        streams.append(plan)
    count = len(streams[0])
    sems = ssend.shape[1] // 2

    def rs_copy(s, k, i):
        peers, kind, r, c, at, _, _, sem_at = streams[s][k]
        box = pl.ds(at + i * r, r)
        return pltpu.make_async_remote_copy(
            src_ref=outbox.at[s, box, pl.ds(0, c)], dst_ref=inbox.at[s, box, pl.ds(0, c)],
            send_sem=ssend.at[s, sem_at + i], recv_sem=srecv.at[s, sem_at + i],
            device_id=partner(peers[i]), device_id_type=MESH)

    def aligned(at):
        row, col = at
        row = pl.multiple_of(row, 16) if not isinstance(row, int) else row
        col = pl.multiple_of(col, 128) if not isinstance(col, int) else col
        return row, col

    def block(s, at, r, c):
        row, col = aligned(at)
        return sums.at[s, pl.ds(row, r), pl.ds(col, c)]

    def ag_copy(s, k, i, incoming):
        peers, kind, r, c, _, keep_at, theirs, sem_at = streams[s][k]
        ref = block(s, theirs[i] if incoming else keep_at, r, c)
        return pltpu.make_async_remote_copy(
            src_ref=ref, dst_ref=ref,
            send_sem=ssend.at[s, sems + sem_at + i], recv_sem=srecv.at[s, sems + sem_at + i],
            device_id=partner(peers[i]), device_id_type=MESH)

    half = width // 2
    core = own_bit(dpb[0])

    def grad(s, which):
        span = pl.ds(pl.multiple_of(which * half, half), half)
        return matmul_tn(lefts[s][:, span], rights[s][...])

    def local(s, at, r, c):
        row, col = aligned((at[0] - streams[s][0][5][0], at[1]))
        return acc.at[s, pl.ds(row, r), pl.ds(col, c)]

    def phase(s, k):
        plan = streams[s]
        if k == 0:
            if s > 0:
                loads[2 + s].wait()
            outbox[s, 0:half, :] = grad(s, 1 - core).astype(bf16)
            rs_copy(s, 0, 0).start()
            return
        if k <= count:
            peers, kind, r, c, at, keep_at, _, _ = plan[k - 1]
            view = local(s, keep_at, r, c)
            total = outbox[s, at : at + r, 0:c].astype(f32) if kind == "whole" else view[...]
            for i in range(len(peers)):
                rs_copy(s, k - 1, i).wait_recv()
                total = total + inbox[s, at + i * r : at + (i + 1) * r, 0:c].astype(f32)
            if k < count:
                view[...] = total
                peers, kind, r, c, at, _, theirs, _ = plan[k]
                for i in range(len(peers)):
                    outbox[s, at + i * r : at + (i + 1) * r, 0:c] = local(s, theirs[i], r, c)[...].astype(bf16)
                    rs_copy(s, k, i).start()
                return
            block(s, keep_at, r, c)[...] = total.astype(bf16)
        g = 2 * count - 1 - k
        if k > count and plan[g + 1][1] != "whole":
            for i in range(len(plan[g + 1][0])):
                ag_copy(s, g + 1, i, True).wait_recv()
        if g >= 0 and plan[g][1] != "whole":
            for i in range(len(plan[g][0])):
                ag_copy(s, g, i, False).start()

    gain_row = gain[...]
    rows = 256

    def norm_block(i, gain_grad):
        span = pl.ds(pl.multiple_of(i * rows, rows), rows)
        grads = (
            matmul_nt(dq[span, :], wq[...]) + matmul_nt(dk[span, :], wk[...]) + matmul_nt(dv[span, :], wv[...])
        )
        x = tokens[span, :].astype(f32)
        inv = lax.rsqrt(jnp.mean(x * x, 1, keepdims=True) + epsilon)
        scaled = grads * gain_row
        mean = jnp.sum(scaled * x, 1, keepdims=True) * (1.0 / width)
        part = inv * (scaled - x * (inv * inv * mean))
        token_grad[span, :] = (middle_grad[span, :] + part).astype(bf16)
        return gain_grad + jnp.sum(grads * (x * inv), 0, keepdims=True)

    slots = returned.shape[0]
    routes = routes_ref[...]
    pad = probs_ref.shape[0]
    hot = lax.broadcasted_iota(jnp.int32, (pad, length), 0) == routes
    gate_row = jnp.sum(jnp.where(hot, probs_ref[...], 0.0), 0, keepdims=True)

    def mix(c):
        at = slice(c, c + BLOCK)
        column = jnp.broadcast_to(slot_ref[0:1, at].astype(f32), (BLOCK, BLOCK)).T
        first = lax.broadcasted_iota(jnp.int32, (BLOCK, LANES), 1).astype(f32)
        spread = jnp.concatenate(
            [(column == first + float(s)).astype(f32).astype(bf16) for s in range(0, slots, LANES)], 1)
        rows_back = dot_nn(spread, returned[...])
        gate = jnp.broadcast_to(gate_row[:, at], (BLOCK, BLOCK)).T
        gate = jnp.concatenate([gate] * (width // LANES), 1)
        mixed[at, :] = (middle[at, :] + gate * rows_back).astype(bf16)

    def small_copy(k):
        return pltpu.make_async_remote_copy(
            src_ref=small_sent.at[k], dst_ref=small_box.at[k],
            send_sem=tsend.at[k], recv_sem=trecv.at[k],
            device_id=partner((every[k],)), device_id_type=MESH)

    def small_phase(k):
        if k == 0:
            gain_grad = lax.fori_loop(0, length // rows, norm_block, jnp.zeros((1, width), f32))
            small_out[...] = small_in[...]
            for i in range(width // LANES):
                small_out[i : i + 1, :] = gain_grad[:, i * LANES : (i + 1) * LANES]
        else:
            small_copy(k - 1).wait_recv()
            small_out[...] = small_out[...] + small_box[k - 1]
        if k < small_count:
            small_sent[k] = small_out[...]
            small_copy(k).start()

    last = 2 * count
    starts = (0, 0, 2, 2)
    stores = [
        pltpu.make_async_copy(sums.at[s], out, store_sem.at[s]) for s, out in enumerate((sum_o, sum_v, sum_k, sum_q))
    ]
    stores.append(pltpu.make_async_copy(token_grad, token_grad_hbm, store_sem.at[4]))
    stores.append(pltpu.make_async_copy(mixed, mixed_hbm, store_sem.at[5]))
    mixes = length // BLOCK
    turns = (1, 1, 4, 5, 6, 6, 8, 8)
    for t in range(max(last + starts[-1], small_count + 3, turns[-1]) + 1):
        for s in range(4):
            if 0 <= t - starts[s] <= last:
                phase(s, t - starts[s])
                if t - starts[s] == last:
                    stores[s].start()
        for s in range(4):
            if t == starts[s]:
                acc[s] = grad(s, core)
        if t == 3:
            for load in loads[6:9]:
                load.wait()
        if 0 <= t - 3 <= small_count:
            small_phase(t - 3)
            if t == 3:
                stores[4].start()
        if t == 1:
            for load in loads[9:]:
                load.wait()
        for c in range(mixes):
            if t == turns[c * len(turns) // mixes]:
                mix(c * BLOCK)
                if c == mixes - 1:
                    stores[5].start()
    for store in stores:
        store.wait()
    for s in range(4):
        for k in range(count):
            for i in range(len(streams[s][k][0])):
                rs_copy(s, k, i).wait_send()
                if streams[s][k][1] != "whole":
                    ag_copy(s, k, i, False).wait_send()
    for k in range(small_count):
        small_copy(k).wait_send()


def reduce_grads(tokens, attended, middle_grad, dq, dk, dv, wq, wk, wv, gain, small,
                 returned, slot, routes_row, probs, middle, dp_size, groups):
    f32, bf16 = jnp.float32, jnp.bfloat16
    length, width = tokens.shape
    dp_bits, expert_bits = dp_size.bit_length() - 1, groups.bit_length() - 1
    count = dp_bits + expert_bits
    steps = fold_steps(width, width, list(range(count)))
    box = sum(step[2] * (3 if step[1] == "quad" else 1) for step in steps)
    messages = sum(3 if step[1] == "quad" else 1 for step in steps)
    vmem = pl.BlockSpec(memory_space=pltpu.VMEM)
    anywhere = pl.BlockSpec(memory_space=pl.ANY)
    sem = pltpu.SemaphoreType.DMA
    shape = jax.ShapeDtypeStruct
    act, square = shape((length, width), bf16), shape((width, width), bf16)
    big = (attended, middle_grad, tokens, dv, dk, dq, wq, wk, wv, returned, middle)
    return pl.pallas_call(
        functools.partial(reduce_kernel, dp_bits=dp_bits, expert_bits=expert_bits),
        out_shape=(square, square, square, square, act, shape(small.shape, f32), act),
        in_specs=[anywhere] * len(big) + [vmem] * 5,
        out_specs=(anywhere,) * 5 + (vmem, anywhere),
        scratch_shapes=[pltpu.VMEM(x.shape, x.dtype) for x in big] + [
            pltpu.VMEM((length, width), bf16),
            pltpu.VMEM((length, width), bf16),
            pltpu.VMEM((4, width, width), bf16),
            pltpu.VMEM((length, width), bf16),
            pltpu.VMEM((length, width), bf16),
            pltpu.VMEM((4, width // 2, width), f32),
            pltpu.VMEM((4, box, width), bf16),
            pltpu.VMEM((4, box, width), bf16),
            pltpu.VMEM((count,) + small.shape, f32),
            pltpu.VMEM((count,) + small.shape, f32),
            sem((len(big),)), sem((6,)),
            sem((4, 2 * messages)), sem((4, 2 * messages)), sem((count,)), sem((count,)),
        ],
        compiler_params=pltpu.CompilerParams(
            collective_id=2, has_side_effects=True, vmem_limit_bytes=62 << 20
        ),
        cost_estimate=pl.CostEstimate(
            flops=14 * length * width * width, bytes_accessed=30 << 20, transcendentals=0
        ),
    )(*big, gain, small, slot, routes_row, probs)


def key_ranges(segment_row):
    first, last = segment_row[::BLOCK], segment_row[BLOCK - 1 :: BLOCK]
    lo = jnp.sum(segment_row[None, :] < first[:, None], 1) // BLOCK
    hi = (jnp.sum(segment_row[None, :] <= last[:, None], 1) + BLOCK - 1) // BLOCK
    return lo.astype(jnp.int32), hi.astype(jnp.int32)


def per_device(
    tokens,
    segments,
    routes,
    cotangent,
    attn_gain,
    ffn_gain,
    query_weight,
    key_weight,
    value_weight,
    output_weight,
    position_bias_grid,
    router_weight,
    expert_in,
    expert_out,
):
    f32, bf16 = jnp.float32, jnp.bfloat16
    token_count, model_width = tokens.shape
    head_count = position_bias_grid.shape[1]
    score_scale = (model_width // head_count) ** (-0.5)
    experts_all = router_weight.shape[1]
    capacity = (5 * token_count + 4 * experts_all - 1) // (4 * experts_all)
    slot_rows = (capacity + 15) // 16 * 16
    slots = experts_all * slot_rows
    groups = lax.axis_size("expert")
    dp_size = lax.axis_size("dp")

    def exchange(rows):
        return lax.all_to_all(rows, "expert", split_axis=0, concat_axis=0, tiled=True)

    routes_row = routes.reshape(1, token_count)
    token_slot, grad_slots = first_slots(routes_row, cotangent, experts_all, capacity, slot_rows)
    grad_arrived = exchange(grad_slots)
    lo, hi = key_ranges(segments[0])
    router_pad = max(experts_all, 16)
    router_t = jnp.pad(router_weight.T, ((0, router_pad - experts_all), (0, 0)))
    gain_one, gain_two = attn_gain[None, :], ffn_gain[None, :]
    queries, key_rows, keys_t, value_rows, attended, log_sums, middle, router_probs, sent, gate_slots = front(
        lo, hi, tokens, segments, token_slot, routes_row, gain_one, gain_two,
        query_weight, key_weight, value_weight, output_weight, position_bias_grid, router_t,
        experts_all, slot_rows, score_scale,
    )
    home_grad, home_gate, produced, keep, give = ffn(
        sent, gate_slots, grad_arrived.reshape(slots, model_width), expert_in[0], expert_out[0], groups, dp_size,
    )
    passed = lax.ppermute(give, "dp", [(i, (i + dp_size // 2) % dp_size) for i in range(dp_size)])
    returned = exchange(produced.reshape(experts_all, slot_rows, model_width)).reshape(slots, model_width)
    query_grad, key_grad, value_grad, middle_grad, small = back(
        lo, hi, home_grad, home_gate, token_slot, routes_row, router_probs, middle, cotangent, segments, gain_two,
        output_weight, router_t, position_bias_grid, queries, key_rows, keys_t, value_rows, log_sums, attended,
        experts_all, slot_rows, score_scale,
    )
    sum_o, sum_v, sum_k, sum_q, token_grad, small, mixed = reduce_grads(
        tokens, attended, middle_grad, query_grad, key_grad, value_grad,
        query_weight, key_weight, value_weight, gain_one, small,
        returned, token_slot, routes_row, router_probs, middle, dp_size, groups,
    )
    (mixed, token_grad, attn_gain_grad, ffn_gain_grad, grad_q, grad_k, grad_v, grad_o, table_grad, router_grad,
     grad_in, grad_out) = finish(
        (sum_q, sum_k, sum_v, sum_o), keep, passed, mixed, token_grad, small, position_bias_grid.shape, experts_all
    )
    return (
        mixed,
        token_grad,
        attn_gain_grad,
        ffn_gain_grad,
        grad_q,
        grad_k,
        grad_v,
        grad_o,
        table_grad.T,
        router_grad.T,
        grad_in[None],
        grad_out[None],
    )


def solution(mesh):
    rows = P(("dp", "expert"), None)
    return jax.shard_map(
        per_device,
        mesh=mesh,
        in_specs=(rows,) * 4 + (P(),) * 8 + (P("expert", None, None),) * 2,
        out_specs=(rows,) * 2 + (P(),) * 8 + (P("expert", None, "dp"), P("expert", "dp", None)),
        check_vma=False,
    )
```

```python
import functools

import jax
import jax.numpy as jnp
from jax import lax
from jax.experimental import pallas as pl
from jax.experimental.pallas import tpu as pltpu
from jax.sharding import PartitionSpec as P

epsilon = 1e-06
precise_setting = lax.Precision.HIGHEST
def matmul(left, right):
    return jnp.dot(left, right, preferred_element_type=jnp.float32)


def matmul_tn(left, right):
    return lax.dot_general(left, right, (((0,), (0,)), ((), ())), preferred_element_type=jnp.float32)


def matmul_nt(left, right):
    return lax.dot_general(left, right, (((1,), (1,)), ((), ())), preferred_element_type=jnp.float32)


bucket_bounds = (12, 16, 23, 32, 46, 64, 91)
masked_score = -1e30
LANES = 128
BLOCK = 128
NEAR = 5
UF = 6
UB = 6


def bucket_of(relative):
    distance = jnp.abs(relative)
    beyond = jnp.zeros_like(distance)
    for threshold in bucket_bounds:
        beyond = beyond + (distance >= threshold).astype(jnp.int32)
    inside = jnp.where(distance < 8, distance, 8 + beyond)
    return inside + 16 * (relative > 0).astype(jnp.int32)


def dot_nt(a, b):
    return lax.dot_general(a, b, (((1,), (1,)), ((), ())), preferred_element_type=jnp.float32)


def dot_nn(a, b):
    return lax.dot_general(a, b, (((1,), (0,)), ((), ())), preferred_element_type=jnp.float32)


def split3(x):
    a = x.astype(jnp.bfloat16)
    r = x - a.astype(jnp.float32)
    b = r.astype(jnp.bfloat16)
    c = (r - b.astype(jnp.float32)).astype(jnp.bfloat16)
    return a, b, c


def fill_bias(diag_ref, bias, pairs):
    for p in range(pairs):
        for d in range(NEAR):
            tiles = []
            for h in (2 * p, 2 * p + 1):
                row = diag_ref[h : h + 1, :]
                if d in (0, NEAR - 1):
                    col = row[:, 511:512] if d == 0 else row[:, 0:1]
                    tiles.append(jnp.broadcast_to(col, (BLOCK, BLOCK)))
                else:
                    base = (3 - d) * BLOCK
                    wide = jnp.broadcast_to(row[:, base : base + 2 * BLOCK], (BLOCK, 2 * BLOCK))
                    tiles.append(pltpu.roll(wide, BLOCK, 1, stride=1, stride_axis=0)[:, :BLOCK])
            bias[p, d] = jnp.concatenate(tiles, 1)


def heads_apart(block, low, extra=None):
    zero = jnp.zeros_like(block)
    first, second = jnp.where(low, block, zero), jnp.where(low, zero, block)
    if extra is not None:
        first, second = jnp.concatenate([first, extra], 1), jnp.concatenate([second, extra], 1)
    return jnp.concatenate([first, second], 0)


def by_count(lo, hi, most, body):
    for n in range(1, most + 1):
        pl.when(hi - lo == n)(functools.partial(body, n))


def own_heads(wide):
    return jnp.concatenate([wide[:64, :LANES], wide[64:128, LANES:]], 0)


def attend(lo_ref, hi_ref, q_ref, k_ref, vt_ref, qm_ref, km_ref, bias, o_ref, lse_ref):
    pairs = q_ref.shape[1] // LANES
    length = q_ref.shape[0]
    nblk = length // BLOCK
    f32, bf16 = jnp.float32, jnp.bfloat16
    low = lax.broadcasted_iota(jnp.int32, (1, LANES), 1) < 64

    def q_block(i, _):
        lo, hi = lo_ref[i], hi_ref[i]
        rows = pl.ds(pl.multiple_of(i * BLOCK, BLOCK), BLOCK)
        start = pl.multiple_of(lo * BLOCK, BLOCK)
        qm = qm_ref[rows, :]

        def body(n):
            span = pl.ds(start, n * BLOCK)
            km = km_ref[span, :]

            def lanes_of(p):
                return pl.ds(pl.multiple_of(p * LANES, LANES), LANES)

            def scores(p):
                qs = heads_apart(q_ref[rows, lanes_of(p)], low, qm)
                return dot_nt(jnp.concatenate([k_ref[span, lanes_of(p)], km], 1), qs)

            def soften(p, st):
                parts = []
                top = None
                for b in range(n):
                    d = jnp.clip(lo + b - i, -2, 2) + 2
                    s = st[b * BLOCK : (b + 1) * BLOCK] + bias[p, d]
                    parts.append(s)
                    top = s if top is None else jnp.maximum(top, s)
                top = jnp.max(top, 0, keepdims=True)
                return jnp.concatenate([jnp.exp(s - top).astype(bf16) for s in parts], 0), top

            def mix(p, probs):
                values = jnp.concatenate([vt_ref[lanes_of(p), span], jnp.ones((16, n * BLOCK), bf16)], 0)
                return dot_nn(values, probs)

            def finish(p, acc, top):
                total = acc[LANES : LANES + 1]
                inv = 1.0 / total
                ot = own_heads(acc)
                ot = jnp.concatenate([ot[:64] * inv[:, :LANES], ot[64:] * inv[:, LANES:]], 0)
                o_ref[rows, lanes_of(p)] = ot.T.astype(bf16)
                lse_ref[i, pl.ds(p, 1), :] = top + jnp.log(total)

            def some(g, _):
                ps = [g * UF + u for u in range(UF)]
                sts = [scores(p) for p in ps]
                soft = [soften(p, st) for p, st in zip(ps, sts)]
                accs = [mix(p, x[0]) for p, x in zip(ps, soft)]
                for p, acc, x in zip(ps, accs, soft):
                    finish(p, acc, x[1])
                return 0
            lax.fori_loop(0, pairs // UF, some, 0)

        by_count(lo, hi, nblk, body)
        return 0
    lax.fori_loop(0, nblk, q_block, 0)


def attend_back(
    lo_ref, hi_ref, q_ref, k_ref, kt_ref, v_ref, lse_ref, do_ref, o_ref, qm_ref, km_ref, bias,
    dq_ref, dk_ref, dv_ref, gsum_ref, gacc, dkacc, dvacc, scale,
):
    length, width = q_ref.shape
    pairs = width // LANES
    nblk = length // BLOCK
    f32, bf16 = jnp.float32, jnp.bfloat16
    low = lax.broadcasted_iota(jnp.int32, (1, LANES), 1) < 64
    pick = (
        lax.broadcasted_iota(jnp.int32, (16, LANES), 0) == lax.broadcasted_iota(jnp.int32, (16, LANES), 1) // 64
    ).astype(f32).astype(bf16)
    gacc[...] = jnp.zeros_like(gacc)
    gsum_ref[...] = jnp.zeros_like(gsum_ref)
    dkacc[...] = jnp.zeros_like(dkacc)
    dvacc[...] = jnp.zeros_like(dvacc)

    def q_block(i, _):
        lo, hi = lo_ref[i], hi_ref[i]
        rows = pl.ds(pl.multiple_of(i * BLOCK, BLOCK), BLOCK)
        start = pl.multiple_of(lo * BLOCK, BLOCK)
        qm = qm_ref[rows, :]

        def body(n):
            span = pl.ds(start, n * BLOCK)
            km = km_ref[span, :]

            def lanes_of(p):
                return pl.ds(pl.multiple_of(p * LANES, LANES), LANES)

            def products(p):
                cols = lanes_of(p)
                qs = heads_apart(q_ref[rows, cols], low, qm)
                dd = do_ref[rows, cols]
                dos = heads_apart(dd, low)
                prod = dd.astype(f32) * o_ref[rows, cols].astype(f32)
                prod_hi = prod.astype(bf16)
                prod_lo = (prod - prod_hi.astype(f32)).astype(bf16)
                inner = dot_nt(pick, prod_hi) + dot_nt(pick, prod_lo)
                inner = jnp.concatenate([inner[0:1], inner[1:2]], 1)
                st = dot_nt(jnp.concatenate([k_ref[span, cols], km], 1), qs)
                dpt = dot_nt(v_ref[span, cols], dos)
                return qs, dos, inner, st, dpt

            def pointwise(p, inner, st, dpt):
                lse = lse_ref[i, pl.ds(p, 1), :]
                probs, grads = [], []
                for b in range(n):
                    d = jnp.clip(lo + b - i, -2, 2) + 2
                    part = slice(b * BLOCK, (b + 1) * BLOCK)
                    prob = jnp.exp(st[part] + bias[p, d] - lse)
                    grad = prob * (dpt[part] - inner)
                    gacc[p, d] += grad
                    probs.append(prob.astype(bf16))
                    grads.append(grad.astype(bf16))
                return jnp.concatenate(probs, 0), jnp.concatenate(grads, 0)

            def back(p, qs, dos, probs, grads):
                cols = lanes_of(p)
                return (
                    dot_nn(probs, dos), dot_nn(grads, qs[:, :LANES]), dot_nn(kt_ref[cols, span], grads)
                )

            def finish(p, dv, dk, dqt):
                cols = lanes_of(p)
                dvacc[span, cols] += dv
                dkacc[span, cols] += dk
                dq_ref[rows, cols] = (own_heads(dqt).T * scale).astype(bf16)

            def some(g, _):
                ps = [g * UB + u for u in range(UB)]
                first = [products(p) for p in ps]
                points = [pointwise(p, *x[2:]) for p, x in zip(ps, first)]
                last = [back(p, *x[:2], *y) for p, x, y in zip(ps, first, points)]
                for p, x in zip(ps, last):
                    finish(p, *x)
                return 0
            lax.fori_loop(0, pairs // UB, some, 0)

        by_count(lo, hi, nblk, body)
        return 0
    lax.fori_loop(0, nblk, q_block, 0)
    dk_ref[...] = dkacc[...].astype(bf16)
    dv_ref[...] = dvacc[...].astype(bf16)
    turn = (
        lax.broadcasted_iota(jnp.int32, (BLOCK, BLOCK), 0) + lax.broadcasted_iota(jnp.int32, (BLOCK, BLOCK), 1)
        == BLOCK - 1
    ).astype(f32).astype(bf16)
    for p in range(pairs):
        for d in range(NEAR):
            t = gacc[p, d]
            if 0 < d < NEAR - 1:
                hi = t.astype(bf16)
                t = dot_nn(turn, hi) + dot_nn(turn, (t - hi.astype(f32)).astype(bf16))
            for u in range(2):
                s = jnp.concatenate([t[:, u * LANES : (u + 1) * LANES], jnp.zeros((BLOCK, LANES), f32)], 1)
                if 0 < d < NEAR - 1:
                    s = pltpu.roll(s, 0, 1, stride=1, stride_axis=0)
                at = d * 16 + 2 * p + u
                gsum_ref[at : at + 1, :] = jnp.sum(s, 0, keepdims=True)


def two(x):
    a = x.astype(jnp.bfloat16)
    return a, (x - a.astype(jnp.float32)).astype(jnp.bfloat16)


def row_pieces(row):
    place = lax.broadcasted_iota(jnp.int32, (16, row.shape[1]), 0)
    a, b, c = [x.astype(jnp.float32) for x in split3(row)]
    return jnp.where(place == 0, a, jnp.where(place == 1, b, jnp.where(place == 2, c, 0.0))).astype(jnp.bfloat16)


def each(count, body):
    if count <= 8:
        for e in range(count):
            body(e)
    else:
        def step(e, _):
            body(e)
            return 0
        lax.fori_loop(0, count, step, 0)


def slot_hot(slot_row, e, slot_rows):
    place = lax.broadcasted_iota(jnp.int32, (slot_rows, slot_row.shape[1]), 0) + e * slot_rows
    return (place == slot_row).astype(jnp.float32).astype(jnp.bfloat16)


def slots_kernel(routes_ref, rows_ref, slot_ref, out_ref, *, experts, capacity, slot_rows):
    f32, bf16 = jnp.float32, jnp.bfloat16
    tokens = routes_ref.shape[1]
    routes = routes_ref[...]
    pad = max(experts, 16)
    hot = (lax.broadcasted_iota(jnp.int32, (pad, tokens), 0) == routes).astype(f32)
    earlier = (
        lax.broadcasted_iota(jnp.int32, (BLOCK, BLOCK), 0) < lax.broadcasted_iota(jnp.int32, (BLOCK, BLOCK), 1)
    ).astype(f32).astype(bf16)
    seen = jnp.zeros((pad, 1), f32)
    ranks = []
    for c in range(0, tokens, BLOCK):
        part = hot[:, c : c + BLOCK]
        ranks.append(jnp.sum((dot_nn(part.astype(bf16), earlier) + seen) * part, 0, keepdims=True))
        seen = seen + jnp.sum(part, 1, keepdims=True)
    rank = jnp.concatenate(ranks, 1).astype(jnp.int32)
    slot = jnp.where(rank < capacity, routes * slot_rows + rank, -1)
    slot_ref[...] = jnp.broadcast_to(slot, slot_ref.shape)

    def pair(e):
        rows = dot_nn(slot_hot(slot, e, 2 * slot_rows), rows_ref[...]).astype(bf16)
        out_ref[pl.ds(2 * e, 2)] = rows.reshape(2, slot_rows, rows.shape[1])
    each(experts // 2, pair)


def first_slots(routes_row, rows, experts, capacity, slot_rows):
    tokens, width = rows.shape
    vmem = pl.BlockSpec(memory_space=pltpu.VMEM)
    return pl.pallas_call(
        functools.partial(slots_kernel, experts=experts, capacity=capacity, slot_rows=slot_rows),
        out_shape=(
            jax.ShapeDtypeStruct((8, tokens), jnp.int32),
            jax.ShapeDtypeStruct((experts, slot_rows, width), jnp.bfloat16),
        ),
        in_specs=[vmem] * 2,
        out_specs=(vmem,) * 2,
        compiler_params=pltpu.CompilerParams(vmem_limit_bytes=63 << 20),
        cost_estimate=pl.CostEstimate(
            flops=2 * experts * slot_rows * tokens * width, bytes_accessed=4 << 20, transcendentals=0
        ),
    )(routes_row, rows)


def fill_masks(segment_row, qm, km):
    f32, bf16 = jnp.float32, jnp.bfloat16
    lane = lax.broadcasted_iota(jnp.int32, (1, LANES), 1)
    for b in range(qm.shape[0] // BLOCK):
        span = slice(b * BLOCK, (b + 1) * BLOCK)
        hot = (lax.broadcasted_iota(jnp.int32, (LANES, BLOCK), 0) == segment_row[:, span]).astype(f32).T
        qm[span, :] = (hot * masked_score).astype(bf16)
        km[span, :] = jnp.where(lane < 8, 1.0 - hot, 0.0).astype(bf16)


def fill_diag(grid_ref, diag, heads):
    bf16 = jnp.bfloat16
    buckets = grid_ref.shape[0]
    relative = 256 - lax.broadcasted_iota(jnp.int32, (buckets, 4 * LANES), 1)
    hot = (lax.broadcasted_iota(jnp.int32, (buckets, 4 * LANES), 0) == bucket_of(relative))
    hot = hot.astype(jnp.float32).astype(bf16)
    grid = jnp.concatenate(
        [grid_ref[...], jnp.zeros((buckets, LANES - heads), jnp.float32)], 1
    ).T[:16]
    total = None
    for piece in split3(grid):
        term = dot_nn(piece, hot)
        total = term if total is None else total + term
    diag[...] = total


def front_kernel(
    lo_ref, hi_ref, tokens, segment_row, slot_ref, routes_ref, gain_one, gain_two, wq, wk, wv, wo, grid_ref, router_t,
    q_ref, k_ref, kt_ref, v_ref, o_ref, lse_ref, middle_ref, probs_ref, xs_ref, gs_ref,
    vt_ref, qm_ref, km_ref, diag, bias, hidden, *, experts, slot_rows, scale,
):
    f32, bf16 = jnp.float32, jnp.bfloat16
    length, width = tokens.shape
    pairs = width // LANES
    nblk = length // BLOCK
    heads = grid_ref.shape[1]
    low = lax.broadcasted_iota(jnp.int32, (1, LANES), 1) < 64
    step = 256

    for b in range(length // step):
        span = slice(b * step, (b + 1) * step)
        x = tokens[span, :].astype(f32)
        inverse = lax.rsqrt(jnp.mean(x * x, 1, keepdims=True) + epsilon)
        normed = (x * inverse * gain_one[...]).astype(bf16)
        q_ref[span, :] = (dot_nn(normed, wq[...]).astype(bf16).astype(f32) * scale).astype(bf16)
        k = dot_nn(normed, wk[...]).astype(bf16)
        k_ref[span, :] = k
        kt_ref[:, span] = k.T
        v = dot_nn(normed, wv[...]).astype(bf16)
        v_ref[span, :] = v
        vt_ref[:, span] = v.T
    fill_masks(segment_row[...], qm_ref, km_ref)
    fill_diag(grid_ref, diag, heads)
    fill_bias(diag, bias, pairs)
    attend(lo_ref, hi_ref, q_ref, k_ref, vt_ref, qm_ref, km_ref, bias, o_ref, lse_ref)

    rw = two(router_t[...])
    routes = routes_ref[...]
    pad = router_t.shape[0]
    place = lax.broadcasted_iota(jnp.int32, (pad, step), 0)
    gates = []
    for b in range(length // step):
        span = slice(b * step, (b + 1) * step)
        middle = tokens[span, :].astype(f32) + dot_nn(o_ref[span, :], wo[...])
        middle_ref[span, :] = middle
        inverse = lax.rsqrt(jnp.mean(middle * middle, 1, keepdims=True) + epsilon)
        parts = two(middle * inverse * gain_two[...])
        hidden[span, :] = parts[0]
        logits = dot_nt(rw[0], parts[0]) + dot_nt(rw[0], parts[1]) + dot_nt(rw[1], parts[0])
        logits = jnp.where(place < experts, logits, -1e30)
        powers = jnp.exp(logits - jnp.max(logits, 0, keepdims=True))
        probs = powers / jnp.sum(powers, 0, keepdims=True)
        probs_ref[:, span] = probs
        gates.append(jnp.sum(jnp.where(place == routes[:, span], probs, 0.0), 0, keepdims=True))
    gates = row_pieces(jnp.concatenate(gates, 1))
    slot = slot_ref[0:1, :]
    lanes = gs_ref.shape[2]

    def one(e):
        hot = slot_hot(slot, e, slot_rows)
        xs_ref[e] = dot_nn(hot, hidden[...]).astype(bf16)
        if lanes > slot_rows:
            hot = jnp.concatenate([hot, jnp.zeros((lanes - slot_rows, length), bf16)], 0)
        row = jnp.sum(dot_nt(gates, hot), 0, keepdims=True)
        gs_ref[e] = jnp.broadcast_to(row, gs_ref.shape[1:])
    each(experts, one)


def front(lo, hi, tokens, segments, slot, routes_row, gain_one, gain_two, wq, wk, wv, wo, grid, router_t, experts, slot_rows, scale):
    length, width = tokens.shape
    heads = grid.shape[1]
    pairs = width // LANES
    nblk = length // BLOCK
    lanes = (slot_rows + LANES - 1) // LANES * LANES
    smem = pl.BlockSpec(memory_space=pltpu.SMEM)
    vmem = pl.BlockSpec(memory_space=pltpu.VMEM)
    f32, bf16 = jnp.float32, jnp.bfloat16
    shape = jax.ShapeDtypeStruct
    act = shape((length, width), bf16)
    return pl.pallas_call(
        functools.partial(front_kernel, experts=experts, slot_rows=slot_rows, scale=scale),
        out_shape=(
            act, act, shape((width, length), bf16), act, act,
            shape((nblk, 8, 2 * LANES), f32), shape((length, width), f32),
            shape((router_t.shape[0], length), f32),
            shape((experts, slot_rows, width), bf16), shape((experts, 8, lanes), f32),
        ),
        in_specs=[smem] * 2 + [vmem] * 12,
        out_specs=(vmem,) * 10,
        scratch_shapes=[
            pltpu.VMEM((width, length), bf16),
            pltpu.VMEM((length, LANES), bf16),
            pltpu.VMEM((length, LANES), bf16),
            pltpu.VMEM((16, 4 * LANES), f32),
            pltpu.VMEM((pairs, NEAR, BLOCK, 2 * LANES), f32),
            pltpu.VMEM((length, width), bf16),
        ],
        compiler_params=pltpu.CompilerParams(vmem_limit_bytes=63 << 20),
        cost_estimate=pl.CostEstimate(
            flops=4 * length * length * width + 12 * length * width * width, bytes_accessed=20 << 20,
            transcendentals=length * length * heads,
        ),
    )(lo, hi, tokens, segments, slot, routes_row, gain_one, gain_two, wq, wk, wv, wo, grid, router_t)


def bucket_sums(gsum_ref):
    bf16 = jnp.bfloat16
    total = jnp.zeros((16, LANES), jnp.float32)
    lane = lax.broadcasted_iota(jnp.int32, (2 * LANES, LANES), 1)
    for d in range(NEAR):
        relative = (d - 2) * BLOCK + BLOCK - 1 - lax.broadcasted_iota(jnp.int32, (2 * LANES, LANES), 0)
        bucket = 15 if d == 0 else 31 if d == NEAR - 1 else bucket_of(relative)
        hot = (lane == bucket).astype(jnp.float32).astype(bf16)
        for piece in split3(gsum_ref[d * 16 : (d + 1) * 16, :]):
            total = total + dot_nn(piece, hot)
    return total


def small_shape(width, experts):
    return (16 + width // LANES * experts + 16, LANES)


def back_kernel(
    lo_ref, hi_ref, home, home_gate, slot_ref, routes_ref, probs_ref, middle_ref, cotangent, segment_row, gain_two,
    wo, router_t, grid_ref, lse_ref, q_hbm, k_hbm, kt_hbm, v_hbm, o_hbm,
    dq_ref, dk_ref, dv_ref, middle_grad_hbm, small,
    q_ref, k_ref, kt_ref, v_ref, o_ref, middle_grad,
    do_ref, qm_ref, km_ref, diag, bias, gacc, dkacc, dvacc, logit, gsum_ref, sems,
    *, experts, slot_rows, scale,
):
    f32, bf16 = jnp.float32, jnp.bfloat16
    length, width = middle_ref.shape
    pairs = width // LANES
    pad = router_t.shape[0]
    heads = grid_ref.shape[1]
    slot = slot_ref[0:1, :]
    loads = [
        pltpu.make_async_copy(there, here, sems.at[i])
        for i, (there, here) in enumerate(zip(
            (q_hbm, k_hbm, kt_hbm, v_hbm, o_hbm), (q_ref, k_ref, kt_ref, v_ref, o_ref)))
    ]
    for load in loads:
        load.start()

    if experts <= 8:
        total = jnp.zeros((16, length), f32)
        for e in range(experts):
            total = total + dot_nn(row_pieces(home_gate[e, 0:1, :])[:, :slot_rows], slot_hot(slot, e, slot_rows))
    else:
        def add(e, total):
            return total + dot_nn(row_pieces(home_gate[e, 0:1, :])[:, :slot_rows], slot_hot(slot, e, slot_rows))
        total = lax.fori_loop(0, experts, add, jnp.zeros((16, length), f32))
    gate_grad = jnp.sum(total, 0, keepdims=True)
    place = lax.broadcasted_iota(jnp.int32, (pad, length), 0)
    hot = place == routes_ref[...]
    probs = probs_ref[...]
    gate = jnp.sum(jnp.where(hot, probs, 0.0), 0, keepdims=True)
    logit[...] = probs * (jnp.where(hot, gate_grad, 0.0) - gate * gate_grad)
    rw = two(router_t[...])
    slots = experts * slot_rows
    router_sum = jnp.zeros((pad, width), f32)
    gain_sum = jnp.zeros((1, width), f32)
    step = 256
    for b in range(length // step):
        span = slice(b * step, (b + 1) * step)
        hots = []
        for c in range(b * step, (b + 1) * step, BLOCK):
            column = jnp.broadcast_to(slot[:, c : c + BLOCK].astype(f32), (BLOCK, BLOCK)).T
            first = lax.broadcasted_iota(jnp.int32, (BLOCK, LANES), 1).astype(f32)
            hots.append(jnp.concatenate(
                [(column == first + float(s)).astype(f32).astype(bf16) for s in range(0, slots, LANES)], 1))
        spread = jnp.concatenate(hots, 0)
        hidden_grad = dot_nn(spread, home[...].reshape(slots, width))
        lg = two(logit[:, span])
        hidden_grad = hidden_grad + (
            matmul_tn(lg[0], rw[0]) + matmul_tn(lg[0], rw[1]) + matmul_tn(lg[1], rw[0])
        )
        middle = middle_ref[span, :]
        inverse = lax.rsqrt(jnp.mean(middle * middle, 1, keepdims=True) + epsilon)
        unit = middle * inverse
        hidden = two(unit * gain_two[...])
        router_sum = router_sum + (dot_nn(lg[0], hidden[0]) + dot_nn(lg[0], hidden[1]) + dot_nn(lg[1], hidden[0]))
        gain_sum = gain_sum + jnp.sum(hidden_grad * unit, 0, keepdims=True)
        scaled = hidden_grad * gain_two[...]
        mean = jnp.mean(scaled * middle, 1, keepdims=True)
        grad = cotangent[span, :].astype(f32) + inverse * (scaled - unit * (inverse * mean))
        middle_grad[span, :] = grad
        do_ref[span, :] = matmul_nt(grad.astype(bf16), wo[...]).astype(bf16)
    store = pltpu.make_async_copy(middle_grad, middle_grad_hbm, sems.at[5])
    store.start()
    small[...] = jnp.zeros_like(small)
    chunks = width // LANES
    for c in range(chunks):
        cols = slice(c * LANES, (c + 1) * LANES)
        small[8 + c : 9 + c, :] = gain_sum[:, cols]
        small[16 + c * experts : 16 + (c + 1) * experts, :] = router_sum[:experts, cols]

    fill_masks(segment_row[...], qm_ref, km_ref)
    fill_diag(grid_ref, diag, heads)
    fill_bias(diag, bias, pairs)
    for load in loads:
        load.wait()
    attend_back(
        lo_ref, hi_ref, q_ref, k_ref, kt_ref, v_ref, lse_ref, do_ref, o_ref, qm_ref, km_ref, bias,
        dq_ref, dk_ref, dv_ref, gsum_ref, gacc, dkacc, dvacc, scale,
    )
    at = 16 + chunks * experts
    small[at : at + 16, :] = bucket_sums(gsum_ref)
    store.wait()


def back(lo, hi, home, home_gate, slot, routes_row, probs, middle, cotangent, segments, gain_two, wo, router_t, grid,
         q, k, kt, v, lse, o, experts, slot_rows, scale):
    length, width = middle.shape
    heads = grid.shape[1]
    pairs = width // LANES
    smem = pl.BlockSpec(memory_space=pltpu.SMEM)
    vmem = pl.BlockSpec(memory_space=pltpu.VMEM)
    f32, bf16 = jnp.float32, jnp.bfloat16
    shape = jax.ShapeDtypeStruct
    act = shape((length, width), bf16)
    anywhere = pl.BlockSpec(memory_space=pl.ANY)
    return pl.pallas_call(
        functools.partial(back_kernel, experts=experts, slot_rows=slot_rows, scale=scale),
        out_shape=(act, act, act, shape((length, width), f32), shape(small_shape(width, experts), f32)),
        in_specs=[smem] * 2 + [vmem] * 13 + [anywhere] * 5,
        out_specs=(vmem, vmem, vmem, anywhere, vmem),
        scratch_shapes=[
            pltpu.VMEM((length, width), bf16),
            pltpu.VMEM((length, width), bf16),
            pltpu.VMEM((width, length), bf16),
            pltpu.VMEM((length, width), bf16),
            pltpu.VMEM((length, width), bf16),
            pltpu.VMEM((length, width), f32),
            pltpu.VMEM((length, width), bf16),
            pltpu.VMEM((length, LANES), bf16),
            pltpu.VMEM((length, LANES), bf16),
            pltpu.VMEM((16, 4 * LANES), f32),
            pltpu.VMEM((pairs, NEAR, BLOCK, 2 * LANES), f32),
            pltpu.VMEM((pairs, NEAR, BLOCK, 2 * LANES), f32),
            pltpu.VMEM((length, width), f32),
            pltpu.VMEM((length, width), f32),
            pltpu.VMEM((router_t.shape[0], length), f32),
            pltpu.VMEM((NEAR * 16, 2 * LANES), f32),
            pltpu.SemaphoreType.DMA((6,)),
        ],
        compiler_params=pltpu.CompilerParams(vmem_limit_bytes=63 << 20),
        cost_estimate=pl.CostEstimate(
            flops=10 * length * length * width + 6 * length * width * width, bytes_accessed=30 << 20,
            transcendentals=length * length * heads,
        ),
    )(lo, hi, home, home_gate, slot, routes_row, probs, middle, cotangent, segments, gain_two, wo, router_t, grid,
      lse, q, k, kt, v, o)


def finish_kernel(
    sum_q, sum_k, sum_v, sum_o, keep, passed, mixed_in, token_in, small,
    mixed_out, token_out, gain_one, gain_two, grad_q, grad_k, grad_v, grad_o, table_t, router_t, grad_in, grad_out,
    low, wide, through, load_sem, store_sem, copy_sem, *, experts,
):
    f32 = jnp.float32
    sources = (sum_o, sum_v, sum_k, sum_q, keep.at[0], keep.at[1], passed.at[0], passed.at[1])
    targets = (grad_o, grad_v, grad_k, grad_q, grad_in, grad_out)
    width = sum_q.shape[0]
    rows = 256
    spans = [pl.ds(r, rows) for r in range(0, width, rows)]
    fetches = [
        pltpu.make_async_copy(x, through.at[i], copy_sem.at[i]) for i, x in enumerate((mixed_in, token_in))
    ]
    copies = [
        pltpu.make_async_copy(through.at[i], x, copy_sem.at[2 + i]) for i, x in enumerate((mixed_out, token_out))
    ]
    loads = [
        [pltpu.make_async_copy(x.at[span], low.at[i, span], load_sem.at[i, j]) for j, span in enumerate(spans)]
        for i, x in enumerate(sources)
    ]
    stores = [
        [pltpu.make_async_copy(wide.at[i, span], x.at[span], store_sem.at[i, j]) for j, span in enumerate(spans)]
        for i, x in enumerate(targets)
    ]
    for i in range(4):
        for load in loads[i]:
            load.start()
    for fetch in fetches:
        fetch.start()
    for i in range(4, 8):
        for load in loads[i]:
            load.start()
    chunks = width // LANES
    gain_one[...] = jnp.concatenate([small[c : c + 1, :] for c in range(chunks)], 1).reshape(width)
    gain_two[...] = jnp.concatenate([small[8 + c : 9 + c, :] for c in range(chunks)], 1).reshape(width)
    for c in range(chunks):
        router_t[:, c * LANES : (c + 1) * LANES] = small[16 + c * experts : 16 + (c + 1) * experts, :]
    at = 16 + chunks * experts
    heads, buckets = table_t.shape
    table_t[...] = small[at : at + heads, :buckets]
    for i in range(4):
        for j, span in enumerate(spans):
            loads[i][j].wait()
            wide[i, span, :] = low[i, span, :].astype(f32)
            stores[i][j].start()
    for fetch, copy in zip(fetches, copies):
        fetch.wait()
        copy.start()
    for i in (4, 5):
        for j, span in enumerate(spans):
            loads[i][j].wait()
            loads[i + 2][j].wait()
            wide[i, span, :] = low[i, span, :].astype(f32) + low[i + 2, span, :].astype(f32)
            stores[i][j].start()
    for i in range(6):
        for store in stores[i]:
            store.wait()
    for copy in copies:
        copy.wait()


def finish(sums, keep, passed, mixed, token_grad, small, grid_shape, experts):
    f32, bf16 = jnp.float32, jnp.bfloat16
    width = sums[0].shape[0]
    vmem = pl.BlockSpec(memory_space=pltpu.VMEM)
    anywhere = pl.BlockSpec(memory_space=pl.ANY)
    shape = jax.ShapeDtypeStruct
    act = shape(mixed.shape, bf16)
    square, row = shape((width, width), f32), shape((width,), f32)
    blocks = width // 256
    return pl.pallas_call(
        functools.partial(finish_kernel, experts=experts),
        out_shape=(act, act, row, row, square, square, square, square, shape(grid_shape[::-1], f32),
                   shape((experts, width), f32), square, square),
        in_specs=[anywhere] * 8 + [vmem],
        out_specs=(anywhere,) * 2 + (vmem, vmem) + (anywhere,) * 4 + (vmem, vmem) + (anywhere,) * 2,
        scratch_shapes=[
            pltpu.VMEM((8, width, width), bf16), pltpu.VMEM((6, width, width), f32),
            pltpu.VMEM((2,) + mixed.shape, bf16),
            pltpu.SemaphoreType.DMA((8, blocks)), pltpu.SemaphoreType.DMA((6, blocks)),
            pltpu.SemaphoreType.DMA((4,)),
        ],
        compiler_params=pltpu.CompilerParams(vmem_limit_bytes=63 << 20),
        cost_estimate=pl.CostEstimate(flops=0, bytes_accessed=30 << 20, transcendentals=0),
    )(*sums, keep, passed, mixed, token_grad, small)


def gelu_parts(v):
    mag = jnp.abs(v)
    t = 1.0 / (1.0 + (0.3275911 * 0.7071067811865476) * mag)
    poly = t * (0.127414796 + t * (-0.142248368 + t * (0.7107068705 + t * (-0.7265760135 + t * 0.5307027145))))
    gauss = jnp.exp(-0.5 * v * v)
    tail = poly * gauss
    phi = jnp.where(v < 0, tail, 1.0 - tail)
    return v * phi, phi + v * gauss * 0.3989422804014327


def flip_bits(index, mask, count):
    out = 0
    bit = 1
    while bit < count:
        a, b = (index // bit) % 2, (mask // bit) % 2
        out = out + bit * (a + b - 2 * a * b)
        bit *= 2
    return out


def ffn_kernel(
    xs, gs, g, win_hbm, wout_hbm,
    home, home_gate, produced, keep, give,
    win, wout, xr, gr, act, pg, gated, igs, ggs, dws, dwr, stage,
    wsem, own_sem, psem, ksem, xsend, xrecv, gsend, grecv, isend, irecv, qsend, qrecv, dsend, drecv,
    *, groups, dp_size, tiles,
):
    f32, bf16 = jnp.float32, jnp.bfloat16
    me = lax.axis_index("expert")
    dp = lax.axis_index("dp")
    core = dp % 2
    sibling = dp + 1 - 2 * core
    half_of = dp // 2
    rows = xs.shape[1]
    width = xs.shape[2]
    hidden = win.shape[1]
    tile = hidden // tiles
    lanes = gs.shape[2]

    def there(peer):
        return (dp, peer)

    load_in = pltpu.make_async_copy(win_hbm, win, wsem.at[0])
    load_out = pltpu.make_async_copy(wout_hbm, wout, wsem.at[1])
    load_in.start()
    load_out.start()
    load_g = pltpu.make_async_copy(g, gated, wsem.at[2])
    load_g.start()

    barrier = pltpu.get_barrier_semaphore()

    def greet(s, _):
        pl.semaphore_signal(
            barrier, inc=1, device_id=there(flip_bits(me, s, groups)), device_id_type=pl.DeviceIdType.MESH
        )
        return 0
    lax.fori_loop(1, groups, greet, 0)
    pl.semaphore_signal(barrier, inc=1, device_id=(sibling, me), device_id_type=pl.DeviceIdType.MESH)
    pl.semaphore_wait(barrier, groups)

    def x_copy(peer, slot):
        return pltpu.make_async_remote_copy(
            src_ref=xs.at[peer], dst_ref=xr.at[slot], send_sem=xsend.at[peer], recv_sem=xrecv.at[slot],
            device_id=there(peer), device_id_type=pl.DeviceIdType.MESH)

    def g_copy(peer, slot):
        return pltpu.make_async_remote_copy(
            src_ref=gs.at[peer], dst_ref=gr.at[slot], send_sem=gsend.at[peer], recv_sem=grecv.at[slot],
            device_id=there(peer), device_id_type=pl.DeviceIdType.MESH)

    def i_copy(peer, slot):
        return pltpu.make_async_remote_copy(
            src_ref=igs.at[peer], dst_ref=home.at[slot], send_sem=isend.at[peer], recv_sem=irecv.at[slot],
            device_id=there(peer), device_id_type=pl.DeviceIdType.MESH)

    def q_copy(peer, slot):
        return pltpu.make_async_remote_copy(
            src_ref=ggs.at[peer], dst_ref=home_gate.at[slot], send_sem=qsend.at[peer], recv_sem=qrecv.at[slot],
            device_id=there(peer), device_id_type=pl.DeviceIdType.MESH)

    def send(i, _):
        odd = (i - 1) % 2
        s = (1 - odd) * (groups - 1 - (i - 1) // 2) + odd * (i // 2)
        peer = flip_bits(me, s, groups)
        x_copy(peer, me).start()
        g_copy(peer, me).start()
        return 0
    lax.fori_loop(1, groups, send, 0)
    own_x = pltpu.make_async_copy(xs.at[me], xr.at[me], own_sem.at[0])
    own_g = pltpu.make_async_copy(gs.at[me], gr.at[me], own_sem.at[1])
    own_x.start()
    own_g.start()
    load_in.wait()
    load_out.wait()
    load_g.wait()

    spot = (
        lax.broadcasted_iota(jnp.int32, (rows, lanes), 0)
        == lax.broadcasted_iota(jnp.int32, (rows, lanes), 1)
    )

    def work(base):
        both = pl.ds(base, 2)
        x = xr[both].reshape(2 * rows, width)
        place = pl.ds(pl.multiple_of(base * rows, rows), 2 * rows)
        gg = gated[place, :]
        gate = jnp.concatenate(
            [jnp.sum(jnp.where(spot, gr[base + u, 0:1, :], 0.0), 1, keepdims=True) for u in range(2)], 0
        )
        gated[place, :] = (gate * gg.astype(f32)).astype(bf16)
        total = jnp.zeros((2 * rows, width), f32)
        gate_grad = jnp.zeros((2 * rows, 1), f32)

        def columns(t):
            return slice(t * tile, (t + 1) * tile)

        def products(t):
            return matmul(x, win[:, columns(t)]), matmul_nt(gg, wout[columns(t), :])

        ahead = products(0)
        for t in range(tiles):
            pre, out_grad = ahead
            if t + 1 < tiles:
                ahead = products(t + 1)
            value, slope = gelu_parts(pre)
            act[place, columns(t)] = value.astype(bf16)
            gate_grad = gate_grad + jnp.sum(value * out_grad, 1, keepdims=True)
            low = (gate * out_grad * slope).astype(bf16)
            pg[place, columns(t)] = low
            total = total + matmul_nt(low, win[:, columns(t)])
        igs[both] = total.astype(bf16).reshape(2, rows, width)
        for u in range(2):
            row = jnp.sum(jnp.where(spot, gate_grad[u * rows : (u + 1) * rows], 0.0), 0, keepdims=True)
            ggs[base + u] = jnp.broadcast_to(row, ggs.shape[1:])

    def arrive(peer):
        x_copy(peer, peer).wait_recv()
        g_copy(peer, peer).wait_recv()

    def back(peer):
        i_copy(peer, me).start()
        q_copy(peer, me).start()

    own_x.wait()
    own_g.wait()
    arrive(flip_bits(me, 1, groups))
    work(me - me % 2)
    own_i = pltpu.make_async_copy(igs.at[me], home.at[me], own_sem.at[0])
    own_q = pltpu.make_async_copy(ggs.at[me], home_gate.at[me], own_sem.at[1])
    own_i.start()
    own_q.start()
    back(flip_bits(me, 1, groups))

    def chunk(j, _):
        peer = flip_bits(me, 2 * j, groups)
        other = flip_bits(me, 2 * j + 1, groups)
        arrive(peer)
        arrive(other)
        work(peer - peer % 2)
        back(peer)
        back(other)
        return 0
    lax.fori_loop(1, groups // 2, chunk, 0)

    def d_copy(k):
        return pltpu.make_async_remote_copy(
            src_ref=dws.at[k % 2], dst_ref=dwr.at[k], send_sem=dsend.at[k], recv_sem=drecv.at[k],
            device_id=(sibling, me), device_id_type=pl.DeviceIdType.MESH)

    part = hidden // dp_size
    flat = groups * rows
    items = [(which, half) for half in (1 - half_of, half_of) for which in range(2)]

    def grad(which, quarter):
        span = pl.ds(pl.multiple_of(quarter * part, part), part)
        if which == 0:
            return matmul_tn(xr[...].reshape(flat, width), pg[:, span])
        return matmul_tn(act[:, span], gated[...])

    for k, (which, half) in enumerate(items):
        if k >= 2:
            d_copy(k - 2).wait_send()
        dws[k % 2] = grad(which, 2 * half + 1 - core).astype(bf16)
        d_copy(k).start()
    outs = [
        pltpu.make_async_copy(dwr.at[0], give.at[0], ksem.at[0]),
        pltpu.make_async_copy(dwr.at[1], give.at[1], ksem.at[1]),
        pltpu.make_async_copy(dwr.at[2], keep.at[0], ksem.at[2]),
        pltpu.make_async_copy(dwr.at[3], keep.at[1], ksem.at[3]),
    ]
    for k, (which, half) in enumerate(items):
        local = grad(which, 2 * half + core)
        d_copy(k).wait_recv()
        dwr[k] = (local + dwr[k].astype(f32)).astype(bf16)
        outs[k].start()

    span = stage.shape[1]
    copies = []
    for b in range(flat // span):
        if b >= 2:
            copies[b - 2].wait()
        stage[b % 2] = matmul(act[b * span : (b + 1) * span, :], wout[...]).astype(bf16)
        copy = pltpu.make_async_copy(stage.at[b % 2], produced.at[pl.ds(b * span, span)], psem.at[b % 2])
        copy.start()
        copies.append(copy)
    for copy in copies[-2:] + outs:
        copy.wait()
    own_i.wait()
    own_q.wait()
    for k in (2, 3):
        d_copy(k).wait_send()

    def finish(s, _):
        peer = flip_bits(me, s, groups)
        x_copy(peer, me).wait_send()
        g_copy(peer, me).wait_send()
        i_copy(peer, me).wait_send()
        q_copy(peer, me).wait_send()
        i_copy(peer, peer).wait_recv()
        q_copy(peer, peer).wait_recv()
        return 0
    lax.fori_loop(1, groups, finish, 0)


def ffn(xs, gs, g, weight_in, weight_out, groups, dp_size, tiles=6):
    f32, bf16 = jnp.float32, jnp.bfloat16
    _, rows, width = xs.shape
    hidden = weight_in.shape[1]
    lanes = gs.shape[2]
    part = hidden // dp_size
    anywhere = pl.BlockSpec(memory_space=pl.ANY)
    sem = pltpu.SemaphoreType.DMA
    flat = groups * rows
    shape = jax.ShapeDtypeStruct
    return pl.pallas_call(
        functools.partial(ffn_kernel, groups=groups, dp_size=dp_size, tiles=tiles),
        out_shape=(
            shape((groups, rows, width), bf16),
            shape((groups, 8, lanes), f32),
            shape((flat, width), bf16),
            shape((2, width, part), bf16),
            shape((2, width, part), bf16),
        ),
        in_specs=[anywhere] * 5,
        out_specs=(anywhere,) * 5,
        scratch_shapes=[
            pltpu.VMEM((width, hidden), bf16),
            pltpu.VMEM((hidden, width), bf16),
            pltpu.VMEM((groups, rows, width), bf16),
            pltpu.VMEM((groups, 8, lanes), f32),
            pltpu.VMEM((flat, hidden), bf16),
            pltpu.VMEM((flat, hidden), bf16),
            pltpu.VMEM((flat, width), bf16),
            pltpu.VMEM((groups, rows, width), bf16),
            pltpu.VMEM((groups, 8, lanes), f32),
            pltpu.VMEM((2, width, part), bf16),
            pltpu.VMEM((4, width, part), bf16),
            pltpu.VMEM((2, flat // 8, width), bf16),
            sem((3,)), sem((2,)), sem((2,)), sem((4,)),
            sem((groups,)), sem((groups,)), sem((groups,)), sem((groups,)),
            sem((groups,)), sem((groups,)), sem((groups,)), sem((groups,)),
            sem((4,)), sem((4,)),
        ],
        compiler_params=pltpu.CompilerParams(
            collective_id=1, has_side_effects=True, vmem_limit_bytes=62 << 20
        ),
        cost_estimate=pl.CostEstimate(
            flops=12 * flat * width * hidden, bytes_accessed=40 << 20, transcendentals=flat * hidden
        ),
    )(xs, gs, g, weight_in, weight_out)


def fold_steps(rows, cols, bits):
    steps = []
    for bit in bits[:3]:
        rows = rows // 2
        steps.append(((bit,), "half", rows, cols))
    rows, cols = rows // 2, cols // 2
    steps.append((tuple(bits[3:5]), "quad", rows, cols))
    for bit in bits[5:]:
        steps.append(((bit,), "whole", rows, cols))
    return steps


def reduce_kernel(
    attended_hbm, middle_grad_hbm, tokens_hbm, dv_hbm, dk_hbm, dq_hbm, wq_hbm, wk_hbm, wv_hbm, returned_hbm, middle_hbm,
    gain, small_in, slot_ref, routes_ref, probs_ref,
    sum_o, sum_v, sum_k, sum_q, token_grad_hbm, small_out, mixed_hbm,
    attended, middle_grad, tokens, dv, dk, dq, wq, wk, wv, returned, middle,
    token_grad, mixed, sums, normed, branch, acc, outbox, inbox, small_box, small_sent, load_sem, store_sem,
    ssend, srecv, tsend, trecv,
    *, dp_bits, expert_bits,
):
    f32, bf16 = jnp.float32, jnp.bfloat16
    dp = lax.axis_index("dp")
    ex = lax.axis_index("expert")
    MESH = pl.DeviceIdType.MESH
    length, width = tokens.shape
    held = (attended, middle_grad, tokens, dv, dk, dq, wq, wk, wv, returned, middle)
    loads = [
        pltpu.make_async_copy(there, here, load_sem.at[i])
        for i, (there, here) in enumerate(zip(
            (attended_hbm, middle_grad_hbm, tokens_hbm, dv_hbm, dk_hbm, dq_hbm, wq_hbm, wk_hbm, wv_hbm,
             returned_hbm, middle_hbm), held))
    ]
    first = 4
    for load in loads[:first]:
        load.start()

    def own_bit(bit):
        axis, place = bit
        return (dp // 2 ** place) % 2 if axis == "dp" else (ex // 2 ** place) % 2

    def partner(bits):
        there = [dp, ex]
        for bit in bits:
            there[bit[0] == "expert"] = there[bit[0] == "expert"] + (1 - 2 * own_bit(bit)) * 2 ** bit[1]
        return tuple(there)

    dpb = [("dp", i) for i in range(dp_bits)]
    exb = [("expert", i) for i in range(expert_bits)]
    orders = [
        [dpb[0], dpb[1], exb[0]] + dpb[2:] + exb[1:],
        [dpb[0], exb[0], dpb[1]] + dpb[2:] + exb[1:],
    ]
    every = dpb + exb
    small_count = len(every)

    barrier = pltpu.get_barrier_semaphore()
    greeted = [(bit,) for bit in every] + [tuple(orders[0][3:5])]
    for bits in greeted:
        pl.semaphore_signal(barrier, inc=1, device_id=partner(bits), device_id_type=MESH)
    pl.semaphore_wait(barrier, len(greeted))

    def prepare(i, _):
        span = pl.ds(pl.multiple_of(i * 256, 256), 256)
        x = tokens[span, :].astype(f32)
        inv = lax.rsqrt(jnp.mean(x * x, 1, keepdims=True) + epsilon)
        normed[span, :] = (x * inv * gain[...]).astype(bf16)
        branch[span, :] = middle_grad[span, :].astype(bf16)
        return 0
    for load in loads[:3]:
        load.wait()
    for load in loads[first:]:
        load.start()
    lax.fori_loop(0, length // 256, prepare, 0)

    lefts = (attended, normed, normed, normed)
    rights = (branch, dv, dk, dq)
    streams = []
    for s in range(4):
        row, col, at, sem_at = 0, 0, 0, 0
        plan = []
        for bits, kind, r, c in fold_steps(width, width, orders[s % 2]):
            mine = [own_bit(bit) for bit in bits]
            if kind == "half":
                peers = [bits]
                keep_at = (row + mine[0] * r, col)
                theirs = [(row + (1 - mine[0]) * r, col)]
            elif kind == "quad":
                peers = [bits[:1], bits[1:], bits]
                keep_at = (row + mine[0] * r, col + mine[1] * c)
                theirs = [
                    (row + (1 - mine[0]) * r, col + mine[1] * c),
                    (row + mine[0] * r, col + (1 - mine[1]) * c),
                    (row + (1 - mine[0]) * r, col + (1 - mine[1]) * c),
                ]
            else:
                peers, keep_at, theirs = [bits], (row, col), [(row, col)]
            plan.append((peers, kind, r, c, at, keep_at, theirs, sem_at))
            row, col = keep_at
            at += r * len(peers)
            sem_at += len(peers)
        streams.append(plan)
    count = len(streams[0])
    sems = ssend.shape[1] // 2

    def rs_copy(s, k, i):
        peers, kind, r, c, at, _, _, sem_at = streams[s][k]
        box = pl.ds(at + i * r, r)
        return pltpu.make_async_remote_copy(
            src_ref=outbox.at[s, box, pl.ds(0, c)], dst_ref=inbox.at[s, box, pl.ds(0, c)],
            send_sem=ssend.at[s, sem_at + i], recv_sem=srecv.at[s, sem_at + i],
            device_id=partner(peers[i]), device_id_type=MESH)

    def aligned(at):
        row, col = at
        row = pl.multiple_of(row, 16) if not isinstance(row, int) else row
        col = pl.multiple_of(col, 128) if not isinstance(col, int) else col
        return row, col

    def block(s, at, r, c):
        row, col = aligned(at)
        return sums.at[s, pl.ds(row, r), pl.ds(col, c)]

    def ag_copy(s, k, i, incoming):
        peers, kind, r, c, _, keep_at, theirs, sem_at = streams[s][k]
        ref = block(s, theirs[i] if incoming else keep_at, r, c)
        return pltpu.make_async_remote_copy(
            src_ref=ref, dst_ref=ref,
            send_sem=ssend.at[s, sems + sem_at + i], recv_sem=srecv.at[s, sems + sem_at + i],
            device_id=partner(peers[i]), device_id_type=MESH)

    half = width // 2
    core = own_bit(dpb[0])

    def grad(s, which):
        span = pl.ds(pl.multiple_of(which * half, half), half)
        return matmul_tn(lefts[s][:, span], rights[s][...])

    def local(s, at, r, c):
        row, col = aligned((at[0] - streams[s][0][5][0], at[1]))
        return acc.at[s, pl.ds(row, r), pl.ds(col, c)]

    def phase(s, k):
        plan = streams[s]
        if k == 0:
            if s > 0:
                loads[2 + s].wait()
            outbox[s, 0:half, :] = grad(s, 1 - core).astype(bf16)
            rs_copy(s, 0, 0).start()
            return
        if k <= count:
            peers, kind, r, c, at, keep_at, _, _ = plan[k - 1]
            view = local(s, keep_at, r, c)
            total = outbox[s, at : at + r, 0:c].astype(f32) if kind == "whole" else view[...]
            for i in range(len(peers)):
                rs_copy(s, k - 1, i).wait_recv()
                total = total + inbox[s, at + i * r : at + (i + 1) * r, 0:c].astype(f32)
            if k < count:
                view[...] = total
                peers, kind, r, c, at, _, theirs, _ = plan[k]
                for i in range(len(peers)):
                    outbox[s, at + i * r : at + (i + 1) * r, 0:c] = local(s, theirs[i], r, c)[...].astype(bf16)
                    rs_copy(s, k, i).start()
                return
            block(s, keep_at, r, c)[...] = total.astype(bf16)
        g = 2 * count - 1 - k
        if k > count and plan[g + 1][1] != "whole":
            for i in range(len(plan[g + 1][0])):
                ag_copy(s, g + 1, i, True).wait_recv()
        if g >= 0 and plan[g][1] != "whole":
            for i in range(len(plan[g][0])):
                ag_copy(s, g, i, False).start()

    gain_row = gain[...]
    rows = 256

    def norm_block(i, gain_grad):
        span = pl.ds(pl.multiple_of(i * rows, rows), rows)
        grads = (
            matmul_nt(dq[span, :], wq[...]) + matmul_nt(dk[span, :], wk[...]) + matmul_nt(dv[span, :], wv[...])
        )
        x = tokens[span, :].astype(f32)
        inv = lax.rsqrt(jnp.mean(x * x, 1, keepdims=True) + epsilon)
        scaled = grads * gain_row
        mean = jnp.sum(scaled * x, 1, keepdims=True) * (1.0 / width)
        part = inv * (scaled - x * (inv * inv * mean))
        token_grad[span, :] = (middle_grad[span, :] + part).astype(bf16)
        return gain_grad + jnp.sum(grads * (x * inv), 0, keepdims=True)

    slots = returned.shape[0]
    routes = routes_ref[...]
    pad = probs_ref.shape[0]
    hot = lax.broadcasted_iota(jnp.int32, (pad, length), 0) == routes
    gate_row = jnp.sum(jnp.where(hot, probs_ref[...], 0.0), 0, keepdims=True)

    def mix(c):
        at = slice(c, c + BLOCK)
        column = jnp.broadcast_to(slot_ref[0:1, at].astype(f32), (BLOCK, BLOCK)).T
        first = lax.broadcasted_iota(jnp.int32, (BLOCK, LANES), 1).astype(f32)
        spread = jnp.concatenate(
            [(column == first + float(s)).astype(f32).astype(bf16) for s in range(0, slots, LANES)], 1)
        rows_back = dot_nn(spread, returned[...])
        gate = jnp.broadcast_to(gate_row[:, at], (BLOCK, BLOCK)).T
        gate = jnp.concatenate([gate] * (width // LANES), 1)
        mixed[at, :] = (middle[at, :] + gate * rows_back).astype(bf16)

    def small_copy(k):
        return pltpu.make_async_remote_copy(
            src_ref=small_sent.at[k], dst_ref=small_box.at[k],
            send_sem=tsend.at[k], recv_sem=trecv.at[k],
            device_id=partner((every[k],)), device_id_type=MESH)

    def small_phase(k):
        if k == 0:
            gain_grad = lax.fori_loop(0, length // rows, norm_block, jnp.zeros((1, width), f32))
            small_out[...] = small_in[...]
            for i in range(width // LANES):
                small_out[i : i + 1, :] = gain_grad[:, i * LANES : (i + 1) * LANES]
        else:
            small_copy(k - 1).wait_recv()
            small_out[...] = small_out[...] + small_box[k - 1]
        if k < small_count:
            small_sent[k] = small_out[...]
            small_copy(k).start()

    last = 2 * count
    starts = (0, 0, 2, 2)
    stores = [
        pltpu.make_async_copy(sums.at[s], out, store_sem.at[s]) for s, out in enumerate((sum_o, sum_v, sum_k, sum_q))
    ]
    stores.append(pltpu.make_async_copy(token_grad, token_grad_hbm, store_sem.at[4]))
    stores.append(pltpu.make_async_copy(mixed, mixed_hbm, store_sem.at[5]))
    mixes = length // BLOCK
    turns = (1, 1, 4, 5, 6, 6, 8, 8)
    for t in range(max(last + starts[-1], small_count + 3, turns[-1]) + 1):
        for s in range(4):
            if 0 <= t - starts[s] <= last:
                phase(s, t - starts[s])
                if t - starts[s] == last:
                    stores[s].start()
        for s in range(4):
            if t == starts[s]:
                acc[s] = grad(s, core)
        if t == 3:
            for load in loads[6:9]:
                load.wait()
        if 0 <= t - 3 <= small_count:
            small_phase(t - 3)
            if t == 3:
                stores[4].start()
        if t == 1:
            for load in loads[9:]:
                load.wait()
        for c in range(mixes):
            if t == turns[c * len(turns) // mixes]:
                mix(c * BLOCK)
                if c == mixes - 1:
                    stores[5].start()
    for store in stores:
        store.wait()
    for s in range(4):
        for k in range(count):
            for i in range(len(streams[s][k][0])):
                rs_copy(s, k, i).wait_send()
                if streams[s][k][1] != "whole":
                    ag_copy(s, k, i, False).wait_send()
    for k in range(small_count):
        small_copy(k).wait_send()


def reduce_grads(tokens, attended, middle_grad, dq, dk, dv, wq, wk, wv, gain, small,
                 returned, slot, routes_row, probs, middle, dp_size, groups):
    f32, bf16 = jnp.float32, jnp.bfloat16
    length, width = tokens.shape
    dp_bits, expert_bits = dp_size.bit_length() - 1, groups.bit_length() - 1
    count = dp_bits + expert_bits
    steps = fold_steps(width, width, list(range(count)))
    box = sum(step[2] * (3 if step[1] == "quad" else 1) for step in steps)
    messages = sum(3 if step[1] == "quad" else 1 for step in steps)
    vmem = pl.BlockSpec(memory_space=pltpu.VMEM)
    anywhere = pl.BlockSpec(memory_space=pl.ANY)
    sem = pltpu.SemaphoreType.DMA
    shape = jax.ShapeDtypeStruct
    act, square = shape((length, width), bf16), shape((width, width), bf16)
    big = (attended, middle_grad, tokens, dv, dk, dq, wq, wk, wv, returned, middle)
    return pl.pallas_call(
        functools.partial(reduce_kernel, dp_bits=dp_bits, expert_bits=expert_bits),
        out_shape=(square, square, square, square, act, shape(small.shape, f32), act),
        in_specs=[anywhere] * len(big) + [vmem] * 5,
        out_specs=(anywhere,) * 5 + (vmem, anywhere),
        scratch_shapes=[pltpu.VMEM(x.shape, x.dtype) for x in big] + [
            pltpu.VMEM((length, width), bf16),
            pltpu.VMEM((length, width), bf16),
            pltpu.VMEM((4, width, width), bf16),
            pltpu.VMEM((length, width), bf16),
            pltpu.VMEM((length, width), bf16),
            pltpu.VMEM((4, width // 2, width), f32),
            pltpu.VMEM((4, box, width), bf16),
            pltpu.VMEM((4, box, width), bf16),
            pltpu.VMEM((count,) + small.shape, f32),
            pltpu.VMEM((count,) + small.shape, f32),
            sem((len(big),)), sem((6,)),
            sem((4, 2 * messages)), sem((4, 2 * messages)), sem((count,)), sem((count,)),
        ],
        compiler_params=pltpu.CompilerParams(
            collective_id=2, has_side_effects=True, vmem_limit_bytes=62 << 20
        ),
        cost_estimate=pl.CostEstimate(
            flops=14 * length * width * width, bytes_accessed=30 << 20, transcendentals=0
        ),
    )(*big, gain, small, slot, routes_row, probs)


def key_ranges(segment_row):
    first, last = segment_row[::BLOCK], segment_row[BLOCK - 1 :: BLOCK]
    lo = jnp.sum(segment_row[None, :] < first[:, None], 1) // BLOCK
    hi = (jnp.sum(segment_row[None, :] <= last[:, None], 1) + BLOCK - 1) // BLOCK
    return lo.astype(jnp.int32), hi.astype(jnp.int32)


def per_device(
    tokens,
    segments,
    routes,
    cotangent,
    attn_gain,
    ffn_gain,
    query_weight,
    key_weight,
    value_weight,
    output_weight,
    position_bias_grid,
    router_weight,
    expert_in,
    expert_out,
):
    f32, bf16 = jnp.float32, jnp.bfloat16
    token_count, model_width = tokens.shape
    head_count = position_bias_grid.shape[1]
    score_scale = (model_width // head_count) ** (-0.5)
    experts_all = router_weight.shape[1]
    capacity = (5 * token_count + 4 * experts_all - 1) // (4 * experts_all)
    slot_rows = (capacity + 15) // 16 * 16
    slots = experts_all * slot_rows
    groups = lax.axis_size("expert")
    dp_size = lax.axis_size("dp")

    def exchange(rows):
        return lax.all_to_all(rows, "expert", split_axis=0, concat_axis=0, tiled=True)

    routes_row = routes.reshape(1, token_count)
    token_slot, grad_slots = first_slots(routes_row, cotangent, experts_all, capacity, slot_rows)
    grad_arrived = exchange(grad_slots)
    lo, hi = key_ranges(segments[0])
    router_pad = max(experts_all, 16)
    router_t = jnp.pad(router_weight.T, ((0, router_pad - experts_all), (0, 0)))
    gain_one, gain_two = attn_gain[None, :], ffn_gain[None, :]
    queries, key_rows, keys_t, value_rows, attended, log_sums, middle, router_probs, sent, gate_slots = front(
        lo, hi, tokens, segments, token_slot, routes_row, gain_one, gain_two,
        query_weight, key_weight, value_weight, output_weight, position_bias_grid, router_t,
        experts_all, slot_rows, score_scale,
    )
    home_grad, home_gate, produced, keep, give = ffn(
        sent, gate_slots, grad_arrived.reshape(slots, model_width), expert_in[0], expert_out[0], groups, dp_size,
    )
    passed = lax.ppermute(give, "dp", [(i, (i + dp_size // 2) % dp_size) for i in range(dp_size)])
    returned = exchange(produced.reshape(experts_all, slot_rows, model_width)).reshape(slots, model_width)
    query_grad, key_grad, value_grad, middle_grad, small = back(
        lo, hi, home_grad, home_gate, token_slot, routes_row, router_probs, middle, cotangent, segments, gain_two,
        output_weight, router_t, position_bias_grid, queries, key_rows, keys_t, value_rows, log_sums, attended,
        experts_all, slot_rows, score_scale,
    )
    sum_o, sum_v, sum_k, sum_q, token_grad, small, mixed = reduce_grads(
        tokens, attended, middle_grad, query_grad, key_grad, value_grad,
        query_weight, key_weight, value_weight, gain_one, small,
        returned, token_slot, routes_row, router_probs, middle, dp_size, groups,
    )
    (mixed, token_grad, attn_gain_grad, ffn_gain_grad, grad_q, grad_k, grad_v, grad_o, table_grad, router_grad,
     grad_in, grad_out) = finish(
        (sum_q, sum_k, sum_v, sum_o), keep, passed, mixed, token_grad, small, position_bias_grid.shape, experts_all
    )
    return (
        mixed,
        token_grad,
        attn_gain_grad,
        ffn_gain_grad,
        grad_q,
        grad_k,
        grad_v,
        grad_o,
        table_grad.T,
        router_grad.T,
        grad_in[None],
        grad_out[None],
    )


def solution(mesh):
    rows = P(("dp", "expert"), None)
    return jax.shard_map(
        per_device,
        mesh=mesh,
        in_specs=(rows,) * 4 + (P(),) * 8 + (P("expert", None, None),) * 2,
        out_specs=(rows,) * 2 + (P(),) * 8 + (P("expert", None, "dp"), P("expert", "dp", None)),
        check_vma=False,
    )
```

```python
import functools

import jax
import jax.numpy as jnp
from jax import lax
from jax.experimental import pallas as pl
from jax.experimental.pallas import tpu as pltpu
from jax.sharding import PartitionSpec as P

epsilon = 1e-06
precise_setting = lax.Precision.HIGHEST
def matmul(left, right):
    return jnp.dot(left, right, preferred_element_type=jnp.float32)


def matmul_tn(left, right):
    return lax.dot_general(left, right, (((0,), (0,)), ((), ())), preferred_element_type=jnp.float32)


def matmul_nt(left, right):
    return lax.dot_general(left, right, (((1,), (1,)), ((), ())), preferred_element_type=jnp.float32)


bucket_bounds = (12, 16, 23, 32, 46, 64, 91)
masked_score = -1e30
LANES = 128
BLOCK = 128
NEAR = 5
UF = 6
UB = 6


def bucket_of(relative):
    distance = jnp.abs(relative)
    beyond = jnp.zeros_like(distance)
    for threshold in bucket_bounds:
        beyond = beyond + (distance >= threshold).astype(jnp.int32)
    inside = jnp.where(distance < 8, distance, 8 + beyond)
    return inside + 16 * (relative > 0).astype(jnp.int32)


def dot_nt(a, b):
    return lax.dot_general(a, b, (((1,), (1,)), ((), ())), preferred_element_type=jnp.float32)


def dot_nn(a, b):
    return lax.dot_general(a, b, (((1,), (0,)), ((), ())), preferred_element_type=jnp.float32)


def split3(x):
    a = x.astype(jnp.bfloat16)
    r = x - a.astype(jnp.float32)
    b = r.astype(jnp.bfloat16)
    c = (r - b.astype(jnp.float32)).astype(jnp.bfloat16)
    return a, b, c


def fill_bias(diag_ref, bias, pairs):
    for p in range(pairs):
        for d in range(NEAR):
            tiles = []
            for h in (2 * p, 2 * p + 1):
                row = diag_ref[h : h + 1, :]
                if d in (0, NEAR - 1):
                    col = row[:, 511:512] if d == 0 else row[:, 0:1]
                    tiles.append(jnp.broadcast_to(col, (BLOCK, BLOCK)))
                else:
                    base = (3 - d) * BLOCK
                    wide = jnp.broadcast_to(row[:, base : base + 2 * BLOCK], (BLOCK, 2 * BLOCK))
                    tiles.append(pltpu.roll(wide, BLOCK, 1, stride=1, stride_axis=0)[:, :BLOCK])
            bias[p, d] = jnp.concatenate(tiles, 1)


def heads_apart(block, low, extra=None):
    zero = jnp.zeros_like(block)
    first, second = jnp.where(low, block, zero), jnp.where(low, zero, block)
    if extra is not None:
        first, second = jnp.concatenate([first, extra], 1), jnp.concatenate([second, extra], 1)
    return jnp.concatenate([first, second], 0)


def by_count(lo, hi, most, body):
    for n in range(1, most + 1):
        pl.when(hi - lo == n)(functools.partial(body, n))


def own_heads(wide):
    return jnp.concatenate([wide[:64, :LANES], wide[64:128, LANES:]], 0)


def attend(lo_ref, hi_ref, q_ref, k_ref, vt_ref, qm_ref, km_ref, bias, o_ref, lse_ref):
    pairs = q_ref.shape[1] // LANES
    length = q_ref.shape[0]
    nblk = length // BLOCK
    f32, bf16 = jnp.float32, jnp.bfloat16
    low = lax.broadcasted_iota(jnp.int32, (1, LANES), 1) < 64

    def q_block(i, _):
        lo, hi = lo_ref[i], hi_ref[i]
        rows = pl.ds(pl.multiple_of(i * BLOCK, BLOCK), BLOCK)
        start = pl.multiple_of(lo * BLOCK, BLOCK)
        qm = qm_ref[rows, :]

        def body(n):
            span = pl.ds(start, n * BLOCK)
            km = km_ref[span, :]

            def lanes_of(p):
                return pl.ds(pl.multiple_of(p * LANES, LANES), LANES)

            def scores(p):
                qs = heads_apart(q_ref[rows, lanes_of(p)], low, qm)
                return dot_nt(jnp.concatenate([k_ref[span, lanes_of(p)], km], 1), qs)

            def soften(p, st):
                parts = []
                top = None
                for b in range(n):
                    d = jnp.clip(lo + b - i, -2, 2) + 2
                    s = st[b * BLOCK : (b + 1) * BLOCK] + bias[p, d]
                    parts.append(s)
                    top = s if top is None else jnp.maximum(top, s)
                top = jnp.max(top, 0, keepdims=True)
                return jnp.concatenate([jnp.exp(s - top).astype(bf16) for s in parts], 0), top

            def mix(p, probs):
                values = jnp.concatenate([vt_ref[lanes_of(p), span], jnp.ones((16, n * BLOCK), bf16)], 0)
                return dot_nn(values, probs)

            def finish(p, acc, top):
                total = acc[LANES : LANES + 1]
                inv = 1.0 / total
                ot = own_heads(acc)
                ot = jnp.concatenate([ot[:64] * inv[:, :LANES], ot[64:] * inv[:, LANES:]], 0)
                o_ref[rows, lanes_of(p)] = ot.T.astype(bf16)
                lse_ref[i, pl.ds(p, 1), :] = top + jnp.log(total)

            def some(g, _):
                ps = [g * UF + u for u in range(UF)]
                sts = [scores(p) for p in ps]
                soft = [soften(p, st) for p, st in zip(ps, sts)]
                accs = [mix(p, x[0]) for p, x in zip(ps, soft)]
                for p, acc, x in zip(ps, accs, soft):
                    finish(p, acc, x[1])
                return 0
            lax.fori_loop(0, pairs // UF, some, 0)

        by_count(lo, hi, nblk, body)
        return 0
    lax.fori_loop(0, nblk, q_block, 0)


def attend_back(
    lo_ref, hi_ref, q_ref, k_ref, kt_ref, v_ref, lse_ref, do_ref, o_ref, qm_ref, km_ref, bias,
    dq_ref, dk_ref, dv_ref, gsum_ref, gacc, dkacc, dvacc, scale,
):
    length, width = q_ref.shape
    pairs = width // LANES
    nblk = length // BLOCK
    f32, bf16 = jnp.float32, jnp.bfloat16
    low = lax.broadcasted_iota(jnp.int32, (1, LANES), 1) < 64
    pick = (
        lax.broadcasted_iota(jnp.int32, (16, LANES), 0) == lax.broadcasted_iota(jnp.int32, (16, LANES), 1) // 64
    ).astype(f32).astype(bf16)
    gacc[...] = jnp.zeros_like(gacc)
    gsum_ref[...] = jnp.zeros_like(gsum_ref)
    dkacc[...] = jnp.zeros_like(dkacc)
    dvacc[...] = jnp.zeros_like(dvacc)

    def q_block(i, _):
        lo, hi = lo_ref[i], hi_ref[i]
        rows = pl.ds(pl.multiple_of(i * BLOCK, BLOCK), BLOCK)
        start = pl.multiple_of(lo * BLOCK, BLOCK)
        qm = qm_ref[rows, :]

        def body(n):
            span = pl.ds(start, n * BLOCK)
            km = km_ref[span, :]

            def lanes_of(p):
                return pl.ds(pl.multiple_of(p * LANES, LANES), LANES)

            def products(p):
                cols = lanes_of(p)
                qs = heads_apart(q_ref[rows, cols], low, qm)
                dd = do_ref[rows, cols]
                dos = heads_apart(dd, low)
                prod = dd.astype(f32) * o_ref[rows, cols].astype(f32)
                prod_hi = prod.astype(bf16)
                prod_lo = (prod - prod_hi.astype(f32)).astype(bf16)
                inner = dot_nt(pick, prod_hi) + dot_nt(pick, prod_lo)
                inner = jnp.concatenate([inner[0:1], inner[1:2]], 1)
                st = dot_nt(jnp.concatenate([k_ref[span, cols], km], 1), qs)
                dpt = dot_nt(v_ref[span, cols], dos)
                return qs, dos, inner, st, dpt

            def pointwise(p, inner, st, dpt):
                lse = lse_ref[i, pl.ds(p, 1), :]
                probs, grads = [], []
                for b in range(n):
                    d = jnp.clip(lo + b - i, -2, 2) + 2
                    part = slice(b * BLOCK, (b + 1) * BLOCK)
                    prob = jnp.exp(st[part] + bias[p, d] - lse)
                    grad = prob * (dpt[part] - inner)
                    gacc[p, d] += grad
                    probs.append(prob.astype(bf16))
                    grads.append(grad.astype(bf16))
                return jnp.concatenate(probs, 0), jnp.concatenate(grads, 0)

            def back(p, qs, dos, probs, grads):
                cols = lanes_of(p)
                return (
                    dot_nn(probs, dos), dot_nn(grads, qs[:, :LANES]), dot_nn(kt_ref[cols, span], grads)
                )

            def finish(p, dv, dk, dqt):
                cols = lanes_of(p)
                dvacc[span, cols] += dv
                dkacc[span, cols] += dk
                dq_ref[rows, cols] = (own_heads(dqt).T * scale).astype(bf16)

            def some(g, _):
                ps = [g * UB + u for u in range(UB)]
                first = [products(p) for p in ps]
                points = [pointwise(p, *x[2:]) for p, x in zip(ps, first)]
                last = [back(p, *x[:2], *y) for p, x, y in zip(ps, first, points)]
                for p, x in zip(ps, last):
                    finish(p, *x)
                return 0
            lax.fori_loop(0, pairs // UB, some, 0)

        by_count(lo, hi, nblk, body)
        return 0
    lax.fori_loop(0, nblk, q_block, 0)
    dk_ref[...] = dkacc[...].astype(bf16)
    dv_ref[...] = dvacc[...].astype(bf16)
    turn = (
        lax.broadcasted_iota(jnp.int32, (BLOCK, BLOCK), 0) + lax.broadcasted_iota(jnp.int32, (BLOCK, BLOCK), 1)
        == BLOCK - 1
    ).astype(f32).astype(bf16)
    for p in range(pairs):
        for d in range(NEAR):
            t = gacc[p, d]
            if 0 < d < NEAR - 1:
                hi = t.astype(bf16)
                t = dot_nn(turn, hi) + dot_nn(turn, (t - hi.astype(f32)).astype(bf16))
            for u in range(2):
                s = jnp.concatenate([t[:, u * LANES : (u + 1) * LANES], jnp.zeros((BLOCK, LANES), f32)], 1)
                if 0 < d < NEAR - 1:
                    s = pltpu.roll(s, 0, 1, stride=1, stride_axis=0)
                at = d * 16 + 2 * p + u
                gsum_ref[at : at + 1, :] = jnp.sum(s, 0, keepdims=True)


def two(x):
    a = x.astype(jnp.bfloat16)
    return a, (x - a.astype(jnp.float32)).astype(jnp.bfloat16)


def row_pieces(row):
    place = lax.broadcasted_iota(jnp.int32, (16, row.shape[1]), 0)
    a, b, c = [x.astype(jnp.float32) for x in split3(row)]
    return jnp.where(place == 0, a, jnp.where(place == 1, b, jnp.where(place == 2, c, 0.0))).astype(jnp.bfloat16)


def each(count, body):
    if count <= 8:
        for e in range(count):
            body(e)
    else:
        def step(e, _):
            body(e)
            return 0
        lax.fori_loop(0, count, step, 0)


def slot_hot(slot_row, e, slot_rows):
    place = lax.broadcasted_iota(jnp.int32, (slot_rows, slot_row.shape[1]), 0) + e * slot_rows
    return (place == slot_row).astype(jnp.float32).astype(jnp.bfloat16)


def slots_kernel(routes_ref, rows_hbm, slot_ref, out_hbm, rows_ref, out_ref, sem, sems, *, experts, capacity, slot_rows):
    f32, bf16 = jnp.float32, jnp.bfloat16
    load = pltpu.make_async_copy(rows_hbm, rows_ref, sem)
    load.start()
    tokens = routes_ref.shape[1]
    routes = routes_ref[...]
    pad = max(experts, 16)
    hot = (lax.broadcasted_iota(jnp.int32, (pad, tokens), 0) == routes).astype(f32)
    earlier = (
        lax.broadcasted_iota(jnp.int32, (BLOCK, BLOCK), 0) < lax.broadcasted_iota(jnp.int32, (BLOCK, BLOCK), 1)
    ).astype(f32).astype(bf16)
    seen = jnp.zeros((pad, 1), f32)
    ranks = []
    for c in range(0, tokens, BLOCK):
        part = hot[:, c : c + BLOCK]
        ranks.append(jnp.sum((dot_nn(part.astype(bf16), earlier) + seen) * part, 0, keepdims=True))
        seen = seen + jnp.sum(part, 1, keepdims=True)
    rank = jnp.concatenate(ranks, 1).astype(jnp.int32)
    slot = jnp.where(rank < capacity, routes * slot_rows + rank, -1)
    slot_ref[...] = jnp.broadcast_to(slot, slot_ref.shape)

    def pair(e):
        rows = dot_nn(slot_hot(slot, e, 2 * slot_rows), rows_ref[...]).astype(bf16)
        out_ref[pl.ds(2 * e, 2)] = rows.reshape(2, slot_rows, rows.shape[1])
        store(e).start()

    def store(e):
        both = pl.ds(2 * e, 2)
        return pltpu.make_async_copy(out_ref.at[both], out_hbm.at[both], sems.at[e])

    def stored(e):
        store(e).wait()
    load.wait()
    each(experts // 2, pair)
    each(experts // 2, stored)


def first_slots(routes_row, rows, experts, capacity, slot_rows):
    tokens, width = rows.shape
    vmem = pl.BlockSpec(memory_space=pltpu.VMEM)
    return pl.pallas_call(
        functools.partial(slots_kernel, experts=experts, capacity=capacity, slot_rows=slot_rows),
        out_shape=(
            jax.ShapeDtypeStruct((8, tokens), jnp.int32),
            jax.ShapeDtypeStruct((experts, slot_rows, width), jnp.bfloat16),
        ),
        in_specs=[vmem, pl.BlockSpec(memory_space=pl.ANY)],
        out_specs=(vmem, pl.BlockSpec(memory_space=pl.ANY)),
        scratch_shapes=[
            pltpu.VMEM((tokens, width), jnp.bfloat16), pltpu.VMEM((experts, slot_rows, width), jnp.bfloat16),
            pltpu.SemaphoreType.DMA, pltpu.SemaphoreType.DMA((experts // 2,)),
        ],
        compiler_params=pltpu.CompilerParams(vmem_limit_bytes=63 << 20),
        cost_estimate=pl.CostEstimate(
            flops=2 * experts * slot_rows * tokens * width, bytes_accessed=4 << 20, transcendentals=0
        ),
    )(routes_row, rows)


def fill_masks(segment_row, qm, km):
    f32, bf16 = jnp.float32, jnp.bfloat16
    lane = lax.broadcasted_iota(jnp.int32, (1, LANES), 1)
    for b in range(qm.shape[0] // BLOCK):
        span = slice(b * BLOCK, (b + 1) * BLOCK)
        hot = (lax.broadcasted_iota(jnp.int32, (LANES, BLOCK), 0) == segment_row[:, span]).astype(f32).T
        qm[span, :] = (hot * masked_score).astype(bf16)
        km[span, :] = jnp.where(lane < 8, 1.0 - hot, 0.0).astype(bf16)


def fill_diag(grid_ref, diag, heads):
    bf16 = jnp.bfloat16
    buckets = grid_ref.shape[0]
    relative = 256 - lax.broadcasted_iota(jnp.int32, (buckets, 4 * LANES), 1)
    hot = (lax.broadcasted_iota(jnp.int32, (buckets, 4 * LANES), 0) == bucket_of(relative))
    hot = hot.astype(jnp.float32).astype(bf16)
    grid = jnp.concatenate(
        [grid_ref[...], jnp.zeros((buckets, LANES - heads), jnp.float32)], 1
    ).T[:16]
    total = None
    for piece in split3(grid):
        term = dot_nn(piece, hot)
        total = term if total is None else total + term
    diag[...] = total


def front_kernel(
    lo_ref, hi_ref, tokens, segment_row, slot_ref, routes_ref, gain_one, gain_two, wq, wk, wv, wo, grid_ref, router_t,
    q_ref, k_ref, kt_ref, v_ref, o_ref, lse_ref, middle_ref, probs_ref, xs_ref, gs_ref,
    vt_ref, qm_ref, km_ref, diag, bias, hidden, *, experts, slot_rows, scale,
):
    f32, bf16 = jnp.float32, jnp.bfloat16
    length, width = tokens.shape
    pairs = width // LANES
    nblk = length // BLOCK
    heads = grid_ref.shape[1]
    low = lax.broadcasted_iota(jnp.int32, (1, LANES), 1) < 64
    step = 256

    for b in range(length // step):
        span = slice(b * step, (b + 1) * step)
        x = tokens[span, :].astype(f32)
        inverse = lax.rsqrt(jnp.mean(x * x, 1, keepdims=True) + epsilon)
        normed = (x * inverse * gain_one[...]).astype(bf16)
        q_ref[span, :] = (dot_nn(normed, wq[...]).astype(bf16).astype(f32) * scale).astype(bf16)
        k = dot_nn(normed, wk[...]).astype(bf16)
        k_ref[span, :] = k
        kt_ref[:, span] = k.T
        v = dot_nn(normed, wv[...]).astype(bf16)
        v_ref[span, :] = v
        vt_ref[:, span] = v.T
    fill_masks(segment_row[...], qm_ref, km_ref)
    fill_diag(grid_ref, diag, heads)
    fill_bias(diag, bias, pairs)
    attend(lo_ref, hi_ref, q_ref, k_ref, vt_ref, qm_ref, km_ref, bias, o_ref, lse_ref)

    rw = two(router_t[...])
    routes = routes_ref[...]
    pad = router_t.shape[0]
    place = lax.broadcasted_iota(jnp.int32, (pad, step), 0)
    gates = []
    for b in range(length // step):
        span = slice(b * step, (b + 1) * step)
        middle = tokens[span, :].astype(f32) + dot_nn(o_ref[span, :], wo[...])
        middle_ref[span, :] = middle
        inverse = lax.rsqrt(jnp.mean(middle * middle, 1, keepdims=True) + epsilon)
        parts = two(middle * inverse * gain_two[...])
        hidden[span, :] = parts[0]
        logits = dot_nt(rw[0], parts[0]) + dot_nt(rw[0], parts[1]) + dot_nt(rw[1], parts[0])
        logits = jnp.where(place < experts, logits, -1e30)
        powers = jnp.exp(logits - jnp.max(logits, 0, keepdims=True))
        probs = powers / jnp.sum(powers, 0, keepdims=True)
        probs_ref[:, span] = probs
        gates.append(jnp.sum(jnp.where(place == routes[:, span], probs, 0.0), 0, keepdims=True))
    gates = row_pieces(jnp.concatenate(gates, 1))
    slot = slot_ref[0:1, :]
    lanes = gs_ref.shape[2]

    def one(e):
        hot = slot_hot(slot, e, slot_rows)
        xs_ref[e] = dot_nn(hot, hidden[...]).astype(bf16)
        if lanes > slot_rows:
            hot = jnp.concatenate([hot, jnp.zeros((lanes - slot_rows, length), bf16)], 0)
        row = jnp.sum(dot_nt(gates, hot), 0, keepdims=True)
        gs_ref[e] = jnp.broadcast_to(row, gs_ref.shape[1:])
    each(experts, one)


def front(lo, hi, tokens, segments, slot, routes_row, gain_one, gain_two, wq, wk, wv, wo, grid, router_t, experts, slot_rows, scale):
    length, width = tokens.shape
    heads = grid.shape[1]
    pairs = width // LANES
    nblk = length // BLOCK
    lanes = (slot_rows + LANES - 1) // LANES * LANES
    smem = pl.BlockSpec(memory_space=pltpu.SMEM)
    vmem = pl.BlockSpec(memory_space=pltpu.VMEM)
    f32, bf16 = jnp.float32, jnp.bfloat16
    shape = jax.ShapeDtypeStruct
    act = shape((length, width), bf16)
    return pl.pallas_call(
        functools.partial(front_kernel, experts=experts, slot_rows=slot_rows, scale=scale),
        out_shape=(
            act, act, shape((width, length), bf16), act, act,
            shape((nblk, 8, 2 * LANES), f32), shape((length, width), f32),
            shape((router_t.shape[0], length), f32),
            shape((experts, slot_rows, width), bf16), shape((experts, 8, lanes), f32),
        ),
        in_specs=[smem] * 2 + [vmem] * 12,
        out_specs=(vmem,) * 10,
        scratch_shapes=[
            pltpu.VMEM((width, length), bf16),
            pltpu.VMEM((length, LANES), bf16),
            pltpu.VMEM((length, LANES), bf16),
            pltpu.VMEM((16, 4 * LANES), f32),
            pltpu.VMEM((pairs, NEAR, BLOCK, 2 * LANES), f32),
            pltpu.VMEM((length, width), bf16),
        ],
        compiler_params=pltpu.CompilerParams(vmem_limit_bytes=63 << 20),
        cost_estimate=pl.CostEstimate(
            flops=4 * length * length * width + 12 * length * width * width, bytes_accessed=20 << 20,
            transcendentals=length * length * heads,
        ),
    )(lo, hi, tokens, segments, slot, routes_row, gain_one, gain_two, wq, wk, wv, wo, grid, router_t)


def bucket_sums(gsum_ref):
    bf16 = jnp.bfloat16
    total = jnp.zeros((16, LANES), jnp.float32)
    lane = lax.broadcasted_iota(jnp.int32, (2 * LANES, LANES), 1)
    for d in range(NEAR):
        relative = (d - 2) * BLOCK + BLOCK - 1 - lax.broadcasted_iota(jnp.int32, (2 * LANES, LANES), 0)
        bucket = 15 if d == 0 else 31 if d == NEAR - 1 else bucket_of(relative)
        hot = (lane == bucket).astype(jnp.float32).astype(bf16)
        for piece in split3(gsum_ref[d * 16 : (d + 1) * 16, :]):
            total = total + dot_nn(piece, hot)
    return total


def small_shape(width, experts):
    return (16 + width // LANES * experts + 16, LANES)


def back_kernel(
    lo_ref, hi_ref, home, home_gate, slot_ref, routes_ref, probs_ref, middle_ref, cotangent, segment_row, gain_two,
    wo, router_t, grid_ref, lse_ref, q_hbm, k_hbm, kt_hbm, v_hbm, o_hbm,
    dq_ref, dk_ref, dv_ref, middle_grad_hbm, small,
    q_ref, k_ref, kt_ref, v_ref, o_ref, middle_grad,
    do_ref, qm_ref, km_ref, diag, bias, gacc, dkacc, dvacc, logit, gsum_ref, sems,
    *, experts, slot_rows, scale,
):
    f32, bf16 = jnp.float32, jnp.bfloat16
    length, width = middle_ref.shape
    pairs = width // LANES
    pad = router_t.shape[0]
    heads = grid_ref.shape[1]
    slot = slot_ref[0:1, :]
    loads = [
        pltpu.make_async_copy(there, here, sems.at[i])
        for i, (there, here) in enumerate(zip(
            (q_hbm, k_hbm, kt_hbm, v_hbm, o_hbm), (q_ref, k_ref, kt_ref, v_ref, o_ref)))
    ]
    for load in loads:
        load.start()

    if experts <= 8:
        total = jnp.zeros((16, length), f32)
        for e in range(experts):
            total = total + dot_nn(row_pieces(home_gate[e, 0:1, :])[:, :slot_rows], slot_hot(slot, e, slot_rows))
    else:
        def add(e, total):
            return total + dot_nn(row_pieces(home_gate[e, 0:1, :])[:, :slot_rows], slot_hot(slot, e, slot_rows))
        total = lax.fori_loop(0, experts, add, jnp.zeros((16, length), f32))
    gate_grad = jnp.sum(total, 0, keepdims=True)
    place = lax.broadcasted_iota(jnp.int32, (pad, length), 0)
    hot = place == routes_ref[...]
    probs = probs_ref[...]
    gate = jnp.sum(jnp.where(hot, probs, 0.0), 0, keepdims=True)
    logit[...] = probs * (jnp.where(hot, gate_grad, 0.0) - gate * gate_grad)
    rw = two(router_t[...])
    stacked = jnp.concatenate([rw[0], rw[1], rw[0]], 0)
    slots = experts * slot_rows
    router_sum = jnp.zeros((pad, width), f32)
    gain_sum = jnp.zeros((1, width), f32)
    step = 256
    for b in range(length // step):
        span = slice(b * step, (b + 1) * step)
        hots = []
        for c in range(b * step, (b + 1) * step, BLOCK):
            column = jnp.broadcast_to(slot[:, c : c + BLOCK].astype(f32), (BLOCK, BLOCK)).T
            first = lax.broadcasted_iota(jnp.int32, (BLOCK, LANES), 1).astype(f32)
            hots.append(jnp.concatenate(
                [(column == first + float(s)).astype(f32).astype(bf16) for s in range(0, slots, LANES)], 1))
        spread = jnp.concatenate(hots, 0)
        hidden_grad = dot_nn(spread, home[...].reshape(slots, width))
        lg = two(logit[:, span])
        hidden_grad = hidden_grad + matmul_tn(jnp.concatenate([lg[0], lg[0], lg[1]], 0), stacked)
        middle = middle_ref[span, :]
        inverse = lax.rsqrt(jnp.mean(middle * middle, 1, keepdims=True) + epsilon)
        unit = middle * inverse
        hidden = two(unit * gain_two[...])
        both = dot_nn(jnp.concatenate(lg, 0), hidden[0])
        router_sum = router_sum + (both[:pad] + both[pad:] + dot_nn(lg[0], hidden[1]))
        gain_sum = gain_sum + jnp.sum(hidden_grad * unit, 0, keepdims=True)
        scaled = hidden_grad * gain_two[...]
        mean = jnp.mean(scaled * middle, 1, keepdims=True)
        grad = cotangent[span, :].astype(f32) + inverse * (scaled - unit * (inverse * mean))
        middle_grad[span, :] = grad
        do_ref[span, :] = matmul_nt(grad.astype(bf16), wo[...]).astype(bf16)
    store = pltpu.make_async_copy(middle_grad, middle_grad_hbm, sems.at[5])
    store.start()
    small[...] = jnp.zeros_like(small)
    chunks = width // LANES
    for c in range(chunks):
        cols = slice(c * LANES, (c + 1) * LANES)
        small[8 + c : 9 + c, :] = gain_sum[:, cols]
        small[16 + c * experts : 16 + (c + 1) * experts, :] = router_sum[:experts, cols]

    fill_masks(segment_row[...], qm_ref, km_ref)
    fill_diag(grid_ref, diag, heads)
    fill_bias(diag, bias, pairs)
    for load in loads:
        load.wait()
    attend_back(
        lo_ref, hi_ref, q_ref, k_ref, kt_ref, v_ref, lse_ref, do_ref, o_ref, qm_ref, km_ref, bias,
        dq_ref, dk_ref, dv_ref, gsum_ref, gacc, dkacc, dvacc, scale,
    )
    at = 16 + chunks * experts
    small[at : at + 16, :] = bucket_sums(gsum_ref)
    store.wait()


def back(lo, hi, home, home_gate, slot, routes_row, probs, middle, cotangent, segments, gain_two, wo, router_t, grid,
         q, k, kt, v, lse, o, experts, slot_rows, scale):
    length, width = middle.shape
    heads = grid.shape[1]
    pairs = width // LANES
    smem = pl.BlockSpec(memory_space=pltpu.SMEM)
    vmem = pl.BlockSpec(memory_space=pltpu.VMEM)
    f32, bf16 = jnp.float32, jnp.bfloat16
    shape = jax.ShapeDtypeStruct
    act = shape((length, width), bf16)
    anywhere = pl.BlockSpec(memory_space=pl.ANY)
    return pl.pallas_call(
        functools.partial(back_kernel, experts=experts, slot_rows=slot_rows, scale=scale),
        out_shape=(act, act, act, shape((length, width), f32), shape(small_shape(width, experts), f32)),
        in_specs=[smem] * 2 + [vmem] * 13 + [anywhere] * 5,
        out_specs=(vmem, vmem, vmem, anywhere, vmem),
        scratch_shapes=[
            pltpu.VMEM((length, width), bf16),
            pltpu.VMEM((length, width), bf16),
            pltpu.VMEM((width, length), bf16),
            pltpu.VMEM((length, width), bf16),
            pltpu.VMEM((length, width), bf16),
            pltpu.VMEM((length, width), f32),
            pltpu.VMEM((length, width), bf16),
            pltpu.VMEM((length, LANES), bf16),
            pltpu.VMEM((length, LANES), bf16),
            pltpu.VMEM((16, 4 * LANES), f32),
            pltpu.VMEM((pairs, NEAR, BLOCK, 2 * LANES), f32),
            pltpu.VMEM((pairs, NEAR, BLOCK, 2 * LANES), f32),
            pltpu.VMEM((length, width), f32),
            pltpu.VMEM((length, width), f32),
            pltpu.VMEM((router_t.shape[0], length), f32),
            pltpu.VMEM((NEAR * 16, 2 * LANES), f32),
            pltpu.SemaphoreType.DMA((6,)),
        ],
        compiler_params=pltpu.CompilerParams(vmem_limit_bytes=63 << 20),
        cost_estimate=pl.CostEstimate(
            flops=10 * length * length * width + 6 * length * width * width, bytes_accessed=30 << 20,
            transcendentals=length * length * heads,
        ),
    )(lo, hi, home, home_gate, slot, routes_row, probs, middle, cotangent, segments, gain_two, wo, router_t, grid,
      lse, q, k, kt, v, o)


def finish_kernel(
    sum_q, sum_k, sum_v, sum_o, keep, passed, returned_in, middle_in, token_in, small, slot_ref, routes_ref, probs_ref,
    mixed_out, token_out, gain_one, gain_two, grad_q, grad_k, grad_v, grad_o, table_t, router_t, grad_in, grad_out,
    low, wide, returned, middle, mixed, token, load_sem, store_sem, copy_sem, mix_sem, *, experts,
):
    f32 = jnp.float32
    sources = (sum_o, sum_v, sum_k, sum_q, keep.at[0], keep.at[1], passed.at[0], passed.at[1])
    targets = (grad_o, grad_v, grad_k, grad_q, grad_in, grad_out)
    width = sum_q.shape[0]
    rows = 256
    spans = [pl.ds(r, rows) for r in range(0, width, rows)]
    fetches = [
        pltpu.make_async_copy(x, y, copy_sem.at[i])
        for i, (x, y) in enumerate(((returned_in, returned), (middle_in, middle), (token_in, token)))
    ]
    copies = [pltpu.make_async_copy(token, token_out, copy_sem.at[3])]
    length = middle.shape[0]
    slots = returned.shape[0]
    for c in range(0, length, BLOCK):
        rows_c = pl.ds(c, BLOCK)
        copies.append(pltpu.make_async_copy(mixed.at[rows_c], mixed_out.at[rows_c], mix_sem.at[c // BLOCK]))
    pad = probs_ref.shape[0]
    hot = lax.broadcasted_iota(jnp.int32, (pad, length), 0) == routes_ref[...]
    gate_row = jnp.sum(jnp.where(hot, probs_ref[...], 0.0), 0, keepdims=True)

    def mix(c):
        at = slice(c, c + BLOCK)
        column = jnp.broadcast_to(slot_ref[0:1, at].astype(f32), (BLOCK, BLOCK)).T
        first = lax.broadcasted_iota(jnp.int32, (BLOCK, LANES), 1).astype(f32)
        spread = jnp.concatenate(
            [(column == first + float(s)).astype(f32).astype(jnp.bfloat16) for s in range(0, slots, LANES)], 1)
        rows_back = dot_nn(spread, returned[...])
        gate = jnp.broadcast_to(gate_row[:, at], (BLOCK, BLOCK)).T
        gate = jnp.concatenate([gate] * (width // LANES), 1)
        mixed[at, :] = (middle[at, :] + gate * rows_back).astype(jnp.bfloat16)

    loads = [
        [pltpu.make_async_copy(x.at[span], low.at[i, span], load_sem.at[i, j]) for j, span in enumerate(spans)]
        for i, x in enumerate(sources)
    ]
    stores = [
        [pltpu.make_async_copy(wide.at[i, span], x.at[span], store_sem.at[i, j]) for j, span in enumerate(spans)]
        for i, x in enumerate(targets)
    ]
    for i in range(4):
        for load in loads[i]:
            load.start()
    for fetch in fetches:
        fetch.start()
    for i in range(4, 8):
        for load in loads[i]:
            load.start()
    chunks = width // LANES
    gain_one[...] = jnp.concatenate([small[c : c + 1, :] for c in range(chunks)], 1).reshape(width)
    gain_two[...] = jnp.concatenate([small[8 + c : 9 + c, :] for c in range(chunks)], 1).reshape(width)
    for c in range(chunks):
        router_t[:, c * LANES : (c + 1) * LANES] = small[16 + c * experts : 16 + (c + 1) * experts, :]
    at = 16 + chunks * experts
    heads, buckets = table_t.shape
    table_t[...] = small[at : at + heads, :buckets]
    for i in range(4):
        for j, span in enumerate(spans):
            loads[i][j].wait()
            wide[i, span, :] = low[i, span, :].astype(f32)
            stores[i][j].start()
    fetches[2].wait()
    copies[0].start()
    for i in (4, 5):
        for j, span in enumerate(spans):
            loads[i][j].wait()
            loads[i + 2][j].wait()
            wide[i, span, :] = low[i, span, :].astype(f32) + low[i + 2, span, :].astype(f32)
            stores[i][j].start()
    for fetch in fetches[:2]:
        fetch.wait()
    for c in range(0, length, BLOCK):
        mix(c)
        copies[1 + c // BLOCK].start()
    for i in range(6):
        for store in stores[i]:
            store.wait()
    for copy in copies:
        copy.wait()


def finish(sums, keep, passed, returned, middle, token_grad, small, slot, routes_row, probs, grid_shape, experts):
    f32, bf16 = jnp.float32, jnp.bfloat16
    width = sums[0].shape[0]
    vmem = pl.BlockSpec(memory_space=pltpu.VMEM)
    anywhere = pl.BlockSpec(memory_space=pl.ANY)
    shape = jax.ShapeDtypeStruct
    act = shape(middle.shape, bf16)
    square, row = shape((width, width), f32), shape((width,), f32)
    blocks = width // 256
    return pl.pallas_call(
        functools.partial(finish_kernel, experts=experts),
        out_shape=(act, act, row, row, square, square, square, square, shape(grid_shape[::-1], f32),
                   shape((experts, width), f32), square, square),
        in_specs=[anywhere] * 9 + [vmem] * 4,
        out_specs=(anywhere,) * 2 + (vmem, vmem) + (anywhere,) * 4 + (vmem, vmem) + (anywhere,) * 2,
        scratch_shapes=[
            pltpu.VMEM((8, width, width), bf16), pltpu.VMEM((6, width, width), f32),
            pltpu.VMEM(returned.shape, bf16), pltpu.VMEM(middle.shape, f32),
            pltpu.VMEM(middle.shape, bf16), pltpu.VMEM(middle.shape, bf16),
            pltpu.SemaphoreType.DMA((8, blocks)), pltpu.SemaphoreType.DMA((6, blocks)),
            pltpu.SemaphoreType.DMA((4,)), pltpu.SemaphoreType.DMA((middle.shape[0] // BLOCK,)),
        ],
        compiler_params=pltpu.CompilerParams(vmem_limit_bytes=63 << 20),
        cost_estimate=pl.CostEstimate(flops=0, bytes_accessed=30 << 20, transcendentals=0),
    )(*sums, keep, passed, returned, middle, token_grad, small, slot, routes_row, probs)


def gelu_parts(v):
    mag = jnp.abs(v)
    t = 1.0 / (1.0 + (0.3275911 * 0.7071067811865476) * mag)
    poly = t * (0.127414796 + t * (-0.142248368 + t * (0.7107068705 + t * (-0.7265760135 + t * 0.5307027145))))
    gauss = jnp.exp(-0.5 * v * v)
    tail = poly * gauss
    phi = jnp.where(v < 0, tail, 1.0 - tail)
    return v * phi, phi + v * gauss * 0.3989422804014327


def flip_bits(index, mask, count):
    out = 0
    bit = 1
    while bit < count:
        a, b = (index // bit) % 2, (mask // bit) % 2
        out = out + bit * (a + b - 2 * a * b)
        bit *= 2
    return out


def ffn_kernel(
    xs, gs, g, win_hbm, wout_hbm,
    home, home_gate, produced, keep, give,
    win, wout, xr, gr, act, pg, gated, igs, ggs, dws, dwr, stage,
    wsem, own_sem, psem, ksem, xsend, xrecv, gsend, grecv, isend, irecv, qsend, qrecv, dsend, drecv,
    *, groups, dp_size, tiles,
):
    f32, bf16 = jnp.float32, jnp.bfloat16
    me = lax.axis_index("expert")
    dp = lax.axis_index("dp")
    core = dp % 2
    sibling = dp + 1 - 2 * core
    half_of = dp // 2
    rows = xs.shape[1]
    width = xs.shape[2]
    hidden = win.shape[1]
    tile = hidden // tiles
    lanes = gs.shape[2]

    def there(peer):
        return (dp, peer)

    load_in = pltpu.make_async_copy(win_hbm, win, wsem.at[0])
    load_out = pltpu.make_async_copy(wout_hbm, wout, wsem.at[1])
    load_in.start()
    load_out.start()
    load_g = pltpu.make_async_copy(g, gated, wsem.at[2])
    load_g.start()

    barrier = pltpu.get_barrier_semaphore()

    def greet(s, _):
        pl.semaphore_signal(
            barrier, inc=1, device_id=there(flip_bits(me, s, groups)), device_id_type=pl.DeviceIdType.MESH
        )
        return 0
    lax.fori_loop(1, groups, greet, 0)
    pl.semaphore_signal(barrier, inc=1, device_id=(sibling, me), device_id_type=pl.DeviceIdType.MESH)
    pl.semaphore_wait(barrier, groups)

    def x_copy(peer, slot):
        return pltpu.make_async_remote_copy(
            src_ref=xs.at[peer], dst_ref=xr.at[slot], send_sem=xsend.at[peer], recv_sem=xrecv.at[slot],
            device_id=there(peer), device_id_type=pl.DeviceIdType.MESH)

    def g_copy(peer, slot):
        return pltpu.make_async_remote_copy(
            src_ref=gs.at[peer], dst_ref=gr.at[slot], send_sem=gsend.at[peer], recv_sem=grecv.at[slot],
            device_id=there(peer), device_id_type=pl.DeviceIdType.MESH)

    def i_copy(peer, slot):
        return pltpu.make_async_remote_copy(
            src_ref=igs.at[peer], dst_ref=home.at[slot], send_sem=isend.at[peer], recv_sem=irecv.at[slot],
            device_id=there(peer), device_id_type=pl.DeviceIdType.MESH)

    def q_copy(peer, slot):
        return pltpu.make_async_remote_copy(
            src_ref=ggs.at[peer], dst_ref=home_gate.at[slot], send_sem=qsend.at[peer], recv_sem=qrecv.at[slot],
            device_id=there(peer), device_id_type=pl.DeviceIdType.MESH)

    def send(i, _):
        odd = (i - 1) % 2
        s = (1 - odd) * (groups - 1 - (i - 1) // 2) + odd * (i // 2)
        peer = flip_bits(me, s, groups)
        x_copy(peer, me).start()
        g_copy(peer, me).start()
        return 0
    lax.fori_loop(1, groups, send, 0)
    own_x = pltpu.make_async_copy(xs.at[me], xr.at[me], own_sem.at[0])
    own_g = pltpu.make_async_copy(gs.at[me], gr.at[me], own_sem.at[1])
    own_x.start()
    own_g.start()
    load_in.wait()
    load_out.wait()
    load_g.wait()

    spot = (
        lax.broadcasted_iota(jnp.int32, (rows, lanes), 0)
        == lax.broadcasted_iota(jnp.int32, (rows, lanes), 1)
    )

    def work(base):
        both = pl.ds(base, 2)
        x = xr[both].reshape(2 * rows, width)
        place = pl.ds(pl.multiple_of(base * rows, rows), 2 * rows)
        gg = gated[place, :]
        gate = jnp.concatenate(
            [jnp.sum(jnp.where(spot, gr[base + u, 0:1, :], 0.0), 1, keepdims=True) for u in range(2)], 0
        )
        gated[place, :] = (gate * gg.astype(f32)).astype(bf16)
        total = jnp.zeros((2 * rows, width), f32)
        gate_grad = jnp.zeros((2 * rows, 1), f32)

        def columns(t):
            return slice(t * tile, (t + 1) * tile)

        def products(t):
            return matmul(x, win[:, columns(t)]), matmul_nt(gg, wout[columns(t), :])

        ahead = products(0)
        for t in range(tiles):
            pre, out_grad = ahead
            if t + 1 < tiles:
                ahead = products(t + 1)
            value, slope = gelu_parts(pre)
            act[place, columns(t)] = value.astype(bf16)
            gate_grad = gate_grad + jnp.sum(value * out_grad, 1, keepdims=True)
            low = (gate * out_grad * slope).astype(bf16)
            pg[place, columns(t)] = low
            total = total + matmul_nt(low, win[:, columns(t)])
        igs[both] = total.astype(bf16).reshape(2, rows, width)
        for u in range(2):
            row = jnp.sum(jnp.where(spot, gate_grad[u * rows : (u + 1) * rows], 0.0), 0, keepdims=True)
            ggs[base + u] = jnp.broadcast_to(row, ggs.shape[1:])

    def arrive(peer):
        x_copy(peer, peer).wait_recv()
        g_copy(peer, peer).wait_recv()

    def back(peer):
        i_copy(peer, me).start()
        q_copy(peer, me).start()

    own_x.wait()
    own_g.wait()
    arrive(flip_bits(me, 1, groups))
    work(me - me % 2)
    own_i = pltpu.make_async_copy(igs.at[me], home.at[me], own_sem.at[0])
    own_q = pltpu.make_async_copy(ggs.at[me], home_gate.at[me], own_sem.at[1])
    own_i.start()
    own_q.start()
    back(flip_bits(me, 1, groups))

    def chunk(j, _):
        peer = flip_bits(me, 2 * j, groups)
        other = flip_bits(me, 2 * j + 1, groups)
        arrive(peer)
        arrive(other)
        work(peer - peer % 2)
        back(peer)
        back(other)
        return 0
    lax.fori_loop(1, groups // 2, chunk, 0)

    def d_copy(k):
        return pltpu.make_async_remote_copy(
            src_ref=dws.at[k % 2], dst_ref=dwr.at[k], send_sem=dsend.at[k], recv_sem=drecv.at[k],
            device_id=(sibling, me), device_id_type=pl.DeviceIdType.MESH)

    part = hidden // dp_size
    flat = groups * rows
    items = [(which, half) for half in (1 - half_of, half_of) for which in range(2)]

    def grad(which, quarter):
        span = pl.ds(pl.multiple_of(quarter * part, part), part)
        if which == 0:
            return matmul_tn(xr[...].reshape(flat, width), pg[:, span])
        return matmul_tn(act[:, span], gated[...])

    for k, (which, half) in enumerate(items):
        if k >= 2:
            d_copy(k - 2).wait_send()
        dws[k % 2] = grad(which, 2 * half + 1 - core).astype(bf16)
        d_copy(k).start()
    outs = [
        pltpu.make_async_copy(dwr.at[0], give.at[0], ksem.at[0]),
        pltpu.make_async_copy(dwr.at[1], give.at[1], ksem.at[1]),
        pltpu.make_async_copy(dwr.at[2], keep.at[0], ksem.at[2]),
        pltpu.make_async_copy(dwr.at[3], keep.at[1], ksem.at[3]),
    ]
    for k, (which, half) in enumerate(items):
        local = grad(which, 2 * half + core)
        d_copy(k).wait_recv()
        dwr[k] = (local + dwr[k].astype(f32)).astype(bf16)
        outs[k].start()

    span = stage.shape[1]
    copies = []
    for b in range(flat // span):
        if b >= 2:
            copies[b - 2].wait()
        stage[b % 2] = matmul(act[b * span : (b + 1) * span, :], wout[...]).astype(bf16)
        copy = pltpu.make_async_copy(stage.at[b % 2], produced.at[pl.ds(b * span, span)], psem.at[b % 2])
        copy.start()
        copies.append(copy)
    for copy in copies[-2:] + outs:
        copy.wait()
    own_i.wait()
    own_q.wait()
    for k in (2, 3):
        d_copy(k).wait_send()

    def finish(s, _):
        peer = flip_bits(me, s, groups)
        x_copy(peer, me).wait_send()
        g_copy(peer, me).wait_send()
        i_copy(peer, me).wait_send()
        q_copy(peer, me).wait_send()
        i_copy(peer, peer).wait_recv()
        q_copy(peer, peer).wait_recv()
        return 0
    lax.fori_loop(1, groups, finish, 0)


def ffn(xs, gs, g, weight_in, weight_out, groups, dp_size, tiles=6):
    f32, bf16 = jnp.float32, jnp.bfloat16
    _, rows, width = xs.shape
    hidden = weight_in.shape[1]
    lanes = gs.shape[2]
    part = hidden // dp_size
    anywhere = pl.BlockSpec(memory_space=pl.ANY)
    sem = pltpu.SemaphoreType.DMA
    flat = groups * rows
    shape = jax.ShapeDtypeStruct
    return pl.pallas_call(
        functools.partial(ffn_kernel, groups=groups, dp_size=dp_size, tiles=tiles),
        out_shape=(
            shape((groups, rows, width), bf16),
            shape((groups, 8, lanes), f32),
            shape((flat, width), bf16),
            shape((2, width, part), bf16),
            shape((2, width, part), bf16),
        ),
        in_specs=[anywhere] * 5,
        out_specs=(anywhere,) * 5,
        scratch_shapes=[
            pltpu.VMEM((width, hidden), bf16),
            pltpu.VMEM((hidden, width), bf16),
            pltpu.VMEM((groups, rows, width), bf16),
            pltpu.VMEM((groups, 8, lanes), f32),
            pltpu.VMEM((flat, hidden), bf16),
            pltpu.VMEM((flat, hidden), bf16),
            pltpu.VMEM((flat, width), bf16),
            pltpu.VMEM((groups, rows, width), bf16),
            pltpu.VMEM((groups, 8, lanes), f32),
            pltpu.VMEM((2, width, part), bf16),
            pltpu.VMEM((4, width, part), bf16),
            pltpu.VMEM((2, flat // 8, width), bf16),
            sem((3,)), sem((2,)), sem((2,)), sem((4,)),
            sem((groups,)), sem((groups,)), sem((groups,)), sem((groups,)),
            sem((groups,)), sem((groups,)), sem((groups,)), sem((groups,)),
            sem((4,)), sem((4,)),
        ],
        compiler_params=pltpu.CompilerParams(
            collective_id=1, has_side_effects=True, vmem_limit_bytes=62 << 20
        ),
        cost_estimate=pl.CostEstimate(
            flops=12 * flat * width * hidden, bytes_accessed=40 << 20, transcendentals=flat * hidden
        ),
    )(xs, gs, g, weight_in, weight_out)


def fold_steps(rows, cols, bits):
    steps = []
    for bit in bits[:3]:
        rows = rows // 2
        steps.append(((bit,), "half", rows, cols))
    rows, cols = rows // 2, cols // 2
    steps.append((tuple(bits[3:5]), "quad", rows, cols))
    for bit in bits[5:]:
        steps.append(((bit,), "whole", rows, cols))
    return steps


NORM = 3


def reduce_kernel(
    attended_hbm, middle_grad_hbm, tokens_hbm, dv_hbm, dk_hbm, dq_hbm, wq_hbm, wk_hbm, wv_hbm,
    gain, small_in,
    sum_o, sum_v, sum_k, sum_q, token_grad_hbm, small_out,
    attended, middle_grad, tokens, dv, dk, dq, wq, wk, wv,
    token_grad, sums, normed, branch, acc, outbox, inbox, small_box, small_sent, load_sem, store_sem,
    ssend, srecv, tsend, trecv,
    *, dp_bits, expert_bits,
):
    f32, bf16 = jnp.float32, jnp.bfloat16
    dp = lax.axis_index("dp")
    ex = lax.axis_index("expert")
    MESH = pl.DeviceIdType.MESH
    length, width = tokens.shape
    held = (attended, middle_grad, tokens, dv, dk, dq, wq, wk, wv)
    loads = [
        pltpu.make_async_copy(there, here, load_sem.at[i])
        for i, (there, here) in enumerate(zip(
            (attended_hbm, middle_grad_hbm, tokens_hbm, dv_hbm, dk_hbm, dq_hbm, wq_hbm, wk_hbm, wv_hbm), held))
    ]
    first = 4
    for load in loads[:first]:
        load.start()

    def own_bit(bit):
        axis, place = bit
        return (dp // 2 ** place) % 2 if axis == "dp" else (ex // 2 ** place) % 2

    def partner(bits):
        there = [dp, ex]
        for bit in bits:
            there[bit[0] == "expert"] = there[bit[0] == "expert"] + (1 - 2 * own_bit(bit)) * 2 ** bit[1]
        return tuple(there)

    dpb = [("dp", i) for i in range(dp_bits)]
    exb = [("expert", i) for i in range(expert_bits)]
    orders = [
        [dpb[0], dpb[1], exb[0]] + dpb[2:] + exb[1:],
        [dpb[0], exb[0], dpb[1]] + dpb[2:] + exb[1:],
    ]
    every = dpb + exb
    small_count = len(every)

    barrier = pltpu.get_barrier_semaphore()
    greeted = [(bit,) for bit in every] + [tuple(orders[0][3:5])]
    for bits in greeted:
        pl.semaphore_signal(barrier, inc=1, device_id=partner(bits), device_id_type=MESH)
    pl.semaphore_wait(barrier, len(greeted))

    def prepare(i, _):
        span = pl.ds(pl.multiple_of(i * 256, 256), 256)
        x = tokens[span, :].astype(f32)
        inv = lax.rsqrt(jnp.mean(x * x, 1, keepdims=True) + epsilon)
        normed[span, :] = (x * inv * gain[...]).astype(bf16)
        branch[span, :] = middle_grad[span, :].astype(bf16)
        return 0
    for load in loads[:3]:
        load.wait()
    for load in loads[first:]:
        load.start()
    lax.fori_loop(0, length // 256, prepare, 0)

    lefts = (attended, normed, normed, normed)
    rights = (branch, dv, dk, dq)
    streams = []
    for s in range(4):
        row, col, at, sem_at = 0, 0, 0, 0
        plan = []
        for bits, kind, r, c in fold_steps(width, width, orders[s % 2]):
            mine = [own_bit(bit) for bit in bits]
            if kind == "half":
                peers = [bits]
                keep_at = (row + mine[0] * r, col)
                theirs = [(row + (1 - mine[0]) * r, col)]
            elif kind == "quad":
                peers = [bits[:1], bits[1:], bits]
                keep_at = (row + mine[0] * r, col + mine[1] * c)
                theirs = [
                    (row + (1 - mine[0]) * r, col + mine[1] * c),
                    (row + mine[0] * r, col + (1 - mine[1]) * c),
                    (row + (1 - mine[0]) * r, col + (1 - mine[1]) * c),
                ]
            else:
                peers, keep_at, theirs = [bits], (row, col), [(row, col)]
            plan.append((peers, kind, r, c, at, keep_at, theirs, sem_at))
            row, col = keep_at
            at += r * len(peers)
            sem_at += len(peers)
        streams.append(plan)
    count = len(streams[0])
    sems = ssend.shape[1] // 2

    def rs_copy(s, k, i):
        peers, kind, r, c, at, _, _, sem_at = streams[s][k]
        box = pl.ds(at + i * r, r)
        return pltpu.make_async_remote_copy(
            src_ref=outbox.at[s, box, pl.ds(0, c)], dst_ref=inbox.at[s, box, pl.ds(0, c)],
            send_sem=ssend.at[s, sem_at + i], recv_sem=srecv.at[s, sem_at + i],
            device_id=partner(peers[i]), device_id_type=MESH)

    def aligned(at):
        row, col = at
        row = pl.multiple_of(row, 16) if not isinstance(row, int) else row
        col = pl.multiple_of(col, 128) if not isinstance(col, int) else col
        return row, col

    def block(s, at, r, c):
        row, col = aligned(at)
        return sums.at[s, pl.ds(row, r), pl.ds(col, c)]

    def ag_copy(s, k, i, incoming):
        peers, kind, r, c, _, keep_at, theirs, sem_at = streams[s][k]
        ref = block(s, theirs[i] if incoming else keep_at, r, c)
        return pltpu.make_async_remote_copy(
            src_ref=ref, dst_ref=ref,
            send_sem=ssend.at[s, sems + sem_at + i], recv_sem=srecv.at[s, sems + sem_at + i],
            device_id=partner(peers[i]), device_id_type=MESH)

    half = width // 2
    core = own_bit(dpb[0])

    def grad(s, which):
        span = pl.ds(pl.multiple_of(which * half, half), half)
        return matmul_tn(lefts[s][:, span], rights[s][...])

    def local(s, at, r, c):
        row, col = aligned((at[0] - streams[s][0][5][0], at[1]))
        return acc.at[s, pl.ds(row, r), pl.ds(col, c)]

    def phase(s, k):
        plan = streams[s]
        if k == 0:
            if s > 0:
                loads[2 + s].wait()
            outbox[s, 0:half, :] = grad(s, 1 - core).astype(bf16)
            rs_copy(s, 0, 0).start()
            return
        if k <= count:
            peers, kind, r, c, at, keep_at, _, _ = plan[k - 1]
            view = local(s, keep_at, r, c)
            total = outbox[s, at : at + r, 0:c].astype(f32) if kind == "whole" else view[...]
            for i in range(len(peers)):
                rs_copy(s, k - 1, i).wait_recv()
                total = total + inbox[s, at + i * r : at + (i + 1) * r, 0:c].astype(f32)
            if k < count:
                view[...] = total
                peers, kind, r, c, at, _, theirs, _ = plan[k]
                for i in range(len(peers)):
                    outbox[s, at + i * r : at + (i + 1) * r, 0:c] = local(s, theirs[i], r, c)[...].astype(bf16)
                    rs_copy(s, k, i).start()
                return
            block(s, keep_at, r, c)[...] = total.astype(bf16)
        g = 2 * count - 1 - k
        if k > count and plan[g + 1][1] != "whole":
            for i in range(len(plan[g + 1][0])):
                ag_copy(s, g + 1, i, True).wait_recv()
        if g >= 0 and plan[g][1] != "whole":
            for i in range(len(plan[g][0])):
                ag_copy(s, g, i, False).start()

    gain_row = gain[...]
    rows = 256

    def norm_block(i, gain_grad):
        span = pl.ds(pl.multiple_of(i * rows, rows), rows)
        grads = (
            matmul_nt(dq[span, :], wq[...]) + matmul_nt(dk[span, :], wk[...]) + matmul_nt(dv[span, :], wv[...])
        )
        x = tokens[span, :].astype(f32)
        inv = lax.rsqrt(jnp.mean(x * x, 1, keepdims=True) + epsilon)
        scaled = grads * gain_row
        mean = jnp.sum(scaled * x, 1, keepdims=True) * (1.0 / width)
        part = inv * (scaled - x * (inv * inv * mean))
        token_grad[span, :] = (middle_grad[span, :] + part).astype(bf16)
        return gain_grad + jnp.sum(grads * (x * inv), 0, keepdims=True)

    def small_copy(k):
        return pltpu.make_async_remote_copy(
            src_ref=small_sent.at[k], dst_ref=small_box.at[k],
            send_sem=tsend.at[k], recv_sem=trecv.at[k],
            device_id=partner((every[k],)), device_id_type=MESH)

    def small_phase(k):
        if k == 0:
            gain_grad = lax.fori_loop(0, length // rows, norm_block, jnp.zeros((1, width), f32))
            small_out[...] = small_in[...]
            for i in range(width // LANES):
                small_out[i : i + 1, :] = gain_grad[:, i * LANES : (i + 1) * LANES]
        else:
            small_copy(k - 1).wait_recv()
            small_out[...] = small_out[...] + small_box[k - 1]
        if k < small_count:
            small_sent[k] = small_out[...]
            small_copy(k).start()

    last = 2 * count
    starts = (0, 0, 2, 2)
    stores = [
        pltpu.make_async_copy(sums.at[s], out, store_sem.at[s]) for s, out in enumerate((sum_o, sum_v, sum_k, sum_q))
    ]
    stores.append(pltpu.make_async_copy(token_grad, token_grad_hbm, store_sem.at[4]))
    for t in range(max(last + starts[-1], small_count + NORM) + 1):
        for s in range(4):
            if 0 <= t - starts[s] <= last:
                phase(s, t - starts[s])
                if t - starts[s] == last:
                    stores[s].start()
        for s in range(4):
            if t == starts[s]:
                acc[s] = grad(s, core)
        if t == NORM:
            for load in loads[6:9]:
                load.wait()
        if 0 <= t - NORM <= small_count:
            small_phase(t - NORM)
            if t == NORM:
                stores[4].start()
    for store in stores:
        store.wait()
    for s in range(4):
        for k in range(count):
            for i in range(len(streams[s][k][0])):
                rs_copy(s, k, i).wait_send()
                if streams[s][k][1] != "whole":
                    ag_copy(s, k, i, False).wait_send()
    for k in range(small_count):
        small_copy(k).wait_send()


def reduce_grads(tokens, attended, middle_grad, dq, dk, dv, wq, wk, wv, gain, small, dp_size, groups):
    f32, bf16 = jnp.float32, jnp.bfloat16
    length, width = tokens.shape
    dp_bits, expert_bits = dp_size.bit_length() - 1, groups.bit_length() - 1
    count = dp_bits + expert_bits
    steps = fold_steps(width, width, list(range(count)))
    box = sum(step[2] * (3 if step[1] == "quad" else 1) for step in steps)
    messages = sum(3 if step[1] == "quad" else 1 for step in steps)
    vmem = pl.BlockSpec(memory_space=pltpu.VMEM)
    anywhere = pl.BlockSpec(memory_space=pl.ANY)
    sem = pltpu.SemaphoreType.DMA
    shape = jax.ShapeDtypeStruct
    act, square = shape((length, width), bf16), shape((width, width), bf16)
    big = (attended, middle_grad, tokens, dv, dk, dq, wq, wk, wv)
    return pl.pallas_call(
        functools.partial(reduce_kernel, dp_bits=dp_bits, expert_bits=expert_bits),
        out_shape=(square, square, square, square, act, shape(small.shape, f32)),
        in_specs=[anywhere] * len(big) + [vmem] * 2,
        out_specs=(anywhere,) * 5 + (vmem,),
        scratch_shapes=[pltpu.VMEM(x.shape, x.dtype) for x in big] + [
            pltpu.VMEM((length, width), bf16),
            pltpu.VMEM((4, width, width), bf16),
            pltpu.VMEM((length, width), bf16),
            pltpu.VMEM((length, width), bf16),
            pltpu.VMEM((4, width // 2, width), f32),
            pltpu.VMEM((4, box, width), bf16),
            pltpu.VMEM((4, box, width), bf16),
            pltpu.VMEM((count,) + small.shape, f32),
            pltpu.VMEM((count,) + small.shape, f32),
            sem((len(big),)), sem((5,)),
            sem((4, 2 * messages)), sem((4, 2 * messages)), sem((count,)), sem((count,)),
        ],
        compiler_params=pltpu.CompilerParams(
            collective_id=2, has_side_effects=True, vmem_limit_bytes=62 << 20
        ),
        cost_estimate=pl.CostEstimate(
            flops=14 * length * width * width, bytes_accessed=30 << 20, transcendentals=0
        ),
    )(*big, gain, small)


def key_ranges(segment_row):
    first, last = segment_row[::BLOCK], segment_row[BLOCK - 1 :: BLOCK]
    lo = jnp.sum(segment_row[None, :] < first[:, None], 1) // BLOCK
    hi = (jnp.sum(segment_row[None, :] <= last[:, None], 1) + BLOCK - 1) // BLOCK
    return lo.astype(jnp.int32), hi.astype(jnp.int32)


def per_device(
    tokens,
    segments,
    routes,
    cotangent,
    attn_gain,
    ffn_gain,
    query_weight,
    key_weight,
    value_weight,
    output_weight,
    position_bias_grid,
    router_weight,
    expert_in,
    expert_out,
):
    f32, bf16 = jnp.float32, jnp.bfloat16
    token_count, model_width = tokens.shape
    head_count = position_bias_grid.shape[1]
    score_scale = (model_width // head_count) ** (-0.5)
    experts_all = router_weight.shape[1]
    capacity = (5 * token_count + 4 * experts_all - 1) // (4 * experts_all)
    slot_rows = (capacity + 15) // 16 * 16
    slots = experts_all * slot_rows
    groups = lax.axis_size("expert")
    dp_size = lax.axis_size("dp")

    def exchange(rows):
        return lax.all_to_all(rows, "expert", split_axis=0, concat_axis=0, tiled=True)

    routes_row = routes.reshape(1, token_count)
    token_slot, grad_slots = first_slots(routes_row, cotangent, experts_all, capacity, slot_rows)
    grad_arrived = exchange(grad_slots)
    lo, hi = key_ranges(segments[0])
    router_pad = max(experts_all, 16)
    router_t = jnp.pad(router_weight.T, ((0, router_pad - experts_all), (0, 0)))
    gain_one, gain_two = attn_gain[None, :], ffn_gain[None, :]
    queries, key_rows, keys_t, value_rows, attended, log_sums, middle, router_probs, sent, gate_slots = front(
        lo, hi, tokens, segments, token_slot, routes_row, gain_one, gain_two,
        query_weight, key_weight, value_weight, output_weight, position_bias_grid, router_t,
        experts_all, slot_rows, score_scale,
    )
    home_grad, home_gate, produced, keep, give = ffn(
        sent, gate_slots, grad_arrived.reshape(slots, model_width), expert_in[0], expert_out[0], groups, dp_size,
    )
    passed = lax.ppermute(give, "dp", [(i, (i + dp_size // 2) % dp_size) for i in range(dp_size)])
    returned = exchange(produced.reshape(experts_all, slot_rows, model_width)).reshape(slots, model_width)
    query_grad, key_grad, value_grad, middle_grad, small = back(
        lo, hi, home_grad, home_gate, token_slot, routes_row, router_probs, middle, cotangent, segments, gain_two,
        output_weight, router_t, position_bias_grid, queries, key_rows, keys_t, value_rows, log_sums, attended,
        experts_all, slot_rows, score_scale,
    )
    sum_o, sum_v, sum_k, sum_q, token_grad, small = reduce_grads(
        tokens, attended, middle_grad, query_grad, key_grad, value_grad,
        query_weight, key_weight, value_weight, gain_one, small, dp_size, groups,
    )
    (mixed, token_grad, attn_gain_grad, ffn_gain_grad, grad_q, grad_k, grad_v, grad_o, table_grad, router_grad,
     grad_in, grad_out) = finish(
        (sum_q, sum_k, sum_v, sum_o), keep, passed, returned, middle, token_grad, small,
        token_slot, routes_row, router_probs, position_bias_grid.shape, experts_all
    )
    return (
        mixed,
        token_grad,
        attn_gain_grad,
        ffn_gain_grad,
        grad_q,
        grad_k,
        grad_v,
        grad_o,
        table_grad.T,
        router_grad.T,
        grad_in[None],
        grad_out[None],
    )


def solution(mesh):
    rows = P(("dp", "expert"), None)
    return jax.shard_map(
        per_device,
        mesh=mesh,
        in_specs=(rows,) * 4 + (P(),) * 8 + (P("expert", None, None),) * 2,
        out_specs=(rows,) * 2 + (P(),) * 8 + (P("expert", None, "dp"), P("expert", "dp", None)),
        check_vma=False,
    )
```

```python
import functools

import jax
import jax.numpy as jnp
from jax import lax
from jax.experimental import pallas as pl
from jax.experimental.pallas import tpu as pltpu
from jax.sharding import PartitionSpec as P

epsilon = 1e-06
precise_setting = lax.Precision.HIGHEST
def matmul(left, right):
    return jnp.dot(left, right, preferred_element_type=jnp.float32)


def matmul_tn(left, right):
    return lax.dot_general(left, right, (((0,), (0,)), ((), ())), preferred_element_type=jnp.float32)


def matmul_nt(left, right):
    return lax.dot_general(left, right, (((1,), (1,)), ((), ())), preferred_element_type=jnp.float32)


bucket_bounds = (12, 16, 23, 32, 46, 64, 91)
masked_score = -1e30
LANES = 128
BLOCK = 128
NEAR = 5
UF = 6
UB = 6


def bucket_of(relative):
    distance = jnp.abs(relative)
    beyond = jnp.zeros_like(distance)
    for threshold in bucket_bounds:
        beyond = beyond + (distance >= threshold).astype(jnp.int32)
    inside = jnp.where(distance < 8, distance, 8 + beyond)
    return inside + 16 * (relative > 0).astype(jnp.int32)


def dot_nt(a, b):
    return lax.dot_general(a, b, (((1,), (1,)), ((), ())), preferred_element_type=jnp.float32)


def dot_nn(a, b):
    return lax.dot_general(a, b, (((1,), (0,)), ((), ())), preferred_element_type=jnp.float32)


def split3(x):
    a = x.astype(jnp.bfloat16)
    r = x - a.astype(jnp.float32)
    b = r.astype(jnp.bfloat16)
    c = (r - b.astype(jnp.float32)).astype(jnp.bfloat16)
    return a, b, c


def fill_bias(diag_ref, bias, pairs):
    for p in range(pairs):
        for d in range(NEAR):
            tiles = []
            for h in (2 * p, 2 * p + 1):
                row = diag_ref[h : h + 1, :]
                if d in (0, NEAR - 1):
                    col = row[:, 511:512] if d == 0 else row[:, 0:1]
                    tiles.append(jnp.broadcast_to(col, (BLOCK, BLOCK)))
                else:
                    base = (3 - d) * BLOCK
                    wide = jnp.broadcast_to(row[:, base : base + 2 * BLOCK], (BLOCK, 2 * BLOCK))
                    tiles.append(pltpu.roll(wide, BLOCK, 1, stride=1, stride_axis=0)[:, :BLOCK])
            bias[p, d] = jnp.concatenate(tiles, 1)


def heads_apart(block, low, extra=None):
    zero = jnp.zeros_like(block)
    first, second = jnp.where(low, block, zero), jnp.where(low, zero, block)
    if extra is not None:
        first, second = jnp.concatenate([first, extra], 1), jnp.concatenate([second, extra], 1)
    return jnp.concatenate([first, second], 0)


def by_count(lo, hi, most, body):
    for n in range(1, most + 1):
        pl.when(hi - lo == n)(functools.partial(body, n))


def own_heads(wide):
    return jnp.concatenate([wide[:64, :LANES], wide[64:128, LANES:]], 0)


def attend(lo_ref, hi_ref, q_ref, k_ref, vt_ref, qm_ref, km_ref, bias, o_ref, lse_ref):
    pairs = q_ref.shape[1] // LANES
    length = q_ref.shape[0]
    nblk = length // BLOCK
    f32, bf16 = jnp.float32, jnp.bfloat16
    low = lax.broadcasted_iota(jnp.int32, (1, LANES), 1) < 64

    def q_block(i, _):
        lo, hi = lo_ref[i], hi_ref[i]
        rows = pl.ds(pl.multiple_of(i * BLOCK, BLOCK), BLOCK)
        start = pl.multiple_of(lo * BLOCK, BLOCK)
        qm = qm_ref[rows, :]

        def body(n):
            span = pl.ds(start, n * BLOCK)
            km = km_ref[span, :]

            def lanes_of(p):
                return pl.ds(pl.multiple_of(p * LANES, LANES), LANES)

            def scores(p):
                qs = heads_apart(q_ref[rows, lanes_of(p)], low, qm)
                return dot_nt(jnp.concatenate([k_ref[span, lanes_of(p)], km], 1), qs)

            def soften(p, st):
                parts = []
                top = None
                for b in range(n):
                    d = jnp.clip(lo + b - i, -2, 2) + 2
                    s = st[b * BLOCK : (b + 1) * BLOCK] + bias[p, d]
                    parts.append(s)
                    top = s if top is None else jnp.maximum(top, s)
                top = jnp.max(top, 0, keepdims=True)
                return jnp.concatenate([jnp.exp(s - top).astype(bf16) for s in parts], 0), top

            def mix(p, probs):
                values = jnp.concatenate([vt_ref[lanes_of(p), span], jnp.ones((16, n * BLOCK), bf16)], 0)
                return dot_nn(values, probs)

            def finish(p, acc, top):
                total = acc[LANES : LANES + 1]
                inv = 1.0 / total
                ot = own_heads(acc)
                ot = jnp.concatenate([ot[:64] * inv[:, :LANES], ot[64:] * inv[:, LANES:]], 0)
                o_ref[rows, lanes_of(p)] = ot.T.astype(bf16)
                lse_ref[i, pl.ds(p, 1), :] = top + jnp.log(total)

            def some(g, _):
                ps = [g * UF + u for u in range(UF)]
                sts = [scores(p) for p in ps]
                soft = [soften(p, st) for p, st in zip(ps, sts)]
                accs = [mix(p, x[0]) for p, x in zip(ps, soft)]
                for p, acc, x in zip(ps, accs, soft):
                    finish(p, acc, x[1])
                return 0
            lax.fori_loop(0, pairs // UF, some, 0)

        by_count(lo, hi, nblk, body)
        return 0
    lax.fori_loop(0, nblk, q_block, 0)


def attend_back(
    lo_ref, hi_ref, q_ref, k_ref, kt_ref, v_ref, lse_ref, do_ref, o_ref, qm_ref, km_ref, bias,
    dq_ref, dk_ref, dv_ref, gsum_ref, gacc, dkacc, dvacc, scale,
):
    length, width = q_ref.shape
    pairs = width // LANES
    nblk = length // BLOCK
    f32, bf16 = jnp.float32, jnp.bfloat16
    low = lax.broadcasted_iota(jnp.int32, (1, LANES), 1) < 64
    pick = (
        lax.broadcasted_iota(jnp.int32, (16, LANES), 0) == lax.broadcasted_iota(jnp.int32, (16, LANES), 1) // 64
    ).astype(f32).astype(bf16)
    gacc[...] = jnp.zeros_like(gacc)
    gsum_ref[...] = jnp.zeros_like(gsum_ref)
    dkacc[...] = jnp.zeros_like(dkacc)
    dvacc[...] = jnp.zeros_like(dvacc)

    def q_block(i, _):
        lo, hi = lo_ref[i], hi_ref[i]
        rows = pl.ds(pl.multiple_of(i * BLOCK, BLOCK), BLOCK)
        start = pl.multiple_of(lo * BLOCK, BLOCK)
        qm = qm_ref[rows, :]

        def body(n):
            span = pl.ds(start, n * BLOCK)
            km = km_ref[span, :]

            def lanes_of(p):
                return pl.ds(pl.multiple_of(p * LANES, LANES), LANES)

            def products(p):
                cols = lanes_of(p)
                qs = heads_apart(q_ref[rows, cols], low, qm)
                dd = do_ref[rows, cols]
                dos = heads_apart(dd, low)
                prod = dd.astype(f32) * o_ref[rows, cols].astype(f32)
                prod_hi = prod.astype(bf16)
                prod_lo = (prod - prod_hi.astype(f32)).astype(bf16)
                inner = dot_nt(pick, prod_hi) + dot_nt(pick, prod_lo)
                inner = jnp.concatenate([inner[0:1], inner[1:2]], 1)
                st = dot_nt(jnp.concatenate([k_ref[span, cols], km], 1), qs)
                dpt = dot_nt(v_ref[span, cols], dos)
                return qs, dos, inner, st, dpt

            def pointwise(p, inner, st, dpt):
                lse = lse_ref[i, pl.ds(p, 1), :]
                probs, grads = [], []
                for b in range(n):
                    d = jnp.clip(lo + b - i, -2, 2) + 2
                    part = slice(b * BLOCK, (b + 1) * BLOCK)
                    prob = jnp.exp(st[part] + bias[p, d] - lse)
                    grad = prob * (dpt[part] - inner)
                    gacc[p, d] += grad
                    probs.append(prob.astype(bf16))
                    grads.append(grad.astype(bf16))
                return jnp.concatenate(probs, 0), jnp.concatenate(grads, 0)

            def back(p, qs, dos, probs, grads):
                cols = lanes_of(p)
                return (
                    dot_nn(probs, dos), dot_nn(grads, qs[:, :LANES]), dot_nn(kt_ref[cols, span], grads)
                )

            def finish(p, dv, dk, dqt):
                cols = lanes_of(p)
                dvacc[span, cols] += dv
                dkacc[span, cols] += dk
                dq_ref[rows, cols] = (own_heads(dqt).T * scale).astype(bf16)

            def some(g, _):
                ps = [g * UB + u for u in range(UB)]
                first = [products(p) for p in ps]
                points = [pointwise(p, *x[2:]) for p, x in zip(ps, first)]
                last = [back(p, *x[:2], *y) for p, x, y in zip(ps, first, points)]
                for p, x in zip(ps, last):
                    finish(p, *x)
                return 0
            lax.fori_loop(0, pairs // UB, some, 0)

        by_count(lo, hi, nblk, body)
        return 0
    lax.fori_loop(0, nblk, q_block, 0)
    dk_ref[...] = dkacc[...].astype(bf16)
    dv_ref[...] = dvacc[...].astype(bf16)
    turn = (
        lax.broadcasted_iota(jnp.int32, (BLOCK, BLOCK), 0) + lax.broadcasted_iota(jnp.int32, (BLOCK, BLOCK), 1)
        == BLOCK - 1
    ).astype(f32).astype(bf16)
    for p in range(pairs):
        for d in range(NEAR):
            t = gacc[p, d]
            if 0 < d < NEAR - 1:
                hi = t.astype(bf16)
                t = dot_nn(turn, hi) + dot_nn(turn, (t - hi.astype(f32)).astype(bf16))
            for u in range(2):
                s = jnp.concatenate([t[:, u * LANES : (u + 1) * LANES], jnp.zeros((BLOCK, LANES), f32)], 1)
                if 0 < d < NEAR - 1:
                    s = pltpu.roll(s, 0, 1, stride=1, stride_axis=0)
                at = d * 16 + 2 * p + u
                gsum_ref[at : at + 1, :] = jnp.sum(s, 0, keepdims=True)


def two(x):
    a = x.astype(jnp.bfloat16)
    return a, (x - a.astype(jnp.float32)).astype(jnp.bfloat16)


def row_pieces(row):
    place = lax.broadcasted_iota(jnp.int32, (16, row.shape[1]), 0)
    a, b, c = [x.astype(jnp.float32) for x in split3(row)]
    return jnp.where(place == 0, a, jnp.where(place == 1, b, jnp.where(place == 2, c, 0.0))).astype(jnp.bfloat16)


def each(count, body):
    if count <= 8:
        for e in range(count):
            body(e)
    else:
        def step(e, _):
            body(e)
            return 0
        lax.fori_loop(0, count, step, 0)


def slot_hot(slot_row, e, slot_rows):
    place = lax.broadcasted_iota(jnp.int32, (slot_rows, slot_row.shape[1]), 0) + e * slot_rows
    return (place == slot_row).astype(jnp.float32).astype(jnp.bfloat16)


def token_hot(slot_row, slots):
    first = lax.broadcasted_iota(jnp.int32, (BLOCK, LANES), 1).astype(jnp.float32)
    blocks = []
    for c in range(0, slot_row.shape[1], BLOCK):
        column = jnp.broadcast_to(slot_row[:, c : c + BLOCK].astype(jnp.float32), (BLOCK, BLOCK)).T
        blocks.append(jnp.concatenate(
            [(column == first + float(s)).astype(jnp.float32).astype(jnp.bfloat16) for s in range(0, slots, LANES)], 1))
    return jnp.concatenate(blocks, 0)


def slots_kernel(routes_ref, rows_ref, slot_ref, out_ref, *, experts, capacity, slot_rows):
    f32, bf16 = jnp.float32, jnp.bfloat16
    tokens = routes_ref.shape[1]
    routes = routes_ref[...]
    pad = max(experts, 16)
    hot = (lax.broadcasted_iota(jnp.int32, (pad, tokens), 0) == routes).astype(f32)
    earlier = (
        lax.broadcasted_iota(jnp.int32, (BLOCK, BLOCK), 0) < lax.broadcasted_iota(jnp.int32, (BLOCK, BLOCK), 1)
    ).astype(f32).astype(bf16)
    seen = jnp.zeros((pad, 1), f32)
    ranks = []
    for c in range(0, tokens, BLOCK):
        part = hot[:, c : c + BLOCK]
        ranks.append(jnp.sum((dot_nn(part.astype(bf16), earlier) + seen) * part, 0, keepdims=True))
        seen = seen + jnp.sum(part, 1, keepdims=True)
    rank = jnp.concatenate(ranks, 1).astype(jnp.int32)
    slot = jnp.where(rank < capacity, routes * slot_rows + rank, -1)
    slot_ref[...] = jnp.broadcast_to(slot, slot_ref.shape)

    rows = dot_nn(slot_hot(slot, 0, experts * slot_rows), rows_ref[...]).astype(bf16)
    out_ref[...] = rows.reshape(out_ref.shape)


def first_slots(routes_row, rows, experts, capacity, slot_rows):
    tokens, width = rows.shape
    vmem = pl.BlockSpec(memory_space=pltpu.VMEM)
    return pl.pallas_call(
        functools.partial(slots_kernel, experts=experts, capacity=capacity, slot_rows=slot_rows),
        out_shape=(
            jax.ShapeDtypeStruct((8, tokens), jnp.int32),
            jax.ShapeDtypeStruct((experts, slot_rows, width), jnp.bfloat16),
        ),
        in_specs=[vmem] * 2,
        out_specs=(vmem,) * 2,
        compiler_params=pltpu.CompilerParams(vmem_limit_bytes=63 << 20),
        cost_estimate=pl.CostEstimate(
            flops=2 * experts * slot_rows * tokens * width, bytes_accessed=4 << 20, transcendentals=0
        ),
    )(routes_row, rows)


def fill_masks(segment_row, qm, km):
    f32, bf16 = jnp.float32, jnp.bfloat16
    lane = lax.broadcasted_iota(jnp.int32, (1, LANES), 1)
    for b in range(qm.shape[0] // BLOCK):
        span = slice(b * BLOCK, (b + 1) * BLOCK)
        hot = (lax.broadcasted_iota(jnp.int32, (LANES, BLOCK), 0) == segment_row[:, span]).astype(f32).T
        qm[span, :] = (hot * masked_score).astype(bf16)
        km[span, :] = jnp.where(lane < 8, 1.0 - hot, 0.0).astype(bf16)


def fill_diag(grid_ref, diag, heads):
    bf16 = jnp.bfloat16
    buckets = grid_ref.shape[0]
    relative = 256 - lax.broadcasted_iota(jnp.int32, (buckets, 4 * LANES), 1)
    hot = (lax.broadcasted_iota(jnp.int32, (buckets, 4 * LANES), 0) == bucket_of(relative))
    hot = hot.astype(jnp.float32).astype(bf16)
    grid = jnp.concatenate(
        [grid_ref[...], jnp.zeros((buckets, LANES - heads), jnp.float32)], 1
    ).T[:16]
    total = None
    for piece in split3(grid):
        term = dot_nn(piece, hot)
        total = term if total is None else total + term
    diag[...] = total


def front_kernel(
    lo_ref, hi_ref, tokens, segment_row, slot_ref, routes_ref, gain_one, gain_two, wq, wk, wv, wo, grid_ref, router_t,
    q_ref, k_ref, kt_ref, v_ref, o_ref, lse_ref, middle_ref, probs_ref, xs_ref, gs_ref,
    vt_ref, qm_ref, km_ref, diag, bias, hidden, *, experts, slot_rows, scale,
):
    f32, bf16 = jnp.float32, jnp.bfloat16
    length, width = tokens.shape
    pairs = width // LANES
    nblk = length // BLOCK
    heads = grid_ref.shape[1]
    low = lax.broadcasted_iota(jnp.int32, (1, LANES), 1) < 64
    step = 256

    for b in range(length // step):
        span = slice(b * step, (b + 1) * step)
        x = tokens[span, :].astype(f32)
        inverse = lax.rsqrt(jnp.mean(x * x, 1, keepdims=True) + epsilon)
        normed = (x * inverse * gain_one[...]).astype(bf16)
        q_ref[span, :] = (dot_nn(normed, wq[...]).astype(bf16).astype(f32) * scale).astype(bf16)
        k = dot_nn(normed, wk[...]).astype(bf16)
        k_ref[span, :] = k
        kt_ref[:, span] = k.T
        v = dot_nn(normed, wv[...]).astype(bf16)
        v_ref[span, :] = v
        vt_ref[:, span] = v.T
    fill_masks(segment_row[...], qm_ref, km_ref)
    fill_diag(grid_ref, diag, heads)
    fill_bias(diag, bias, pairs)
    attend(lo_ref, hi_ref, q_ref, k_ref, vt_ref, qm_ref, km_ref, bias, o_ref, lse_ref)

    rw = two(router_t[...])
    routes = routes_ref[...]
    pad = router_t.shape[0]
    place = lax.broadcasted_iota(jnp.int32, (pad, step), 0)
    gates = []
    for b in range(length // step):
        span = slice(b * step, (b + 1) * step)
        middle = tokens[span, :].astype(f32) + dot_nn(o_ref[span, :], wo[...])
        middle_ref[span, :] = middle
        inverse = lax.rsqrt(jnp.mean(middle * middle, 1, keepdims=True) + epsilon)
        parts = two(middle * inverse * gain_two[...])
        hidden[span, :] = parts[0]
        logits = dot_nt(rw[0], parts[0]) + dot_nt(rw[0], parts[1]) + dot_nt(rw[1], parts[0])
        logits = jnp.where(place < experts, logits, -1e30)
        powers = jnp.exp(logits - jnp.max(logits, 0, keepdims=True))
        probs = powers / jnp.sum(powers, 0, keepdims=True)
        probs_ref[:, span] = probs
        gates.append(jnp.sum(jnp.where(place == routes[:, span], probs, 0.0), 0, keepdims=True))
    gates = row_pieces(jnp.concatenate(gates, 1))
    slot = slot_ref[0:1, :]
    lanes = gs_ref.shape[2]

    def one(e):
        hot = slot_hot(slot, e, slot_rows)
        xs_ref[e] = dot_nn(hot, hidden[...]).astype(bf16)
        if lanes > slot_rows:
            hot = jnp.concatenate([hot, jnp.zeros((lanes - slot_rows, length), bf16)], 0)
        row = jnp.sum(dot_nt(gates, hot), 0, keepdims=True)
        gs_ref[e] = jnp.broadcast_to(row, gs_ref.shape[1:])
    each(experts, one)


def front(lo, hi, tokens, segments, slot, routes_row, gain_one, gain_two, wq, wk, wv, wo, grid, router_t, experts, slot_rows, scale):
    length, width = tokens.shape
    heads = grid.shape[1]
    pairs = width // LANES
    nblk = length // BLOCK
    lanes = (slot_rows + LANES - 1) // LANES * LANES
    smem = pl.BlockSpec(memory_space=pltpu.SMEM)
    vmem = pl.BlockSpec(memory_space=pltpu.VMEM)
    f32, bf16 = jnp.float32, jnp.bfloat16
    shape = jax.ShapeDtypeStruct
    act = shape((length, width), bf16)
    return pl.pallas_call(
        functools.partial(front_kernel, experts=experts, slot_rows=slot_rows, scale=scale),
        out_shape=(
            act, act, shape((width, length), bf16), act, act,
            shape((nblk, 8, 2 * LANES), f32), shape((length, width), f32),
            shape((router_t.shape[0], length), f32),
            shape((experts, slot_rows, width), bf16), shape((experts, 8, lanes), f32),
        ),
        in_specs=[smem] * 2 + [vmem] * 12,
        out_specs=(vmem,) * 10,
        scratch_shapes=[
            pltpu.VMEM((width, length), bf16),
            pltpu.VMEM((length, LANES), bf16),
            pltpu.VMEM((length, LANES), bf16),
            pltpu.VMEM((16, 4 * LANES), f32),
            pltpu.VMEM((pairs, NEAR, BLOCK, 2 * LANES), f32),
            pltpu.VMEM((length, width), bf16),
        ],
        compiler_params=pltpu.CompilerParams(vmem_limit_bytes=63 << 20),
        cost_estimate=pl.CostEstimate(
            flops=4 * length * length * width + 12 * length * width * width, bytes_accessed=20 << 20,
            transcendentals=length * length * heads,
        ),
    )(lo, hi, tokens, segments, slot, routes_row, gain_one, gain_two, wq, wk, wv, wo, grid, router_t)


def bucket_sums(gsum_ref):
    bf16 = jnp.bfloat16
    total = jnp.zeros((16, LANES), jnp.float32)
    lane = lax.broadcasted_iota(jnp.int32, (2 * LANES, LANES), 1)
    for d in range(NEAR):
        relative = (d - 2) * BLOCK + BLOCK - 1 - lax.broadcasted_iota(jnp.int32, (2 * LANES, LANES), 0)
        bucket = 15 if d == 0 else 31 if d == NEAR - 1 else bucket_of(relative)
        hot = (lane == bucket).astype(jnp.float32).astype(bf16)
        for piece in split3(gsum_ref[d * 16 : (d + 1) * 16, :]):
            total = total + dot_nn(piece, hot)
    return total


def small_shape(width, experts):
    return (16 + width // LANES * experts + 16, LANES)


def back_kernel(
    lo_ref, hi_ref, home, home_gate, slot_ref, routes_ref, probs_ref, middle_ref, cotangent, segment_row, gain_two,
    wo, router_t, grid_ref, lse_ref, q_hbm, k_hbm, kt_hbm, v_hbm, o_hbm,
    dq_ref, dk_ref, dv_ref, middle_grad_hbm, small,
    q_ref, k_ref, kt_ref, v_ref, o_ref, middle_grad,
    do_ref, qm_ref, km_ref, diag, bias, gacc, dkacc, dvacc, logit, gsum_ref, sems,
    *, experts, slot_rows, scale,
):
    f32, bf16 = jnp.float32, jnp.bfloat16
    length, width = middle_ref.shape
    pairs = width // LANES
    pad = router_t.shape[0]
    heads = grid_ref.shape[1]
    slot = slot_ref[0:1, :]
    loads = [
        pltpu.make_async_copy(there, here, sems.at[i])
        for i, (there, here) in enumerate(zip(
            (q_hbm, k_hbm, kt_hbm, v_hbm, o_hbm), (q_ref, k_ref, kt_ref, v_ref, o_ref)))
    ]
    for load in loads:
        load.start()

    if experts <= 8:
        total = jnp.zeros((16, length), f32)
        for e in range(experts):
            total = total + dot_nn(row_pieces(home_gate[e, 0:1, :])[:, :slot_rows], slot_hot(slot, e, slot_rows))
    else:
        def add(e, total):
            return total + dot_nn(row_pieces(home_gate[e, 0:1, :])[:, :slot_rows], slot_hot(slot, e, slot_rows))
        total = lax.fori_loop(0, experts, add, jnp.zeros((16, length), f32))
    gate_grad = jnp.sum(total, 0, keepdims=True)
    place = lax.broadcasted_iota(jnp.int32, (pad, length), 0)
    hot = place == routes_ref[...]
    probs = probs_ref[...]
    gate = jnp.sum(jnp.where(hot, probs, 0.0), 0, keepdims=True)
    logit[...] = probs * (jnp.where(hot, gate_grad, 0.0) - gate * gate_grad)
    rw = two(router_t[...])
    stacked = jnp.concatenate([rw[0], rw[1], rw[0]], 0)
    slots = experts * slot_rows
    dkacc[...] = dot_nn(token_hot(slot, slots), home[...].reshape(slots, width))
    router_sum = jnp.zeros((pad, width), f32)
    gain_sum = jnp.zeros((1, width), f32)
    step = 256
    for b in range(length // step):
        span = slice(b * step, (b + 1) * step)
        lg = two(logit[:, span])
        hidden_grad = dkacc[span, :] + matmul_tn(jnp.concatenate([lg[0], lg[0], lg[1]], 0), stacked)
        middle = middle_ref[span, :]
        inverse = lax.rsqrt(jnp.mean(middle * middle, 1, keepdims=True) + epsilon)
        unit = middle * inverse
        hidden = two(unit * gain_two[...])
        both = dot_nn(jnp.concatenate(lg, 0), hidden[0])
        router_sum = router_sum + (both[:pad] + both[pad:] + dot_nn(lg[0], hidden[1]))
        gain_sum = gain_sum + jnp.sum(hidden_grad * unit, 0, keepdims=True)
        scaled = hidden_grad * gain_two[...]
        mean = jnp.mean(scaled * middle, 1, keepdims=True)
        grad = cotangent[span, :].astype(f32) + inverse * (scaled - unit * (inverse * mean))
        middle_grad[span, :] = grad
        dq_ref[span, :] = grad.astype(bf16)
    store = pltpu.make_async_copy(middle_grad, middle_grad_hbm, sems.at[5])
    store.start()
    do_ref[...] = matmul_nt(dq_ref[...], wo[...]).astype(bf16)
    small[...] = jnp.zeros_like(small)
    chunks = width // LANES
    for c in range(chunks):
        cols = slice(c * LANES, (c + 1) * LANES)
        small[8 + c : 9 + c, :] = gain_sum[:, cols]
        small[16 + c * experts : 16 + (c + 1) * experts, :] = router_sum[:experts, cols]

    fill_masks(segment_row[...], qm_ref, km_ref)
    fill_diag(grid_ref, diag, heads)
    fill_bias(diag, bias, pairs)
    for load in loads:
        load.wait()
    attend_back(
        lo_ref, hi_ref, q_ref, k_ref, kt_ref, v_ref, lse_ref, do_ref, o_ref, qm_ref, km_ref, bias,
        dq_ref, dk_ref, dv_ref, gsum_ref, gacc, dkacc, dvacc, scale,
    )
    at = 16 + chunks * experts
    small[at : at + 16, :] = bucket_sums(gsum_ref)
    store.wait()


def back(lo, hi, home, home_gate, slot, routes_row, probs, middle, cotangent, segments, gain_two, wo, router_t, grid,
         q, k, kt, v, lse, o, experts, slot_rows, scale):
    length, width = middle.shape
    heads = grid.shape[1]
    pairs = width // LANES
    smem = pl.BlockSpec(memory_space=pltpu.SMEM)
    vmem = pl.BlockSpec(memory_space=pltpu.VMEM)
    f32, bf16 = jnp.float32, jnp.bfloat16
    shape = jax.ShapeDtypeStruct
    act = shape((length, width), bf16)
    anywhere = pl.BlockSpec(memory_space=pl.ANY)
    return pl.pallas_call(
        functools.partial(back_kernel, experts=experts, slot_rows=slot_rows, scale=scale),
        out_shape=(act, act, act, shape((length, width), f32), shape(small_shape(width, experts), f32)),
        in_specs=[smem] * 2 + [vmem] * 13 + [anywhere] * 5,
        out_specs=(vmem, vmem, vmem, anywhere, vmem),
        scratch_shapes=[
            pltpu.VMEM((length, width), bf16),
            pltpu.VMEM((length, width), bf16),
            pltpu.VMEM((width, length), bf16),
            pltpu.VMEM((length, width), bf16),
            pltpu.VMEM((length, width), bf16),
            pltpu.VMEM((length, width), f32),
            pltpu.VMEM((length, width), bf16),
            pltpu.VMEM((length, LANES), bf16),
            pltpu.VMEM((length, LANES), bf16),
            pltpu.VMEM((16, 4 * LANES), f32),
            pltpu.VMEM((pairs, NEAR, BLOCK, 2 * LANES), f32),
            pltpu.VMEM((pairs, NEAR, BLOCK, 2 * LANES), f32),
            pltpu.VMEM((length, width), f32),
            pltpu.VMEM((length, width), f32),
            pltpu.VMEM((router_t.shape[0], length), f32),
            pltpu.VMEM((NEAR * 16, 2 * LANES), f32),
            pltpu.SemaphoreType.DMA((6,)),
        ],
        compiler_params=pltpu.CompilerParams(vmem_limit_bytes=63 << 20),
        cost_estimate=pl.CostEstimate(
            flops=10 * length * length * width + 6 * length * width * width, bytes_accessed=30 << 20,
            transcendentals=length * length * heads,
        ),
    )(lo, hi, home, home_gate, slot, routes_row, probs, middle, cotangent, segments, gain_two, wo, router_t, grid,
      lse, q, k, kt, v, o)


def finish_kernel(
    sum_q, sum_k, sum_v, sum_o, keep, passed, returned_in, middle_in, token_in, small, slot_ref, routes_ref, probs_ref,
    mixed_out, token_out, gain_one, gain_two, grad_q, grad_k, grad_v, grad_o, table_t, router_t, grad_in, grad_out,
    low, wide, returned, middle, mixed, token, load_sem, store_sem, copy_sem, mix_sem, *, experts,
):
    f32 = jnp.float32
    sources = (sum_o, sum_v, sum_k, sum_q, keep.at[0], keep.at[1], passed.at[0], passed.at[1])
    targets = (grad_o, grad_v, grad_k, grad_q, grad_in, grad_out)
    width = sum_q.shape[0]
    rows = 256
    spans = [pl.ds(r, rows) for r in range(0, width, rows)]
    fetches = [
        pltpu.make_async_copy(x, y, copy_sem.at[i])
        for i, (x, y) in enumerate(((returned_in, returned), (middle_in, middle), (token_in, token)))
    ]
    copies = [pltpu.make_async_copy(token, token_out, copy_sem.at[3])]
    length = middle.shape[0]
    slots = returned.shape[0]
    for c in range(0, length, BLOCK):
        rows_c = pl.ds(c, BLOCK)
        copies.append(pltpu.make_async_copy(mixed.at[rows_c], mixed_out.at[rows_c], mix_sem.at[c // BLOCK]))
    pad = probs_ref.shape[0]
    hot = lax.broadcasted_iota(jnp.int32, (pad, length), 0) == routes_ref[...]
    gate_row = jnp.sum(jnp.where(hot, probs_ref[...], 0.0), 0, keepdims=True)

    def mix(c, rows_back):
        at = slice(c, c + BLOCK)
        gate = jnp.broadcast_to(gate_row[:, at], (BLOCK, BLOCK)).T
        gate = jnp.concatenate([gate] * (width // LANES), 1)
        mixed[at, :] = (middle[at, :] + gate * rows_back[at]).astype(jnp.bfloat16)

    loads = [
        [pltpu.make_async_copy(x.at[span], low.at[i, span], load_sem.at[i, j]) for j, span in enumerate(spans)]
        for i, x in enumerate(sources)
    ]
    stores = [
        [pltpu.make_async_copy(wide.at[i, span], x.at[span], store_sem.at[i, j]) for j, span in enumerate(spans)]
        for i, x in enumerate(targets)
    ]
    fetches[0].start()
    for i in range(4):
        for load in loads[i]:
            load.start()
    for fetch in fetches[1:]:
        fetch.start()
    for i in range(4, 8):
        for load in loads[i]:
            load.start()
    chunks = width // LANES
    gain_one[...] = jnp.concatenate([small[c : c + 1, :] for c in range(chunks)], 1).reshape(width)
    gain_two[...] = jnp.concatenate([small[8 + c : 9 + c, :] for c in range(chunks)], 1).reshape(width)
    for c in range(chunks):
        router_t[:, c * LANES : (c + 1) * LANES] = small[16 + c * experts : 16 + (c + 1) * experts, :]
    at = 16 + chunks * experts
    heads, buckets = table_t.shape
    table_t[...] = small[at : at + heads, :buckets]
    fetches[0].wait()
    rows_back = dot_nn(token_hot(slot_ref[0:1, :], slots), returned[...])
    for i in range(4):
        for j, span in enumerate(spans):
            loads[i][j].wait()
            wide[i, span, :] = low[i, span, :].astype(f32)
            stores[i][j].start()
    fetches[2].wait()
    copies[0].start()
    for i in (4, 5):
        for j, span in enumerate(spans):
            loads[i][j].wait()
            loads[i + 2][j].wait()
            wide[i, span, :] = low[i, span, :].astype(f32) + low[i + 2, span, :].astype(f32)
            stores[i][j].start()
    fetches[1].wait()
    for c in range(0, length, BLOCK):
        mix(c, rows_back)
        copies[1 + c // BLOCK].start()
    for i in range(6):
        for store in stores[i]:
            store.wait()
    for copy in copies:
        copy.wait()


def finish(sums, keep, passed, returned, middle, token_grad, small, slot, routes_row, probs, grid_shape, experts):
    f32, bf16 = jnp.float32, jnp.bfloat16
    width = sums[0].shape[0]
    vmem = pl.BlockSpec(memory_space=pltpu.VMEM)
    anywhere = pl.BlockSpec(memory_space=pl.ANY)
    shape = jax.ShapeDtypeStruct
    act = shape(middle.shape, bf16)
    square, row = shape((width, width), f32), shape((width,), f32)
    blocks = width // 256
    return pl.pallas_call(
        functools.partial(finish_kernel, experts=experts),
        out_shape=(act, act, row, row, square, square, square, square, shape(grid_shape[::-1], f32),
                   shape((experts, width), f32), square, square),
        in_specs=[anywhere] * 9 + [vmem] * 4,
        out_specs=(anywhere,) * 2 + (vmem, vmem) + (anywhere,) * 4 + (vmem, vmem) + (anywhere,) * 2,
        scratch_shapes=[
            pltpu.VMEM((8, width, width), bf16), pltpu.VMEM((6, width, width), f32),
            pltpu.VMEM(returned.shape, bf16), pltpu.VMEM(middle.shape, f32),
            pltpu.VMEM(middle.shape, bf16), pltpu.VMEM(middle.shape, bf16),
            pltpu.SemaphoreType.DMA((8, blocks)), pltpu.SemaphoreType.DMA((6, blocks)),
            pltpu.SemaphoreType.DMA((4,)), pltpu.SemaphoreType.DMA((middle.shape[0] // BLOCK,)),
        ],
        compiler_params=pltpu.CompilerParams(vmem_limit_bytes=63 << 20),
        cost_estimate=pl.CostEstimate(flops=0, bytes_accessed=30 << 20, transcendentals=0),
    )(*sums, keep, passed, returned, middle, token_grad, small, slot, routes_row, probs)


def gelu_parts(v):
    mag = jnp.abs(v)
    t = 1.0 / (1.0 + (0.3275911 * 0.7071067811865476) * mag)
    poly = t * (0.127414796 + t * (-0.142248368 + t * (0.7107068705 + t * (-0.7265760135 + t * 0.5307027145))))
    gauss = jnp.exp(-0.5 * v * v)
    tail = poly * gauss
    phi = jnp.where(v < 0, tail, 1.0 - tail)
    return v * phi, phi + v * gauss * 0.3989422804014327


def flip_bits(index, mask, count):
    out = 0
    bit = 1
    while bit < count:
        a, b = (index // bit) % 2, (mask // bit) % 2
        out = out + bit * (a + b - 2 * a * b)
        bit *= 2
    return out


def ffn_kernel(
    xs, gs, g, win_hbm, wout_hbm,
    home, home_gate, produced, keep, give,
    win, wout, xr, gr, act, pg, gated, igs, ggs, dws, dwr, stage,
    wsem, own_sem, psem, ksem, xsend, xrecv, gsend, grecv, isend, irecv, qsend, qrecv, dsend, drecv,
    *, groups, dp_size, tiles,
):
    f32, bf16 = jnp.float32, jnp.bfloat16
    me = lax.axis_index("expert")
    dp = lax.axis_index("dp")
    core = dp % 2
    sibling = dp + 1 - 2 * core
    half_of = dp // 2
    rows = xs.shape[1]
    width = xs.shape[2]
    hidden = win.shape[1]
    tile = hidden // tiles
    lanes = gs.shape[2]

    def there(peer):
        return (dp, peer)

    load_in = pltpu.make_async_copy(win_hbm, win, wsem.at[0])
    load_out = pltpu.make_async_copy(wout_hbm, wout, wsem.at[1])
    load_in.start()
    load_out.start()
    load_g = pltpu.make_async_copy(g, gated, wsem.at[2])
    load_g.start()

    barrier = pltpu.get_barrier_semaphore()

    def greet(s, _):
        pl.semaphore_signal(
            barrier, inc=1, device_id=there(flip_bits(me, s, groups)), device_id_type=pl.DeviceIdType.MESH
        )
        return 0
    lax.fori_loop(1, groups, greet, 0)
    pl.semaphore_signal(barrier, inc=1, device_id=(sibling, me), device_id_type=pl.DeviceIdType.MESH)
    pl.semaphore_wait(barrier, groups)

    def x_copy(peer, slot):
        return pltpu.make_async_remote_copy(
            src_ref=xs.at[peer], dst_ref=xr.at[slot], send_sem=xsend.at[peer], recv_sem=xrecv.at[slot],
            device_id=there(peer), device_id_type=pl.DeviceIdType.MESH)

    def g_copy(peer, slot):
        return pltpu.make_async_remote_copy(
            src_ref=gs.at[peer], dst_ref=gr.at[slot], send_sem=gsend.at[peer], recv_sem=grecv.at[slot],
            device_id=there(peer), device_id_type=pl.DeviceIdType.MESH)

    def i_copy(peer, slot):
        return pltpu.make_async_remote_copy(
            src_ref=igs.at[peer], dst_ref=home.at[slot], send_sem=isend.at[peer], recv_sem=irecv.at[slot],
            device_id=there(peer), device_id_type=pl.DeviceIdType.MESH)

    def q_copy(peer, slot):
        return pltpu.make_async_remote_copy(
            src_ref=ggs.at[peer], dst_ref=home_gate.at[slot], send_sem=qsend.at[peer], recv_sem=qrecv.at[slot],
            device_id=there(peer), device_id_type=pl.DeviceIdType.MESH)

    def send(i, _):
        odd = (i - 1) % 2
        s = (1 - odd) * (groups - 1 - (i - 1) // 2) + odd * (i // 2)
        peer = flip_bits(me, s, groups)
        x_copy(peer, me).start()
        g_copy(peer, me).start()
        return 0
    lax.fori_loop(1, groups, send, 0)
    own_x = pltpu.make_async_copy(xs.at[me], xr.at[me], own_sem.at[0])
    own_g = pltpu.make_async_copy(gs.at[me], gr.at[me], own_sem.at[1])
    own_x.start()
    own_g.start()
    load_in.wait()
    load_out.wait()
    load_g.wait()

    spot = (
        lax.broadcasted_iota(jnp.int32, (rows, lanes), 0)
        == lax.broadcasted_iota(jnp.int32, (rows, lanes), 1)
    )

    def work(base):
        both = pl.ds(base, 2)
        x = xr[both].reshape(2 * rows, width)
        place = pl.ds(pl.multiple_of(base * rows, rows), 2 * rows)
        gg = gated[place, :]
        gate = jnp.concatenate(
            [jnp.sum(jnp.where(spot, gr[base + u, 0:1, :], 0.0), 1, keepdims=True) for u in range(2)], 0
        )
        gated[place, :] = (gate * gg.astype(f32)).astype(bf16)
        total = jnp.zeros((2 * rows, width), f32)
        gate_grad = jnp.zeros((2 * rows, 1), f32)

        def columns(t):
            return slice(t * tile, (t + 1) * tile)

        def products(t):
            return matmul(x, win[:, columns(t)]), matmul_nt(gg, wout[columns(t), :])

        ahead = products(0)
        for t in range(tiles):
            pre, out_grad = ahead
            if t + 1 < tiles:
                ahead = products(t + 1)
            value, slope = gelu_parts(pre)
            act[place, columns(t)] = value.astype(bf16)
            gate_grad = gate_grad + jnp.sum(value * out_grad, 1, keepdims=True)
            low = (gate * out_grad * slope).astype(bf16)
            pg[place, columns(t)] = low
            total = total + matmul_nt(low, win[:, columns(t)])
        igs[both] = total.astype(bf16).reshape(2, rows, width)
        for u in range(2):
            row = jnp.sum(jnp.where(spot, gate_grad[u * rows : (u + 1) * rows], 0.0), 0, keepdims=True)
            ggs[base + u] = jnp.broadcast_to(row, ggs.shape[1:])

    def arrive(peer):
        x_copy(peer, peer).wait_recv()
        g_copy(peer, peer).wait_recv()

    def back(peer):
        i_copy(peer, me).start()
        q_copy(peer, me).start()

    own_x.wait()
    own_g.wait()
    arrive(flip_bits(me, 1, groups))
    work(me - me % 2)
    own_i = pltpu.make_async_copy(igs.at[me], home.at[me], own_sem.at[0])
    own_q = pltpu.make_async_copy(ggs.at[me], home_gate.at[me], own_sem.at[1])
    own_i.start()
    own_q.start()
    back(flip_bits(me, 1, groups))

    def chunk(j, _):
        peer = flip_bits(me, 2 * j, groups)
        other = flip_bits(me, 2 * j + 1, groups)
        arrive(peer)
        arrive(other)
        work(peer - peer % 2)
        back(peer)
        back(other)
        return 0
    lax.fori_loop(1, groups // 2, chunk, 0)

    def d_copy(k):
        return pltpu.make_async_remote_copy(
            src_ref=dws.at[k % 2], dst_ref=dwr.at[k], send_sem=dsend.at[k], recv_sem=drecv.at[k],
            device_id=(sibling, me), device_id_type=pl.DeviceIdType.MESH)

    part = hidden // dp_size
    flat = groups * rows
    items = [(which, half) for half in (1 - half_of, half_of) for which in range(2)]

    def grad(which, quarter):
        span = pl.ds(pl.multiple_of(quarter * part, part), part)
        if which == 0:
            return matmul_tn(xr[...].reshape(flat, width), pg[:, span])
        return matmul_tn(act[:, span], gated[...])

    for k, (which, half) in enumerate(items):
        if k >= 2:
            d_copy(k - 2).wait_send()
        dws[k % 2] = grad(which, 2 * half + 1 - core).astype(bf16)
        d_copy(k).start()
    outs = [
        pltpu.make_async_copy(dwr.at[0], give.at[0], ksem.at[0]),
        pltpu.make_async_copy(dwr.at[1], give.at[1], ksem.at[1]),
        pltpu.make_async_copy(dwr.at[2], keep.at[0], ksem.at[2]),
        pltpu.make_async_copy(dwr.at[3], keep.at[1], ksem.at[3]),
    ]
    for k, (which, half) in enumerate(items):
        local = grad(which, 2 * half + core)
        d_copy(k).wait_recv()
        dwr[k] = (local + dwr[k].astype(f32)).astype(bf16)
        outs[k].start()

    span = stage.shape[1]
    copies = []
    for b in range(flat // span):
        if b >= 2:
            copies[b - 2].wait()
        stage[b % 2] = matmul(act[b * span : (b + 1) * span, :], wout[...]).astype(bf16)
        copy = pltpu.make_async_copy(stage.at[b % 2], produced.at[pl.ds(b * span, span)], psem.at[b % 2])
        copy.start()
        copies.append(copy)
    for copy in copies[-2:] + outs:
        copy.wait()
    own_i.wait()
    own_q.wait()
    for k in (2, 3):
        d_copy(k).wait_send()

    def finish(s, _):
        peer = flip_bits(me, s, groups)
        x_copy(peer, me).wait_send()
        g_copy(peer, me).wait_send()
        i_copy(peer, me).wait_send()
        q_copy(peer, me).wait_send()
        i_copy(peer, peer).wait_recv()
        q_copy(peer, peer).wait_recv()
        return 0
    lax.fori_loop(1, groups, finish, 0)


def ffn(xs, gs, g, weight_in, weight_out, groups, dp_size, tiles=6):
    f32, bf16 = jnp.float32, jnp.bfloat16
    _, rows, width = xs.shape
    hidden = weight_in.shape[1]
    lanes = gs.shape[2]
    part = hidden // dp_size
    anywhere = pl.BlockSpec(memory_space=pl.ANY)
    sem = pltpu.SemaphoreType.DMA
    flat = groups * rows
    shape = jax.ShapeDtypeStruct
    return pl.pallas_call(
        functools.partial(ffn_kernel, groups=groups, dp_size=dp_size, tiles=tiles),
        out_shape=(
            shape((groups, rows, width), bf16),
            shape((groups, 8, lanes), f32),
            shape((flat, width), bf16),
            shape((2, width, part), bf16),
            shape((2, width, part), bf16),
        ),
        in_specs=[anywhere] * 5,
        out_specs=(anywhere,) * 5,
        scratch_shapes=[
            pltpu.VMEM((width, hidden), bf16),
            pltpu.VMEM((hidden, width), bf16),
            pltpu.VMEM((groups, rows, width), bf16),
            pltpu.VMEM((groups, 8, lanes), f32),
            pltpu.VMEM((flat, hidden), bf16),
            pltpu.VMEM((flat, hidden), bf16),
            pltpu.VMEM((flat, width), bf16),
            pltpu.VMEM((groups, rows, width), bf16),
            pltpu.VMEM((groups, 8, lanes), f32),
            pltpu.VMEM((2, width, part), bf16),
            pltpu.VMEM((4, width, part), bf16),
            pltpu.VMEM((2, flat // 8, width), bf16),
            sem((3,)), sem((2,)), sem((2,)), sem((4,)),
            sem((groups,)), sem((groups,)), sem((groups,)), sem((groups,)),
            sem((groups,)), sem((groups,)), sem((groups,)), sem((groups,)),
            sem((4,)), sem((4,)),
        ],
        compiler_params=pltpu.CompilerParams(
            collective_id=1, has_side_effects=True, vmem_limit_bytes=62 << 20
        ),
        cost_estimate=pl.CostEstimate(
            flops=12 * flat * width * hidden, bytes_accessed=40 << 20, transcendentals=flat * hidden
        ),
    )(xs, gs, g, weight_in, weight_out)


def fold_steps(rows, cols, bits):
    steps = []
    for bit in bits[:3]:
        rows = rows // 2
        steps.append(((bit,), "half", rows, cols))
    rows, cols = rows // 2, cols // 2
    steps.append((tuple(bits[3:5]), "quad", rows, cols))
    for bit in bits[5:]:
        steps.append(((bit,), "whole", rows, cols))
    return steps


NORM = 3


def reduce_kernel(
    attended_hbm, middle_grad_hbm, tokens_hbm, dv_hbm, dk_hbm, dq_hbm, wq_hbm, wk_hbm, wv_hbm,
    gain, small_in,
    sum_o, sum_v, sum_k, sum_q, token_grad_hbm, small_out,
    attended, middle_grad, tokens, dv, dk, dq, wq, wk, wv,
    token_grad, sums, normed, branch, acc, outbox, inbox, small_box, small_sent, load_sem, store_sem,
    ssend, srecv, tsend, trecv,
    *, dp_bits, expert_bits,
):
    f32, bf16 = jnp.float32, jnp.bfloat16
    dp = lax.axis_index("dp")
    ex = lax.axis_index("expert")
    MESH = pl.DeviceIdType.MESH
    length, width = tokens.shape
    held = (attended, middle_grad, tokens, dv, dk, dq, wq, wk, wv)
    loads = [
        pltpu.make_async_copy(there, here, load_sem.at[i])
        for i, (there, here) in enumerate(zip(
            (attended_hbm, middle_grad_hbm, tokens_hbm, dv_hbm, dk_hbm, dq_hbm, wq_hbm, wk_hbm, wv_hbm), held))
    ]
    first = 4
    for load in loads[:first]:
        load.start()

    def own_bit(bit):
        axis, place = bit
        return (dp // 2 ** place) % 2 if axis == "dp" else (ex // 2 ** place) % 2

    def partner(bits):
        there = [dp, ex]
        for bit in bits:
            there[bit[0] == "expert"] = there[bit[0] == "expert"] + (1 - 2 * own_bit(bit)) * 2 ** bit[1]
        return tuple(there)

    dpb = [("dp", i) for i in range(dp_bits)]
    exb = [("expert", i) for i in range(expert_bits)]
    orders = [
        [dpb[0], dpb[1], exb[0]] + dpb[2:] + exb[1:],
        [dpb[0], exb[0], dpb[1]] + dpb[2:] + exb[1:],
    ]
    every = dpb + exb
    small_count = len(every)

    barrier = pltpu.get_barrier_semaphore()
    greeted = [(bit,) for bit in every] + [tuple(orders[0][3:5])]
    for bits in greeted:
        pl.semaphore_signal(barrier, inc=1, device_id=partner(bits), device_id_type=MESH)
    pl.semaphore_wait(barrier, len(greeted))

    def prepare(i, _):
        span = pl.ds(pl.multiple_of(i * 256, 256), 256)
        x = tokens[span, :].astype(f32)
        inv = lax.rsqrt(jnp.mean(x * x, 1, keepdims=True) + epsilon)
        normed[span, :] = (x * inv * gain[...]).astype(bf16)
        branch[span, :] = middle_grad[span, :].astype(bf16)
        return 0
    for load in loads[:3]:
        load.wait()
    for load in loads[first:]:
        load.start()
    lax.fori_loop(0, length // 256, prepare, 0)

    lefts = (attended, normed, normed, normed)
    rights = (branch, dv, dk, dq)
    streams = []
    for s in range(4):
        row, col, at, sem_at = 0, 0, 0, 0
        plan = []
        for bits, kind, r, c in fold_steps(width, width, orders[s % 2]):
            mine = [own_bit(bit) for bit in bits]
            if kind == "half":
                peers = [bits]
                keep_at = (row + mine[0] * r, col)
                theirs = [(row + (1 - mine[0]) * r, col)]
            elif kind == "quad":
                peers = [bits[:1], bits[1:], bits]
                keep_at = (row + mine[0] * r, col + mine[1] * c)
                theirs = [
                    (row + (1 - mine[0]) * r, col + mine[1] * c),
                    (row + mine[0] * r, col + (1 - mine[1]) * c),
                    (row + (1 - mine[0]) * r, col + (1 - mine[1]) * c),
                ]
            else:
                peers, keep_at, theirs = [bits], (row, col), [(row, col)]
            plan.append((peers, kind, r, c, at, keep_at, theirs, sem_at))
            row, col = keep_at
            at += r * len(peers)
            sem_at += len(peers)
        streams.append(plan)
    count = len(streams[0])
    sems = ssend.shape[1] // 2

    def rs_copy(s, k, i):
        peers, kind, r, c, at, _, _, sem_at = streams[s][k]
        box = pl.ds(at + i * r, r)
        return pltpu.make_async_remote_copy(
            src_ref=outbox.at[s, box, pl.ds(0, c)], dst_ref=inbox.at[s, box, pl.ds(0, c)],
            send_sem=ssend.at[s, sem_at + i], recv_sem=srecv.at[s, sem_at + i],
            device_id=partner(peers[i]), device_id_type=MESH)

    def aligned(at):
        row, col = at
        row = pl.multiple_of(row, 16) if not isinstance(row, int) else row
        col = pl.multiple_of(col, 128) if not isinstance(col, int) else col
        return row, col

    def block(s, at, r, c):
        row, col = aligned(at)
        return sums.at[s, pl.ds(row, r), pl.ds(col, c)]

    def ag_copy(s, k, i, incoming):
        peers, kind, r, c, _, keep_at, theirs, sem_at = streams[s][k]
        ref = block(s, theirs[i] if incoming else keep_at, r, c)
        return pltpu.make_async_remote_copy(
            src_ref=ref, dst_ref=ref,
            send_sem=ssend.at[s, sems + sem_at + i], recv_sem=srecv.at[s, sems + sem_at + i],
            device_id=partner(peers[i]), device_id_type=MESH)

    half = width // 2
    core = own_bit(dpb[0])

    def grad(s, which):
        span = pl.ds(pl.multiple_of(which * half, half), half)
        return matmul_tn(lefts[s][:, span], rights[s][...])

    def local(s, at, r, c):
        row, col = aligned((at[0] - streams[s][0][5][0], at[1]))
        return acc.at[s, pl.ds(row, r), pl.ds(col, c)]

    def phase(s, k):
        plan = streams[s]
        if k == 0:
            if s > 0:
                loads[2 + s].wait()
            outbox[s, 0:half, :] = grad(s, 1 - core).astype(bf16)
            rs_copy(s, 0, 0).start()
            return
        if k <= count:
            peers, kind, r, c, at, keep_at, _, _ = plan[k - 1]
            view = local(s, keep_at, r, c)
            total = outbox[s, at : at + r, 0:c].astype(f32) if kind == "whole" else view[...]
            for i in range(len(peers)):
                rs_copy(s, k - 1, i).wait_recv()
                total = total + inbox[s, at + i * r : at + (i + 1) * r, 0:c].astype(f32)
            if k < count:
                view[...] = total
                peers, kind, r, c, at, _, theirs, _ = plan[k]
                for i in range(len(peers)):
                    outbox[s, at + i * r : at + (i + 1) * r, 0:c] = local(s, theirs[i], r, c)[...].astype(bf16)
                    rs_copy(s, k, i).start()
                return
            block(s, keep_at, r, c)[...] = total.astype(bf16)
        g = 2 * count - 1 - k
        if k > count and plan[g + 1][1] != "whole":
            for i in range(len(plan[g + 1][0])):
                ag_copy(s, g + 1, i, True).wait_recv()
        if g >= 0 and plan[g][1] != "whole":
            for i in range(len(plan[g][0])):
                ag_copy(s, g, i, False).start()

    gain_row = gain[...]
    rows = 256

    def norm_block(i, gain_grad):
        span = pl.ds(pl.multiple_of(i * rows, rows), rows)
        grads = (
            matmul_nt(dq[span, :], wq[...]) + matmul_nt(dk[span, :], wk[...]) + matmul_nt(dv[span, :], wv[...])
        )
        x = tokens[span, :].astype(f32)
        inv = lax.rsqrt(jnp.mean(x * x, 1, keepdims=True) + epsilon)
        scaled = grads * gain_row
        mean = jnp.sum(scaled * x, 1, keepdims=True) * (1.0 / width)
        part = inv * (scaled - x * (inv * inv * mean))
        token_grad[span, :] = (middle_grad[span, :] + part).astype(bf16)
        return gain_grad + jnp.sum(grads * (x * inv), 0, keepdims=True)

    def small_copy(k):
        return pltpu.make_async_remote_copy(
            src_ref=small_sent.at[k], dst_ref=small_box.at[k],
            send_sem=tsend.at[k], recv_sem=trecv.at[k],
            device_id=partner((every[k],)), device_id_type=MESH)

    def small_phase(k):
        if k == 0:
            gain_grad = lax.fori_loop(0, length // rows, norm_block, jnp.zeros((1, width), f32))
            small_out[...] = small_in[...]
            for i in range(width // LANES):
                small_out[i : i + 1, :] = gain_grad[:, i * LANES : (i + 1) * LANES]
        else:
            small_copy(k - 1).wait_recv()
            small_out[...] = small_out[...] + small_box[k - 1]
        if k < small_count:
            small_sent[k] = small_out[...]
            small_copy(k).start()

    last = 2 * count
    starts = (0, 0, 2, 2)
    stores = [
        pltpu.make_async_copy(sums.at[s], out, store_sem.at[s]) for s, out in enumerate((sum_o, sum_v, sum_k, sum_q))
    ]
    stores.append(pltpu.make_async_copy(token_grad, token_grad_hbm, store_sem.at[4]))
    for t in range(max(last + starts[-1], small_count + NORM) + 1):
        for s in range(4):
            if 0 <= t - starts[s] <= last:
                phase(s, t - starts[s])
                if t - starts[s] == last:
                    stores[s].start()
        for s in range(4):
            if t == starts[s]:
                acc[s] = grad(s, core)
        if t == NORM:
            for load in loads[6:9]:
                load.wait()
        if 0 <= t - NORM <= small_count:
            small_phase(t - NORM)
            if t == NORM:
                stores[4].start()
    for store in stores:
        store.wait()
    for s in range(4):
        for k in range(count):
            for i in range(len(streams[s][k][0])):
                rs_copy(s, k, i).wait_send()
                if streams[s][k][1] != "whole":
                    ag_copy(s, k, i, False).wait_send()
    for k in range(small_count):
        small_copy(k).wait_send()


def reduce_grads(tokens, attended, middle_grad, dq, dk, dv, wq, wk, wv, gain, small, dp_size, groups):
    f32, bf16 = jnp.float32, jnp.bfloat16
    length, width = tokens.shape
    dp_bits, expert_bits = dp_size.bit_length() - 1, groups.bit_length() - 1
    count = dp_bits + expert_bits
    steps = fold_steps(width, width, list(range(count)))
    box = sum(step[2] * (3 if step[1] == "quad" else 1) for step in steps)
    messages = sum(3 if step[1] == "quad" else 1 for step in steps)
    vmem = pl.BlockSpec(memory_space=pltpu.VMEM)
    anywhere = pl.BlockSpec(memory_space=pl.ANY)
    sem = pltpu.SemaphoreType.DMA
    shape = jax.ShapeDtypeStruct
    act, square = shape((length, width), bf16), shape((width, width), bf16)
    big = (attended, middle_grad, tokens, dv, dk, dq, wq, wk, wv)
    return pl.pallas_call(
        functools.partial(reduce_kernel, dp_bits=dp_bits, expert_bits=expert_bits),
        out_shape=(square, square, square, square, act, shape(small.shape, f32)),
        in_specs=[anywhere] * len(big) + [vmem] * 2,
        out_specs=(anywhere,) * 5 + (vmem,),
        scratch_shapes=[pltpu.VMEM(x.shape, x.dtype) for x in big] + [
            pltpu.VMEM((length, width), bf16),
            pltpu.VMEM((4, width, width), bf16),
            pltpu.VMEM((length, width), bf16),
            pltpu.VMEM((length, width), bf16),
            pltpu.VMEM((4, width // 2, width), f32),
            pltpu.VMEM((4, box, width), bf16),
            pltpu.VMEM((4, box, width), bf16),
            pltpu.VMEM((count,) + small.shape, f32),
            pltpu.VMEM((count,) + small.shape, f32),
            sem((len(big),)), sem((5,)),
            sem((4, 2 * messages)), sem((4, 2 * messages)), sem((count,)), sem((count,)),
        ],
        compiler_params=pltpu.CompilerParams(
            collective_id=2, has_side_effects=True, vmem_limit_bytes=62 << 20
        ),
        cost_estimate=pl.CostEstimate(
            flops=14 * length * width * width, bytes_accessed=30 << 20, transcendentals=0
        ),
    )(*big, gain, small)


def key_ranges(segment_row):
    first, last = segment_row[::BLOCK], segment_row[BLOCK - 1 :: BLOCK]
    lo = jnp.sum(segment_row[None, :] < first[:, None], 1) // BLOCK
    hi = (jnp.sum(segment_row[None, :] <= last[:, None], 1) + BLOCK - 1) // BLOCK
    return lo.astype(jnp.int32), hi.astype(jnp.int32)


def per_device(
    tokens,
    segments,
    routes,
    cotangent,
    attn_gain,
    ffn_gain,
    query_weight,
    key_weight,
    value_weight,
    output_weight,
    position_bias_grid,
    router_weight,
    expert_in,
    expert_out,
):
    f32, bf16 = jnp.float32, jnp.bfloat16
    token_count, model_width = tokens.shape
    head_count = position_bias_grid.shape[1]
    score_scale = (model_width // head_count) ** (-0.5)
    experts_all = router_weight.shape[1]
    capacity = (5 * token_count + 4 * experts_all - 1) // (4 * experts_all)
    slot_rows = (capacity + 15) // 16 * 16
    slots = experts_all * slot_rows
    groups = lax.axis_size("expert")
    dp_size = lax.axis_size("dp")

    def exchange(rows):
        return lax.all_to_all(rows, "expert", split_axis=0, concat_axis=0, tiled=True)

    routes_row = routes.reshape(1, token_count)
    token_slot, grad_slots = first_slots(routes_row, cotangent, experts_all, capacity, slot_rows)
    grad_arrived = exchange(grad_slots)
    lo, hi = key_ranges(segments[0])
    router_pad = max(experts_all, 16)
    router_t = jnp.pad(router_weight.T, ((0, router_pad - experts_all), (0, 0)))
    gain_one, gain_two = attn_gain[None, :], ffn_gain[None, :]
    queries, key_rows, keys_t, value_rows, attended, log_sums, middle, router_probs, sent, gate_slots = front(
        lo, hi, tokens, segments, token_slot, routes_row, gain_one, gain_two,
        query_weight, key_weight, value_weight, output_weight, position_bias_grid, router_t,
        experts_all, slot_rows, score_scale,
    )
    home_grad, home_gate, produced, keep, give = ffn(
        sent, gate_slots, grad_arrived.reshape(slots, model_width), expert_in[0], expert_out[0], groups, dp_size,
    )
    passed = lax.ppermute(give, "dp", [(i, (i + dp_size // 2) % dp_size) for i in range(dp_size)])
    returned = exchange(produced.reshape(experts_all, slot_rows, model_width)).reshape(slots, model_width)
    query_grad, key_grad, value_grad, middle_grad, small = back(
        lo, hi, home_grad, home_gate, token_slot, routes_row, router_probs, middle, cotangent, segments, gain_two,
        output_weight, router_t, position_bias_grid, queries, key_rows, keys_t, value_rows, log_sums, attended,
        experts_all, slot_rows, score_scale,
    )
    sum_o, sum_v, sum_k, sum_q, token_grad, small = reduce_grads(
        tokens, attended, middle_grad, query_grad, key_grad, value_grad,
        query_weight, key_weight, value_weight, gain_one, small, dp_size, groups,
    )
    (mixed, token_grad, attn_gain_grad, ffn_gain_grad, grad_q, grad_k, grad_v, grad_o, table_grad, router_grad,
     grad_in, grad_out) = finish(
        (sum_q, sum_k, sum_v, sum_o), keep, passed, returned, middle, token_grad, small,
        token_slot, routes_row, router_probs, position_bias_grid.shape, experts_all
    )
    return (
        mixed,
        token_grad,
        attn_gain_grad,
        ffn_gain_grad,
        grad_q,
        grad_k,
        grad_v,
        grad_o,
        table_grad.T,
        router_grad.T,
        grad_in[None],
        grad_out[None],
    )


def solution(mesh):
    rows = P(("dp", "expert"), None)
    return jax.shard_map(
        per_device,
        mesh=mesh,
        in_specs=(rows,) * 4 + (P(),) * 8 + (P("expert", None, None),) * 2,
        out_specs=(rows,) * 2 + (P(),) * 8 + (P("expert", None, "dp"), P("expert", "dp", None)),
        check_vma=False,
    )
```

```python
import functools

import jax
import jax.numpy as jnp
from jax import lax
from jax.experimental import pallas as pl
from jax.experimental.pallas import tpu as pltpu
from jax.sharding import PartitionSpec as P

epsilon = 1e-06
precise_setting = lax.Precision.HIGHEST
def matmul(left, right):
    return jnp.dot(left, right, preferred_element_type=jnp.float32)


def matmul_tn(left, right):
    return lax.dot_general(left, right, (((0,), (0,)), ((), ())), preferred_element_type=jnp.float32)


def matmul_nt(left, right):
    return lax.dot_general(left, right, (((1,), (1,)), ((), ())), preferred_element_type=jnp.float32)


bucket_bounds = (12, 16, 23, 32, 46, 64, 91)
masked_score = -1e30
LANES = 128
BLOCK = 128
NEAR = 5
UF = 6
UB = 6


def bucket_of(relative):
    distance = jnp.abs(relative)
    beyond = jnp.zeros_like(distance)
    for threshold in bucket_bounds:
        beyond = beyond + (distance >= threshold).astype(jnp.int32)
    inside = jnp.where(distance < 8, distance, 8 + beyond)
    return inside + 16 * (relative > 0).astype(jnp.int32)


def dot_nt(a, b):
    return lax.dot_general(a, b, (((1,), (1,)), ((), ())), preferred_element_type=jnp.float32)


def dot_nn(a, b):
    return lax.dot_general(a, b, (((1,), (0,)), ((), ())), preferred_element_type=jnp.float32)


def split3(x):
    a = x.astype(jnp.bfloat16)
    r = x - a.astype(jnp.float32)
    b = r.astype(jnp.bfloat16)
    c = (r - b.astype(jnp.float32)).astype(jnp.bfloat16)
    return a, b, c


def fill_bias(diag_ref, bias, pairs):
    for p in range(pairs):
        for d in range(NEAR):
            tiles = []
            for h in (2 * p, 2 * p + 1):
                row = diag_ref[h : h + 1, :]
                if d in (0, NEAR - 1):
                    col = row[:, 511:512] if d == 0 else row[:, 0:1]
                    tiles.append(jnp.broadcast_to(col, (BLOCK, BLOCK)))
                else:
                    base = (3 - d) * BLOCK
                    wide = jnp.broadcast_to(row[:, base : base + 2 * BLOCK], (BLOCK, 2 * BLOCK))
                    tiles.append(pltpu.roll(wide, BLOCK, 1, stride=1, stride_axis=0)[:, :BLOCK])
            bias[p, d] = jnp.concatenate(tiles, 1)


def heads_apart(block, low, extra=None):
    zero = jnp.zeros_like(block)
    first, second = jnp.where(low, block, zero), jnp.where(low, zero, block)
    if extra is not None:
        first, second = jnp.concatenate([first, extra], 1), jnp.concatenate([second, extra], 1)
    return jnp.concatenate([first, second], 0)


def by_count(lo, hi, most, body):
    for n in range(1, most + 1):
        pl.when(hi - lo == n)(functools.partial(body, n))


def own_heads(wide):
    return jnp.concatenate([wide[:64, :LANES], wide[64:128, LANES:]], 0)


def attend(lo_ref, hi_ref, q_ref, k_ref, vt_ref, qm_ref, km_ref, bias, o_ref, lse_ref):
    pairs = q_ref.shape[1] // LANES
    length = q_ref.shape[0]
    nblk = length // BLOCK
    f32, bf16 = jnp.float32, jnp.bfloat16
    low = lax.broadcasted_iota(jnp.int32, (1, LANES), 1) < 64

    def q_block(i, _):
        lo, hi = lo_ref[i], hi_ref[i]
        rows = pl.ds(pl.multiple_of(i * BLOCK, BLOCK), BLOCK)
        start = pl.multiple_of(lo * BLOCK, BLOCK)
        qm = qm_ref[rows, :]

        def body(n):
            span = pl.ds(start, n * BLOCK)
            km = km_ref[span, :]

            def lanes_of(p):
                return pl.ds(pl.multiple_of(p * LANES, LANES), LANES)

            def scores(p):
                qs = heads_apart(q_ref[rows, lanes_of(p)], low, qm)
                return dot_nt(jnp.concatenate([k_ref[span, lanes_of(p)], km], 1), qs)

            def soften(p, st):
                parts = []
                top = None
                for b in range(n):
                    d = jnp.clip(lo + b - i, -2, 2) + 2
                    s = st[b * BLOCK : (b + 1) * BLOCK] + bias[p, d]
                    parts.append(s)
                    top = s if top is None else jnp.maximum(top, s)
                top = jnp.max(top, 0, keepdims=True)
                return jnp.concatenate([jnp.exp(s - top).astype(bf16) for s in parts], 0), top

            def mix(p, probs):
                values = jnp.concatenate([vt_ref[lanes_of(p), span], jnp.ones((16, n * BLOCK), bf16)], 0)
                return dot_nn(values, probs)

            def finish(p, acc, top):
                total = acc[LANES : LANES + 1]
                inv = 1.0 / total
                ot = own_heads(acc)
                ot = jnp.concatenate([ot[:64] * inv[:, :LANES], ot[64:] * inv[:, LANES:]], 0)
                o_ref[rows, lanes_of(p)] = ot.T.astype(bf16)
                lse_ref[i, pl.ds(p, 1), :] = top + jnp.log(total)

            def some(g, _):
                ps = [g * UF + u for u in range(UF)]
                sts = [scores(p) for p in ps]
                soft = [soften(p, st) for p, st in zip(ps, sts)]
                accs = [mix(p, x[0]) for p, x in zip(ps, soft)]
                for p, acc, x in zip(ps, accs, soft):
                    finish(p, acc, x[1])
                return 0
            lax.fori_loop(0, pairs // UF, some, 0)

        by_count(lo, hi, nblk, body)
        return 0
    lax.fori_loop(0, nblk, q_block, 0)


def attend_back(
    lo_ref, hi_ref, q_ref, k_ref, kt_ref, v_ref, lse_ref, do_ref, o_ref, qm_ref, km_ref, bias,
    dq_ref, dk_ref, dv_ref, gsum_ref, gacc, dkacc, dvacc, scale,
):
    length, width = q_ref.shape
    pairs = width // LANES
    nblk = length // BLOCK
    f32, bf16 = jnp.float32, jnp.bfloat16
    low = lax.broadcasted_iota(jnp.int32, (1, LANES), 1) < 64
    pick = (
        lax.broadcasted_iota(jnp.int32, (16, LANES), 0) == lax.broadcasted_iota(jnp.int32, (16, LANES), 1) // 64
    ).astype(f32).astype(bf16)
    gacc[...] = jnp.zeros_like(gacc)
    gsum_ref[...] = jnp.zeros_like(gsum_ref)
    dkacc[...] = jnp.zeros_like(dkacc)
    dvacc[...] = jnp.zeros_like(dvacc)

    def q_block(i, _):
        lo, hi = lo_ref[i], hi_ref[i]
        rows = pl.ds(pl.multiple_of(i * BLOCK, BLOCK), BLOCK)
        start = pl.multiple_of(lo * BLOCK, BLOCK)
        qm = qm_ref[rows, :]

        def body(n):
            span = pl.ds(start, n * BLOCK)
            km = km_ref[span, :]

            def lanes_of(p):
                return pl.ds(pl.multiple_of(p * LANES, LANES), LANES)

            def products(p):
                cols = lanes_of(p)
                qs = heads_apart(q_ref[rows, cols], low, qm)
                dd = do_ref[rows, cols]
                dos = heads_apart(dd, low)
                prod = dd.astype(f32) * o_ref[rows, cols].astype(f32)
                prod_hi = prod.astype(bf16)
                prod_lo = (prod - prod_hi.astype(f32)).astype(bf16)
                inner = dot_nt(pick, prod_hi) + dot_nt(pick, prod_lo)
                inner = jnp.concatenate([inner[0:1], inner[1:2]], 1)
                st = dot_nt(jnp.concatenate([k_ref[span, cols], km], 1), qs)
                dpt = dot_nt(v_ref[span, cols], dos)
                return qs, dos, inner, st, dpt

            def pointwise(p, inner, st, dpt):
                lse = lse_ref[i, pl.ds(p, 1), :]
                probs, grads = [], []
                for b in range(n):
                    d = jnp.clip(lo + b - i, -2, 2) + 2
                    part = slice(b * BLOCK, (b + 1) * BLOCK)
                    prob = jnp.exp(st[part] + bias[p, d] - lse)
                    grad = prob * (dpt[part] - inner)
                    gacc[p, d] += grad
                    probs.append(prob.astype(bf16))
                    grads.append(grad.astype(bf16))
                return jnp.concatenate(probs, 0), jnp.concatenate(grads, 0)

            def back(p, qs, dos, probs, grads):
                cols = lanes_of(p)
                return (
                    dot_nn(probs, dos), dot_nn(grads, qs[:, :LANES]), dot_nn(kt_ref[cols, span], grads)
                )

            def finish(p, dv, dk, dqt):
                cols = lanes_of(p)
                dvacc[span, cols] += dv
                dkacc[span, cols] += dk
                dq_ref[rows, cols] = (own_heads(dqt).T * scale).astype(bf16)

            def some(g, _):
                ps = [g * UB + u for u in range(UB)]
                first = [products(p) for p in ps]
                points = [pointwise(p, *x[2:]) for p, x in zip(ps, first)]
                last = [back(p, *x[:2], *y) for p, x, y in zip(ps, first, points)]
                for p, x in zip(ps, last):
                    finish(p, *x)
                return 0
            lax.fori_loop(0, pairs // UB, some, 0)

        by_count(lo, hi, nblk, body)
        return 0
    lax.fori_loop(0, nblk, q_block, 0)
    dk_ref[...] = dkacc[...].astype(bf16)
    dv_ref[...] = dvacc[...].astype(bf16)
    turn = (
        lax.broadcasted_iota(jnp.int32, (BLOCK, BLOCK), 0) + lax.broadcasted_iota(jnp.int32, (BLOCK, BLOCK), 1)
        == BLOCK - 1
    ).astype(f32).astype(bf16)
    for p in range(pairs):
        for d in range(NEAR):
            t = gacc[p, d]
            if 0 < d < NEAR - 1:
                hi = t.astype(bf16)
                t = dot_nn(turn, hi) + dot_nn(turn, (t - hi.astype(f32)).astype(bf16))
            for u in range(2):
                s = jnp.concatenate([t[:, u * LANES : (u + 1) * LANES], jnp.zeros((BLOCK, LANES), f32)], 1)
                if 0 < d < NEAR - 1:
                    s = pltpu.roll(s, 0, 1, stride=1, stride_axis=0)
                at = d * 16 + 2 * p + u
                gsum_ref[at : at + 1, :] = jnp.sum(s, 0, keepdims=True)


def two(x):
    a = x.astype(jnp.bfloat16)
    return a, (x - a.astype(jnp.float32)).astype(jnp.bfloat16)


def row_pieces(row):
    place = lax.broadcasted_iota(jnp.int32, (16, row.shape[1]), 0)
    a, b, c = [x.astype(jnp.float32) for x in split3(row)]
    return jnp.where(place == 0, a, jnp.where(place == 1, b, jnp.where(place == 2, c, 0.0))).astype(jnp.bfloat16)


def each(count, body):
    if count <= 8:
        for e in range(count):
            body(e)
    else:
        def step(e, _):
            body(e)
            return 0
        lax.fori_loop(0, count, step, 0)


def slot_hot(slot_row, e, slot_rows):
    place = lax.broadcasted_iota(jnp.int32, (slot_rows, slot_row.shape[1]), 0) + e * slot_rows
    return (place == slot_row).astype(jnp.float32).astype(jnp.bfloat16)


def token_hot(slot_row, slots):
    first = lax.broadcasted_iota(jnp.int32, (BLOCK, LANES), 1).astype(jnp.float32)
    blocks = []
    for c in range(0, slot_row.shape[1], BLOCK):
        column = jnp.broadcast_to(slot_row[:, c : c + BLOCK].astype(jnp.float32), (BLOCK, BLOCK)).T
        blocks.append(jnp.concatenate(
            [(column == first + float(s)).astype(jnp.float32).astype(jnp.bfloat16) for s in range(0, slots, LANES)], 1))
    return jnp.concatenate(blocks, 0)


def slots_kernel(routes_ref, rows_ref, slot_ref, out_ref, *, experts, capacity, slot_rows):
    f32, bf16 = jnp.float32, jnp.bfloat16
    tokens = routes_ref.shape[1]
    routes = routes_ref[...]
    pad = max(experts, 16)
    hot = (lax.broadcasted_iota(jnp.int32, (pad, tokens), 0) == routes).astype(f32)
    earlier = (
        lax.broadcasted_iota(jnp.int32, (BLOCK, BLOCK), 0) < lax.broadcasted_iota(jnp.int32, (BLOCK, BLOCK), 1)
    ).astype(f32).astype(bf16)
    seen = jnp.zeros((pad, 1), f32)
    ranks = []
    for c in range(0, tokens, BLOCK):
        part = hot[:, c : c + BLOCK]
        ranks.append(jnp.sum((dot_nn(part.astype(bf16), earlier) + seen) * part, 0, keepdims=True))
        seen = seen + jnp.sum(part, 1, keepdims=True)
    rank = jnp.concatenate(ranks, 1).astype(jnp.int32)
    slot = jnp.where(rank < capacity, routes * slot_rows + rank, -1)
    slot_ref[...] = jnp.broadcast_to(slot, slot_ref.shape)

    rows = dot_nn(slot_hot(slot, 0, experts * slot_rows), rows_ref[...]).astype(bf16)
    out_ref[...] = rows.reshape(out_ref.shape)


def first_slots(routes_row, rows, experts, capacity, slot_rows):
    tokens, width = rows.shape
    vmem = pl.BlockSpec(memory_space=pltpu.VMEM)
    return pl.pallas_call(
        functools.partial(slots_kernel, experts=experts, capacity=capacity, slot_rows=slot_rows),
        out_shape=(
            jax.ShapeDtypeStruct((8, tokens), jnp.int32),
            jax.ShapeDtypeStruct((experts, slot_rows, width), jnp.bfloat16),
        ),
        in_specs=[vmem] * 2,
        out_specs=(vmem,) * 2,
        compiler_params=pltpu.CompilerParams(vmem_limit_bytes=63 << 20),
        cost_estimate=pl.CostEstimate(
            flops=2 * experts * slot_rows * tokens * width, bytes_accessed=4 << 20, transcendentals=0
        ),
    )(routes_row, rows)


def fill_masks(segment_row, qm, km):
    f32, bf16 = jnp.float32, jnp.bfloat16
    lane = lax.broadcasted_iota(jnp.int32, (1, LANES), 1)
    for b in range(qm.shape[0] // BLOCK):
        span = slice(b * BLOCK, (b + 1) * BLOCK)
        hot = (lax.broadcasted_iota(jnp.int32, (LANES, BLOCK), 0) == segment_row[:, span]).astype(f32).T
        qm[span, :] = (hot * masked_score).astype(bf16)
        km[span, :] = jnp.where(lane < 8, 1.0 - hot, 0.0).astype(bf16)


def fill_diag(grid_ref, diag, heads):
    bf16 = jnp.bfloat16
    buckets = grid_ref.shape[0]
    relative = 256 - lax.broadcasted_iota(jnp.int32, (buckets, 4 * LANES), 1)
    hot = (lax.broadcasted_iota(jnp.int32, (buckets, 4 * LANES), 0) == bucket_of(relative))
    hot = hot.astype(jnp.float32).astype(bf16)
    grid = jnp.concatenate(
        [grid_ref[...], jnp.zeros((buckets, LANES - heads), jnp.float32)], 1
    ).T[:16]
    total = None
    for piece in split3(grid):
        term = dot_nn(piece, hot)
        total = term if total is None else total + term
    diag[...] = total


def front_kernel(
    lo_ref, hi_ref, tokens, segment_row, slot_ref, routes_ref, gain_one, gain_two, wq, wk, wv, wo, grid_ref, router_t,
    q_ref, k_ref, kt_ref, v_ref, o_ref, lse_ref, middle_ref, probs_ref, xs_ref, gs_ref,
    vt_ref, qm_ref, km_ref, diag, bias, hidden, *, experts, slot_rows, scale,
):
    f32, bf16 = jnp.float32, jnp.bfloat16
    length, width = tokens.shape
    pairs = width // LANES
    nblk = length // BLOCK
    heads = grid_ref.shape[1]
    low = lax.broadcasted_iota(jnp.int32, (1, LANES), 1) < 64
    step = 256

    for b in range(length // step):
        span = slice(b * step, (b + 1) * step)
        x = tokens[span, :].astype(f32)
        inverse = lax.rsqrt(jnp.mean(x * x, 1, keepdims=True) + epsilon)
        normed = (x * inverse * gain_one[...]).astype(bf16)
        q_ref[span, :] = (dot_nn(normed, wq[...]).astype(bf16).astype(f32) * scale).astype(bf16)
        k = dot_nn(normed, wk[...]).astype(bf16)
        k_ref[span, :] = k
        kt_ref[:, span] = k.T
        v = dot_nn(normed, wv[...]).astype(bf16)
        v_ref[span, :] = v
        vt_ref[:, span] = v.T
    fill_masks(segment_row[...], qm_ref, km_ref)
    fill_diag(grid_ref, diag, heads)
    fill_bias(diag, bias, pairs)
    attend(lo_ref, hi_ref, q_ref, k_ref, vt_ref, qm_ref, km_ref, bias, o_ref, lse_ref)

    rw = two(router_t[...])
    routes = routes_ref[...]
    pad = router_t.shape[0]
    place = lax.broadcasted_iota(jnp.int32, (pad, step), 0)
    gates = []
    for b in range(length // step):
        span = slice(b * step, (b + 1) * step)
        middle = tokens[span, :].astype(f32) + dot_nn(o_ref[span, :], wo[...])
        middle_ref[span, :] = middle
        inverse = lax.rsqrt(jnp.mean(middle * middle, 1, keepdims=True) + epsilon)
        parts = two(middle * inverse * gain_two[...])
        hidden[span, :] = parts[0]
        logits = dot_nt(rw[0], parts[0]) + dot_nt(rw[0], parts[1]) + dot_nt(rw[1], parts[0])
        logits = jnp.where(place < experts, logits, -1e30)
        powers = jnp.exp(logits - jnp.max(logits, 0, keepdims=True))
        probs = powers / jnp.sum(powers, 0, keepdims=True)
        probs_ref[:, span] = probs
        gates.append(jnp.sum(jnp.where(place == routes[:, span], probs, 0.0), 0, keepdims=True))
    gates = row_pieces(jnp.concatenate(gates, 1))
    slot = slot_ref[0:1, :]
    lanes = gs_ref.shape[2]

    def one(e):
        hot = slot_hot(slot, e, slot_rows)
        xs_ref[e] = dot_nn(hot, hidden[...]).astype(bf16)
        if lanes > slot_rows:
            hot = jnp.concatenate([hot, jnp.zeros((lanes - slot_rows, length), bf16)], 0)
        row = jnp.sum(dot_nt(gates, hot), 0, keepdims=True)
        gs_ref[e] = jnp.broadcast_to(row, gs_ref.shape[1:])
    each(experts, one)


def front(lo, hi, tokens, segments, slot, routes_row, gain_one, gain_two, wq, wk, wv, wo, grid, router_t, experts, slot_rows, scale):
    length, width = tokens.shape
    heads = grid.shape[1]
    pairs = width // LANES
    nblk = length // BLOCK
    lanes = (slot_rows + LANES - 1) // LANES * LANES
    smem = pl.BlockSpec(memory_space=pltpu.SMEM)
    vmem = pl.BlockSpec(memory_space=pltpu.VMEM)
    f32, bf16 = jnp.float32, jnp.bfloat16
    shape = jax.ShapeDtypeStruct
    act = shape((length, width), bf16)
    return pl.pallas_call(
        functools.partial(front_kernel, experts=experts, slot_rows=slot_rows, scale=scale),
        out_shape=(
            act, act, shape((width, length), bf16), act, act,
            shape((nblk, 8, 2 * LANES), f32), shape((length, width), f32),
            shape((router_t.shape[0], length), f32),
            shape((experts, slot_rows, width), bf16), shape((experts, 8, lanes), f32),
        ),
        in_specs=[smem] * 2 + [vmem] * 12,
        out_specs=(vmem,) * 10,
        scratch_shapes=[
            pltpu.VMEM((width, length), bf16),
            pltpu.VMEM((length, LANES), bf16),
            pltpu.VMEM((length, LANES), bf16),
            pltpu.VMEM((16, 4 * LANES), f32),
            pltpu.VMEM((pairs, NEAR, BLOCK, 2 * LANES), f32),
            pltpu.VMEM((length, width), bf16),
        ],
        compiler_params=pltpu.CompilerParams(vmem_limit_bytes=63 << 20),
        cost_estimate=pl.CostEstimate(
            flops=4 * length * length * width + 12 * length * width * width, bytes_accessed=20 << 20,
            transcendentals=length * length * heads,
        ),
    )(lo, hi, tokens, segments, slot, routes_row, gain_one, gain_two, wq, wk, wv, wo, grid, router_t)


def bucket_sums(gsum_ref):
    bf16 = jnp.bfloat16
    total = jnp.zeros((16, LANES), jnp.float32)
    lane = lax.broadcasted_iota(jnp.int32, (2 * LANES, LANES), 1)
    for d in range(NEAR):
        relative = (d - 2) * BLOCK + BLOCK - 1 - lax.broadcasted_iota(jnp.int32, (2 * LANES, LANES), 0)
        bucket = 15 if d == 0 else 31 if d == NEAR - 1 else bucket_of(relative)
        hot = (lane == bucket).astype(jnp.float32).astype(bf16)
        for piece in split3(gsum_ref[d * 16 : (d + 1) * 16, :]):
            total = total + dot_nn(piece, hot)
    return total


def small_shape(width, experts):
    return (16 + width // LANES * experts + 16, LANES)


def back_kernel(
    lo_ref, hi_ref, home, home_gate, slot_ref, routes_ref, probs_ref, middle_ref, cotangent, segment_row, gain_two,
    wo, router_t, grid_ref, lse_ref, q_hbm, k_hbm, kt_hbm, v_hbm, o_hbm,
    dq_ref, dk_ref, dv_ref, middle_grad_hbm, small,
    q_ref, k_ref, kt_ref, v_ref, o_ref, middle_grad,
    do_ref, qm_ref, km_ref, diag, bias, gacc, dkacc, dvacc, logit, gsum_ref, sems,
    *, experts, slot_rows, scale,
):
    f32, bf16 = jnp.float32, jnp.bfloat16
    length, width = middle_ref.shape
    pairs = width // LANES
    pad = router_t.shape[0]
    heads = grid_ref.shape[1]
    slot = slot_ref[0:1, :]
    loads = [
        pltpu.make_async_copy(there, here, sems.at[i])
        for i, (there, here) in enumerate(zip(
            (q_hbm, k_hbm, kt_hbm, v_hbm, o_hbm), (q_ref, k_ref, kt_ref, v_ref, o_ref)))
    ]
    for load in loads:
        load.start()

    if experts <= 8:
        total = jnp.zeros((16, length), f32)
        for e in range(experts):
            total = total + dot_nn(row_pieces(home_gate[e, 0:1, :])[:, :slot_rows], slot_hot(slot, e, slot_rows))
    else:
        def add(e, total):
            return total + dot_nn(row_pieces(home_gate[e, 0:1, :])[:, :slot_rows], slot_hot(slot, e, slot_rows))
        total = lax.fori_loop(0, experts, add, jnp.zeros((16, length), f32))
    gate_grad = jnp.sum(total, 0, keepdims=True)
    place = lax.broadcasted_iota(jnp.int32, (pad, length), 0)
    hot = place == routes_ref[...]
    probs = probs_ref[...]
    gate = jnp.sum(jnp.where(hot, probs, 0.0), 0, keepdims=True)
    logit[...] = probs * (jnp.where(hot, gate_grad, 0.0) - gate * gate_grad)
    rw = two(router_t[...])
    stacked = jnp.concatenate([rw[0], rw[1], rw[0]], 0)
    slots = experts * slot_rows
    dkacc[...] = dot_nn(token_hot(slot, slots), home[...].reshape(slots, width))
    router_sum = jnp.zeros((pad, width), f32)
    gain_sum = jnp.zeros((1, width), f32)
    step = 256
    for b in range(length // step):
        span = slice(b * step, (b + 1) * step)
        lg = two(logit[:, span])
        hidden_grad = dkacc[span, :] + matmul_tn(jnp.concatenate([lg[0], lg[0], lg[1]], 0), stacked)
        middle = middle_ref[span, :]
        inverse = lax.rsqrt(jnp.mean(middle * middle, 1, keepdims=True) + epsilon)
        unit = middle * inverse
        hidden = two(unit * gain_two[...])
        both = dot_nn(jnp.concatenate(lg, 0), hidden[0])
        router_sum = router_sum + (both[:pad] + both[pad:] + dot_nn(lg[0], hidden[1]))
        gain_sum = gain_sum + jnp.sum(hidden_grad * unit, 0, keepdims=True)
        scaled = hidden_grad * gain_two[...]
        mean = jnp.mean(scaled * middle, 1, keepdims=True)
        grad = cotangent[span, :].astype(f32) + inverse * (scaled - unit * (inverse * mean))
        middle_grad[span, :] = grad
        dq_ref[span, :] = grad.astype(bf16)
    store = pltpu.make_async_copy(middle_grad, middle_grad_hbm, sems.at[5])
    store.start()
    do_ref[...] = matmul_nt(dq_ref[...], wo[...]).astype(bf16)
    small[...] = jnp.zeros_like(small)
    chunks = width // LANES
    for c in range(chunks):
        cols = slice(c * LANES, (c + 1) * LANES)
        small[8 + c : 9 + c, :] = gain_sum[:, cols]
        small[16 + c * experts : 16 + (c + 1) * experts, :] = router_sum[:experts, cols]

    fill_masks(segment_row[...], qm_ref, km_ref)
    fill_diag(grid_ref, diag, heads)
    fill_bias(diag, bias, pairs)
    for load in loads:
        load.wait()
    attend_back(
        lo_ref, hi_ref, q_ref, k_ref, kt_ref, v_ref, lse_ref, do_ref, o_ref, qm_ref, km_ref, bias,
        dq_ref, dk_ref, dv_ref, gsum_ref, gacc, dkacc, dvacc, scale,
    )
    at = 16 + chunks * experts
    small[at : at + 16, :] = bucket_sums(gsum_ref)
    store.wait()


def back(lo, hi, home, home_gate, slot, routes_row, probs, middle, cotangent, segments, gain_two, wo, router_t, grid,
         q, k, kt, v, lse, o, experts, slot_rows, scale):
    length, width = middle.shape
    heads = grid.shape[1]
    pairs = width // LANES
    smem = pl.BlockSpec(memory_space=pltpu.SMEM)
    vmem = pl.BlockSpec(memory_space=pltpu.VMEM)
    f32, bf16 = jnp.float32, jnp.bfloat16
    shape = jax.ShapeDtypeStruct
    act = shape((length, width), bf16)
    anywhere = pl.BlockSpec(memory_space=pl.ANY)
    return pl.pallas_call(
        functools.partial(back_kernel, experts=experts, slot_rows=slot_rows, scale=scale),
        out_shape=(act, act, act, shape((length, width), f32), shape(small_shape(width, experts), f32)),
        in_specs=[smem] * 2 + [vmem] * 13 + [anywhere] * 5,
        out_specs=(vmem, vmem, vmem, anywhere, vmem),
        scratch_shapes=[
            pltpu.VMEM((length, width), bf16),
            pltpu.VMEM((length, width), bf16),
            pltpu.VMEM((width, length), bf16),
            pltpu.VMEM((length, width), bf16),
            pltpu.VMEM((length, width), bf16),
            pltpu.VMEM((length, width), f32),
            pltpu.VMEM((length, width), bf16),
            pltpu.VMEM((length, LANES), bf16),
            pltpu.VMEM((length, LANES), bf16),
            pltpu.VMEM((16, 4 * LANES), f32),
            pltpu.VMEM((pairs, NEAR, BLOCK, 2 * LANES), f32),
            pltpu.VMEM((pairs, NEAR, BLOCK, 2 * LANES), f32),
            pltpu.VMEM((length, width), f32),
            pltpu.VMEM((length, width), f32),
            pltpu.VMEM((router_t.shape[0], length), f32),
            pltpu.VMEM((NEAR * 16, 2 * LANES), f32),
            pltpu.SemaphoreType.DMA((6,)),
        ],
        compiler_params=pltpu.CompilerParams(vmem_limit_bytes=63 << 20),
        cost_estimate=pl.CostEstimate(
            flops=10 * length * length * width + 6 * length * width * width, bytes_accessed=30 << 20,
            transcendentals=length * length * heads,
        ),
    )(lo, hi, home, home_gate, slot, routes_row, probs, middle, cotangent, segments, gain_two, wo, router_t, grid,
      lse, q, k, kt, v, o)


def finish_kernel(
    sum_q, sum_k, sum_v, sum_o, keep, passed, returned_in, middle_in, token_in, small, slot_ref, routes_ref, probs_ref,
    mixed_out, token_out, gain_one, gain_two, grad_q, grad_k, grad_v, grad_o, table_t, router_t, grad_in, grad_out,
    low, wide, returned, middle, mixed, token, load_sem, store_sem, copy_sem, mix_sem, *, experts,
):
    f32 = jnp.float32
    sources = (sum_o, sum_v, sum_k, sum_q, keep.at[0], keep.at[1], passed.at[0], passed.at[1])
    targets = (grad_o, grad_v, grad_k, grad_q, grad_in, grad_out)
    width = sum_q.shape[0]
    rows = 256
    spans = [pl.ds(r, rows) for r in range(0, width, rows)]
    fetches = [
        pltpu.make_async_copy(x, y, copy_sem.at[i])
        for i, (x, y) in enumerate(((returned_in, returned), (middle_in, middle), (token_in, token)))
    ]
    copies = [pltpu.make_async_copy(token, token_out, copy_sem.at[3])]
    length = middle.shape[0]
    slots = returned.shape[0]
    for c in range(0, length, BLOCK):
        rows_c = pl.ds(c, BLOCK)
        copies.append(pltpu.make_async_copy(mixed.at[rows_c], mixed_out.at[rows_c], mix_sem.at[c // BLOCK]))
    pad = probs_ref.shape[0]
    hot = lax.broadcasted_iota(jnp.int32, (pad, length), 0) == routes_ref[...]
    gate_row = jnp.sum(jnp.where(hot, probs_ref[...], 0.0), 0, keepdims=True)

    def mix(c, rows_back):
        at = slice(c, c + BLOCK)
        gate = jnp.broadcast_to(gate_row[:, at], (BLOCK, BLOCK)).T
        gate = jnp.concatenate([gate] * (width // LANES), 1)
        mixed[at, :] = (middle[at, :] + gate * rows_back[at]).astype(jnp.bfloat16)

    loads = [
        [pltpu.make_async_copy(x.at[span], low.at[i, span], load_sem.at[i, j]) for j, span in enumerate(spans)]
        for i, x in enumerate(sources)
    ]
    stores = [
        [pltpu.make_async_copy(wide.at[i, span], x.at[span], store_sem.at[i, j]) for j, span in enumerate(spans)]
        for i, x in enumerate(targets)
    ]
    for i in range(4):
        for load in loads[i]:
            load.start()
    for fetch in fetches:
        fetch.start()
    for i in range(4, 8):
        for load in loads[i]:
            load.start()
    chunks = width // LANES
    gain_one[...] = jnp.concatenate([small[c : c + 1, :] for c in range(chunks)], 1).reshape(width)
    gain_two[...] = jnp.concatenate([small[8 + c : 9 + c, :] for c in range(chunks)], 1).reshape(width)
    for c in range(chunks):
        router_t[:, c * LANES : (c + 1) * LANES] = small[16 + c * experts : 16 + (c + 1) * experts, :]
    at = 16 + chunks * experts
    heads, buckets = table_t.shape
    table_t[...] = small[at : at + heads, :buckets]
    for i in range(4):
        for j, span in enumerate(spans):
            loads[i][j].wait()
            wide[i, span, :] = low[i, span, :].astype(f32)
            stores[i][j].start()
    fetches[0].wait()
    rows_back = dot_nn(token_hot(slot_ref[0:1, :], slots), returned[...])
    fetches[2].wait()
    copies[0].start()
    for i in (4, 5):
        for j, span in enumerate(spans):
            loads[i][j].wait()
            loads[i + 2][j].wait()
            wide[i, span, :] = low[i, span, :].astype(f32) + low[i + 2, span, :].astype(f32)
            stores[i][j].start()
    fetches[1].wait()
    for c in range(0, length, BLOCK):
        mix(c, rows_back)
        copies[1 + c // BLOCK].start()
    for i in range(6):
        for store in stores[i]:
            store.wait()
    for copy in copies:
        copy.wait()


def finish(sums, keep, passed, returned, middle, token_grad, small, slot, routes_row, probs, grid_shape, experts):
    f32, bf16 = jnp.float32, jnp.bfloat16
    width = sums[0].shape[0]
    vmem = pl.BlockSpec(memory_space=pltpu.VMEM)
    anywhere = pl.BlockSpec(memory_space=pl.ANY)
    shape = jax.ShapeDtypeStruct
    act = shape(middle.shape, bf16)
    square, row = shape((width, width), f32), shape((width,), f32)
    blocks = width // 256
    return pl.pallas_call(
        functools.partial(finish_kernel, experts=experts),
        out_shape=(act, act, row, row, square, square, square, square, shape(grid_shape[::-1], f32),
                   shape((experts, width), f32), square, square),
        in_specs=[anywhere] * 9 + [vmem] * 4,
        out_specs=(anywhere,) * 2 + (vmem, vmem) + (anywhere,) * 4 + (vmem, vmem) + (anywhere,) * 2,
        scratch_shapes=[
            pltpu.VMEM((8, width, width), bf16), pltpu.VMEM((6, width, width), f32),
            pltpu.VMEM(returned.shape, bf16), pltpu.VMEM(middle.shape, f32),
            pltpu.VMEM(middle.shape, bf16), pltpu.VMEM(middle.shape, bf16),
            pltpu.SemaphoreType.DMA((8, blocks)), pltpu.SemaphoreType.DMA((6, blocks)),
            pltpu.SemaphoreType.DMA((4,)), pltpu.SemaphoreType.DMA((middle.shape[0] // BLOCK,)),
        ],
        compiler_params=pltpu.CompilerParams(vmem_limit_bytes=63 << 20),
        cost_estimate=pl.CostEstimate(flops=0, bytes_accessed=30 << 20, transcendentals=0),
    )(*sums, keep, passed, returned, middle, token_grad, small, slot, routes_row, probs)


def gelu_parts(v):
    mag = jnp.abs(v)
    t = 1.0 / (1.0 + (0.3275911 * 0.7071067811865476) * mag)
    poly = t * (0.127414796 + t * (-0.142248368 + t * (0.7107068705 + t * (-0.7265760135 + t * 0.5307027145))))
    gauss = jnp.exp(-0.5 * v * v)
    tail = poly * gauss
    phi = jnp.where(v < 0, tail, 1.0 - tail)
    return v * phi, phi + v * gauss * 0.3989422804014327


def flip_bits(index, mask, count):
    out = 0
    bit = 1
    while bit < count:
        a, b = (index // bit) % 2, (mask // bit) % 2
        out = out + bit * (a + b - 2 * a * b)
        bit *= 2
    return out


def ffn_kernel(
    xs, gs, g, win_hbm, wout_hbm,
    home, home_gate, produced, keep, give,
    win, wout, xr, gr, act, pg, gated, igs, ggs, dws, dwr, stage,
    wsem, own_sem, psem, ksem, xsend, xrecv, gsend, grecv, isend, irecv, qsend, qrecv, dsend, drecv,
    *, groups, dp_size, tiles,
):
    f32, bf16 = jnp.float32, jnp.bfloat16
    me = lax.axis_index("expert")
    dp = lax.axis_index("dp")
    core = dp % 2
    sibling = dp + 1 - 2 * core
    half_of = dp // 2
    rows = xs.shape[1]
    width = xs.shape[2]
    hidden = win.shape[1]
    tile = hidden // tiles
    lanes = gs.shape[2]

    def there(peer):
        return (dp, peer)

    load_in = pltpu.make_async_copy(win_hbm, win, wsem.at[0])
    load_out = pltpu.make_async_copy(wout_hbm, wout, wsem.at[1])
    load_in.start()
    load_out.start()
    load_g = pltpu.make_async_copy(g, gated, wsem.at[2])
    load_g.start()

    barrier = pltpu.get_barrier_semaphore()

    def greet(s, _):
        pl.semaphore_signal(
            barrier, inc=1, device_id=there(flip_bits(me, s, groups)), device_id_type=pl.DeviceIdType.MESH
        )
        return 0
    lax.fori_loop(1, groups, greet, 0)
    pl.semaphore_signal(barrier, inc=1, device_id=(sibling, me), device_id_type=pl.DeviceIdType.MESH)
    pl.semaphore_wait(barrier, groups)

    def x_copy(peer, slot):
        return pltpu.make_async_remote_copy(
            src_ref=xs.at[peer], dst_ref=xr.at[slot], send_sem=xsend.at[peer], recv_sem=xrecv.at[slot],
            device_id=there(peer), device_id_type=pl.DeviceIdType.MESH)

    def g_copy(peer, slot):
        return pltpu.make_async_remote_copy(
            src_ref=gs.at[peer], dst_ref=gr.at[slot], send_sem=gsend.at[peer], recv_sem=grecv.at[slot],
            device_id=there(peer), device_id_type=pl.DeviceIdType.MESH)

    def i_copy(peer, slot):
        return pltpu.make_async_remote_copy(
            src_ref=igs.at[peer], dst_ref=home.at[slot], send_sem=isend.at[peer], recv_sem=irecv.at[slot],
            device_id=there(peer), device_id_type=pl.DeviceIdType.MESH)

    def q_copy(peer, slot):
        return pltpu.make_async_remote_copy(
            src_ref=ggs.at[peer], dst_ref=home_gate.at[slot], send_sem=qsend.at[peer], recv_sem=qrecv.at[slot],
            device_id=there(peer), device_id_type=pl.DeviceIdType.MESH)

    def send(i, _):
        odd = (i - 1) % 2
        s = (1 - odd) * (groups - 1 - (i - 1) // 2) + odd * (i // 2)
        peer = flip_bits(me, s, groups)
        x_copy(peer, me).start()
        g_copy(peer, me).start()
        return 0
    lax.fori_loop(1, groups, send, 0)
    own_x = pltpu.make_async_copy(xs.at[me], xr.at[me], own_sem.at[0])
    own_g = pltpu.make_async_copy(gs.at[me], gr.at[me], own_sem.at[1])
    own_x.start()
    own_g.start()
    load_in.wait()
    load_out.wait()
    load_g.wait()

    spot = (
        lax.broadcasted_iota(jnp.int32, (rows, lanes), 0)
        == lax.broadcasted_iota(jnp.int32, (rows, lanes), 1)
    )

    def work(base):
        both = pl.ds(base, 2)
        x = xr[both].reshape(2 * rows, width)
        place = pl.ds(pl.multiple_of(base * rows, rows), 2 * rows)
        gg = gated[place, :]
        gate = jnp.concatenate(
            [jnp.sum(jnp.where(spot, gr[base + u, 0:1, :], 0.0), 1, keepdims=True) for u in range(2)], 0
        )
        gated[place, :] = (gate * gg.astype(f32)).astype(bf16)
        total = jnp.zeros((2 * rows, width), f32)
        gate_grad = jnp.zeros((2 * rows, 1), f32)

        def columns(t):
            return slice(t * tile, (t + 1) * tile)

        def products(t):
            return matmul(x, win[:, columns(t)]), matmul_nt(gg, wout[columns(t), :])

        ahead = products(0)
        for t in range(tiles):
            pre, out_grad = ahead
            if t + 1 < tiles:
                ahead = products(t + 1)
            value, slope = gelu_parts(pre)
            act[place, columns(t)] = value.astype(bf16)
            gate_grad = gate_grad + jnp.sum(value * out_grad, 1, keepdims=True)
            low = (gate * out_grad * slope).astype(bf16)
            pg[place, columns(t)] = low
            total = total + matmul_nt(low, win[:, columns(t)])
        igs[both] = total.astype(bf16).reshape(2, rows, width)
        for u in range(2):
            row = jnp.sum(jnp.where(spot, gate_grad[u * rows : (u + 1) * rows], 0.0), 0, keepdims=True)
            ggs[base + u] = jnp.broadcast_to(row, ggs.shape[1:])

    def arrive(peer):
        x_copy(peer, peer).wait_recv()
        g_copy(peer, peer).wait_recv()

    def back(peer):
        i_copy(peer, me).start()
        q_copy(peer, me).start()

    own_x.wait()
    own_g.wait()
    arrive(flip_bits(me, 1, groups))
    work(me - me % 2)
    own_i = pltpu.make_async_copy(igs.at[me], home.at[me], own_sem.at[0])
    own_q = pltpu.make_async_copy(ggs.at[me], home_gate.at[me], own_sem.at[1])
    own_i.start()
    own_q.start()
    back(flip_bits(me, 1, groups))

    def chunk(j, _):
        peer = flip_bits(me, 2 * j, groups)
        other = flip_bits(me, 2 * j + 1, groups)
        arrive(peer)
        arrive(other)
        work(peer - peer % 2)
        back(peer)
        back(other)
        return 0
    lax.fori_loop(1, groups // 2, chunk, 0)

    def d_copy(k):
        return pltpu.make_async_remote_copy(
            src_ref=dws.at[k % 2], dst_ref=dwr.at[k], send_sem=dsend.at[k], recv_sem=drecv.at[k],
            device_id=(sibling, me), device_id_type=pl.DeviceIdType.MESH)

    part = hidden // dp_size
    flat = groups * rows
    items = [(which, half) for half in (1 - half_of, half_of) for which in range(2)]

    def grad(which, quarter):
        span = pl.ds(pl.multiple_of(quarter * part, part), part)
        if which == 0:
            return matmul_tn(xr[...].reshape(flat, width), pg[:, span])
        return matmul_tn(act[:, span], gated[...])

    for k, (which, half) in enumerate(items):
        if k >= 2:
            d_copy(k - 2).wait_send()
        dws[k % 2] = grad(which, 2 * half + 1 - core).astype(bf16)
        d_copy(k).start()
    outs = [
        pltpu.make_async_copy(dwr.at[0], give.at[0], ksem.at[0]),
        pltpu.make_async_copy(dwr.at[1], give.at[1], ksem.at[1]),
        pltpu.make_async_copy(dwr.at[2], keep.at[0], ksem.at[2]),
        pltpu.make_async_copy(dwr.at[3], keep.at[1], ksem.at[3]),
    ]
    for k, (which, half) in enumerate(items):
        local = grad(which, 2 * half + core)
        d_copy(k).wait_recv()
        dwr[k] = (local + dwr[k].astype(f32)).astype(bf16)
        outs[k].start()

    span = stage.shape[1]
    copies = []
    for b in range(flat // span):
        if b >= 2:
            copies[b - 2].wait()
        stage[b % 2] = matmul(act[b * span : (b + 1) * span, :], wout[...]).astype(bf16)
        copy = pltpu.make_async_copy(stage.at[b % 2], produced.at[pl.ds(b * span, span)], psem.at[b % 2])
        copy.start()
        copies.append(copy)
    for copy in copies[-2:] + outs:
        copy.wait()
    own_i.wait()
    own_q.wait()
    for k in (2, 3):
        d_copy(k).wait_send()

    def finish(s, _):
        peer = flip_bits(me, s, groups)
        x_copy(peer, me).wait_send()
        g_copy(peer, me).wait_send()
        i_copy(peer, me).wait_send()
        q_copy(peer, me).wait_send()
        i_copy(peer, peer).wait_recv()
        q_copy(peer, peer).wait_recv()
        return 0
    lax.fori_loop(1, groups, finish, 0)


def ffn(xs, gs, g, weight_in, weight_out, groups, dp_size, tiles=6):
    f32, bf16 = jnp.float32, jnp.bfloat16
    _, rows, width = xs.shape
    hidden = weight_in.shape[1]
    lanes = gs.shape[2]
    part = hidden // dp_size
    anywhere = pl.BlockSpec(memory_space=pl.ANY)
    sem = pltpu.SemaphoreType.DMA
    flat = groups * rows
    shape = jax.ShapeDtypeStruct
    return pl.pallas_call(
        functools.partial(ffn_kernel, groups=groups, dp_size=dp_size, tiles=tiles),
        out_shape=(
            shape((groups, rows, width), bf16),
            shape((groups, 8, lanes), f32),
            shape((flat, width), bf16),
            shape((2, width, part), bf16),
            shape((2, width, part), bf16),
        ),
        in_specs=[anywhere] * 5,
        out_specs=(anywhere,) * 5,
        scratch_shapes=[
            pltpu.VMEM((width, hidden), bf16),
            pltpu.VMEM((hidden, width), bf16),
            pltpu.VMEM((groups, rows, width), bf16),
            pltpu.VMEM((groups, 8, lanes), f32),
            pltpu.VMEM((flat, hidden), bf16),
            pltpu.VMEM((flat, hidden), bf16),
            pltpu.VMEM((flat, width), bf16),
            pltpu.VMEM((groups, rows, width), bf16),
            pltpu.VMEM((groups, 8, lanes), f32),
            pltpu.VMEM((2, width, part), bf16),
            pltpu.VMEM((4, width, part), bf16),
            pltpu.VMEM((2, flat // 8, width), bf16),
            sem((3,)), sem((2,)), sem((2,)), sem((4,)),
            sem((groups,)), sem((groups,)), sem((groups,)), sem((groups,)),
            sem((groups,)), sem((groups,)), sem((groups,)), sem((groups,)),
            sem((4,)), sem((4,)),
        ],
        compiler_params=pltpu.CompilerParams(
            collective_id=1, has_side_effects=True, vmem_limit_bytes=62 << 20
        ),
        cost_estimate=pl.CostEstimate(
            flops=12 * flat * width * hidden, bytes_accessed=40 << 20, transcendentals=flat * hidden
        ),
    )(xs, gs, g, weight_in, weight_out)


def fold_steps(rows, cols, bits):
    steps = []
    for bit in bits[:3]:
        rows = rows // 2
        steps.append(((bit,), "half", rows, cols))
    rows, cols = rows // 2, cols // 2
    steps.append((tuple(bits[3:5]), "quad", rows, cols))
    for bit in bits[5:]:
        steps.append(((bit,), "whole", rows, cols))
    return steps


NORM = 3


def reduce_kernel(
    attended_hbm, middle_grad_hbm, tokens_hbm, dv_hbm, dk_hbm, dq_hbm, wq_hbm, wk_hbm, wv_hbm,
    gain, small_in,
    sum_o, sum_v, sum_k, sum_q, token_grad_hbm, small_out,
    attended, middle_grad, tokens, dv, dk, dq, wq, wk, wv,
    token_grad, sums, normed, branch, acc, outbox, inbox, small_box, small_sent, load_sem, store_sem,
    ssend, srecv, tsend, trecv,
    *, dp_bits, expert_bits,
):
    f32, bf16 = jnp.float32, jnp.bfloat16
    dp = lax.axis_index("dp")
    ex = lax.axis_index("expert")
    MESH = pl.DeviceIdType.MESH
    length, width = tokens.shape
    held = (attended, middle_grad, tokens, dv, dk, dq, wq, wk, wv)
    loads = [
        pltpu.make_async_copy(there, here, load_sem.at[i])
        for i, (there, here) in enumerate(zip(
            (attended_hbm, middle_grad_hbm, tokens_hbm, dv_hbm, dk_hbm, dq_hbm, wq_hbm, wk_hbm, wv_hbm), held))
    ]
    first = 4
    for load in loads[:first]:
        load.start()

    def own_bit(bit):
        axis, place = bit
        return (dp // 2 ** place) % 2 if axis == "dp" else (ex // 2 ** place) % 2

    def partner(bits):
        there = [dp, ex]
        for bit in bits:
            there[bit[0] == "expert"] = there[bit[0] == "expert"] + (1 - 2 * own_bit(bit)) * 2 ** bit[1]
        return tuple(there)

    dpb = [("dp", i) for i in range(dp_bits)]
    exb = [("expert", i) for i in range(expert_bits)]
    orders = [
        [dpb[0], dpb[1], exb[0]] + dpb[2:] + exb[1:],
        [dpb[0], exb[0], dpb[1]] + dpb[2:] + exb[1:],
    ]
    every = dpb + exb
    small_count = len(every)

    barrier = pltpu.get_barrier_semaphore()
    greeted = [(bit,) for bit in every] + [tuple(orders[0][3:5])]
    for bits in greeted:
        pl.semaphore_signal(barrier, inc=1, device_id=partner(bits), device_id_type=MESH)
    pl.semaphore_wait(barrier, len(greeted))

    def prepare(i, _):
        span = pl.ds(pl.multiple_of(i * 256, 256), 256)
        x = tokens[span, :].astype(f32)
        inv = lax.rsqrt(jnp.mean(x * x, 1, keepdims=True) + epsilon)
        normed[span, :] = (x * inv * gain[...]).astype(bf16)
        branch[span, :] = middle_grad[span, :].astype(bf16)
        return 0
    for load in loads[:3]:
        load.wait()
    for load in loads[first:]:
        load.start()
    lax.fori_loop(0, length // 256, prepare, 0)

    lefts = (attended, normed, normed, normed)
    rights = (branch, dv, dk, dq)
    streams = []
    for s in range(4):
        row, col, at, sem_at = 0, 0, 0, 0
        plan = []
        for bits, kind, r, c in fold_steps(width, width, orders[s % 2]):
            mine = [own_bit(bit) for bit in bits]
            if kind == "half":
                peers = [bits]
                keep_at = (row + mine[0] * r, col)
                theirs = [(row + (1 - mine[0]) * r, col)]
            elif kind == "quad":
                peers = [bits[:1], bits[1:], bits]
                keep_at = (row + mine[0] * r, col + mine[1] * c)
                theirs = [
                    (row + (1 - mine[0]) * r, col + mine[1] * c),
                    (row + mine[0] * r, col + (1 - mine[1]) * c),
                    (row + (1 - mine[0]) * r, col + (1 - mine[1]) * c),
                ]
            else:
                peers, keep_at, theirs = [bits], (row, col), [(row, col)]
            plan.append((peers, kind, r, c, at, keep_at, theirs, sem_at))
            row, col = keep_at
            at += r * len(peers)
            sem_at += len(peers)
        streams.append(plan)
    count = len(streams[0])
    sems = ssend.shape[1] // 2

    def rs_copy(s, k, i):
        peers, kind, r, c, at, _, _, sem_at = streams[s][k]
        box = pl.ds(at + i * r, r)
        return pltpu.make_async_remote_copy(
            src_ref=outbox.at[s, box, pl.ds(0, c)], dst_ref=inbox.at[s, box, pl.ds(0, c)],
            send_sem=ssend.at[s, sem_at + i], recv_sem=srecv.at[s, sem_at + i],
            device_id=partner(peers[i]), device_id_type=MESH)

    def aligned(at):
        row, col = at
        row = pl.multiple_of(row, 16) if not isinstance(row, int) else row
        col = pl.multiple_of(col, 128) if not isinstance(col, int) else col
        return row, col

    def block(s, at, r, c):
        row, col = aligned(at)
        return sums.at[s, pl.ds(row, r), pl.ds(col, c)]

    def ag_copy(s, k, i, incoming):
        peers, kind, r, c, _, keep_at, theirs, sem_at = streams[s][k]
        ref = block(s, theirs[i] if incoming else keep_at, r, c)
        return pltpu.make_async_remote_copy(
            src_ref=ref, dst_ref=ref,
            send_sem=ssend.at[s, sems + sem_at + i], recv_sem=srecv.at[s, sems + sem_at + i],
            device_id=partner(peers[i]), device_id_type=MESH)

    half = width // 2
    core = own_bit(dpb[0])

    def grad(s, which):
        span = pl.ds(pl.multiple_of(which * half, half), half)
        return matmul_tn(lefts[s][:, span], rights[s][...])

    def local(s, at, r, c):
        row, col = aligned((at[0] - streams[s][0][5][0], at[1]))
        return acc.at[s, pl.ds(row, r), pl.ds(col, c)]

    def phase(s, k):
        plan = streams[s]
        if k == 0:
            if s > 0:
                loads[2 + s].wait()
            outbox[s, 0:half, :] = grad(s, 1 - core).astype(bf16)
            rs_copy(s, 0, 0).start()
            return
        if k <= count:
            peers, kind, r, c, at, keep_at, _, _ = plan[k - 1]
            view = local(s, keep_at, r, c)
            total = outbox[s, at : at + r, 0:c].astype(f32) if kind == "whole" else view[...]
            for i in range(len(peers)):
                rs_copy(s, k - 1, i).wait_recv()
                total = total + inbox[s, at + i * r : at + (i + 1) * r, 0:c].astype(f32)
            if k < count:
                view[...] = total
                peers, kind, r, c, at, _, theirs, _ = plan[k]
                for i in range(len(peers)):
                    outbox[s, at + i * r : at + (i + 1) * r, 0:c] = local(s, theirs[i], r, c)[...].astype(bf16)
                    rs_copy(s, k, i).start()
                return
            block(s, keep_at, r, c)[...] = total.astype(bf16)
        g = 2 * count - 1 - k
        if k > count and plan[g + 1][1] != "whole":
            for i in range(len(plan[g + 1][0])):
                ag_copy(s, g + 1, i, True).wait_recv()
        if g >= 0 and plan[g][1] != "whole":
            for i in range(len(plan[g][0])):
                ag_copy(s, g, i, False).start()

    gain_row = gain[...]
    rows = 256

    def norm_block(i, gain_grad):
        span = pl.ds(pl.multiple_of(i * rows, rows), rows)
        grads = (
            matmul_nt(dq[span, :], wq[...]) + matmul_nt(dk[span, :], wk[...]) + matmul_nt(dv[span, :], wv[...])
        )
        x = tokens[span, :].astype(f32)
        inv = lax.rsqrt(jnp.mean(x * x, 1, keepdims=True) + epsilon)
        scaled = grads * gain_row
        mean = jnp.sum(scaled * x, 1, keepdims=True) * (1.0 / width)
        part = inv * (scaled - x * (inv * inv * mean))
        token_grad[span, :] = (middle_grad[span, :] + part).astype(bf16)
        return gain_grad + jnp.sum(grads * (x * inv), 0, keepdims=True)

    def small_copy(k):
        return pltpu.make_async_remote_copy(
            src_ref=small_sent.at[k], dst_ref=small_box.at[k],
            send_sem=tsend.at[k], recv_sem=trecv.at[k],
            device_id=partner((every[k],)), device_id_type=MESH)

    def small_phase(k):
        if k == 0:
            gain_grad = lax.fori_loop(0, length // rows, norm_block, jnp.zeros((1, width), f32))
            small_out[...] = small_in[...]
            for i in range(width // LANES):
                small_out[i : i + 1, :] = gain_grad[:, i * LANES : (i + 1) * LANES]
        else:
            small_copy(k - 1).wait_recv()
            small_out[...] = small_out[...] + small_box[k - 1]
        if k < small_count:
            small_sent[k] = small_out[...]
            small_copy(k).start()

    last = 2 * count
    starts = (0, 0, 2, 2)
    stores = [
        pltpu.make_async_copy(sums.at[s], out, store_sem.at[s]) for s, out in enumerate((sum_o, sum_v, sum_k, sum_q))
    ]
    stores.append(pltpu.make_async_copy(token_grad, token_grad_hbm, store_sem.at[4]))
    for t in range(max(last + starts[-1], small_count + NORM) + 1):
        for s in range(4):
            if 0 <= t - starts[s] <= last:
                phase(s, t - starts[s])
                if t - starts[s] == last:
                    stores[s].start()
        for s in range(4):
            if t == starts[s]:
                acc[s] = grad(s, core)
        if t == NORM:
            for load in loads[6:9]:
                load.wait()
        if 0 <= t - NORM <= small_count:
            small_phase(t - NORM)
            if t == NORM:
                stores[4].start()
    for store in stores:
        store.wait()
    for s in range(4):
        for k in range(count):
            for i in range(len(streams[s][k][0])):
                rs_copy(s, k, i).wait_send()
                if streams[s][k][1] != "whole":
                    ag_copy(s, k, i, False).wait_send()
    for k in range(small_count):
        small_copy(k).wait_send()


def reduce_grads(tokens, attended, middle_grad, dq, dk, dv, wq, wk, wv, gain, small, dp_size, groups):
    f32, bf16 = jnp.float32, jnp.bfloat16
    length, width = tokens.shape
    dp_bits, expert_bits = dp_size.bit_length() - 1, groups.bit_length() - 1
    count = dp_bits + expert_bits
    steps = fold_steps(width, width, list(range(count)))
    box = sum(step[2] * (3 if step[1] == "quad" else 1) for step in steps)
    messages = sum(3 if step[1] == "quad" else 1 for step in steps)
    vmem = pl.BlockSpec(memory_space=pltpu.VMEM)
    anywhere = pl.BlockSpec(memory_space=pl.ANY)
    sem = pltpu.SemaphoreType.DMA
    shape = jax.ShapeDtypeStruct
    act, square = shape((length, width), bf16), shape((width, width), bf16)
    big = (attended, middle_grad, tokens, dv, dk, dq, wq, wk, wv)
    return pl.pallas_call(
        functools.partial(reduce_kernel, dp_bits=dp_bits, expert_bits=expert_bits),
        out_shape=(square, square, square, square, act, shape(small.shape, f32)),
        in_specs=[anywhere] * len(big) + [vmem] * 2,
        out_specs=(anywhere,) * 5 + (vmem,),
        scratch_shapes=[pltpu.VMEM(x.shape, x.dtype) for x in big] + [
            pltpu.VMEM((length, width), bf16),
            pltpu.VMEM((4, width, width), bf16),
            pltpu.VMEM((length, width), bf16),
            pltpu.VMEM((length, width), bf16),
            pltpu.VMEM((4, width // 2, width), f32),
            pltpu.VMEM((4, box, width), bf16),
            pltpu.VMEM((4, box, width), bf16),
            pltpu.VMEM((count,) + small.shape, f32),
            pltpu.VMEM((count,) + small.shape, f32),
            sem((len(big),)), sem((5,)),
            sem((4, 2 * messages)), sem((4, 2 * messages)), sem((count,)), sem((count,)),
        ],
        compiler_params=pltpu.CompilerParams(
            collective_id=2, has_side_effects=True, vmem_limit_bytes=62 << 20
        ),
        cost_estimate=pl.CostEstimate(
            flops=14 * length * width * width, bytes_accessed=30 << 20, transcendentals=0
        ),
    )(*big, gain, small)


def key_ranges(segment_row):
    first, last = segment_row[::BLOCK], segment_row[BLOCK - 1 :: BLOCK]
    lo = jnp.sum(segment_row[None, :] < first[:, None], 1) // BLOCK
    hi = (jnp.sum(segment_row[None, :] <= last[:, None], 1) + BLOCK - 1) // BLOCK
    return lo.astype(jnp.int32), hi.astype(jnp.int32)


def per_device(
    tokens,
    segments,
    routes,
    cotangent,
    attn_gain,
    ffn_gain,
    query_weight,
    key_weight,
    value_weight,
    output_weight,
    position_bias_grid,
    router_weight,
    expert_in,
    expert_out,
):
    f32, bf16 = jnp.float32, jnp.bfloat16
    token_count, model_width = tokens.shape
    head_count = position_bias_grid.shape[1]
    score_scale = (model_width // head_count) ** (-0.5)
    experts_all = router_weight.shape[1]
    capacity = (5 * token_count + 4 * experts_all - 1) // (4 * experts_all)
    slot_rows = (capacity + 15) // 16 * 16
    slots = experts_all * slot_rows
    groups = lax.axis_size("expert")
    dp_size = lax.axis_size("dp")

    def exchange(rows):
        return lax.all_to_all(rows, "expert", split_axis=0, concat_axis=0, tiled=True)

    routes_row = routes.reshape(1, token_count)
    token_slot, grad_slots = first_slots(routes_row, cotangent, experts_all, capacity, slot_rows)
    grad_arrived = exchange(grad_slots)
    lo, hi = key_ranges(segments[0])
    router_pad = max(experts_all, 16)
    router_t = jnp.pad(router_weight.T, ((0, router_pad - experts_all), (0, 0)))
    gain_one, gain_two = attn_gain[None, :], ffn_gain[None, :]
    queries, key_rows, keys_t, value_rows, attended, log_sums, middle, router_probs, sent, gate_slots = front(
        lo, hi, tokens, segments, token_slot, routes_row, gain_one, gain_two,
        query_weight, key_weight, value_weight, output_weight, position_bias_grid, router_t,
        experts_all, slot_rows, score_scale,
    )
    home_grad, home_gate, produced, keep, give = ffn(
        sent, gate_slots, grad_arrived.reshape(slots, model_width), expert_in[0], expert_out[0], groups, dp_size,
    )
    passed = lax.ppermute(give, "dp", [(i, (i + dp_size // 2) % dp_size) for i in range(dp_size)])
    returned = exchange(produced.reshape(experts_all, slot_rows, model_width)).reshape(slots, model_width)
    query_grad, key_grad, value_grad, middle_grad, small = back(
        lo, hi, home_grad, home_gate, token_slot, routes_row, router_probs, middle, cotangent, segments, gain_two,
        output_weight, router_t, position_bias_grid, queries, key_rows, keys_t, value_rows, log_sums, attended,
        experts_all, slot_rows, score_scale,
    )
    sum_o, sum_v, sum_k, sum_q, token_grad, small = reduce_grads(
        tokens, attended, middle_grad, query_grad, key_grad, value_grad,
        query_weight, key_weight, value_weight, gain_one, small, dp_size, groups,
    )
    (mixed, token_grad, attn_gain_grad, ffn_gain_grad, grad_q, grad_k, grad_v, grad_o, table_grad, router_grad,
     grad_in, grad_out) = finish(
        (sum_q, sum_k, sum_v, sum_o), keep, passed, returned, middle, token_grad, small,
        token_slot, routes_row, router_probs, position_bias_grid.shape, experts_all
    )
    return (
        mixed,
        token_grad,
        attn_gain_grad,
        ffn_gain_grad,
        grad_q,
        grad_k,
        grad_v,
        grad_o,
        table_grad.T,
        router_grad.T,
        grad_in[None],
        grad_out[None],
    )


def solution(mesh):
    rows = P(("dp", "expert"), None)
    return jax.shard_map(
        per_device,
        mesh=mesh,
        in_specs=(rows,) * 4 + (P(),) * 8 + (P("expert", None, None),) * 2,
        out_specs=(rows,) * 2 + (P(),) * 8 + (P("expert", None, "dp"), P("expert", "dp", None)),
        check_vma=False,
    )
```
